32 devices in a mesh: dp: 8 (over z, y), fsdp: 4 (over x, core).
Axes of the slice: x: 2, y: 2, z: 4, core: 2. Of those that a mesh axis runs over, the one named last changes fastest.
Arguments:
- inputs: bfloat16 [32768, 512], P(('dp', 'fsdp')), may hold values from -6 to 6
- memory: bfloat16 [65536, 512], P(('dp', 'fsdp')), may hold values from -6 to 6
- seg_lengths: int32 [32, 16], P(('dp', 'fsdp')), may hold values from 1 to 256, 1024 in all within a row
- mem_lengths: int32 [32, 17], P(('dp', 'fsdp')), may hold values from 1 to 256, 2048 in all within a row
- self_query: bfloat16 [262144], P(('dp', 'fsdp')), may hold values from -0.25 to 0.25
- self_key: bfloat16 [262144], P(('dp', 'fsdp')), may hold values from -0.25 to 0.25
- self_value: bfloat16 [262144], P(('dp', 'fsdp')), may hold values from -0.25 to 0.25
- self_out: bfloat16 [262144], P(('dp', 'fsdp')), may hold values from -1 to 1
- cross_query: bfloat16 [262144], P(('dp', 'fsdp')), may hold values from -0.25 to 0.25
- cross_key: bfloat16 [262144], P(('dp', 'fsdp')), may hold values from -0.25 to 0.25
- cross_value: bfloat16 [262144], P(('dp', 'fsdp')), may hold values from -0.25 to 0.25
- cross_out: bfloat16 [262144], P(('dp', 'fsdp')), may hold values from -1 to 1
- ffn_in: bfloat16 [1048576], P(('dp', 'fsdp')), may hold values from -0.25 to 0.25
- ffn_out: bfloat16 [1048576], P(('dp', 'fsdp')), may hold values from -0.125 to 0.125
- norm_params: float32 [3072], P(('dp', 'fsdp')), may hold values from -1.2 to 1.45
- cotangent: bfloat16 [32768, 512], P(('dp', 'fsdp')), may hold values from -6 to 6
Outputs:
- block_output: bfloat16 [32768, 512], P(('dp', 'fsdp'))
- grad_inputs: bfloat16 [32768, 512], P(('dp', 'fsdp'))
- grad_memory: bfloat16 [65536, 512], P(('dp', 'fsdp'))
- grad_self_query: float32 [262144], P(('dp', 'fsdp'))
- grad_self_key: float32 [262144], P(('dp', 'fsdp'))
- grad_self_value: float32 [262144], P(('dp', 'fsdp'))
- grad_self_out: float32 [262144], P(('dp', 'fsdp'))
- grad_cross_query: float32 [262144], P(('dp', 'fsdp'))
- grad_cross_key: float32 [262144], P(('dp', 'fsdp'))
- grad_cross_value: float32 [262144], P(('dp', 'fsdp'))
- grad_cross_out: float32 [262144], P(('dp', 'fsdp'))
- grad_ffn_in: float32 [1048576], P(('dp', 'fsdp'))
- grad_ffn_out: float32 [1048576], P(('dp', 'fsdp'))
- grad_norm_params: float32 [3072], P(('dp', 'fsdp'))
The draws below stay inside these ranges and needn't reach their ends.
Inputs may be any that keep to these rules, and one draw needn't show every extreme that they name: `seg_lengths`: each row sums to 1024. `mem_lengths`: each row sums to 2048; the last entry counts padding rows at the end of the stream's memory.
All inputs are finite; a program needn't handle non-finite values.
Results may differ from the reference program's by a relative error of at most 0.03.
Values may be sent and summed in bfloat16 or wider, within the bound.
No kernel may reach another device: no remote copies, remote signals or barrier semaphores. Data moves between devices by JAX's collectives and lax.ppermute only.
A program may use at most 256 MiB of HBM per device.

```python
import math
import jax
import jax.numpy as jnp
import numpy as np
from jax import lax

D = 512
HEADS = 8
HD = 64
FF = 2048
STREAM = 1024
MOST = 256
SEGS = 16
MEM = 2048
TOKENS = 32768
MEMTOK = 65536
DEVICES = 32


def draw_norm_params(key, part):
    key = jax.random.fold_in(key, 7)
    noise_draw = jnp.clip(jax.random.normal(key, (6, D), jnp.float32), -3.0, 3.0)
    row_parity = jnp.arange(6, dtype=jnp.int32)[:, None] % 2
    entries = jnp.where(row_parity == 0, 1.0 + 0.15 * noise_draw, 0.4 * noise_draw)
    return entries.reshape(6 * D).astype(jnp.float32)


def with_spikes(values, own_key, source, target, blocks, factor):
    def block_of(axis_at):
        return (jnp.arange(values.shape[axis_at]) // (values.shape[axis_at] // blocks)).reshape((-1,) + (1,) * (values.ndim - 1 - axis_at))

    near = jax.random.permutation(own_key, blocks)[block_of(target)]
    far = (block_of(target) + blocks // 2) % blocks
    return jnp.where((block_of(source) == near) | (block_of(source) == far), factor * values, values)


def block_scale(key, extent, cuts, least, top_value):
    def one(axis_at, blocks):
        heights = jax.random.uniform(jax.random.fold_in(jax.random.fold_in(key, 6), axis_at), (blocks,), jnp.float32, least / len(cuts), top_value / len(cuts))
        return jnp.repeat(jnp.exp(heights), extent[axis_at] // blocks).reshape((-1,) + (1,) * (len(extent) - axis_at - 1))

    level = one(*cuts[0])
    for cut in cuts[1:]:
        level = level * one(*cut)
    return level


def split_up(amount, total, limit, skew):
    portions = [(1 << 20) // math.isqrt(rank ** skew) + 1 for rank in range(2, amount + 1)]
    rest, given = total - limit - (amount - 1), [1] * (amount - 1)
    while rest > 0:
        candidates = [i for i in range(amount - 1) if given[i] < limit]
        whole, remaining = sum([portions[i] for i in candidates]), rest
        for i in candidates:
            more = min(limit - given[i], max(1, remaining * portions[i] // whole), rest)
            given[i] = given[i] + more
            rest = rest - more
    return np.array([limit] + given)


def uneven_parts(own_key, number_of, total, most, slope):
    if number_of == 2:
        one = jax.random.randint(own_key, (), max(1, total - most), min(most, total - 1) + 1)
        return jnp.stack([one, total - one])
    sizes = jnp.asarray(split_up(number_of, total, most, slope), jnp.int32)
    couples = (number_of - 1) // 2
    source_of, receiver = sizes[1:1 + 2 * couples:2], sizes[2:2 + 2 * couples:2]
    margin = jnp.minimum(source_of - 1, most - receiver)
    shifted = jax.random.randint(jax.random.fold_in(own_key, 1), (couples,), 0, 1 << 20) % (margin + 1)
    sizes = sizes.at[1:1 + 2 * couples:2].set(source_of - shifted).at[2:2 + 2 * couples:2].set(receiver + shifted)
    return sizes[jax.random.permutation(jax.random.fold_in(own_key, 2), number_of)]


def bell_draw(stream_key, extent, scale, reach, shards=(), kind=jnp.bfloat16):
    factor_of = block_scale(stream_key, extent, shards, -0.22, 0.18) if shards else 1.0
    array = jax.random.normal(stream_key, extent, jnp.float32) * scale * factor_of
    return jnp.minimum(jnp.maximum(array, -reach), reach).astype(kind)


def bell_draw_with(own_key, extent, width, reach, cuts, heavy, held_as=jnp.bfloat16):
    array = width * jax.random.normal(own_key, extent, jnp.float32)
    if cuts:
        array = array * block_scale(own_key, extent, cuts, -0.22, 0.18)
    return jnp.clip(with_spikes(array, jax.random.fold_in(own_key, 3), *heavy), -reach, reach).astype(held_as)


def setup_inputs(seed: int = 0) -> dict:
    key_of = jax.random.split(jax.random.key(seed), 17)
    inputs = bell_draw_with(key_of[0], (TOKENS, D), 1.0, 6.0, ((0, 32),), (0, 1, 32, 2.75))
    memory = bell_draw_with(key_of[1], (MEMTOK, D), 1.0, 6.0, ((0, 32),), (0, 1, 32, 2.75))
    seg_lengths = jax.vmap(lambda own: uneven_parts(own, SEGS, STREAM, MOST, 2))(jax.random.split(key_of[2], DEVICES)).reshape((DEVICES, SEGS)).astype(jnp.int32)
    mem_lengths = jax.vmap(lambda own: uneven_parts(own, SEGS + 1, MEM, MOST, 2))(jax.random.split(key_of[3], DEVICES)).reshape((DEVICES, SEGS + 1)).astype(jnp.int32)
    self_query = bell_draw(key_of[4], (D * D,), D ** -0.5, 0.25, ((0, 32),))
    self_key = bell_draw(key_of[5], (D * D,), D ** -0.5, 0.25, ((0, 32),))
    self_value = bell_draw(key_of[6], (D * D,), D ** -0.5, 0.25, ((0, 32),))
    self_out = bell_draw(key_of[7], (D * D,), (D // 16) ** -0.5, 1.0, ((0, 32),))
    cross_query = bell_draw(key_of[8], (D * D,), D ** -0.5, 0.25, ((0, 32),))
    cross_key = bell_draw(key_of[9], (D * D,), D ** -0.5, 0.25, ((0, 32),))
    cross_value = bell_draw(key_of[10], (D * D,), D ** -0.5, 0.25, ((0, 32),))
    cross_out = bell_draw(key_of[11], (D * D,), (D // 16) ** -0.5, 1.0, ((0, 32),))
    ffn_in = bell_draw(key_of[12], (D * FF,), D ** -0.5, 0.25, ((0, 32),))
    ffn_out = bell_draw(key_of[13], (FF * D,), FF ** -0.5, 0.125, ((0, 32),))
    norm_params = draw_norm_params(jax.random.fold_in(key_of[16], 71), 0)
    cotangent = bell_draw(key_of[15], (TOKENS, D), 1.0, 6.0, ((0, 32),))
    return {"inputs": inputs, "memory": memory, "seg_lengths": seg_lengths, "mem_lengths": mem_lengths, "self_query": self_query, "self_key": self_key, "self_value": self_value, "self_out": self_out, "cross_query": cross_query, "cross_key": cross_key, "cross_value": cross_value, "cross_out": cross_out, "ffn_in": ffn_in, "ffn_out": ffn_out, "norm_params": norm_params, "cotangent": cotangent}


masked_score = -1e+30
norm_eps = 1e-05

@jax.custom_vjp
def low(v):
    return lax.optimization_barrier(v.astype(jnp.bfloat16)).astype(jnp.float32)

@jax.custom_vjp
def low_back(v):
    return v

def low_keep(v):
    return (low(v), None)

def low_pass(kept, grad):
    return (grad,)

def back_keep(v):
    return (v, None)

def back_low(kept, grad):
    return (low(grad),)
low.defvjp(low_keep, low_pass)
low_back.defvjp(back_keep, back_low)

def precise(left, right):
    return jnp.dot(left, right, precision=lax.Precision.HIGHEST)

def layer_norm(source, gain_row, shift_row):
    row_mean = lax.optimization_barrier(jnp.mean(source, axis=-1, keepdims=True))
    centered = source - row_mean
    variance = lax.optimization_barrier(jnp.mean(centered * centered, axis=-1, keepdims=True))
    return centered * lax.rsqrt(variance + norm_eps) * gain_row + shift_row

def gelu_tanh(source):
    return 0.5 * source * (1.0 + jnp.tanh(0.7978845608028654 * (source + 0.044715 * source * source * source)))

def segment_ids(lengths, row_count):
    ends = jnp.cumsum(lengths).astype(jnp.int32)
    places = jnp.arange(row_count, dtype=jnp.int32)
    return lax.optimization_barrier(jnp.sum((places[:, None] >= ends[None, :]).astype(jnp.int32), axis=1)).astype(jnp.int32)

def split_heads(source):
    return source.reshape(source.shape[0], HEADS, HD)

def attend(queries, keys, values, allowed):
    scores = jnp.einsum('thd,shd->hts', queries, keys, precision=lax.Precision.HIGHEST) * HD ** (-0.5)
    scores = jnp.where(allowed[None], low_back(scores), masked_score)
    row_max = lax.optimization_barrier(jnp.max(scores, axis=-1, keepdims=True))
    raised = jnp.exp(scores - row_max)
    weights = low(raised / lax.optimization_barrier(jnp.sum(raised, axis=-1, keepdims=True)))
    mixed = jnp.einsum('hts,shd->thd', weights, values, precision=lax.Precision.HIGHEST)
    return low(low_back(mixed.reshape(mixed.shape[0], D)))

def stream_layer(pieces, params):
    inputs_row, memory_row, seg_row, mem_row = pieces
    self_query, self_key, self_value, self_out, cross_query, cross_key, cross_value, cross_out, ffn_in, ffn_out, norms = params
    query_ids = segment_ids(seg_row, STREAM)
    memory_ids = segment_ids(mem_row, MEM)
    places = jnp.arange(STREAM, dtype=jnp.int32)
    self_allowed = (query_ids[:, None] == query_ids[None, :]) & (places[None, :] <= places[:, None])
    cross_allowed = query_ids[:, None] == memory_ids[None, :]
    queries = low(low_back(precise(inputs_row, self_query)))
    keys = low(low_back(precise(inputs_row, self_key)))
    values = low(low_back(precise(inputs_row, self_value)))
    self_mixed = attend(split_heads(queries), split_heads(keys), split_heads(values), self_allowed)
    residual_one = inputs_row + low_back(precise(self_mixed, self_out))
    first_norm = layer_norm(residual_one, norms[0], norms[1])
    first_low = low(first_norm)
    cross_queries = low(low_back(precise(first_low, cross_query)))
    cross_keys = low(low_back(precise(memory_row, cross_key)))
    cross_values = low(low_back(precise(memory_row, cross_value)))
    cross_mixed = attend(split_heads(cross_queries), split_heads(cross_keys), split_heads(cross_values), cross_allowed)
    residual_two = first_norm + low_back(precise(cross_mixed, cross_out))
    second_norm = layer_norm(residual_two, norms[2], norms[3])
    second_low = low(second_norm)
    hidden_pre = low_back(precise(second_low, ffn_in))
    active = low(gelu_tanh(hidden_pre))
    residual_three = second_norm + low_back(precise(active, ffn_out)) + inputs_row
    return layer_norm(residual_three, norms[4], norms[5])

def as_matrix(flat, rows):
    return flat.astype(jnp.float32).reshape(rows, -1)

def reference(inputs, memory, seg_lengths, mem_lengths, self_query, self_key, self_value, self_out, cross_query, cross_key, cross_value, cross_out, ffn_in, ffn_out, norm_params, cotangent):
    stream_count = TOKENS // STREAM
    params = (as_matrix(self_query, D), as_matrix(self_key, D), as_matrix(self_value, D), as_matrix(self_out, D), as_matrix(cross_query, D), as_matrix(cross_key, D), as_matrix(cross_value, D), as_matrix(cross_out, D), as_matrix(ffn_in, D), as_matrix(ffn_out, FF), as_matrix(norm_params, 6))
    inputs_all = inputs.astype(jnp.float32).reshape(stream_count, STREAM, D)
    memory_all = memory.astype(jnp.float32).reshape(stream_count, MEM, D)

    def forward(inputs_given, memory_given, weights_given):

        def one_stream(pieces):
            return stream_layer(pieces, weights_given)
        return lax.map(jax.checkpoint(one_stream), (inputs_given, memory_given, seg_lengths, mem_lengths))
    outputs, pullback = jax.vjp(forward, inputs_all, memory_all, params)
    grad_in, grad_mem, grad_params = pullback(cotangent.astype(jnp.float32).reshape(stream_count, STREAM, D))
    return (outputs.reshape(TOKENS, D).astype(jnp.bfloat16), grad_in.reshape(TOKENS, D).astype(jnp.bfloat16), grad_mem.reshape(MEMTOK, D).astype(jnp.bfloat16), grad_params[0].reshape(-1), grad_params[1].reshape(-1), grad_params[2].reshape(-1), grad_params[3].reshape(-1), grad_params[4].reshape(-1), grad_params[5].reshape(-1), grad_params[6].reshape(-1), grad_params[7].reshape(-1), grad_params[8].reshape(-1), grad_params[9].reshape(-1), grad_params[10].reshape(-1))
```

```python
import functools
import jax
import jax.numpy as jnp
from jax import lax
from jax.experimental import pallas as pl
from jax.experimental.pallas import tpu as pltpu
from jax.sharding import PartitionSpec as P

HD = 64
LANES = 128
MOST = 256
masked_score = -1e30
norm_eps = 1e-05
bf16, f32 = jnp.bfloat16, jnp.float32
NT = (((1,), (1,)), ((), ()))
TN = (((0,), (0,)), ((), ()))
NN = (((1,), (0,)), ((), ()))


def mm(left, right, dims=NN):
    return lax.dot_general(left, right, dims, preferred_element_type=f32)


def norm_rows(source):
    mean = jnp.mean(source, axis=-1, keepdims=True)
    centered = source - mean
    variance = jnp.mean(centered * centered, axis=-1, keepdims=True)
    rstd = lax.rsqrt(variance + norm_eps)
    return centered * rstd, rstd


def lane_below(rows):
    return lax.broadcasted_iota(jnp.int32, (rows, LANES), 1) < HD


def head_part(pair, which, low):
    return jnp.where(low == (which == 0), pair, jnp.zeros_like(pair))


def values_with_ones(values, low):
    parts = []
    for p in range(values.shape[1] // LANES):
        pair = values[:, p * LANES : (p + 1) * LANES]
        one = jnp.ones_like(pair)
        parts.append(jnp.where(low, pair, one))
        parts.append(jnp.where(low, pltpu.roll(pair, HD, 1), one))
    return jnp.concatenate(parts, axis=1)


def self_forward_kernel(
    block, x_ref, wq_ref, wk_ref, wv_ref, wo_ref, wcq_ref, norms_ref, idc_ref, idr_ref,
    q_ref, k_ref, v_ref, o_ref, l_ref, r1_ref, h1b_ref, q2_ref, k_all, vx_all,
):
    step = pl.program_id(0)
    rows, width = x_ref.shape
    total = k_all.shape[0]
    window = MOST + block
    pairs = width // LANES
    x = x_ref[...]
    q = mm(x, wq_ref[...]).astype(bf16)
    k = mm(x, wk_ref[...]).astype(bf16)
    v = mm(x, wv_ref[...]).astype(bf16)
    q_ref[...] = q
    k_ref[...] = k
    v_ref[...] = v
    low_rows = lane_below(rows)

    @pl.when(step == 0)
    def _():
        k_all[...] = jnp.zeros_like(k_all)
        vx_all[...] = jnp.zeros_like(vx_all)

    base = pl.multiple_of(step * rows, rows)
    k_all[pl.ds(base, rows), :] = k
    vx_all[pl.ds(base, rows), :] = values_with_ones(v, low_rows)
    scaled = q * jnp.asarray(HD ** -0.5, bf16)
    low = lane_below(block)
    lane = lax.broadcasted_iota(jnp.int32, (block, LANES), 1)
    for sub in range(rows // block):
        start = pl.multiple_of(jnp.maximum(base + sub * block - MOST, 0), LANES)
        ids_q = idc_ref[sub * block : (sub + 1) * block, :]
        ids_k = idr_ref[:, pl.ds(start, window)]
        pos_q = base + sub * block + lax.broadcasted_iota(jnp.int32, (block, window), 0)
        pos_k = start + lax.broadcasted_iota(jnp.int32, (block, window), 1)
        bias = jnp.where((ids_q == ids_k) & (pos_k <= pos_q), 0.0, masked_score).astype(f32)
        totals = jnp.zeros((block, LANES), f32)
        for p in range(pairs):
            cols = slice(p * LANES, (p + 1) * LANES)
            qp = scaled[sub * block : (sub + 1) * block, cols]
            kp = k_all[pl.ds(start, window), cols]
            mixed = []
            for h in range(2):
                s = mm(head_part(qp, h, low), kp, NT) + bias
                m = jnp.max(s, axis=1, keepdims=True)
                e = jnp.exp(s - m).astype(bf16)
                head = 2 * p + h
                o = mm(e, vx_all[pl.ds(start, window), head * LANES : (head + 1) * LANES])
                l = pltpu.roll(o, HD, 1)
                mixed.append(o / l)
                totals = jnp.where(lane == head, m + jnp.log(jnp.where(low, l, 1.0)[:, :1]), totals)
            o_ref[sub * block : (sub + 1) * block, cols] = jnp.where(
                low, mixed[0], pltpu.roll(mixed[1], HD, 1)
            ).astype(bf16)
        l_ref[:, sub * block : (sub + 1) * block] = totals.T[: 2 * pairs, :]
    r1 = x.astype(f32) + mm(o_ref[...], wo_ref[...])
    r1_ref[...] = r1
    n, _ = norm_rows(r1)
    h1b = (n * norms_ref[0:1, :] + norms_ref[1:2, :]).astype(bf16)
    h1b_ref[...] = h1b
    q2_ref[...] = mm(h1b, wcq_ref[...]).astype(bf16)


def whole(a):
    return pl.BlockSpec(a.shape, lambda *_: (0,) * a.ndim)


def self_forward(x, wq, wk, wv, wo, wcq, norms, idc, idr, rows=256, block=128, vmem=48 * 2**20):
    total, width = x.shape
    heads = width // HD
    steps = total // rows
    rowspec = lambda w: pl.BlockSpec((rows, w), lambda i: (i, 0))
    full = jax.ShapeDtypeStruct((total, width), bf16)
    return pl.pallas_call(
        functools.partial(self_forward_kernel, block),
        grid=(steps,),
        in_specs=[rowspec(width)] + [whole(a) for a in (wq, wk, wv, wo, wcq, norms)] + [rowspec(1), whole(idr)],
        out_specs=[rowspec(width)] * 4 + [pl.BlockSpec((heads, rows), lambda i: (0, i))] + [rowspec(width)] * 3,
        out_shape=[full] * 4
        + [jax.ShapeDtypeStruct((heads, total), f32), jax.ShapeDtypeStruct((total, width), f32), full, full],
        scratch_shapes=[pltpu.VMEM((total, width), bf16), pltpu.VMEM((total, 2 * width), bf16)],
        compiler_params=pltpu.CompilerParams(vmem_limit_bytes=vmem),
        name="self_forward",
    )(x, wq, wk, wv, wo, wcq, norms, idc, idr)


def cross_forward_kernel(
    tile, ranges_ref, q2_ref, k2_ref, v2_ref, r1_ref, wco_ref, norms_ref, idc_ref, idr_ref,
    o_ref, l_ref, r2_ref, vx_all, s_all, acc,
):
    step = pl.program_id(0)
    rows, width = q2_ref.shape
    keys = k2_ref.shape[0]
    pairs = width // LANES

    @pl.when(step == 0)
    def _():
        def fill(j, _):
            at = pl.ds(pl.multiple_of(j * tile, tile), tile)
            vx_all[at, :] = values_with_ones(v2_ref[at, :], lane_below(tile))
            return 0

        lax.fori_loop(0, keys // tile, fill, 0)

    low = lane_below(rows)
    lane = lax.broadcasted_iota(jnp.int32, (rows, LANES), 1)
    scaled = q2_ref[...] * jnp.asarray(HD ** -0.5, bf16)
    ids_q = idc_ref[...]
    first, count = ranges_ref[0, step], ranges_ref[1, step]

    def place(j):
        wanted = (first + j * (tile // LANES)) * LANES
        return wanted, pl.multiple_of(jnp.minimum(wanted, keys - tile), LANES)

    def scores(j, tops):
        wanted, start = place(j)
        pos = start + lax.broadcasted_iota(jnp.int32, (1, tile), 1)
        ids_k = jnp.where(pos >= wanted, idr_ref[:, pl.ds(start, tile)], -1)
        bias = jnp.where(ids_q == ids_k, 0.0, masked_score).astype(f32)
        new = []
        for p in range(pairs):
            cols = slice(p * LANES, (p + 1) * LANES)
            kp = k2_ref[pl.ds(start, tile), cols]
            for h in range(2):
                s = mm(head_part(scaled[:, cols], h, low), kp, NT) + bias
                s_all[2 * p + h, j] = s
                top = s[:, :LANES]
                for c in range(1, tile // LANES):
                    top = jnp.maximum(top, s[:, c * LANES : (c + 1) * LANES])
                tops[2 * p + h] = jnp.maximum(tops[2 * p + h], top)
        return 0

    acc[...] = jnp.full(acc.shape, masked_score, f32)
    lax.fori_loop(0, count, lambda j, c: scores(j, acc), 0)
    peaks = [jnp.max(acc[head], axis=1, keepdims=True) for head in range(2 * pairs)]
    for head in range(2 * pairs):
        acc[head] = jnp.zeros((rows, LANES), f32)

    def mix(j, _):
        wanted, start = place(j)
        for head in range(2 * pairs):
            e = jnp.exp(s_all[head, j] - peaks[head]).astype(bf16)
            acc[head] += mm(e, vx_all[pl.ds(start, tile), head * LANES : (head + 1) * LANES])
        return 0

    lax.fori_loop(0, count, mix, 0)
    totals = jnp.zeros((rows, LANES), f32)
    for p in range(pairs):
        mixed = []
        for h in range(2):
            head = 2 * p + h
            o = acc[head]
            l = pltpu.roll(o, HD, 1)
            mixed.append(o / l)
            totals = jnp.where(lane == head, peaks[head] + jnp.log(jnp.where(low, l, 1.0)[:, :1]), totals)
        o_ref[:, p * LANES : (p + 1) * LANES] = jnp.where(
            low, mixed[0], pltpu.roll(mixed[1], HD, 1)
        ).astype(bf16)
    l_ref[...] = totals.T[: 2 * pairs, :]
    n1, _ = norm_rows(r1_ref[...])
    h1 = n1 * norms_ref[0:1, :] + norms_ref[1:2, :]
    r2_ref[...] = h1 + mm(o_ref[...], wco_ref[...])


def cross_forward(ranges, q2, k2, v2, r1, wco, norms, idc, idr, rows=256, tile=256, vmem=56 * 2**20):
    total, width = q2.shape
    keys = k2.shape[0]
    heads = width // HD
    rowspec = lambda w: pl.BlockSpec((rows, w), lambda i, *_: (i, 0))
    return pl.pallas_call(
        functools.partial(cross_forward_kernel, tile),
        grid_spec=pltpu.PrefetchScalarGridSpec(
            num_scalar_prefetch=1,
            grid=(total // rows,),
            in_specs=[rowspec(width), whole(k2), whole(v2), rowspec(width), whole(wco), whole(norms), rowspec(1), whole(idr)],
            out_specs=[rowspec(width), pl.BlockSpec((heads, rows), lambda i, *_: (0, i)), rowspec(width)],
            scratch_shapes=[
                pltpu.VMEM((keys, 2 * width), bf16),
                pltpu.VMEM((heads, keys // tile, rows, tile), f32),
                pltpu.VMEM((heads, rows, LANES), f32),
            ],
        ),
        out_shape=[
            jax.ShapeDtypeStruct((total, width), bf16),
            jax.ShapeDtypeStruct((heads, total), f32),
            jax.ShapeDtypeStruct((total, width), f32),
        ],
        compiler_params=pltpu.CompilerParams(vmem_limit_bytes=vmem),
        name="cross_forward",
    )(ranges, q2, k2, v2, r1, wco, norms, idc, idr)


def norm_back(incoming, normal, rstd, gain):
    m = incoming * gain
    return rstd * (
        m - jnp.mean(m, axis=-1, keepdims=True) - normal * jnp.mean(m * normal, axis=-1, keepdims=True)
    )


def head_sums(left, right):
    width = left.shape[1]
    prod = left.astype(f32) * right.astype(f32)
    heads = width // HD
    own = lax.broadcasted_iota(jnp.int32, (heads, width), 1) // HD == lax.broadcasted_iota(
        jnp.int32, (heads, width), 0
    )
    return lax.dot_general(
        own.astype(f32), prod, NT, preferred_element_type=f32, precision=lax.Precision.HIGHEST
    )


def column_sums(a):
    return jnp.sum(a, axis=0, keepdims=True)


def ffn_kernel(
    r2_ref, x_ref, cot_ref, o2_ref, win_ref, wout_ref, wco_ref, norms_ref,
    out_ref, dr3_ref, dr2_ref, do2_ref, delta_ref, gin_ref, gout_ref, gco_ref, gn_ref, gin, gout, gco,
):
    step = pl.program_id(0)
    last = pl.num_programs(0) - 1

    @pl.when(step == 0)
    def _():
        gin[...] = jnp.zeros_like(gin)
        gout[...] = jnp.zeros_like(gout)
        gco[...] = jnp.zeros_like(gco)
        gn_ref[...] = jnp.zeros_like(gn_ref)

    n2, rstd2 = norm_rows(r2_ref[...])
    h2 = n2 * norms_ref[2:3, :] + norms_ref[3:4, :]
    h2b = h2.astype(bf16)
    u = mm(h2b, win_ref[...])
    square = u * u
    t = jnp.tanh(0.7978845608028654 * u * (1.0 + 0.044715 * square))
    half = 0.5 * (1.0 + t)
    act = (u * half).astype(bf16)
    slope = half + 0.5 * u * (1.0 - t * t) * (0.7978845608028654 * (1.0 + 3 * 0.044715 * square))
    r3 = h2 + mm(act, wout_ref[...]) + x_ref[...].astype(f32)
    n3, rstd3 = norm_rows(r3)
    gain3 = norms_ref[4:5, :]
    out_ref[...] = (n3 * gain3 + norms_ref[5:6, :]).astype(bf16)
    e = cot_ref[...].astype(f32)
    gn_ref[2:3, :] += column_sums(e * n3)
    gn_ref[3:4, :] += column_sums(e)
    dr3 = norm_back(e, n3, rstd3, gain3)
    dr3_ref[...] = dr3
    dfb = dr3.astype(bf16)
    gout[...] += mm(act, dfb, TN)
    du = (mm(dfb, wout_ref[...], NT) * slope).astype(bf16)
    gin[...] += mm(h2b, du, TN)
    dh2 = dr3 + mm(du, win_ref[...], NT)
    gn_ref[0:1, :] += column_sums(dh2 * n2)
    gn_ref[1:2, :] += column_sums(dh2)
    dr2 = norm_back(dh2, n2, rstd2, norms_ref[2:3, :])
    dr2_ref[...] = dr2
    da2 = dr2.astype(bf16)
    o2 = o2_ref[...]
    gco[...] += mm(o2, da2, TN)
    do2 = mm(da2, wco_ref[...], NT).astype(bf16)
    do2_ref[...] = do2
    delta_ref[...] = head_sums(do2, o2)

    @pl.when(step == last)
    def _():
        gin_ref[...] = gin[...].astype(bf16)
        gout_ref[...] = gout[...].astype(bf16)
        gco_ref[...] = gco[...].astype(bf16)


def ffn(r2, x, cot, o2, win, wout, wco, norms, rows=256, vmem=56 * 2**20):
    total, width = x.shape
    heads = width // HD
    hidden = win.shape[1]
    rowspec = lambda w: pl.BlockSpec((rows, w), lambda i: (i, 0))
    fixed = lambda s: pl.BlockSpec(s, lambda i: (0, 0))
    sds = jax.ShapeDtypeStruct
    return pl.pallas_call(
        ffn_kernel,
        grid=(total // rows,),
        in_specs=[rowspec(width)] * 4 + [whole(a) for a in (win, wout, wco, norms)],
        out_specs=[rowspec(width)] * 4
        + [pl.BlockSpec((heads, rows), lambda i: (0, i)), fixed((width, hidden)), fixed((hidden, width)), fixed((width, width)), fixed((4, width))],
        out_shape=[
            sds((total, width), bf16), sds((total, width), f32), sds((total, width), f32), sds((total, width), bf16),
            sds((heads, total), f32), sds((width, hidden), bf16), sds((hidden, width), bf16), sds((width, width), bf16), sds((4, width), f32),
        ],
        scratch_shapes=[pltpu.VMEM((width, hidden), f32), pltpu.VMEM((hidden, width), f32), pltpu.VMEM((width, width), f32)],
        compiler_params=pltpu.CompilerParams(vmem_limit_bytes=vmem),
        name="ffn",
    )(r2, x, cot, o2, win, wout, wco, norms)


def tile_back(kp, vp, qp, dop, bias, logs, deltas, low_k):
    dks, dvs, dss, kms = [], [], [], []
    for h in range(2):
        km = head_part(kp, h, low_k)
        s = mm(km, qp, NT) + bias
        e = jnp.exp(s - logs[h])
        dp = mm(head_part(vp, h, low_k), dop, NT)
        ds = (e * (dp - deltas[h])).astype(bf16)
        dvs.append(mm(e.astype(bf16), dop))
        dks.append(mm(ds, qp))
        dss.append(ds)
        kms.append(km)
    dq = mm(jnp.concatenate(dss, axis=0), jnp.concatenate(kms, axis=0), TN)
    return jnp.where(low_k, dks[0], dks[1]), jnp.where(low_k, dvs[0], dvs[1]), dq


def cross_backward_kernel(
    tile, ranges_ref, q2_ref, k2_ref, v2_ref, do_ref, l_ref, delta_ref, idr_ref, idc_ref,
    dq_ref, dk_ref, dv_ref, dk, dv, dq,
):
    step = pl.program_id(0)
    rows, width = q2_ref.shape
    keys = k2_ref.shape[0]
    pairs = width // LANES

    @pl.when(step == 0)
    def _():
        dk[...] = jnp.zeros_like(dk)
        dv[...] = jnp.zeros_like(dv)

    dq[...] = jnp.zeros_like(dq)
    scaled = q2_ref[...] * jnp.asarray(HD ** -0.5, bf16)
    do = do_ref[...]
    ids_q = idr_ref[...]
    low_k = lane_below(tile)
    first, count = ranges_ref[0, step], ranges_ref[1, step]

    def one(j, _):
        wanted = (first + j * (tile // LANES)) * LANES
        start = pl.multiple_of(jnp.minimum(wanted, keys - tile), LANES)
        at = pl.ds(start, tile)
        pos = start + lax.broadcasted_iota(jnp.int32, (tile, 1), 0)
        ids_k = jnp.where(pos >= wanted, idc_ref[at, :], -1)
        bias = jnp.where(ids_q == ids_k, 0.0, masked_score).astype(f32)
        for p in range(pairs):
            cols = slice(p * LANES, (p + 1) * LANES)
            logs = [l_ref[2 * p + h : 2 * p + h + 1, :] for h in range(2)]
            deltas = [delta_ref[2 * p + h : 2 * p + h + 1, :] for h in range(2)]
            gk, gv, gq = tile_back(
                k2_ref[at, cols], v2_ref[at, cols], scaled[:, cols], do[:, cols], bias, logs, deltas, low_k
            )
            dk[at, cols] += gk
            dv[at, cols] += gv
            dq[:, cols] += gq
        return 0

    lax.fori_loop(0, count, one, 0)
    dq_ref[...] = (dq[...] * HD ** -0.5).astype(bf16)

    @pl.when(step == pl.num_programs(0) - 1)
    def _():
        dk_ref[...] = dk[...].astype(bf16)
        dv_ref[...] = dv[...].astype(bf16)


def cross_backward(ranges, q2, k2, v2, do, l, delta, idr, idc, rows=256, tile=256, vmem=56 * 2**20):
    total, width = q2.shape
    keys = k2.shape[0]
    heads = width // HD
    rowspec = lambda w: pl.BlockSpec((rows, w), lambda i, *_: (i, 0))
    cols = lambda h: pl.BlockSpec((h, rows), lambda i, *_: (0, i))
    sds = jax.ShapeDtypeStruct
    return pl.pallas_call(
        functools.partial(cross_backward_kernel, tile),
        grid_spec=pltpu.PrefetchScalarGridSpec(
            num_scalar_prefetch=1,
            grid=(total // rows,),
            in_specs=[rowspec(width), whole(k2), whole(v2), rowspec(width), cols(heads), cols(heads), cols(1), whole(idc)],
            out_specs=[rowspec(width), pl.BlockSpec((keys, width), lambda i, *_: (0, 0)), pl.BlockSpec((keys, width), lambda i, *_: (0, 0))],
            scratch_shapes=[pltpu.VMEM((keys, width), f32), pltpu.VMEM((keys, width), f32), pltpu.VMEM((rows, width), f32)],
        ),
        out_shape=[sds((total, width), bf16), sds((keys, width), bf16), sds((keys, width), bf16)],
        compiler_params=pltpu.CompilerParams(vmem_limit_bytes=vmem),
        name="cross_backward",
    )(ranges, q2, k2, v2, do, l, delta, idr, idc)


def between_kernel(
    r1_ref, dr2_ref, dq2_ref, h1b_ref, o1_ref, wcq_ref, wso_ref, norms_ref,
    dr1_ref, do1_ref, delta_ref, grads_ref, gn_ref, gcq, gso,
):
    step = pl.program_id(0)

    @pl.when(step == 0)
    def _():
        gcq[...] = jnp.zeros_like(gcq)
        gso[...] = jnp.zeros_like(gso)
        gn_ref[...] = jnp.zeros_like(gn_ref)

    dq2 = dq2_ref[...]
    dh1 = dr2_ref[...] + mm(dq2, wcq_ref[...], NT)
    n1, rstd1 = norm_rows(r1_ref[...])
    gn_ref[0:1, :] += column_sums(dh1 * n1)
    gn_ref[1:2, :] += column_sums(dh1)
    dr1 = norm_back(dh1, n1, rstd1, norms_ref[0:1, :])
    dr1_ref[...] = dr1
    da1 = dr1.astype(bf16)
    o1 = o1_ref[...]
    do1 = mm(da1, wso_ref[...], NT).astype(bf16)
    do1_ref[...] = do1
    delta_ref[...] = head_sums(do1, o1)
    gcq[...] += mm(h1b_ref[...], dq2, TN)
    gso[...] += mm(o1, da1, TN)

    @pl.when(step == pl.num_programs(0) - 1)
    def _():
        grads_ref[0] = gcq[...].astype(bf16)
        grads_ref[1] = gso[...].astype(bf16)


def between(r1, dr2, dq2, h1b, o1, wcq, wso, norms, rows=256, vmem=40 * 2**20):
    total, width = r1.shape
    heads = width // HD
    rowspec = lambda w: pl.BlockSpec((rows, w), lambda i: (i, 0))
    fixed = lambda s: pl.BlockSpec(s, lambda i: (0, 0))
    sds = jax.ShapeDtypeStruct
    return pl.pallas_call(
        between_kernel,
        grid=(total // rows,),
        in_specs=[rowspec(width)] * 5 + [whole(a) for a in (wcq, wso, norms)],
        out_specs=[rowspec(width)] * 2 + [pl.BlockSpec((heads, rows), lambda i: (0, i)), pl.BlockSpec((2, width, width), lambda i: (0, 0, 0)), fixed((2, width))],
        out_shape=[sds((total, width), f32), sds((total, width), bf16), sds((heads, total), f32), sds((2, width, width), bf16), sds((2, width), f32)],
        scratch_shapes=[pltpu.VMEM((width, width), f32), pltpu.VMEM((width, width), f32)],
        compiler_params=pltpu.CompilerParams(vmem_limit_bytes=vmem),
        name="between",
    )(r1, dr2, dq2, h1b, o1, wcq, wso, norms)


def self_backward_kernel(
    block, q_ref, k_ref, v_ref, do_ref, l_ref, delta_ref, idc_ref, idr_ref, x_ref, wq_ref, wk_ref, wv_ref, dr1_ref, dr3_ref,
    gx_ref, grads_ref, dq, dk, dv, gq, gk, gv,
):
    step = pl.program_id(0)
    rows, width = k_ref.shape
    total = q_ref.shape[0]
    window = MOST + block
    pairs = width // LANES

    @pl.when(step == 0)
    def _():
        dq[...] = jnp.zeros_like(dq)
        gq[...] = jnp.zeros_like(gq)
        gk[...] = jnp.zeros_like(gk)
        gv[...] = jnp.zeros_like(gv)

    base = pl.multiple_of(step * rows, rows)
    low_k = lane_below(block)
    for sub in range(rows // block):
        here = slice(sub * block, (sub + 1) * block)
        start = pl.multiple_of(jnp.minimum(base + sub * block, total - window), LANES)
        at = pl.ds(start, window)
        pos_k = base + sub * block + lax.broadcasted_iota(jnp.int32, (block, window), 0)
        pos_q = start + lax.broadcasted_iota(jnp.int32, (block, window), 1)
        bias = jnp.where((idc_ref[here, :] == idr_ref[:, at]) & (pos_k <= pos_q), 0.0, masked_score).astype(f32)
        for p in range(pairs):
            cols = slice(p * LANES, (p + 1) * LANES)
            logs = [l_ref[2 * p + h : 2 * p + h + 1, at] for h in range(2)]
            deltas = [delta_ref[2 * p + h : 2 * p + h + 1, at] for h in range(2)]
            hk, hv, hq = tile_back(
                k_ref[here, cols], v_ref[here, cols], q_ref[at, cols] * jnp.asarray(HD ** -0.5, bf16), do_ref[at, cols],
                bias, logs, deltas, low_k,
            )
            dk[here, cols] = hk.astype(bf16)
            dv[here, cols] = hv.astype(bf16)
            dq[at, cols] += hq
    x = x_ref[...]
    dqb = (dq[pl.ds(base, rows), :] * HD ** -0.5).astype(bf16)
    dkb, dvb = dk[...], dv[...]
    gx = dr1_ref[...] + dr3_ref[...] + mm(dqb, wq_ref[...], NT) + mm(dkb, wk_ref[...], NT) + mm(dvb, wv_ref[...], NT)
    gx_ref[...] = gx.astype(bf16)
    gq[...] += mm(x, dqb, TN)
    gk[...] += mm(x, dkb, TN)
    gv[...] += mm(x, dvb, TN)

    @pl.when(step == pl.num_programs(0) - 1)
    def _():
        grads_ref[0] = gq[...].astype(bf16)
        grads_ref[1] = gk[...].astype(bf16)
        grads_ref[2] = gv[...].astype(bf16)


def self_backward(q, k, v, do, l, delta, idc, idr, x, wq, wk, wv, dr1, dr3, rows=256, block=256, vmem=48 * 2**20):
    total, width = x.shape
    rowspec = lambda w: pl.BlockSpec((rows, w), lambda i: (i, 0))
    fixed = lambda s: pl.BlockSpec(s, lambda i: (0, 0))
    sds = jax.ShapeDtypeStruct
    return pl.pallas_call(
        functools.partial(self_backward_kernel, block),
        grid=(total // rows,),
        in_specs=[whole(q), rowspec(width), rowspec(width), whole(do), whole(l), whole(delta), rowspec(1), whole(idr), rowspec(width)]
        + [whole(a) for a in (wq, wk, wv)] + [rowspec(width)] * 2,
        out_specs=[rowspec(width), pl.BlockSpec((3, width, width), lambda i: (0, 0, 0))],
        out_shape=[sds((total, width), bf16), sds((3, width, width), bf16)],
        scratch_shapes=[pltpu.VMEM((total, width), f32), pltpu.VMEM((rows, width), bf16), pltpu.VMEM((rows, width), bf16)]
        + [pltpu.VMEM((width, width), f32)] * 3,
        compiler_params=pltpu.CompilerParams(vmem_limit_bytes=vmem),
        name="self_backward",
    )(q, k, v, do, l, delta, idc, idr, x, wq, wk, wv, dr1, dr3)


def segment_ids(lengths, row_count):
    ends = jnp.cumsum(lengths)
    places = jnp.arange(row_count, dtype=jnp.int32)
    return jnp.sum((places[:, None] >= ends[None, :]).astype(jnp.int32), axis=1)


def cross_ranges(seg, mem, total, rows, tile):
    ends = jnp.cumsum(seg)
    starts = jnp.arange(0, total, rows, dtype=jnp.int32)
    head = starts[:, None] >= ends[None, :]
    tail = (starts + rows - 1)[:, None] >= ends[None, :]
    mem = mem[: seg.shape[0]]
    low = jnp.sum(jnp.where(head, mem[None, :], 0), axis=1)
    before = jnp.concatenate([jnp.ones((starts.shape[0], 1), bool), tail[:, :-1]], axis=1)
    high = jnp.sum(jnp.where(before, mem[None, :], 0), axis=1)
    first = low // LANES
    count = (high - first * LANES + tile - 1) // tile
    return jnp.stack([first, count]).astype(jnp.int32)


def index_bits():
    sizes = lax.axis_size("dp"), lax.axis_size("fsdp")
    count = (sizes[0] * sizes[1]).bit_length() - 1
    me = lax.axis_index("dp") * sizes[1] + lax.axis_index("fsdp")
    return count, me


def swap(x, b):
    count = lax.axis_size("dp") * lax.axis_size("fsdp")
    return lax.ppermute(x, ("dp", "fsdp"), [(i, i ^ (1 << b)) for i in range(count)])


def gather(x, order, lead=0):
    _, me = index_bits()
    have = []
    for b in order:
        mine = (me >> b) & 1 == 0
        other = swap(x, b)
        place = lead + sum(1 for h in have if h > b)
        x = jnp.stack([jnp.where(mine, x, other), jnp.where(mine, other, x)], axis=place)
        have.append(b)
    return x.reshape(x.shape[:lead] + (-1, x.shape[-1]))


def scatter_sum(x, order, lead=0, kind=bf16):
    count, me = index_bits()
    x = x.reshape(x.shape[:lead] + (2,) * count + (-1, x.shape[-1]))
    have = list(range(count))
    for b in order:
        mine = (me >> b) & 1
        place = lead + sum(1 for h in have if h > b)
        other = swap(lax.dynamic_index_in_dim(x, 1 - mine, place, keepdims=False), b)
        own = lax.dynamic_index_in_dim(x, mine, place, keepdims=False)
        have.remove(b)
        x = own.astype(f32) + other.astype(f32)
        if have:
            x = x.astype(kind)
    return x


def body(
    inputs, memory, seg_lengths, mem_lengths, self_query, self_key, self_value, self_out,
    cross_query, cross_key, cross_value, cross_out, ffn_in, ffn_out, norm_params, cotangent,
):
    total, width = inputs.shape
    keys = memory.shape[0]
    count, _ = index_bits()
    up, down = list(range(count)), list(range(count))[::-1]
    tile = 256

    def rows_of(flat, columns):
        return flat.reshape(-1, columns)

    first = gather(jnp.stack([rows_of(w, width) for w in (self_query, self_key, self_value)]), down, 1)
    wsq, wsk, wsv = first[0], first[1], first[2]
    second = gather(
        jnp.stack([rows_of(w, width) for w in (self_out, cross_query, cross_key, cross_value, cross_out)]), down, 1
    )
    wso, wcq, wck, wcv, wco = (second[i] for i in range(5))
    win = gather(rows_of(ffn_in, ffn_in.shape[0] * (1 << count) // width), down)
    wout = gather(rows_of(ffn_out, width), down)
    norms = gather(norm_params.reshape(1, -1), down).reshape(6, width)

    qid, mid = segment_ids(seg_lengths[0], total), segment_ids(mem_lengths[0], keys)
    qc, qr, mc, mr = qid[:, None], qid[None, :], mid[:, None], mid[None, :]
    ranges = cross_ranges(seg_lengths[0], mem_lengths[0], total, 256, tile)
    q1, k1, v1, o1, l1, r1, h1b, q2 = self_forward(inputs, wsq, wsk, wsv, wso, wcq, norms, qc, qr, block=256)
    k2 = mm(memory, wck).astype(bf16)
    v2 = mm(memory, wcv).astype(bf16)
    o2, l2, r2 = cross_forward(ranges, q2, k2, v2, r1, wco, norms, qc, mr, tile=tile)
    out, dr3, dr2, do2, delta2, gfi, gfo, gco, gn23 = ffn(r2, inputs, cotangent, o2, win, wout, wco, norms)
    gfi, gfo, gco = (scatter_sum(g, up) for g in (gfi, gfo, gco))
    dq2, dk2, dv2 = cross_backward(ranges, q2, k2, v2, do2, l2, delta2, qr, mc, tile=tile)
    gckv = scatter_sum(jnp.stack([mm(memory, dk2, TN).astype(bf16), mm(memory, dv2, TN).astype(bf16)]), up, 1)
    dr1, do1, delta1, gcqso, gn1 = between(r1, dr2, dq2, h1b, o1, wcq, wso, norms)
    gcqso = scatter_sum(gcqso, up, 1)
    gn = scatter_sum(jnp.concatenate([gn1, gn23]).reshape(1 << count, -1), up, kind=f32)
    gx, gself = self_backward(q1, k1, v1, do1, l1, delta1, qc, qr, inputs, wsq, wsk, wsv, dr1, dr3)
    gself = scatter_sum(gself, up, 1)
    gm = (mm(dk2, wck, NT) + mm(dv2, wcv, NT)).astype(bf16)
    flat = lambda g: g.reshape(-1)
    return (
        out, gx, gm, flat(gself[0]), flat(gself[1]), flat(gself[2]), flat(gcqso[1]),
        flat(gcqso[0]), flat(gckv[0]), flat(gckv[1]), flat(gco), flat(gfi), flat(gfo), flat(gn),
    )


def solution(mesh):
    rows, flat = P(("dp", "fsdp"), None), P(("dp", "fsdp"))
    return jax.shard_map(
        body,
        mesh=mesh,
        in_specs=(rows,) * 4 + (flat,) * 11 + (rows,),
        out_specs=(rows,) * 3 + (flat,) * 11,
        check_vma=False,
    )
```

```python
import functools
import jax
import jax.numpy as jnp
from jax import lax
from jax.experimental import pallas as pl
from jax.experimental.pallas import tpu as pltpu
from jax.sharding import PartitionSpec as P

HD = 64
LANES = 128
MOST = 256
masked_score = -1e30
norm_eps = 1e-05
bf16, f32 = jnp.bfloat16, jnp.float32
NT = (((1,), (1,)), ((), ()))
TN = (((0,), (0,)), ((), ()))
NN = (((1,), (0,)), ((), ()))


def mm(left, right, dims=NN):
    return lax.dot_general(left, right, dims, preferred_element_type=f32)


def norm_rows(source):
    mean = jnp.mean(source, axis=-1, keepdims=True)
    centered = source - mean
    variance = jnp.mean(centered * centered, axis=-1, keepdims=True)
    rstd = lax.rsqrt(variance + norm_eps)
    return centered * rstd, rstd


def lane_below(rows):
    return lax.broadcasted_iota(jnp.int32, (rows, LANES), 1) < HD


def column_of(row):
    return jnp.broadcast_to(row, (LANES, row.shape[1])).T


def head_part(pair, which, low):
    return jnp.where(low == (which == 0), pair, jnp.zeros_like(pair))


def values_with_ones(values, low):
    parts = []
    for p in range(values.shape[1] // LANES):
        pair = values[:, p * LANES : (p + 1) * LANES]
        one = jnp.ones_like(pair)
        parts.append(jnp.where(low, pair, one))
        parts.append(jnp.where(low, pltpu.roll(pair, HD, 1), one))
    return jnp.concatenate(parts, axis=1)


def self_forward_kernel(block, x_ref, wq_ref, wk_ref, wv_ref, idr_ref, *rest):
    q_ref, k_ref, v_ref, o_ref, l_ref, k_all, vx_all = rest[-7:]
    step = pl.program_id(0)
    rows = x_ref.shape[0]
    width = k_ref.shape[1]
    window = MOST + block
    pairs = width // LANES
    x = x_ref[...]
    q = mm(x, wq_ref[0]).astype(bf16)
    k = mm(x, wk_ref[0]).astype(bf16)
    v = mm(x, wv_ref[0]).astype(bf16)
    q_ref[...] = q
    k_ref[...] = k
    v_ref[...] = v

    @pl.when(step == 0)
    def _():
        k_all[...] = jnp.zeros_like(k_all)
        vx_all[...] = jnp.zeros_like(vx_all)

    base = pl.multiple_of(step * rows, rows)
    k_all[pl.ds(base, rows), :] = k
    vx_all[pl.ds(base, rows), :] = values_with_ones(v, lane_below(rows))
    scaled = q * jnp.asarray(HD ** -0.5, bf16)
    low = lane_below(block)
    lane = lax.broadcasted_iota(jnp.int32, (block, LANES), 1)
    for sub in range(rows // block):
        start = pl.multiple_of(jnp.maximum(base + sub * block - MOST, 0), LANES)
        ids_q = column_of(idr_ref[:, pl.ds(base + sub * block, block)])[:, :1]
        ids_k = idr_ref[:, pl.ds(start, window)]
        pos_q = base + sub * block + lax.broadcasted_iota(jnp.int32, (block, window), 0)
        pos_k = start + lax.broadcasted_iota(jnp.int32, (block, window), 1)
        bias = jnp.where((ids_q == ids_k) & (pos_k <= pos_q), 0.0, masked_score).astype(f32)
        totals = jnp.zeros((block, LANES), f32)
        for p in range(pairs):
            cols = slice(p * LANES, (p + 1) * LANES)
            qp = scaled[sub * block : (sub + 1) * block, cols]
            kp = k_all[pl.ds(start, window), cols]
            mixed = []
            for h in range(2):
                s = mm(head_part(qp, h, low), kp, NT) + bias
                m = jnp.max(s, axis=1, keepdims=True)
                e = jnp.exp(s - m).astype(bf16)
                head = 2 * p + h
                o = mm(e, vx_all[pl.ds(start, window), head * LANES : (head + 1) * LANES])
                l = pltpu.roll(o, HD, 1)
                mixed.append(o / l)
                totals = jnp.where(lane == head, m + jnp.log(jnp.where(low, l, 1.0)[:, :1]), totals)
            o_ref[sub * block : (sub + 1) * block, cols] = jnp.where(
                low, mixed[0], pltpu.roll(mixed[1], HD, 1)
            ).astype(bf16)
        l_ref[:, sub * block : (sub + 1) * block] = totals.T[: 2 * pairs, :]


def whole(a):
    return pl.BlockSpec(a.shape, lambda *_: (0,) * a.ndim)


def part(weights, index, columns, half):
    return pl.BlockSpec((1, weights.shape[1], columns), lambda *_: (index, 0, half))


def params(us, vmem):
    return dict(
        compiler_params=pltpu.CompilerParams(vmem_limit_bytes=vmem * 2**20),
        cost_estimate=pl.CostEstimate(flops=us * 10**9, bytes_accessed=2**20, transcendentals=0),
    )


apart = pl.BlockSpec(memory_space=pl.ANY)


def self_forward(x, weights, idr, half, after, rows=256, block=256):
    total, width = x.shape
    columns = width // 2
    heads = columns // HD
    rowspec = lambda w: pl.BlockSpec((rows, w), lambda i: (i, 0))
    full = jax.ShapeDtypeStruct((total, columns), bf16)
    return pl.pallas_call(
        functools.partial(self_forward_kernel, block),
        grid=(total // rows,),
        in_specs=[rowspec(width)] + [part(weights, i, columns, half) for i in range(3)] + [whole(idr)]
        + [apart] * len(after),
        out_specs=[rowspec(columns)] * 4 + [pl.BlockSpec((heads, rows), lambda i: (0, i))],
        out_shape=[full] * 4 + [jax.ShapeDtypeStruct((heads, total), f32)],
        scratch_shapes=[pltpu.VMEM((total, columns), bf16), pltpu.VMEM((total, 2 * columns), bf16)],
        name="self_forward",
        **params(8, 24),
    )(x, weights, weights, weights, idr, *after)


def project_memory_kernel(memory_ref, wk_ref, wv_ref, k_ref, v_ref):
    memory = memory_ref[...]
    k_ref[...] = mm(memory, wk_ref[0]).astype(bf16)
    v_ref[...] = mm(memory, wv_ref[0]).astype(bf16)


def project_memory(memory, weights, index, rows=512):
    keys, width = memory.shape
    rowspec = pl.BlockSpec((rows, width), lambda i: (i, 0))
    return pl.pallas_call(
        project_memory_kernel,
        grid=(keys // rows,),
        in_specs=[rowspec, part(weights, index, width, 0), part(weights, index + 1, width, 0)],
        out_specs=[rowspec] * 2,
        out_shape=[jax.ShapeDtypeStruct((keys, width), bf16)] * 2,
        name="project_memory",
        **params(5, 24),
    )(memory, weights, weights)


def cross_forward_kernel(
    tile, ranges_ref, x_ref, oa_ref, ob_ref, wso_ref, wcq_ref, wco_ref, norms_ref, k2_ref, v2_ref, idq_ref, idr_ref,
    r1_ref, h1b_ref, q2_ref, o_ref, l_ref, r2_ref, vx_all, s_all, acc,
):
    step = pl.program_id(0)
    rows, width = x_ref.shape
    keys = k2_ref.shape[0]
    pairs = width // LANES

    @pl.when(step == 0)
    def _():
        def fill(j, _):
            at = pl.ds(pl.multiple_of(j * tile, tile), tile)
            vx_all[at, :] = values_with_ones(v2_ref[at, :], lane_below(tile))
            return 0

        lax.fori_loop(0, keys // tile, fill, 0)

    half = width // 2
    r1 = x_ref[...].astype(f32) + mm(oa_ref[...], wso_ref[0, :half, :]) + mm(ob_ref[...], wso_ref[0, half:, :])
    r1_ref[...] = r1
    n1, _ = norm_rows(r1)
    h1 = n1 * norms_ref[0:1, :] + norms_ref[1:2, :]
    h1b = h1.astype(bf16)
    h1b_ref[...] = h1b
    q2 = mm(h1b, wcq_ref[0]).astype(bf16)
    q2_ref[...] = q2
    low = lane_below(rows)
    lane = lax.broadcasted_iota(jnp.int32, (rows, LANES), 1)
    scaled = q2 * jnp.asarray(HD ** -0.5, bf16)
    ids_q = column_of(idq_ref[...])[:, :1]
    first, count = ranges_ref[0, step], ranges_ref[1, step]

    def place(j):
        wanted = (first + j * (tile // LANES)) * LANES
        return wanted, pl.multiple_of(jnp.minimum(wanted, keys - tile), LANES)

    def scores(j, tops):
        wanted, start = place(j)
        pos = start + lax.broadcasted_iota(jnp.int32, (1, tile), 1)
        ids_k = jnp.where(pos >= wanted, idr_ref[:, pl.ds(start, tile)], -1)
        bias = jnp.where(ids_q == ids_k, 0.0, masked_score).astype(f32)
        new = []
        for p in range(pairs):
            cols = slice(p * LANES, (p + 1) * LANES)
            kp = k2_ref[pl.ds(start, tile), cols]
            for h in range(2):
                s = mm(head_part(scaled[:, cols], h, low), kp, NT) + bias
                s_all[2 * p + h, j] = s
                top = s[:, :LANES]
                for c in range(1, tile // LANES):
                    top = jnp.maximum(top, s[:, c * LANES : (c + 1) * LANES])
                tops[2 * p + h] = jnp.maximum(tops[2 * p + h], top)
        return 0

    acc[...] = jnp.full(acc.shape, masked_score, f32)
    lax.fori_loop(0, count, lambda j, c: scores(j, acc), 0)
    peaks = [jnp.max(acc[head], axis=1, keepdims=True) for head in range(2 * pairs)]
    for head in range(2 * pairs):
        acc[head] = jnp.zeros((rows, LANES), f32)

    def mix(j, _):
        wanted, start = place(j)
        for head in range(2 * pairs):
            e = jnp.exp(s_all[head, j] - peaks[head]).astype(bf16)
            acc[head] += mm(e, vx_all[pl.ds(start, tile), head * LANES : (head + 1) * LANES])
        return 0

    lax.fori_loop(0, count, mix, 0)
    totals = jnp.zeros((rows, LANES), f32)
    for p in range(pairs):
        mixed = []
        for h in range(2):
            head = 2 * p + h
            o = acc[head]
            l = pltpu.roll(o, HD, 1)
            mixed.append(o / l)
            totals = jnp.where(lane == head, peaks[head] + jnp.log(jnp.where(low, l, 1.0)[:, :1]), totals)
        o_ref[:, p * LANES : (p + 1) * LANES] = jnp.where(
            low, mixed[0], pltpu.roll(mixed[1], HD, 1)
        ).astype(bf16)
    l_ref[...] = totals.T[: 2 * pairs, :]
    r2_ref[...] = h1 + mm(o_ref[...], wco_ref[0])


def cross_forward(ranges, x, oa, ob, weights, norms, k2, v2, idq, idr, rows=256, tile=256):
    total, width = x.shape
    keys = k2.shape[0]
    heads = width // HD
    rowspec = lambda w: pl.BlockSpec((rows, w), lambda i, *_: (i, 0))
    sds = jax.ShapeDtypeStruct
    return pl.pallas_call(
        functools.partial(cross_forward_kernel, tile),
        grid_spec=pltpu.PrefetchScalarGridSpec(
            num_scalar_prefetch=1,
            grid=(total // rows,),
            in_specs=[rowspec(width), rowspec(width // 2), rowspec(width // 2)]
            + [part(weights, i, width, 0) for i in range(3)]
            + [whole(norms), whole(k2), whole(v2), pl.BlockSpec((1, rows), lambda i, *_: (0, i)), whole(idr)],
            out_specs=[rowspec(width)] * 4 + [pl.BlockSpec((heads, rows), lambda i, *_: (0, i)), rowspec(width)],
            scratch_shapes=[
                pltpu.VMEM((keys, 2 * width), bf16),
                pltpu.VMEM((heads, keys // tile, rows, tile), f32),
                pltpu.VMEM((heads, rows, LANES), f32),
            ],
        ),
        out_shape=[
            sds((total, width), f32), sds((total, width), bf16), sds((total, width), bf16),
            sds((total, width), bf16), sds((heads, total), f32), sds((total, width), f32),
        ],
        name="cross_forward",
        **params(28, 50),
    )(ranges, x, oa, ob, weights, weights, weights, norms, k2, v2, idq, idr)


def norm_back(incoming, normal, rstd, gain):
    m = incoming * gain
    return rstd * (
        m - jnp.mean(m, axis=-1, keepdims=True) - normal * jnp.mean(m * normal, axis=-1, keepdims=True)
    )


def head_sums(left, right):
    width = left.shape[1]
    prod = left.astype(f32) * right.astype(f32)
    heads = width // HD
    own = lax.broadcasted_iota(jnp.int32, (heads, width), 1) // HD == lax.broadcasted_iota(
        jnp.int32, (heads, width), 0
    )
    return lax.dot_general(
        own.astype(f32), prod, NT, preferred_element_type=f32, precision=lax.Precision.HIGHEST
    )


def column_sums(a):
    return jnp.sum(a, axis=0, keepdims=True)


def spread(keep_ref, send_ref, core, write):
    def one(j, _):
        write(2 * j + core, keep_ref, j)
        write(2 * j + 1 - core, send_ref, j)
        return 0

    lax.fori_loop(0, keep_ref.shape[0], one, 0)


def ffn_kernel(
    core_ref, r2_ref, x_ref, cot_ref, o2_ref, w_ref, wco_ref, norms_ref,
    out_ref, dr3_ref, dr2_ref, do2_ref, delta_ref, keep_ref, send_ref, gn_ref, gin, gout, gco,
):
    step = pl.program_id(0)
    last = pl.num_programs(0) - 1
    width = x_ref.shape[1]
    blocks = w_ref.shape[1] // 2

    @pl.when(step == 0)
    def _():
        gin[...] = jnp.zeros_like(gin)
        gout[...] = jnp.zeros_like(gout)
        gco[...] = jnp.zeros_like(gco)
        gn_ref[...] = jnp.zeros_like(gn_ref)

    win = [w_ref[:, c].reshape(width, width) for c in range(blocks)]
    wout = w_ref[:, blocks:].reshape(blocks * width, width)
    n2, rstd2 = norm_rows(r2_ref[...])
    h2 = n2 * norms_ref[2:3, :] + norms_ref[3:4, :]
    h2b = h2.astype(bf16)
    acts, slopes = [], []
    ff = jnp.zeros(h2.shape, f32)
    for c in range(blocks):
        u = mm(h2b, win[c])
        square = u * u
        t = jnp.tanh(0.7978845608028654 * u * (1.0 + 0.044715 * square))
        half = 0.5 * (1.0 + t)
        act = (u * half).astype(bf16)
        slopes.append(half + 0.5 * u * (1.0 - t * t) * (0.7978845608028654 * (1.0 + 3 * 0.044715 * square)))
        acts.append(act)
        ff += mm(act, wout[c * width : (c + 1) * width, :])
    r3 = h2 + ff + x_ref[...].astype(f32)
    n3, rstd3 = norm_rows(r3)
    gain3 = norms_ref[4:5, :]
    out_ref[...] = (n3 * gain3 + norms_ref[5:6, :]).astype(bf16)
    e = cot_ref[...].astype(f32)
    gn_ref[2:3, :] += column_sums(e * n3)
    gn_ref[3:4, :] += column_sums(e)
    dr3 = norm_back(e, n3, rstd3, gain3)
    dr3_ref[...] = dr3
    dfb = dr3.astype(bf16)
    dh2 = dr3
    for c in range(blocks):
        rows = slice(c * width, (c + 1) * width)
        gout[rows, :] += mm(acts[c], dfb, TN)
        du = (mm(dfb, wout[rows, :], NT) * slopes[c]).astype(bf16)
        gin[:, rows] += mm(h2b, du, TN)
        dh2 += mm(du, win[c], NT)
    gn_ref[0:1, :] += column_sums(dh2 * n2)
    gn_ref[1:2, :] += column_sums(dh2)
    dr2 = norm_back(dh2, n2, rstd2, norms_ref[2:3, :])
    dr2_ref[...] = dr2
    da2 = dr2.astype(bf16)
    o2 = o2_ref[...]
    gco[...] += mm(o2, da2, TN)
    do2 = mm(da2, wco_ref[0], NT).astype(bf16)
    do2_ref[...] = do2
    delta_ref[...] = head_sums(do2, o2)

    @pl.when(step == last)
    def _():
        r = keep_ref.shape[2]

        def write(device, ref, j):
            here = pl.ds(pl.multiple_of(device * r, r), r)
            for c in range(blocks):
                ref[j, c] = gin[here, c * width : (c + 1) * width].astype(bf16)
            ref[j, blocks] = gco[here, :].astype(bf16)
            there = pl.ds(pl.multiple_of(device * blocks * r, blocks * r), blocks * r)
            ref[j, blocks + 1 :] = gout[there, :].astype(bf16).reshape(blocks, r, width)

        spread(keep_ref, send_ref, core_ref[0], write)


def ffn(core, pairs, r2, x, cot, o2, w, weights, index, norms, rows=256):
    total, width = x.shape
    heads = width // HD
    blocks = w.shape[1] // 2
    rowspec = lambda w: pl.BlockSpec((rows, w), lambda i: (i, 0))
    sds = jax.ShapeDtypeStruct
    side = sds((pairs, 2 * blocks + 1, width // (2 * pairs), width), bf16)
    return pl.pallas_call(
        ffn_kernel,
        grid=(total // rows,),
        in_specs=[pl.BlockSpec(memory_space=pltpu.SMEM)] + [rowspec(width)] * 4 + [whole(w), part(weights, index, width, 0), whole(norms)],
        out_specs=[rowspec(width)] * 4
        + [pl.BlockSpec((heads, rows), lambda i: (0, i)), whole(side), whole(side), pl.BlockSpec((4, width), lambda i: (0, 0))],
        out_shape=[
            sds((total, width), bf16), sds((total, width), f32), sds((total, width), f32), sds((total, width), bf16),
            sds((heads, total), f32), side, side, sds((4, width), f32),
        ],
        scratch_shapes=[pltpu.VMEM((width, blocks * width), f32), pltpu.VMEM((blocks * width, width), f32), pltpu.VMEM((width, width), f32)],
        name="ffn",
        **params(32, 50),
    )(core, r2, x, cot, o2, w, weights, norms)


def tile_back(kp, vp, qp, dop, bias, logs, deltas, low_k):
    dks, dvs, dss, kms = [], [], [], []
    for h in range(2):
        km = head_part(kp, h, low_k)
        s = mm(km, qp, NT) + bias
        e = jnp.exp(s - logs[h])
        dp = mm(head_part(vp, h, low_k), dop, NT)
        ds = (e * (dp - deltas[h])).astype(bf16)
        dvs.append(mm(e.astype(bf16), dop))
        dks.append(mm(ds, qp))
        dss.append(ds)
        kms.append(km)
    dq = mm(jnp.concatenate(dss, axis=0), jnp.concatenate(kms, axis=0), TN)
    return jnp.where(low_k, dks[0], dks[1]), jnp.where(low_k, dvs[0], dvs[1]), dq


def cross_backward_kernel(tile, half, ranges_ref, q2_ref, k2_ref, v2_ref, do_ref, l_ref, delta_ref, idr_ref, idk_ref, *rest):
    dq_ref, dk_ref, dv_ref, dk, dv, dq = rest[-6:]
    step = pl.program_id(0)
    rows, width = q2_ref.shape
    keys = k2_ref.shape[0]
    pairs = width // LANES

    @pl.when(step == 0)
    def _():
        dk[...] = jnp.zeros_like(dk)
        dv[...] = jnp.zeros_like(dv)

    dq[...] = jnp.zeros_like(dq)
    scaled = q2_ref[...] * jnp.asarray(HD ** -0.5, bf16)
    do = do_ref[...]
    ids_q = idr_ref[...]
    low_k = lane_below(tile)
    first, count = ranges_ref[0, step], ranges_ref[1, step]

    def one(j, _):
        wanted = (first + j * (tile // LANES)) * LANES
        start = pl.multiple_of(jnp.minimum(wanted, keys - tile), LANES)
        at = pl.ds(start, tile)
        pos = start + lax.broadcasted_iota(jnp.int32, (1, tile), 1)
        ids_k = column_of(jnp.where(pos >= wanted, idk_ref[:, at], -1))[:, :1]
        bias = jnp.where(ids_q == ids_k, 0.0, masked_score).astype(f32)
        for p in range(pairs):
            cols = slice(p * LANES, (p + 1) * LANES)
            heads = [2 * (half * pairs + p) + h for h in range(2)]
            logs = [l_ref[h : h + 1, :] for h in heads]
            deltas = [delta_ref[h : h + 1, :] for h in heads]
            gk, gv, gq = tile_back(
                k2_ref[at, cols], v2_ref[at, cols], scaled[:, cols], do[:, cols], bias, logs, deltas, low_k
            )
            dk[at, cols] += gk
            dv[at, cols] += gv
            dq[:, cols] += gq
        return 0

    lax.fori_loop(0, count, one, 0)
    dq_ref[...] = (dq[...] * HD ** -0.5).astype(bf16)

    @pl.when(step == pl.num_programs(0) - 1)
    def _():
        dk_ref[...] = dk[...].astype(bf16)
        dv_ref[...] = dv[...].astype(bf16)


def cross_backward(ranges, q2, k2, v2, do, l, delta, idr, idk, half, after, rows=256, tile=256):
    total, width = q2.shape
    keys = k2.shape[0]
    heads = width // HD
    columns = width // 2
    rowspec = lambda w: pl.BlockSpec((rows, columns), lambda i, *_: (i, w))
    allrows = lambda w: pl.BlockSpec((keys, columns), lambda i, *_: (0, w))
    cols = lambda h: pl.BlockSpec((h, rows), lambda i, *_: (0, i))
    sds = jax.ShapeDtypeStruct
    return pl.pallas_call(
        functools.partial(cross_backward_kernel, tile, half),
        grid_spec=pltpu.PrefetchScalarGridSpec(
            num_scalar_prefetch=1,
            grid=(total // rows,),
            in_specs=[rowspec(half), allrows(half), allrows(half), rowspec(half), cols(heads), cols(heads), cols(1), whole(idk)]
            + [apart] * len(after),
            out_specs=[rowspec(0), allrows(0), allrows(0)],
            scratch_shapes=[pltpu.VMEM((keys, columns), f32), pltpu.VMEM((keys, columns), f32), pltpu.VMEM((rows, columns), f32)],
        ),
        out_shape=[sds((total, columns), bf16), sds((keys, columns), bf16), sds((keys, columns), bf16)],
        name="cross_backward",
        **params(18, 40),
    )(ranges, q2, k2, v2, do, l, delta, idr, idk, *after)


def memory_weight_kernel(memory_ref, ka_ref, kb_ref, va_ref, vb_ref, *rest):
    grads_ref, total = rest[-2:]
    step = pl.program_id(0)

    @pl.when(step == 0)
    def _():
        total[...] = jnp.zeros_like(total)

    memory = memory_ref[...]
    half = ka_ref.shape[1]
    for i, ref in enumerate((ka_ref, kb_ref, va_ref, vb_ref)):
        total[i // 2, :, (i % 2) * half : (i % 2 + 1) * half] += mm(memory, ref[...], TN)

    @pl.when(step == pl.num_programs(0) - 1)
    def _():
        grads_ref[...] = total[...].astype(bf16)


def memory_weights(memory, ka, kb, va, vb, after, rows=512):
    keys, width = memory.shape
    rowspec = lambda w: pl.BlockSpec((rows, w), lambda i: (i, 0))
    return pl.pallas_call(
        memory_weight_kernel,
        grid=(keys // rows,),
        in_specs=[rowspec(width)] + [rowspec(width // 2)] * 4 + [apart] * len(after),
        out_specs=pl.BlockSpec((2, width, width), lambda i: (0, 0, 0)),
        out_shape=jax.ShapeDtypeStruct((2, width, width), bf16),
        scratch_shapes=[pltpu.VMEM((2, width, width), f32)],
        name="memory_weights",
        **params(6, 24),
    )(memory, ka, kb, va, vb, *after)


def memory_grad_kernel(ka_ref, kb_ref, va_ref, vb_ref, wk_ref, wv_ref, *rest):
    half = ka_ref.shape[1]
    total = mm(ka_ref[...], wk_ref[0, :, :half], NT) + mm(kb_ref[...], wk_ref[0, :, half:], NT)
    total += mm(va_ref[...], wv_ref[0, :, :half], NT) + mm(vb_ref[...], wv_ref[0, :, half:], NT)
    rest[-1][...] = total.astype(bf16)


def memory_grad(ka, kb, va, vb, weights, index, after, rows=512):
    keys, width = ka.shape[0], weights.shape[2]
    rowspec = lambda w: pl.BlockSpec((rows, w), lambda i: (i, 0))
    return pl.pallas_call(
        memory_grad_kernel,
        grid=(keys // rows,),
        in_specs=[rowspec(width // 2)] * 4 + [part(weights, index, width, 0), part(weights, index + 1, width, 0)] + [apart] * len(after),
        out_specs=rowspec(width),
        out_shape=jax.ShapeDtypeStruct((keys, width), bf16),
        name="memory_grad",
        **params(4, 24),
    )(ka, kb, va, vb, weights, weights, *after)


def between_kernel(
    core_ref, gckv_ref, gn23_ref, r1_ref, dr2_ref, dr3_ref, dqa_ref, dqb_ref, h1b_ref, oa_ref, ob_ref, wso_ref, wcq_ref, norms_ref, *rest
):
    dsum_ref, do1_ref, delta_ref, keep_ref, send_ref, gn_ref, total = rest[-7:]
    step = pl.program_id(0)

    @pl.when(step == 0)
    def _():
        total[...] = jnp.zeros_like(total)
        gn_ref[...] = jnp.zeros_like(gn_ref)

    dq2 = jnp.concatenate([dqa_ref[...], dqb_ref[...]], axis=1)
    dh1 = dr2_ref[...] + mm(dq2, wcq_ref[0], NT)
    n1, rstd1 = norm_rows(r1_ref[...])
    gn_ref[0:1, :] += column_sums(dh1 * n1)
    gn_ref[1:2, :] += column_sums(dh1)
    dr1 = norm_back(dh1, n1, rstd1, norms_ref[0:1, :])
    dsum_ref[...] = dr1 + dr3_ref[...]
    da1 = dr1.astype(bf16)
    o1 = jnp.concatenate([oa_ref[...], ob_ref[...]], axis=1)
    do1 = mm(da1, wso_ref[0], NT).astype(bf16)
    do1_ref[...] = do1
    delta_ref[...] = head_sums(do1, o1)
    total[0] += mm(h1b_ref[...], dq2, TN)
    total[1] += mm(o1, da1, TN)

    @pl.when(step == pl.num_programs(0) - 1)
    def _():
        gn_ref[2:6, :] = gn23_ref[...]
        r, width = keep_ref.shape[2:]
        norm_part = jnp.concatenate([gn_ref[...], jnp.zeros((r - 8, width), f32)]).astype(bf16)

        def write(device, ref, j):
            here = pl.ds(pl.multiple_of(device * r, r), r)
            for i in range(2):
                ref[j, i] = gckv_ref[i, here, :]
                ref[j, 2 + i] = total[i, here, :].astype(bf16)
            ref[j, 4] = norm_part

        spread(keep_ref, send_ref, core_ref[0], write)


def between(core, pairs, gckv, gn23, r1, dr2, dr3, dqa, dqb, h1b, oa, ob, weights, norms, after, rows=256):
    total, width = r1.shape
    heads = width // HD
    rowspec = lambda w: pl.BlockSpec((rows, w), lambda i: (i, 0))
    sds = jax.ShapeDtypeStruct
    side = sds((pairs, 5, width // (2 * pairs), width), bf16)
    return pl.pallas_call(
        between_kernel,
        grid=(total // rows,),
        in_specs=[pl.BlockSpec(memory_space=pltpu.SMEM), whole(gckv), whole(gn23)]
        + [rowspec(width)] * 3 + [rowspec(width // 2)] * 2 + [rowspec(width)] + [rowspec(width // 2)] * 2
        + [part(weights, 0, width, 0), part(weights, 1, width, 0), whole(norms)] + [apart] * len(after),
        out_specs=[rowspec(width)] * 2
        + [pl.BlockSpec((heads, rows), lambda i: (0, i)), whole(side), whole(side), pl.BlockSpec((8, width), lambda i: (0, 0))],
        out_shape=[sds((total, width), f32), sds((total, width), bf16), sds((heads, total), f32), side, side, sds((8, width), f32)],
        scratch_shapes=[pltpu.VMEM((2, width, width), f32)],
        name="between",
        **params(7, 32),
    )(core, gckv, gn23, r1, dr2, dr3, dqa, dqb, h1b, oa, ob, weights, weights, norms, *after)


def self_backward_kernel(
    block, half, q_ref, k_ref, v_ref, do_ref, l_ref, delta_ref, idr_ref, x_ref, wq_ref, wk_ref, wv_ref, sofar_ref, *rest
):
    if half:
        core_ref, before_ref = rest[:2]
        gx_ref, keep_ref, send_ref, dq, dk, dv, total_grad = rest[-7:]
    else:
        gx_ref, grads_ref, dq, dk, dv, total_grad = rest[-6:]
    step = pl.program_id(0)
    rows, width = k_ref.shape
    total = q_ref.shape[0]
    window = MOST + block
    pairs = width // LANES

    @pl.when(step == 0)
    def _():
        dq[...] = jnp.zeros_like(dq)
        total_grad[...] = jnp.zeros_like(total_grad)

    base = pl.multiple_of(step * rows, rows)
    low_k = lane_below(block)
    for sub in range(rows // block):
        here = slice(sub * block, (sub + 1) * block)
        start = pl.multiple_of(jnp.minimum(base + sub * block, total - window), LANES)
        at = pl.ds(start, window)
        pos_k = base + sub * block + lax.broadcasted_iota(jnp.int32, (block, window), 0)
        pos_q = start + lax.broadcasted_iota(jnp.int32, (block, window), 1)
        ids_k = column_of(idr_ref[:, pl.ds(base + sub * block, block)])[:, :1]
        bias = jnp.where((ids_k == idr_ref[:, at]) & (pos_k <= pos_q), 0.0, masked_score).astype(f32)
        for p in range(pairs):
            cols = slice(p * LANES, (p + 1) * LANES)
            logs = [l_ref[2 * p + h : 2 * p + h + 1, at] for h in range(2)]
            heads = [2 * (half * pairs + p) + h for h in range(2)]
            deltas = [delta_ref[h : h + 1, at] for h in heads]
            hk, hv, hq = tile_back(
                k_ref[here, cols], v_ref[here, cols], q_ref[at, cols] * jnp.asarray(HD ** -0.5, bf16), do_ref[at, cols],
                bias, logs, deltas, low_k,
            )
            dk[here, cols] = hk.astype(bf16)
            dv[here, cols] = hv.astype(bf16)
            dq[at, cols] += hq
    x = x_ref[...]
    grads = (dq[pl.ds(base, rows), :] * HD ** -0.5).astype(bf16), dk[...], dv[...]
    gx = sofar_ref[...]
    for i, (grad, w_ref) in enumerate(zip(grads, (wq_ref, wk_ref, wv_ref))):
        gx += mm(grad, w_ref[0], NT)
        total_grad[i] += mm(x, grad, TN)
    gx_ref[...] = gx.astype(gx_ref.dtype)

    @pl.when(step == pl.num_programs(0) - 1)
    def _():
        if not half:
            grads_ref[...] = total_grad[...].astype(bf16)
            return
        r = keep_ref.shape[2]

        def write(device, ref, j):
            place = pl.ds(pl.multiple_of(device * r, r), r)
            for i in range(3):
                ref[j, i, :, :width] = before_ref[i, place, :]
                ref[j, i, :, width:] = total_grad[i, place, :].astype(bf16)

        spread(keep_ref, send_ref, core_ref[0], write)


def self_backward(q, k, v, do, l, delta, idr, x, weights, sofar, half, after, core=None, before=None, pairs=1, rows=256, block=256):
    total, width = x.shape
    columns = width // 2
    kind = bf16 if half else f32
    sides = [jax.ShapeDtypeStruct((pairs, 3, width // (2 * pairs), width), bf16)] * 2
    if not half:
        sides = [jax.ShapeDtypeStruct((3, width, columns), bf16)]
    more = [core, before] if half else []
    rowspec = lambda w: pl.BlockSpec((rows, w), lambda i: (i, 0))
    sds = jax.ShapeDtypeStruct
    return pl.pallas_call(
        functools.partial(self_backward_kernel, block, half),
        grid=(total // rows,),
        in_specs=[whole(q), rowspec(columns), rowspec(columns), pl.BlockSpec((total, columns), lambda i: (0, half)), whole(l), whole(delta), whole(idr), rowspec(width)]
        + [part(weights, i, columns, half) for i in range(3)] + [rowspec(width)]
        + ([pl.BlockSpec(memory_space=pltpu.SMEM), whole(before)] if half else []) + [apart] * len(after),
        out_specs=[rowspec(width)] + [whole(side) for side in sides],
        out_shape=[sds((total, width), kind)] + sides,
        scratch_shapes=[pltpu.VMEM((total, columns), f32), pltpu.VMEM((rows, columns), bf16), pltpu.VMEM((rows, columns), bf16), pltpu.VMEM((3, width, columns), f32)],
        name="self_backward",
        **params(10, 40),
    )(q, k, v, do, l, delta, idr, x, weights, weights, weights, sofar, *more, *after)


def add_split_kernel(count, here_ref, *refs):
    places = refs[0].shape[1]
    for m in range(places):
        at = here_ref[0] ^ m
        total = refs[0][:, at].astype(f32)
        for ref in refs[1:count]:
            total += ref[:, at].astype(f32)
        refs[count + m][...] = total.astype(bf16)


def add_split(here, parts, outer, places):
    tail = parts[0].shape[1:]
    parts = [p.reshape((outer, places) + tail) for p in parts]
    out = pl.pallas_call(
        functools.partial(add_split_kernel, len(parts)),
        grid=(outer,),
        in_specs=[pl.BlockSpec(memory_space=pltpu.SMEM)] + [pl.BlockSpec((1, places) + tail, lambda i: (i, 0, 0, 0, 0))] * len(parts),
        out_specs=[pl.BlockSpec((1,) + tail, lambda i: (i, 0, 0, 0))] * places,
        out_shape=[jax.ShapeDtypeStruct((outer,) + tail, bf16)] * places,
        name="add_split",
        **params(3, 24),
    )(here, *parts)
    return list(out)


def segment_ids(lengths, row_count):
    ends = jnp.cumsum(lengths)
    places = jnp.arange(row_count, dtype=jnp.int32)
    return jnp.sum((places[:, None] >= ends[None, :]).astype(jnp.int32), axis=1)


def cross_ranges(seg, mem, total, rows, tile):
    ends = jnp.cumsum(seg)
    starts = jnp.arange(0, total, rows, dtype=jnp.int32)
    head = starts[:, None] >= ends[None, :]
    tail = (starts + rows - 1)[:, None] >= ends[None, :]
    mem = mem[: seg.shape[0]]
    low = jnp.sum(jnp.where(head, mem[None, :], 0), axis=1)
    before = jnp.concatenate([jnp.ones((starts.shape[0], 1), bool), tail[:, :-1]], axis=1)
    high = jnp.sum(jnp.where(before, mem[None, :], 0), axis=1)
    first = low // LANES
    count = (high - first * LANES + tile - 1) // tile
    return jnp.stack([first, count]).astype(jnp.int32)


def mesh_size():
    return lax.axis_size("dp") * lax.axis_size("fsdp")


def position():
    return lax.axis_index("dp") * lax.axis_size("fsdp") + lax.axis_index("fsdp")


def bit_groups():
    count = mesh_size().bit_length() - 1
    groups = [(0, 1)]
    while groups[-1][0] + groups[-1][1] < count:
        low = groups[-1][0] + groups[-1][1]
        groups.append((low, min(2, count - low)))
    return groups


def swap(x, mask):
    return lax.ppermute(x, ("dp", "fsdp"), [(i, i ^ mask) for i in range(mesh_size())])


def place_in(group):
    return (position() >> group[0]) & ((1 << group[1]) - 1)


def tie(x, *after):
    return lax.optimization_barrier((x, *after))[0] if after else x


def gather_step(x, group):
    low, width = group
    here = place_in(group)
    blocks = [x] + [swap(x, m << low) for m in range(1, 1 << width)]
    for j in range(width):
        flip = (here >> j) & 1 == 1
        blocks = [jnp.where(flip, blocks[p ^ (1 << j)], blocks[p]) for p in range(1 << width)]
    return jnp.stack(blocks, axis=x.ndim - 2)


def gathered(x):
    return x.reshape(x.shape[:1] + (-1, x.shape[-1]))


def swap_pieces(parts, group, after=()):
    return [parts[0]] + tie([swap(parts[m], m << group[0]) for m in range(1, len(parts))], *after)


def next_pieces(parts, groups, done):
    group = groups[done]
    outer = 1 << sum(g[1] for g in groups[done + 1 :])
    return add_split(place_in(group).reshape(1).astype(jnp.int32), parts, outer, 1 << group[1])


def norm_parts(norm_params, size):
    parts, left = [], norm_params
    for _ in range(3):
        part = left.astype(bf16)
        parts.append(part)
        left = left - part.astype(f32)
    flat = jnp.concatenate(parts)
    return jnp.pad(flat, (0, size - flat.size))


def resplit(keep, send, devices, core, squares):
    halves = jnp.concatenate([keep, send])
    width = halves.shape[-1]
    first = halves[:, :squares].transpose(1, 0, 2, 3).reshape(squares, devices, -1, width).transpose(1, 0, 2, 3)
    rows = first.shape[2]
    if halves.shape[1] > squares:
        rest = halves[:, squares:].reshape(devices, halves.shape[1] - squares, rows, width)
        first = jnp.concatenate([first, rest], axis=1)
    both = first.reshape(devices // 2, 2, -1, rows, width)
    return [lax.dynamic_index_in_dim(both, core ^ m, 1, keepdims=False) for m in range(2)]


def body(
    inputs, memory, seg_lengths, mem_lengths, self_query, self_key, self_value, self_out,
    cross_query, cross_key, cross_value, cross_out, ffn_in, ffn_out, norm_params, cotangent,
):
    total, width = inputs.shape
    keys = memory.shape[0]
    devices = mesh_size()
    groups = bit_groups()
    down = groups[::-1]
    tile = 256
    shard = norm_params.shape[0]
    size = self_query.shape[0]
    own_rows = size // width
    blocks = ffn_in.shape[0] // size
    whole_tiles = own_rows % 16 == 0
    core = place_in(groups[0]).reshape(1).astype(jnp.int32)

    first = jnp.concatenate([self_query, self_key, self_value]).reshape(3, own_rows, width)
    others = jnp.concatenate(
        [self_out, cross_query, cross_out, cross_key, cross_value, norm_parts(norm_params, size), ffn_out, ffn_in]
    ).reshape(-1, own_rows, width)
    second = others[:6]
    fi = others[6 + blocks :].reshape(own_rows, blocks, width).transpose(1, 0, 2)
    ffn_own = jnp.concatenate([fi, others[6 : 6 + blocks]]).reshape(-1, width)
    first = gather_step(first, down[0])
    second, ffn_own = tie((second, ffn_own), first)
    for g in down[1:]:
        second = gather_step(second, down[down.index(g) - 1])
        first = gather_step(first, g)
        if g == down[-2]:
            ffn_own = tie(ffn_own, first)
        second = tie(second, first)
    first = gathered(first)
    ffn_all = lax.all_gather(ffn_own, ("dp", "fsdp"), axis=0, tiled=True).reshape(devices, 2 * blocks, own_rows, width)
    if not whole_tiles:
        fi = ffn_all[:, :blocks].transpose(1, 0, 2, 3).reshape(1, blocks, width, width)
        ffn_all = jnp.concatenate([fi, ffn_all[:, blocks:].reshape(1, blocks, width, width)], axis=1)
    pairs = devices // 2 if whole_tiles else 1
    part_of = core if whole_tiles else jnp.zeros_like(core)

    qid, mid = segment_ids(seg_lengths[0], total)[None, :], segment_ids(mem_lengths[0], keys)[None, :]
    ranges = cross_ranges(seg_lengths[0], mem_lengths[0], total, 256, tile)

    qa, ka, va, oa, la = self_forward(inputs, first, qid, 0, [])
    qb, kb, vb, ob, lb = self_forward(inputs, first, qid, 1, [second, la])
    second = gathered(gather_step(second, down[-1]))
    norm_all = second[5].reshape(devices, -1)[:, : 3 * shard].astype(f32).reshape(devices, 3, shard)
    norms = jnp.sum(norm_all, axis=1).reshape(6, width)
    k2, v2 = project_memory(memory, second, 3)
    r1, h1b, q2, o2, l2, r2 = cross_forward(ranges, inputs, oa, ob, second, norms, k2, v2, qid, mid, tile=tile)
    out, dr3, dr2, do2, delta2, keep, send, gn23 = ffn(part_of, pairs, r2, inputs, cotangent, o2, ffn_all, second, 2, norms)

    one = [keep, send] if whole_tiles else resplit(keep, send, devices, core[0], blocks + 1)
    dq2a, dk2a, dv2a = cross_backward(ranges, q2, k2, v2, do2, l2, delta2, qid, mid, 0, [one[1]], tile=tile)
    one = next_pieces(swap_pieces(one, groups[0], [dq2a]), groups, 1)
    dq2b, dk2b, dv2b = cross_backward(ranges, q2, k2, v2, do2, l2, delta2, qid, mid, 1, one[1:], tile=tile)
    gckv = memory_weights(memory, dk2a, dk2b, dv2a, dv2b, [])
    dsum, do1, delta1, keep, send, gn = between(
        part_of, pairs, gckv, gn23, r1, dr2, dr3, dq2a, dq2b, h1b, oa, ob, second, norms, []
    )
    two = [keep, send]
    if not whole_tiles:
        two = resplit(keep, send, devices, core[0], 5)
        own_norms = jnp.pad(gn[:6].astype(bf16).reshape(devices, -1), ((0, 0), (0, size - shard)))
        own_norms = own_norms.reshape(devices // 2, 2, own_rows, width)
        two = [two[m].at[:, 4].set(lax.dynamic_index_in_dim(own_norms, core[0] ^ m, 1, keepdims=False)) for m in range(2)]
    one = next_pieces(swap_pieces(one, groups[1], [do1]), groups, 2)
    gxa, gsa = self_backward(qa, ka, va, do1, la, delta1, qid, inputs, first, dsum, 0, one[1:] + [two[1]])
    two = next_pieces(swap_pieces(two, groups[0], [gsa]), groups, 1)
    gx, keep, send = self_backward(
        qb, kb, vb, do1, lb, delta1, qid, inputs, first, gxa, 1, two[1:], core=part_of, before=gsa, pairs=pairs
    )
    three = [keep, send] if whole_tiles else resplit(keep, send, devices, core[0], 3)
    three = next_pieces(swap_pieces(three, groups[0]), groups, 1)
    two = next_pieces(swap_pieces(two, groups[1], [gx]), groups, 2)
    gm = memory_grad(dk2a, dk2b, dv2a, dv2b, second, 3, three[1:])
    for i in range(2, len(groups)):
        three = next_pieces(swap_pieces(three, groups[i - 1]), groups, i)
        if i > 2:
            one = next_pieces(swap_pieces(one, groups[i - 1]), groups, i)
            two = next_pieces(swap_pieces(two, groups[i - 1]), groups, i)
    one, two, three = (
        sum(p.astype(f32) for p in swap_pieces(chain, groups[-1])).reshape(-1, own_rows, width) for chain in (one, two, three)
    )

    def flat(g):
        return g.reshape(-1)

    gn = flat(two[4])[:shard]
    if whole_tiles:
        gn = lax.dynamic_slice_in_dim(flat(two[4][:6]), position() * shard, shard)
    return (
        out, gx, gm, flat(three[0]), flat(three[1]), flat(three[2]), flat(two[3]),
        flat(two[2]), flat(two[0]), flat(two[1]), flat(one[blocks]), flat(one[:blocks].transpose(1, 0, 2)), flat(one[blocks + 1 :]), gn,
    )


def solution(mesh):
    rows, flat = P(("dp", "fsdp"), None), P(("dp", "fsdp"))
    return jax.shard_map(
        body,
        mesh=mesh,
        in_specs=(rows,) * 4 + (flat,) * 11 + (rows,),
        out_specs=(rows,) * 3 + (flat,) * 11,
        check_vma=False,
    )
```

```python
import functools
import jax
import jax.numpy as jnp
from jax import lax
from jax.experimental import pallas as pl
from jax.experimental.pallas import tpu as pltpu
from jax.sharding import PartitionSpec as P

HD = 64
LANES = 128
MOST = 256
QROWS = 128
FORWARD_ITEMS = 2
BACKWARD_ITEMS = 3
FFN_CHUNK = 256
masked_score = -1e30
norm_eps = 1e-05
bf16, f32 = jnp.bfloat16, jnp.float32
NT = (((1,), (1,)), ((), ()))
TN = (((0,), (0,)), ((), ()))
NN = (((1,), (0,)), ((), ()))


def mm(left, right, dims=NN):
    return lax.dot_general(left, right, dims, preferred_element_type=f32)


def norm_rows(source):
    mean = jnp.mean(source, axis=-1, keepdims=True)
    centered = source - mean
    variance = jnp.mean(centered * centered, axis=-1, keepdims=True)
    rstd = lax.rsqrt(variance + norm_eps)
    return centered * rstd, rstd


def lane_below(rows):
    return lax.broadcasted_iota(jnp.int32, (rows, LANES), 1) < HD


def column_of(row):
    return jnp.broadcast_to(row, (LANES, row.shape[1])).T


def head_part(pair, which, low):
    return jnp.where(low == (which == 0), pair, jnp.zeros_like(pair))


def values_with_ones(values):
    parts = []
    for p in range(values.shape[1] // LANES):
        pair = values[:, p * LANES : (p + 1) * LANES]
        parts += [pair, jnp.ones_like(pair)]
    return jnp.concatenate(parts, axis=1)


def finish_heads(at, top, tot, acc, write):
    shape = acc.shape[0], at.size if hasattr(at, "size") else at.stop - at.start, LANES
    lane = lax.broadcasted_iota(jnp.int32, shape[1:], 1)
    sums, tops = jnp.ones(shape[1:], f32), jnp.zeros(shape[1:], f32)
    for p in range(shape[0]):
        total = tot[p, at, :]
        write(p, (acc[p, at, :] / total).astype(bf16))
        sums = jnp.where(lane % HD == p, total, sums)
        tops = jnp.where(lane == p, top[2 * p, at, :], jnp.where(lane == HD + p, top[2 * p + 1, at, :], tops))
    return tops + jnp.log(sums)


def column_at(head):
    return head % 2 * HD + head // 2


def item_at(items_ref, n, idk_ref, ids_q, keys, tile, block, causal):
    begin = pl.multiple_of(items_ref[0, n] * block, block)
    wanted = items_ref[1, n] * LANES
    start = pl.multiple_of(jnp.minimum(wanted, keys - tile), LANES)
    at = pl.ds(begin, block)
    pos = start + lax.broadcasted_iota(jnp.int32, (1, tile), 1)
    ids_k = jnp.where(pos >= wanted, idk_ref[:, pl.ds(start, tile)], -1)
    allowed = ids_q[at, :1] == ids_k
    if causal:
        allowed &= pos <= begin + lax.broadcasted_iota(jnp.int32, (block, 1), 0)
    return at, pl.ds(start, tile), jnp.where(allowed, 0.0, masked_score).astype(f32)


def attend(items_ref, idk_ref, ids_q, q_all, k_all, vx_all, top, tot, acc, tile, block, causal):
    keys, width = k_all.shape
    pairs = width // LANES
    heads = 2 * pairs
    low = lane_below(block)
    top[...] = jnp.full(top.shape, masked_score, f32)
    tot[...] = jnp.zeros(tot.shape, f32)
    acc[...] = jnp.zeros(acc.shape, f32)

    def some(i, _):
        loads, made = [], []
        for t in range(FORWARD_ITEMS):
            at, there, bias = item_at(items_ref, FORWARD_ITEMS * i + t, idk_ref, ids_q, keys, tile, block, causal)
            loads.append((at, there, bias))
            for p in range(pairs):
                cols = slice(p * LANES, (p + 1) * LANES)
                part = q_all[at, cols]
                both = jnp.concatenate([head_part(part, h, low) for h in range(2)])
                made.append(mm(both, k_all[there, cols], NT))
        weights, scales = [], []
        for t, (at, there, bias) in enumerate(loads):
            for head in range(heads):
                s = made[t * pairs + head // 2][head % 2 * block : (head % 2 + 1) * block] + bias
                old = top[head, at, :]
                new = jnp.maximum(old, jnp.max(s, axis=1, keepdims=True))
                top[head, at, :] = new
                scales.append(jnp.exp(old - new))
                weights.append(jnp.exp(s - jnp.concatenate([new] * (tile // LANES), axis=1)).astype(bf16))
        mixed = [
            mm(jnp.concatenate(weights[t * heads + 2 * p : t * heads + 2 * p + 2]), vx_all[there, 2 * p * LANES : 2 * (p + 1) * LANES])
            for t, (_, there, _) in enumerate(loads) for p in range(pairs)
        ]
        for t, (at, _, _) in enumerate(loads):
            for p in range(pairs):
                n = t * pairs + p
                scale = jnp.where(low, scales[2 * n], scales[2 * n + 1])
                o = mixed[n]
                acc[p, at, :] = acc[p, at, :] * scale + jnp.where(low, o[:block, :LANES], o[block:, :LANES])
                tot[p, at, :] = tot[p, at, :] * scale + jnp.where(low, o[:block, LANES:], o[block:, LANES:])
        return 0

    lax.fori_loop(0, items_ref[2, 0], some, 0)


def attend_back(items_ref, idk_ref, ids_q, q_all, do_ref, k_ref, v_ref, l_ref, delta_ref, dq, dk, dv, tile, block, first_log, first_head, causal):
    keys, width = k_ref.shape
    pairs = width // LANES
    low = lane_below(block)

    def some(i, _):
        loads, scores, grads = [], [], []
        for t in range(BACKWARD_ITEMS):
            at, there, bias = item_at(items_ref, BACKWARD_ITEMS * i + t, idk_ref, ids_q, keys, tile, block, causal)
            loads.append((at, there, bias))
            for p in range(pairs):
                cols = slice(p * LANES, (p + 1) * LANES)
                q, do = q_all[at, cols], do_ref[at, cols]
                qs = jnp.concatenate([head_part(q, h, low) for h in range(2)])
                dos = jnp.concatenate([head_part(do, h, low) for h in range(2)])
                scores.append((mm(qs, k_ref[there, cols], NT), qs))
                grads.append((mm(dos, v_ref[there, cols], NT), dos))
        weights, slopes = [], []
        for t, (at, there, bias) in enumerate(loads):
            logs, deltas = l_ref[at, :], delta_ref[at, :]
            for p in range(pairs):
                es, ds = [], []
                for h in range(2):
                    lane = column_at(first_log + 2 * p + h)
                    other = column_at(first_head + 2 * p + h)
                    rows = slice(h * block, (h + 1) * block)
                    e = jnp.exp(scores[t * pairs + p][0][rows] + bias - logs[:, lane : lane + 1])
                    es.append(e.astype(bf16))
                    ds.append((e * (grads[t * pairs + p][0][rows] - deltas[:, other : other + 1])).astype(bf16))
                weights.append(jnp.concatenate(es))
                slopes.append(jnp.concatenate(ds))
        for t, (at, there, _) in enumerate(loads):
            for p in range(pairs):
                cols = slice(p * LANES, (p + 1) * LANES)
                n = t * pairs + p
                gq = mm(slopes[n], k_ref[there, cols])
                gk = mm(slopes[n], scores[n][1], TN)
                gv = mm(weights[n], grads[n][1], TN)
                dq[at, cols] += jnp.where(low, gq[:block], gq[block:])
                dk[there, cols] += gk
                dv[there, cols] += gv
        return 0

    lax.fori_loop(0, items_ref[3, 0], some, 0)


def self_forward_kernel(tile, block, items_ref, x_ref, wq_ref, wk_ref, wv_ref, idr_ref, *rest):
    q_ref, k_ref, v_ref, o_ref, l_ref, q_all, k_all, vx_all, ids_all, top, tot, acc = rest[-12:]
    step = pl.program_id(0)
    rows = x_ref.shape[0]
    total, width = k_all.shape
    turns = total // rows

    @pl.when(step < turns)
    def _():
        x = x_ref[...]
        q = mm(x, wq_ref[0]).astype(bf16)
        k = mm(x, wk_ref[0]).astype(bf16)
        v = mm(x, wv_ref[0]).astype(bf16)
        q_ref[...] = q
        k_ref[...] = k
        v_ref[...] = v
        here = pl.ds(pl.multiple_of(step * rows, rows), rows)
        q_all[here, :] = q * jnp.asarray(HD ** -0.5, bf16)
        k_all[here, :] = k
        vx_all[here, :] = values_with_ones(v)
        ids_all[here, :] = column_of(idr_ref[:, here])

    @pl.when(step == turns)
    def _():
        attend(items_ref, idr_ref, ids_all, q_all, k_all, vx_all, top, tot, acc, tile, block, True)
        size = 2 * block
        for j in range(total // size):
            at = slice(j * size, (j + 1) * size)

            def write(p, value):
                o_ref[at, p * LANES : (p + 1) * LANES] = value

            l_ref[at, :] = finish_heads(at, top, tot, acc, write)


def whole(a):
    return pl.BlockSpec(a.shape, lambda *_: (0,) * a.ndim)


def part(weights, index, columns, half):
    return pl.BlockSpec((1, weights.shape[1], columns), lambda *_: (index, 0, half))


def params(us, vmem):
    return dict(
        compiler_params=pltpu.CompilerParams(vmem_limit_bytes=vmem * 2**20),
        cost_estimate=pl.CostEstimate(flops=us * 10**9, bytes_accessed=2**20, transcendentals=0),
    )


apart = pl.BlockSpec(memory_space=pl.ANY)


def out_array(shape, dtype):
    return pltpu.HBM(shape, dtype)


def placed(*arrays):
    return [pltpu.with_memory_space_constraint(a, pltpu.HBM) for a in arrays]


def self_forward(items, x, weights, idr, half, after, turns=4, block=QROWS, tile=256):
    total, width = x.shape
    columns = width // 2
    heads = columns // HD
    rows = total // turns
    early = lambda w: pl.BlockSpec((rows, w), lambda i, *_: (jnp.minimum(i, turns - 1), 0))
    fixed = lambda w: pl.BlockSpec((total, w), lambda i, *_: (0, 0))
    sds = out_array
    full = sds((total, columns), bf16)
    return pl.pallas_call(
        functools.partial(self_forward_kernel, tile, block),
        grid_spec=pltpu.PrefetchScalarGridSpec(
            num_scalar_prefetch=1,
            grid=(turns + 1,),
            in_specs=[early(width)] + [part(weights, i, columns, half) for i in range(3)] + [whole(idr)] + [apart] * len(after),
            out_specs=[early(columns)] * 3 + [fixed(columns), fixed(LANES)],
            scratch_shapes=[
                pltpu.VMEM((total, columns), bf16), pltpu.VMEM((total, columns), bf16), pltpu.VMEM((total, 2 * columns), bf16),
                pltpu.VMEM((total, LANES), jnp.int32),
                pltpu.VMEM((heads, total, LANES), f32), pltpu.VMEM((heads // 2, total, LANES), f32), pltpu.VMEM((heads // 2, total, LANES), f32),
            ],
        ),
        out_shape=[full] * 4 + [sds((total, LANES), f32)],
        name="self_forward",
        **params(6, 24),
    )(items, *placed(x, weights, weights, weights), idr, *after)


def cross_forward_kernel(
    tile, block, items_ref, memory_ref, wk_ref, wv_ref, x_ref, oa_ref, ob_ref, wso_ref, wcq_ref, wco_ref, norms_ref, idr_ref, idk_ref,
    k2_ref, v2_ref, r1_ref, h1b_ref, q2_ref, o_ref, l_ref, r2_ref, k_all, vx_all, q_all, h_all, ids_all, top, tot, acc,
):
    step = pl.program_id(0)
    rows, width = x_ref.shape
    keys = k_all.shape[0]
    turns = pl.num_programs(0) // 2

    @pl.when(step < turns)
    def _():
        per = memory_ref.shape[0]
        memory = memory_ref[...]
        half = width // 2
        r1 = x_ref[...].astype(f32) + mm(oa_ref[...], wso_ref[0, :half, :]) + mm(ob_ref[...], wso_ref[0, half:, :])
        k2 = mm(memory, wk_ref[0]).astype(bf16)
        r1_ref[...] = r1.astype(bf16)
        n1, _ = norm_rows(r1)
        v2 = mm(memory, wv_ref[0]).astype(bf16)
        h1 = n1 * norms_ref[0:1, :] + norms_ref[1:2, :]
        h1b = h1.astype(bf16)
        h1b_ref[...] = h1b
        q2 = mm(h1b, wcq_ref[0]).astype(bf16)
        q2_ref[...] = q2
        k2_ref[...] = k2
        v2_ref[...] = v2
        here = pl.ds(pl.multiple_of(step * rows, rows), rows)
        q_all[here, :] = q2 * jnp.asarray(HD ** -0.5, bf16)
        h_all[here, :] = h1
        ids_all[here, :] = column_of(idr_ref[:, here])
        there = pl.ds(pl.multiple_of(step * per, per), per)
        k_all[there, :] = k2
        vx_all[there, :] = values_with_ones(v2)

    @pl.when(step == turns)
    def _():
        attend(items_ref, idk_ref, ids_all, q_all, k_all, vx_all, top, tot, acc, tile, block, False)

    @pl.when(step >= turns)
    def _():
        for sub in range(rows // block):
            inner = slice(sub * block, (sub + 1) * block)
            at = pl.ds(pl.multiple_of((step - turns) * rows + sub * block, block), block)

            def write(p, value):
                o_ref[inner, p * LANES : (p + 1) * LANES] = value

            l_ref[inner, :] = finish_heads(at, top, tot, acc, write)
        here = pl.ds(pl.multiple_of((step - turns) * rows, rows), rows)
        r2_ref[...] = h_all[here, :] + mm(o_ref[...], wco_ref[0])


def cross_forward(items, memory, x, oa, ob, weights, norms, idr, idk, turns=4, block=QROWS, tile=256):
    total, width = x.shape
    keys = memory.shape[0]
    heads = width // HD
    rows, per = total // turns, keys // turns
    early = lambda r, w: pl.BlockSpec((r, w), lambda i, *_: (jnp.minimum(i, turns - 1), 0))
    late = lambda w: pl.BlockSpec((rows, w), lambda i, *_: (jnp.maximum(i - turns, 0), 0))
    sds = out_array
    return pl.pallas_call(
        functools.partial(cross_forward_kernel, tile, block),
        grid_spec=pltpu.PrefetchScalarGridSpec(
            num_scalar_prefetch=1,
            grid=(2 * turns,),
            in_specs=[early(per, width), part(weights, 3, width, 0), part(weights, 4, width, 0)]
            + [early(rows, width), early(rows, width // 2), early(rows, width // 2)]
            + [part(weights, i, width, 0) for i in range(3)]
            + [whole(norms), whole(idr), whole(idk)],
            out_specs=[early(per, width)] * 2 + [early(rows, width)] * 3 + [late(width), late(LANES), late(width)],
            scratch_shapes=[
                pltpu.VMEM((keys, width), bf16),
                pltpu.VMEM((keys, 2 * width), bf16),
                pltpu.VMEM((total, width), bf16),
                pltpu.VMEM((total, width), f32),
                pltpu.VMEM((total, LANES), jnp.int32),
                pltpu.VMEM((heads, total, LANES), f32),
                pltpu.VMEM((heads // 2, total, LANES), f32),
                pltpu.VMEM((heads // 2, total, LANES), f32),
            ],
        ),
        out_shape=[
            sds((keys, width), bf16), sds((keys, width), bf16), sds((total, width), bf16), sds((total, width), bf16),
            sds((total, width), bf16), sds((total, width), bf16), sds((total, LANES), f32), sds((total, width), f32),
        ],
        name="cross_forward",
        **params(24, 44),
    )(items, *placed(memory, weights, weights, x, oa, ob, weights, weights, weights), norms, idr, idk)


def norm_back(incoming, normal, rstd, gain):
    m = incoming * gain
    return rstd * (
        m - jnp.mean(m, axis=-1, keepdims=True) - normal * jnp.mean(m * normal, axis=-1, keepdims=True)
    )


def head_columns(left, right):
    width = left.shape[1]
    prod = left.astype(f32) * right.astype(f32)
    lane = lax.broadcasted_iota(jnp.int32, (width, LANES), 1)
    own = lax.broadcasted_iota(jnp.int32, (width, LANES), 0) // HD == 2 * (lane % HD) + lane // HD
    own = own.astype(bf16)
    high = prod.astype(bf16)
    low = (prod - high.astype(f32)).astype(bf16)
    return mm(high, own) + mm(low, own)


def column_sums(a):
    return jnp.sum(a, axis=0, keepdims=True)


def spread(keep_ref, send_ref, core, write):
    def one(j, _):
        write(2 * j + core, keep_ref, j)
        write(2 * j + 1 - core, send_ref, j)
        return 0

    lax.fori_loop(0, keep_ref.shape[0], one, 0)


def ffn_kernel(
    core_ref, r2_ref, x_ref, cot_ref, o2_ref, w_ref, wco_ref, norms_ref,
    out_ref, dr3_ref, dr2_ref, do2_ref, delta_ref, keep_ref, send_ref, gn_ref, gin, gout, gco,
):
    step = pl.program_id(0)
    last = pl.num_programs(0) - 1
    width = x_ref.shape[1]
    blocks = w_ref.shape[1] // 2

    @pl.when(step == 0)
    def _():
        gin[...] = jnp.zeros_like(gin)
        gout[...] = jnp.zeros_like(gout)
        gco[...] = jnp.zeros_like(gco)
        gn_ref[...] = jnp.zeros_like(gn_ref)

    win = [w_ref[:, c].reshape(width, width) for c in range(blocks)]
    wout = w_ref[:, blocks:].reshape(blocks * width, width)
    n2, rstd2 = norm_rows(r2_ref[...])
    h2 = n2 * norms_ref[2:3, :] + norms_ref[3:4, :]
    h2b = h2.astype(bf16)
    chunk = min(FFN_CHUNK, width)
    parts = blocks * width // chunk
    per = width // chunk

    def win_part(c):
        return win[c // per][:, (c % per) * chunk : (c % per + 1) * chunk]

    acts, slopes, hidden = [], [], [mm(h2b, win_part(0))]
    ff = jnp.zeros(h2.shape, f32)
    for c in range(parts):
        if c + 1 < parts:
            hidden.append(mm(h2b, win_part(c + 1)))
        u = hidden[c]
        square = u * u
        t = jnp.tanh(u * (0.7978845608028654 + (0.7978845608028654 * 0.044715) * square))
        half = 0.5 + 0.5 * t
        acts.append((u * half).astype(bf16))
        rise = u * (0.5 * 0.7978845608028654 + (0.5 * 0.7978845608028654 * 3 * 0.044715) * square)
        slopes.append(half + (1.0 - t * t) * rise)
        if c:
            ff += mm(acts[c - 1], wout[(c - 1) * chunk : c * chunk, :])
    ff += mm(acts[-1], wout[(parts - 1) * chunk :, :])
    r3 = h2 + ff + x_ref[...].astype(f32)
    n3, rstd3 = norm_rows(r3)
    gain3 = norms_ref[4:5, :]
    out_ref[...] = (n3 * gain3 + norms_ref[5:6, :]).astype(bf16)
    e = cot_ref[...].astype(f32)
    gn_ref[2:3, :] += column_sums(e * n3)
    gn_ref[3:4, :] += column_sums(e)
    dr3 = norm_back(e, n3, rstd3, gain3)
    dr3_ref[...] = dr3.astype(bf16)
    dfb = dr3.astype(bf16)
    dh2 = dr3
    raw, made = [mm(dfb, wout[:chunk, :], NT)], []
    for c in range(parts + 1):
        if c + 1 < parts:
            raw.append(mm(dfb, wout[(c + 1) * chunk : (c + 2) * chunk, :], NT))
        if c < parts:
            gout[c * chunk : (c + 1) * chunk, :] += mm(acts[c], dfb, TN)
            made.append((raw[c] * slopes[c]).astype(bf16))
        if c:
            gin[:, (c - 1) * chunk : c * chunk] += mm(h2b, made[c - 1], TN)
            dh2 += mm(made[c - 1], win_part(c - 1), NT)
    gn_ref[0:1, :] += column_sums(dh2 * n2)
    gn_ref[1:2, :] += column_sums(dh2)
    dr2 = norm_back(dh2, n2, rstd2, norms_ref[2:3, :])
    da2 = dr2.astype(bf16)
    dr2_ref[...] = da2
    o2 = o2_ref[...]
    gco[...] += mm(o2, da2, TN)
    do2 = mm(da2, wco_ref[0], NT).astype(bf16)
    do2_ref[...] = do2
    delta_ref[...] = head_columns(do2, o2)

    @pl.when(step == last)
    def _():
        r = keep_ref.shape[2]

        def write(device, ref, j):
            here = pl.ds(pl.multiple_of(device * r, r), r)
            for c in range(blocks):
                ref[j, c] = gin[here, c * width : (c + 1) * width].astype(bf16)
            ref[j, blocks] = gco[here, :].astype(bf16)
            there = pl.ds(pl.multiple_of(device * blocks * r, blocks * r), blocks * r)
            ref[j, blocks + 1 :] = gout[there, :].astype(bf16).reshape(blocks, r, width)

        spread(keep_ref, send_ref, core_ref[0], write)


def ffn(core, pairs, r2, x, cot, o2, w, weights, index, norms, rows=512):
    total, width = x.shape
    blocks = w.shape[1] // 2
    rowspec = lambda w: pl.BlockSpec((rows, w), lambda i: (i, 0))
    sds = out_array
    side = jax.ShapeDtypeStruct((pairs, 2 * blocks + 1, width // (2 * pairs), width), bf16)
    return pl.pallas_call(
        ffn_kernel,
        grid=(total // rows,),
        in_specs=[pl.BlockSpec(memory_space=pltpu.SMEM)] + [rowspec(width)] * 4 + [whole(w), part(weights, index, width, 0), whole(norms)],
        out_specs=[rowspec(width)] * 4
        + [rowspec(LANES), whole(side), whole(side), pl.BlockSpec((4, width), lambda i: (0, 0))],
        out_shape=[
            sds((total, width), bf16), sds((total, width), bf16), sds((total, width), bf16), sds((total, width), bf16),
            sds((total, LANES), f32), side, side, sds((4, width), f32),
        ],
        scratch_shapes=[pltpu.VMEM((width, blocks * width), f32), pltpu.VMEM((blocks * width, width), f32), pltpu.VMEM((width, width), f32)],
        name="ffn",
        **params(32, 50),
    )(core, *placed(r2, x, cot, o2, w, weights), norms)


def cross_backward_kernel(
    tile, block, half, items_ref, q2_ref, k2_ref, v2_ref, do_ref, l_ref, delta_ref, idr_ref, idk_ref, memory_ref, *rest
):
    dq_ref, dk_ref, dv_ref, grads_ref, q_all, ids_all, dq, dk, dv, grads = rest[-10:]
    step = pl.program_id(0)
    total, width = q2_ref.shape

    @pl.when(step == 0)
    def _():
        dq[...] = jnp.zeros_like(dq)
        dk[...] = jnp.zeros_like(dk)
        dv[...] = jnp.zeros_like(dv)
        grads[...] = jnp.zeros_like(grads)
        q_all[...] = q2_ref[...] * jnp.asarray(HD ** -0.5, bf16)
        for j in range(total // block):
            ids_all[j * block : (j + 1) * block, :] = column_of(idr_ref[:, j * block : (j + 1) * block])
        attend_back(
            items_ref, idk_ref, ids_all, q_all, do_ref, k2_ref, v2_ref, l_ref, delta_ref, dq, dk, dv, tile, block,
            2 * half * (width // LANES), 2 * half * (width // LANES), False,
        )

    memory = memory_ref[...]
    per = memory.shape[0]
    here = pl.ds(pl.multiple_of(step * per, per), per)
    for i, (ref, out_ref) in enumerate(((dk, dk_ref), (dv, dv_ref))):
        grad = ref[here, :].astype(bf16)
        out_ref[...] = grad
        grads[i] += mm(memory, grad, TN)
    rows = dq_ref.shape[0]
    dq_ref[...] = (dq[pl.ds(pl.multiple_of(step * rows, rows), rows), :] * HD ** -0.5).astype(bf16)

    @pl.when(step == pl.num_programs(0) - 1)
    def _():
        grads_ref[...] = grads[...].astype(bf16)


def cross_backward(items, q2, k2, v2, do, l, delta, idr, idk, memory, half, after, turns=4, block=QROWS, tile=256):
    total, width = q2.shape
    keys = k2.shape[0]
    columns = width // 2
    cols = lambda r: pl.BlockSpec((r, columns), lambda i, *_: (0, half))
    rowspec = lambda r, w: pl.BlockSpec((r, w), lambda i, *_: (i, 0))
    sds = out_array
    grad = jax.ShapeDtypeStruct((2, width, columns), bf16)
    return pl.pallas_call(
        functools.partial(cross_backward_kernel, tile, block, half),
        grid_spec=pltpu.PrefetchScalarGridSpec(
            num_scalar_prefetch=1,
            grid=(turns,),
            in_specs=[cols(total), cols(keys), cols(keys), cols(total)]
            + [whole(l), whole(delta), whole(idr), whole(idk), rowspec(keys // turns, width)] + [apart] * len(after),
            out_specs=[rowspec(total // turns, columns), rowspec(keys // turns, columns), rowspec(keys // turns, columns), whole(grad)],
            scratch_shapes=[
                pltpu.VMEM((total, columns), bf16), pltpu.VMEM((total, LANES), jnp.int32), pltpu.VMEM((total, columns), f32),
                pltpu.VMEM((keys, columns), f32), pltpu.VMEM((keys, columns), f32), pltpu.VMEM((2, width, columns), f32),
            ],
        ),
        out_shape=[sds((total, columns), bf16), sds((keys, columns), bf16), sds((keys, columns), bf16), grad],
        name="cross_backward",
        **params(12, 40),
    )(items, *placed(q2, k2, v2, do, l, delta), idr, idk, *placed(memory), *after)


def memory_grad_kernel(ka_ref, kb_ref, va_ref, vb_ref, wk_ref, wv_ref, *rest):
    half = ka_ref.shape[1]
    total = mm(ka_ref[...], wk_ref[0, :, :half], NT) + mm(kb_ref[...], wk_ref[0, :, half:], NT)
    total += mm(va_ref[...], wv_ref[0, :, :half], NT) + mm(vb_ref[...], wv_ref[0, :, half:], NT)
    rest[-1][...] = total.astype(bf16)


def memory_grad(ka, kb, va, vb, weights, index, after, rows=512):
    keys, width = ka.shape[0], weights.shape[2]
    rowspec = lambda w: pl.BlockSpec((rows, w), lambda i: (i, 0))
    return pl.pallas_call(
        memory_grad_kernel,
        grid=(keys // rows,),
        in_specs=[rowspec(width // 2)] * 4 + [part(weights, index, width, 0), part(weights, index + 1, width, 0)] + [apart] * len(after),
        out_specs=rowspec(width),
        out_shape=jax.ShapeDtypeStruct((keys, width), bf16),
        name="memory_grad",
        **params(4, 24),
    )(*placed(ka, kb, va, vb, weights, weights), *after)


def between_kernel(
    core_ref, ga_ref, gb_ref, gn23_ref, r1_ref, dr2_ref, dr3_ref, dqa_ref, dqb_ref, h1b_ref, oa_ref, ob_ref, wso_ref, wcq_ref, norms_ref, *rest
):
    dsum_ref, do1_ref, delta_ref, keep_ref, send_ref, gn_ref, total = rest[-7:]
    step = pl.program_id(0)

    @pl.when(step == 0)
    def _():
        total[...] = jnp.zeros_like(total)
        gn_ref[...] = jnp.zeros_like(gn_ref)

    dq2 = jnp.concatenate([dqa_ref[...], dqb_ref[...]], axis=1)
    dh1 = dr2_ref[...].astype(f32) + mm(dq2, wcq_ref[0], NT)
    n1, rstd1 = norm_rows(r1_ref[...].astype(f32))
    gn_ref[0:1, :] += column_sums(dh1 * n1)
    gn_ref[1:2, :] += column_sums(dh1)
    dr1 = norm_back(dh1, n1, rstd1, norms_ref[0:1, :])
    dsum_ref[...] = (dr1 + dr3_ref[...].astype(f32)).astype(bf16)
    da1 = dr1.astype(bf16)
    o1 = jnp.concatenate([oa_ref[...], ob_ref[...]], axis=1)
    do1 = mm(da1, wso_ref[0], NT).astype(bf16)
    do1_ref[...] = do1
    delta_ref[...] = head_columns(do1, o1)
    total[0] += mm(h1b_ref[...], dq2, TN)
    total[1] += mm(o1, da1, TN)

    @pl.when(step == pl.num_programs(0) - 1)
    def _():
        gn_ref[2:6, :] = gn23_ref[...]
        r, width = keep_ref.shape[2:]
        norm_part = jnp.concatenate([gn_ref[...], jnp.zeros((r - 8, width), f32)]).astype(bf16)

        def write(device, ref, j):
            here = pl.ds(pl.multiple_of(device * r, r), r)
            for i in range(2):
                ref[j, i, :, : width // 2] = ga_ref[i, here, :]
                ref[j, i, :, width // 2 :] = gb_ref[i, here, :]
                ref[j, 2 + i] = total[i, here, :].astype(bf16)
            ref[j, 4] = norm_part

        spread(keep_ref, send_ref, core_ref[0], write)


def between(core, pairs, ga, gb, gn23, r1, dr2, dr3, dqa, dqb, h1b, oa, ob, weights, norms, after, rows=256):
    total, width = r1.shape
    rowspec = lambda w: pl.BlockSpec((rows, w), lambda i: (i, 0))
    sds = out_array
    side = jax.ShapeDtypeStruct((pairs, 5, width // (2 * pairs), width), bf16)
    return pl.pallas_call(
        between_kernel,
        grid=(total // rows,),
        in_specs=[pl.BlockSpec(memory_space=pltpu.SMEM), whole(ga), whole(gb), whole(gn23)]
        + [rowspec(width)] * 3 + [rowspec(width // 2)] * 2 + [rowspec(width)] + [rowspec(width // 2)] * 2
        + [part(weights, 0, width, 0), part(weights, 1, width, 0), whole(norms)] + [apart] * len(after),
        out_specs=[rowspec(width)] * 2
        + [rowspec(LANES), whole(side), whole(side), pl.BlockSpec((8, width), lambda i: (0, 0))],
        out_shape=[sds((total, width), bf16), sds((total, width), bf16), sds((total, LANES), f32), side, side, sds((8, width), f32)],
        scratch_shapes=[pltpu.VMEM((2, width, width), f32)],
        name="between",
        **params(7, 32),
    )(core, ga, gb, gn23, *placed(r1, dr2, dr3, dqa, dqb, h1b, oa, ob, weights, weights), norms, *after)


def self_backward_kernel(
    tile, block, half, items_ref, q_ref, k_ref, v_ref, do_ref, l_ref, delta_ref, idr_ref, x_ref, wq_ref, wk_ref, wv_ref, sofar_ref, *rest
):
    if half:
        core_ref, before_ref = rest[:2]
        gx_ref, keep_ref, send_ref, q_all, ids_all, dq, dk, dv, grads = rest[-9:]
    else:
        gx_ref, grads_ref, q_all, ids_all, dq, dk, dv, grads = rest[-8:]
    step = pl.program_id(0)
    total, width = q_ref.shape

    @pl.when(step == 0)
    def _():
        dq[...] = jnp.zeros_like(dq)
        dk[...] = jnp.zeros_like(dk)
        dv[...] = jnp.zeros_like(dv)
        grads[...] = jnp.zeros_like(grads)
        q_all[...] = q_ref[...] * jnp.asarray(HD ** -0.5, bf16)
        for j in range(total // block):
            ids_all[j * block : (j + 1) * block, :] = column_of(idr_ref[:, j * block : (j + 1) * block])
        attend_back(
            items_ref, idr_ref, ids_all, q_all, do_ref, k_ref, v_ref, l_ref, delta_ref, dq, dk, dv, tile, block,
            0, 2 * half * (width // LANES), True,
        )

    x = x_ref[...]
    rows = x.shape[0]
    here = pl.ds(pl.multiple_of(step * rows, rows), rows)
    gx = sofar_ref[...].astype(f32)
    parts = (dq[here, :] * HD ** -0.5).astype(bf16), dk[here, :].astype(bf16), dv[here, :].astype(bf16)
    for i, (grad, w_ref) in enumerate(zip(parts, (wq_ref, wk_ref, wv_ref))):
        gx += mm(grad, w_ref[0], NT)
        grads[i] += mm(x, grad, TN)
    gx_ref[...] = gx.astype(bf16)

    @pl.when(step == pl.num_programs(0) - 1)
    def _():
        if not half:
            grads_ref[...] = grads[...].astype(bf16)
            return
        r = keep_ref.shape[2]

        def write(device, ref, j):
            place = pl.ds(pl.multiple_of(device * r, r), r)
            for i in range(3):
                ref[j, i, :, :width] = before_ref[i, place, :]
                ref[j, i, :, width:] = grads[i, place, :].astype(bf16)

        spread(keep_ref, send_ref, core_ref[0], write)


def self_backward(
    items, q, k, v, do, l, delta, idr, x, weights, sofar, half, after, core=None, before=None, pairs=1, turns=4, block=QROWS, tile=256
):
    total, width = x.shape
    columns = width // 2
    sds = out_array
    sides = [jax.ShapeDtypeStruct((pairs, 3, width // (2 * pairs), width), bf16)] * 2 if half else [jax.ShapeDtypeStruct((3, width, columns), bf16)]
    more = [core, before] if half else []
    rowspec = lambda w: pl.BlockSpec((total // turns, w), lambda i, *_: (i, 0))
    return pl.pallas_call(
        functools.partial(self_backward_kernel, tile, block, half),
        grid_spec=pltpu.PrefetchScalarGridSpec(
            num_scalar_prefetch=1,
            grid=(turns,),
            in_specs=[whole(q), whole(k), whole(v), pl.BlockSpec((total, columns), lambda i, *_: (0, half)), whole(l), whole(delta), whole(idr)]
            + [rowspec(width)] + [part(weights, i, columns, half) for i in range(3)] + [rowspec(width)]
            + ([pl.BlockSpec(memory_space=pltpu.SMEM), whole(before)] if half else []) + [apart] * len(after),
            out_specs=[rowspec(width)] + [whole(side) for side in sides],
            scratch_shapes=[
                pltpu.VMEM((total, columns), bf16), pltpu.VMEM((total, LANES), jnp.int32),
                pltpu.VMEM((total, columns), f32), pltpu.VMEM((total, columns), f32), pltpu.VMEM((total, columns), f32),
                pltpu.VMEM((3, width, columns), f32),
            ],
        ),
        out_shape=[sds((total, width), bf16)] + sides,
        name="self_backward",
        **params(10, 32),
    )(items, *placed(q, k, v, do, l, delta), idr, *placed(x, weights, weights, weights, sofar), *more, *after)


def add_split_kernel(count, here_ref, *refs):
    places = refs[0].shape[1]
    for m in range(places):
        at = here_ref[0] ^ m
        total = refs[0][:, at].astype(f32)
        for ref in refs[1:count]:
            total += ref[:, at].astype(f32)
        refs[count + m][...] = total.astype(bf16)


def add_split(here, parts, outer, places):
    tail = parts[0].shape[1:]
    parts = [p.reshape((outer, places) + tail) for p in parts]
    out = pl.pallas_call(
        functools.partial(add_split_kernel, len(parts)),
        grid=(outer,),
        in_specs=[pl.BlockSpec(memory_space=pltpu.SMEM)] + [pl.BlockSpec((1, places) + tail, lambda i: (i, 0, 0, 0, 0))] * len(parts),
        out_specs=[pl.BlockSpec((1,) + tail, lambda i: (i, 0, 0, 0))] * places,
        out_shape=[jax.ShapeDtypeStruct((outer,) + tail, bf16)] * places,
        name="add_split",
        **params(3, 24),
    )(here, *parts)
    return list(out)


def own_block(shape):
    return pl.BlockSpec(shape, lambda *_: (0,) * len(shape))


def pack_kernel(moves, count, *refs):
    ins, out_ref, wide = refs[:count], refs[count], refs[count + 1 :]
    rows = out_ref.shape[1]
    for ref, w in zip(ins, wide):
        w[...] = ref[...].astype(f32)
    for source, begin, step, square, block in moves:
        value = wide[source][pl.ds(begin, rows, stride=step), :]
        out_ref[square, :, block * LANES : (block + 1) * LANES] = value.astype(bf16)


def pack(arrays, moves, squares, rows, width, name):
    arrays = [a.reshape(-1, LANES) for a in arrays]
    return pl.pallas_call(
        functools.partial(pack_kernel, moves, len(arrays)),
        in_specs=[own_block(a.shape) for a in arrays],
        out_specs=own_block((squares, rows, width)),
        out_shape=jax.ShapeDtypeStruct((squares, rows, width), bf16),
        scratch_shapes=[pltpu.VMEM(a.shape, f32) for a in arrays],
        name=name,
        **params(1, 16),
    )(*arrays)


def square_moves(source, square, width):
    blocks = width // LANES
    return [(source, b, blocks, square, b) for b in range(blocks)]


def finish_kernel(moves, count, *refs):
    ins, outs = refs[:count], refs[count:]
    rows = ins[0].shape[1]
    for square, block, out, begin, step in moves:
        cols = slice(block * LANES, (block + 1) * LANES)
        total = ins[0][square, :, cols].astype(f32)
        for ref in ins[1:]:
            total += ref[square, :, cols].astype(f32)
        if step:
            outs[out][pl.ds(begin, rows, stride=step), :] = total
        else:
            outs[out][:, cols] = total


def finish(parts, moves, shapes, name):
    return pl.pallas_call(
        functools.partial(finish_kernel, moves, len(parts)),
        in_specs=[own_block(p.shape) for p in parts],
        out_specs=[own_block(s) for s in shapes],
        out_shape=[jax.ShapeDtypeStruct(s, f32) for s in shapes],
        name=name,
        **params(1, 16),
    )(*parts)


def segment_ids(lengths, row_count):
    ends = jnp.cumsum(lengths)
    places = jnp.arange(row_count, dtype=jnp.int32)
    return jnp.sum((places[:, None] >= ends[None, :]).astype(jnp.int32), axis=1)


def item_list(first, high, keys, block, tile):
    blocks = first.shape[0]
    count = (high - first * LANES + tile - 1) // tile
    upto = jnp.cumsum(count)
    most = blocks * (keys // tile)
    place = jnp.arange(most + FORWARD_ITEMS * BACKWARD_ITEMS, dtype=jnp.int32)
    passed = place[:, None] >= upto[None, :]
    which = jnp.minimum(jnp.sum(passed, axis=1), blocks - 1)
    skipped = jnp.sum(jnp.where(passed, count[None, :], 0), axis=1)
    mine = which[:, None] == jnp.arange(blocks)[None, :]
    begin = jnp.sum(jnp.where(mine, first[None, :], 0), axis=1) + (place - skipped) * (tile // LANES)
    begin = jnp.where(place < upto[-1], begin, keys // LANES)
    turns = [jnp.broadcast_to((upto[-1] + n - 1) // n, place.shape) for n in (FORWARD_ITEMS, BACKWARD_ITEMS)]
    return jnp.stack([which, begin] + turns).astype(jnp.int32)


def cross_items(seg, mem, total, keys, block=QROWS, tile=256):
    ends = jnp.cumsum(seg)
    starts = jnp.arange(0, total, block, dtype=jnp.int32)
    mem = mem[: seg.shape[0]]
    low = jnp.sum(jnp.where(starts[:, None] >= ends[None, :], mem[None, :], 0), axis=1)
    before = jnp.concatenate([jnp.zeros((1,), jnp.int32), ends[:-1].astype(jnp.int32)])
    high = jnp.sum(jnp.where((starts + block - 1)[:, None] >= before[None, :], mem[None, :], 0), axis=1)
    return item_list(low // LANES, high, keys, block, tile)


def self_items(seg, total, block=QROWS, tile=256):
    ends = jnp.cumsum(seg)
    starts = jnp.arange(0, total, block, dtype=jnp.int32)
    low = jnp.sum(jnp.where(starts[:, None] >= ends[None, :], seg[None, :], 0), axis=1)
    return item_list(low // LANES, starts + block, total, block, tile)


def mesh_size():
    return lax.axis_size("dp") * lax.axis_size("fsdp")


def position():
    return lax.axis_index("dp") * lax.axis_size("fsdp") + lax.axis_index("fsdp")


def bit_groups():
    count = mesh_size().bit_length() - 1
    groups = [(0, 1)]
    while groups[-1][0] + groups[-1][1] < count:
        low = groups[-1][0] + groups[-1][1]
        groups.append((low, min(2, count - low)))
    return groups


def swap(x, mask):
    return lax.ppermute(x, ("dp", "fsdp"), [(i, i ^ mask) for i in range(mesh_size())])


def place_in(group):
    return (position() >> group[0]) & ((1 << group[1]) - 1)


def tie(x, *after):
    return lax.optimization_barrier((x, *after))[0] if after else x


def gather_step(x, group, after=()):
    low, width = group
    here = place_in(group)
    blocks = [x] + tie([swap(x, m << low) for m in range(1, 1 << width)], *after)
    for j in range(width):
        flip = (here >> j) & 1 == 1
        blocks = [jnp.where(flip, blocks[p ^ (1 << j)], blocks[p]) for p in range(1 << width)]
    return jnp.stack(blocks, axis=x.ndim - 2)


def gathered(x):
    return x.reshape(x.shape[:1] + (-1, x.shape[-1]))


def swap_pieces(parts, group, after=()):
    return [parts[0]] + tie([swap(parts[m], m << group[0]) for m in range(1, len(parts))], *after)


def next_pieces(parts, groups, done):
    group = groups[done]
    outer = 1 << sum(g[1] for g in groups[done + 1 :])
    return add_split(place_in(group).reshape(1).astype(jnp.int32), parts, outer, 1 << group[1])


def norm_parts(norm_params, size):
    parts, left = [], norm_params
    for _ in range(3):
        part = left.astype(bf16)
        parts.append(jnp.pad(part, (0, LANES - part.size)))
        left = left - part.astype(f32)
    flat = jnp.concatenate(parts)
    return jnp.pad(flat, (0, size - flat.size))


def resplit(keep, send, devices, core, squares):
    halves = jnp.concatenate([keep, send])
    width = halves.shape[-1]
    first = halves[:, :squares].transpose(1, 0, 2, 3).reshape(squares, devices, -1, width).transpose(1, 0, 2, 3)
    rows = first.shape[2]
    if halves.shape[1] > squares:
        rest = halves[:, squares:].reshape(devices, halves.shape[1] - squares, rows, width)
        first = jnp.concatenate([first, rest], axis=1)
    both = first.reshape(devices // 2, 2, -1, rows, width)
    return [lax.dynamic_index_in_dim(both, core ^ m, 1, keepdims=False) for m in range(2)]


def body(
    inputs, memory, seg_lengths, mem_lengths, self_query, self_key, self_value, self_out,
    cross_query, cross_key, cross_value, cross_out, ffn_in, ffn_out, norm_params, cotangent,
):
    total, width = inputs.shape
    keys = memory.shape[0]
    devices = mesh_size()
    groups = bit_groups()
    down = groups[::-1]
    shard = norm_params.shape[0]
    size = self_query.shape[0]
    own_rows = size // width
    blocks = ffn_in.shape[0] // size
    whole_tiles = own_rows % 16 == 0
    core = place_in(groups[0]).reshape(1).astype(jnp.int32)

    firsts = (self_query, self_key, self_value)
    seconds = (self_out, cross_query, cross_out, cross_key, cross_value, norm_parts(norm_params, size))
    if whole_tiles:
        lane_blocks = width // LANES
        three = [m for i in range(3) for m in square_moves(i, i, width)]
        six = three + [m for i in range(3, 6) for m in square_moves(i, i, width)]
        wide = [(0, c * lane_blocks + b, blocks * lane_blocks, c, b) for c in range(blocks) for b in range(lane_blocks)]
        tall = [(1, j * own_rows * lane_blocks + b, lane_blocks, blocks + j, b) for j in range(blocks) for b in range(lane_blocks)]
        first = pack(firsts, three, 3, own_rows, width, "pack_self")
        second = pack(tie(seconds, first), six, 6, own_rows, width, "pack_cross")
        ffn_own = pack(tie((ffn_in, ffn_out), first), wide + tall, 2 * blocks, own_rows, width, "pack_ffn")
    else:
        first = jnp.concatenate(firsts).reshape(3, own_rows, width)
        second = jnp.concatenate(seconds).reshape(6, own_rows, width)
        fi = ffn_in.reshape(own_rows, blocks, width).transpose(1, 0, 2)
        ffn_own = jnp.concatenate([fi, ffn_out.reshape(blocks, own_rows, width)])
    for i, g in enumerate(down[:-1]):
        first = gather_step(first, g, [second] if i else [])
        if i < len(down) - 2:
            second = gather_step(second, g)
    early = second
    first = gathered(gather_step(first, down[-1]))
    ffn_all = lax.all_gather(ffn_own.reshape(-1, width), ("dp", "fsdp"), axis=0, tiled=True)
    ffn_all = ffn_all.reshape(devices, 2 * blocks, own_rows, width)
    if not whole_tiles:
        fi = ffn_all[:, :blocks].transpose(1, 0, 2, 3).reshape(1, blocks, width, width)
        ffn_all = jnp.concatenate([fi, ffn_all[:, blocks:].reshape(1, blocks, width, width)], axis=1)
    pairs = devices // 2 if whole_tiles else 1
    part_of = core if whole_tiles else jnp.zeros_like(core)

    qid, mid = segment_ids(seg_lengths[0], total)[None, :], segment_ids(mem_lengths[0], keys)[None, :]
    own_items = self_items(seg_lengths[0], total)
    items = cross_items(seg_lengths[0], mem_lengths[0], total, keys)

    qa, ka, va, oa, la = self_forward(own_items, inputs, first, qid, 0, [early])
    second = gather_step(second, down[-2], [la])
    qb, kb, vb, ob, lb = self_forward(own_items, inputs, first, qid, 1, [second])
    second = gathered(gather_step(second, down[-1], [lb]))
    norm_all = second[5].reshape(devices, -1)[:, : 3 * LANES].reshape(devices, 3, LANES)[:, :, :shard].astype(f32)
    norms = jnp.sum(norm_all, axis=1).reshape(6, width)
    k2, v2, r1, h1b, q2, o2, l2, r2 = cross_forward(items, memory, inputs, oa, ob, second, norms, qid, mid)
    out, dr3, dr2, do2, delta2, keep, send, gn23 = ffn(part_of, pairs, r2, inputs, cotangent, o2, ffn_all, second, 2, norms)

    one = [keep, send] if whole_tiles else resplit(keep, send, devices, core[0], blocks + 1)
    dq2a, dk2a, dv2a, gckva = cross_backward(items, q2, k2, v2, do2, l2, delta2, qid, mid, memory, 0, [one[1]])
    one = next_pieces(swap_pieces(one, groups[0], [dq2a]), groups, 1)
    dq2b, dk2b, dv2b, gckvb = cross_backward(items, q2, k2, v2, do2, l2, delta2, qid, mid, memory, 1, one[1:])
    dsum, do1, delta1, keep, send, gn = between(
        part_of, pairs, gckva, gckvb, gn23, r1, dr2, dr3, dq2a, dq2b, h1b, oa, ob, second, norms, []
    )
    two = [keep, send]
    if not whole_tiles:
        two = resplit(keep, send, devices, core[0], 5)
        own_norms = jnp.pad(gn[:6].astype(bf16).reshape(devices, -1), ((0, 0), (0, size - shard)))
        own_norms = own_norms.reshape(devices // 2, 2, own_rows, width)
        two = [two[m].at[:, 4].set(lax.dynamic_index_in_dim(own_norms, core[0] ^ m, 1, keepdims=False)) for m in range(2)]
    one = next_pieces(swap_pieces(one, groups[1], [do1]), groups, 2)
    gxa, gsa = self_backward(own_items, qa, ka, va, do1, la, delta1, qid, inputs, first, dsum, 0, one[1:] + [two[1]])
    two = next_pieces(swap_pieces(two, groups[0], [gsa]), groups, 1)
    gx, keep, send = self_backward(
        own_items, qb, kb, vb, do1, lb, delta1, qid, inputs, first, gxa, 1, two[1:], core=part_of, before=gsa, pairs=pairs
    )
    three = [keep, send] if whole_tiles else resplit(keep, send, devices, core[0], 3)
    three = next_pieces(swap_pieces(three, groups[0]), groups, 1)
    two = next_pieces(swap_pieces(two, groups[1], [three[1]]), groups, 2)
    gm = memory_grad(dk2a, dk2b, dv2a, dv2b, second, 3, two[1:])
    for i in range(2, len(groups)):
        three = next_pieces(swap_pieces(three, groups[i - 1]), groups, i)
        if i > 2:
            one = next_pieces(swap_pieces(one, groups[i - 1]), groups, i)
            two = next_pieces(swap_pieces(two, groups[i - 1]), groups, i)

    def flat(g):
        return g.reshape(-1)

    chains = [swap_pieces(one, groups[-1], [two[1]]), swap_pieces(two, groups[-1]), swap_pieces(three, groups[-1])]
    chains = [[p.reshape(-1, own_rows, width) for p in chain] for chain in chains]
    if whole_tiles:
        lane_rows = size // LANES
        square, long = (lane_rows, LANES), (blocks * lane_rows, LANES)

        moves = [(c, b, 0, c * lane_blocks + b, blocks * lane_blocks) for c in range(blocks) for b in range(lane_blocks)]
        moves += [(blocks, b, 1, b, lane_blocks) for b in range(lane_blocks)]
        moves += [
            (blocks + 1 + j, b, 2, j * own_rows * lane_blocks + b, lane_blocks) for j in range(blocks) for b in range(lane_blocks)
        ]
        gfi, gco, gfo = finish(chains[0], moves, [long, square, long], "finish_ffn")
        moves = [(i, b, i, b, lane_blocks) for i in range(4) for b in range(lane_blocks)] + [(4, b, 4, 0, 0) for b in range(lane_blocks)]
        gck, gcv, gcq, gso, gn = finish(chains[1], moves, [square] * 4 + [(own_rows, width)], "finish_cross")
        gn = lax.dynamic_slice_in_dim(flat(gn[:6]), position() * shard, shard)
        moves = [(i, b, i, b, lane_blocks) for i in range(3) for b in range(lane_blocks)]
        gsq, gsk, gsv = finish(chains[2], moves, [square] * 3, "finish_self")
    else:
        one, two, three = (sum(p.astype(f32) for p in chain) for chain in chains)
        gfi, gco, gfo = one[:blocks].transpose(1, 0, 2), one[blocks], one[blocks + 1 :]
        gck, gcv, gcq, gso, gn = two[0], two[1], two[2], two[3], flat(two[4])[:shard]
        gsq, gsk, gsv = three[0], three[1], three[2]
    return (out, gx, gm) + tuple(flat(g) for g in (gsq, gsk, gsv, gso, gcq, gck, gcv, gco, gfi, gfo, gn))


def solution(mesh):
    rows, flat = P(("dp", "fsdp"), None), P(("dp", "fsdp"))
    return jax.shard_map(
        body,
        mesh=mesh,
        in_specs=(rows,) * 4 + (flat,) * 11 + (rows,),
        out_specs=(rows,) * 3 + (flat,) * 11,
        check_vma=False,
    )
```

```python
import functools
import jax
import jax.numpy as jnp
from jax import lax
from jax.experimental import pallas as pl
from jax.experimental.pallas import tpu as pltpu
from jax.sharding import PartitionSpec as P

HD = 64
LANES = 128
MOST = 256
QROWS = 128
FORWARD_ITEMS = 2
BACKWARD_ITEMS = 3
FFN_CHUNK = 256
masked_score = -1e30
norm_eps = 1e-05
bf16, f32 = jnp.bfloat16, jnp.float32
NT = (((1,), (1,)), ((), ()))
TN = (((0,), (0,)), ((), ()))
NN = (((1,), (0,)), ((), ()))


def mm(left, right, dims=NN):
    return lax.dot_general(left, right, dims, preferred_element_type=f32)


def norm_rows(source):
    mean = jnp.mean(source, axis=-1, keepdims=True)
    centered = source - mean
    variance = jnp.mean(centered * centered, axis=-1, keepdims=True)
    rstd = lax.rsqrt(variance + norm_eps)
    return centered * rstd, rstd


def lane_below(rows):
    return lax.broadcasted_iota(jnp.int32, (rows, LANES), 1) < HD


def column_of(row):
    return jnp.broadcast_to(row, (LANES, row.shape[1])).T


def head_part(pair, which, low):
    return jnp.where(low == (which == 0), pair, jnp.zeros_like(pair))


def values_with_ones(values):
    parts = []
    for p in range(values.shape[1] // LANES):
        pair = values[:, p * LANES : (p + 1) * LANES]
        parts += [pair, jnp.ones_like(pair)]
    return jnp.concatenate(parts, axis=1)


def finish_heads(at, top, tot, acc, write):
    shape = acc.shape[0], at.size if hasattr(at, "size") else at.stop - at.start, LANES
    lane = lax.broadcasted_iota(jnp.int32, shape[1:], 1)
    sums, tops = jnp.ones(shape[1:], f32), jnp.zeros(shape[1:], f32)
    for p in range(shape[0]):
        total = tot[p, at, :]
        write(p, (acc[p, at, :] / total).astype(bf16))
        sums = jnp.where(lane % HD == p, total, sums)
        tops = jnp.where(lane == p, top[2 * p, at, :], jnp.where(lane == HD + p, top[2 * p + 1, at, :], tops))
    return tops + jnp.log(sums)


def column_at(head):
    return head % 2 * HD + head // 2


def item_at(items_ref, n, idk_ref, ids_q, keys, tile, block, causal):
    begin = pl.multiple_of(items_ref[0, n] * block, block)
    wanted = items_ref[1, n] * LANES
    start = pl.multiple_of(jnp.minimum(wanted, keys - tile), LANES)
    at = pl.ds(begin, block)
    pos = start + lax.broadcasted_iota(jnp.int32, (1, tile), 1)
    ids_k = jnp.where(pos >= wanted, idk_ref[:, pl.ds(start, tile)], -1)
    allowed = ids_q[at, :1] == ids_k
    if causal:
        allowed &= pos <= begin + lax.broadcasted_iota(jnp.int32, (block, 1), 0)
    return at, pl.ds(start, tile), jnp.where(allowed, 0.0, masked_score).astype(f32)


def attend(items_ref, idk_ref, ids_q, q_all, k_all, vx_all, top, tot, acc, tile, block, causal):
    keys, width = k_all.shape
    pairs = width // LANES
    heads = 2 * pairs
    low = lane_below(block)
    top[...] = jnp.full(top.shape, masked_score, f32)
    tot[...] = jnp.zeros(tot.shape, f32)
    acc[...] = jnp.zeros(acc.shape, f32)

    def some(i, _):
        loads, made = [], []
        for t in range(FORWARD_ITEMS):
            at, there, bias = item_at(items_ref, FORWARD_ITEMS * i + t, idk_ref, ids_q, keys, tile, block, causal)
            loads.append((at, there, bias))
            for p in range(pairs):
                cols = slice(p * LANES, (p + 1) * LANES)
                part = q_all[at, cols]
                both = jnp.concatenate([head_part(part, h, low) for h in range(2)])
                made.append(mm(both, k_all[there, cols], NT))
        weights, scales = [], []
        for t, (at, there, bias) in enumerate(loads):
            for head in range(heads):
                s = made[t * pairs + head // 2][head % 2 * block : (head % 2 + 1) * block] + bias
                old = top[head, at, :]
                new = jnp.maximum(old, jnp.max(s, axis=1, keepdims=True))
                top[head, at, :] = new
                scales.append(jnp.exp(old - new))
                weights.append(jnp.exp(s - jnp.concatenate([new] * (tile // LANES), axis=1)).astype(bf16))
        mixed = [
            mm(jnp.concatenate(weights[t * heads + 2 * p : t * heads + 2 * p + 2]), vx_all[there, 2 * p * LANES : 2 * (p + 1) * LANES])
            for t, (_, there, _) in enumerate(loads) for p in range(pairs)
        ]
        for t, (at, _, _) in enumerate(loads):
            for p in range(pairs):
                n = t * pairs + p
                scale = jnp.where(low, scales[2 * n], scales[2 * n + 1])
                o = mixed[n]
                acc[p, at, :] = acc[p, at, :] * scale + jnp.where(low, o[:block, :LANES], o[block:, :LANES])
                tot[p, at, :] = tot[p, at, :] * scale + jnp.where(low, o[:block, LANES:], o[block:, LANES:])
        return 0

    lax.fori_loop(0, items_ref[2, 0], some, 0)


def attend_back(items_ref, idk_ref, ids_q, q_all, do_ref, k_ref, v_ref, l_ref, delta_ref, dq, dk, dv, tile, block, first_head, causal):
    keys, width = k_ref.shape
    pairs = width // LANES
    low = lane_below(block)

    def some(i, _):
        loads, scores, grads = [], [], []
        for t in range(BACKWARD_ITEMS):
            at, there, bias = item_at(items_ref, BACKWARD_ITEMS * i + t, idk_ref, ids_q, keys, tile, block, causal)
            loads.append((at, there, bias))
            for p in range(pairs):
                cols = slice(p * LANES, (p + 1) * LANES)
                q, do = q_all[at, cols], do_ref[at, cols]
                qs = jnp.concatenate([head_part(q, h, low) for h in range(2)])
                dos = jnp.concatenate([head_part(do, h, low) for h in range(2)])
                scores.append((mm(qs, k_ref[there, cols], NT), qs))
                grads.append((mm(dos, v_ref[there, cols], NT), dos))
        weights, slopes = [], []
        for t, (at, there, bias) in enumerate(loads):
            logs, deltas = l_ref[at, :], delta_ref[at, :]
            for p in range(pairs):
                es, ds = [], []
                for h in range(2):
                    lane = column_at(first_head + 2 * p + h)
                    rows = slice(h * block, (h + 1) * block)
                    e = jnp.exp(scores[t * pairs + p][0][rows] + bias - logs[:, lane : lane + 1])
                    es.append(e.astype(bf16))
                    ds.append((e * (grads[t * pairs + p][0][rows] - deltas[:, lane : lane + 1])).astype(bf16))
                weights.append(jnp.concatenate(es))
                slopes.append(jnp.concatenate(ds))
        for t, (at, there, _) in enumerate(loads):
            for p in range(pairs):
                cols = slice(p * LANES, (p + 1) * LANES)
                n = t * pairs + p
                gq = mm(slopes[n], k_ref[there, cols])
                gk = mm(slopes[n], scores[n][1], TN)
                gv = mm(weights[n], grads[n][1], TN)
                dq[at, cols] += jnp.where(low, gq[:block], gq[block:])
                dk[there, cols] += gk
                dv[there, cols] += gv
        return 0

    lax.fori_loop(0, items_ref[2, 1], some, 0)


def self_forward_kernel(tile, block, items_ref, x_ref, wq_ref, wk_ref, wv_ref, idr_ref, *rest):
    q_ref, k_ref, v_ref, o_ref, l_ref, q_all, k_all, vx_all, ids_all, top, tot, acc = rest[-12:]
    step = pl.program_id(0)
    rows = x_ref.shape[0]
    total, width = k_all.shape
    turns = total // rows

    @pl.when(step < turns)
    def _():
        x = x_ref[...]
        q = mm(x, wq_ref[0]).astype(bf16)
        k = mm(x, wk_ref[0]).astype(bf16)
        v = mm(x, wv_ref[0]).astype(bf16)
        q_ref[...] = q
        k_ref[...] = k
        v_ref[...] = v
        here = pl.ds(pl.multiple_of(step * rows, rows), rows)
        q_all[here, :] = q * jnp.asarray(HD ** -0.5, bf16)
        k_all[here, :] = k
        vx_all[here, :] = values_with_ones(v)
        ids_all[here, :] = column_of(idr_ref[:, here])

    @pl.when(step == turns)
    def _():
        attend(items_ref, idr_ref, ids_all, q_all, k_all, vx_all, top, tot, acc, tile, block, True)
        size = 2 * block
        for j in range(total // size):
            at = slice(j * size, (j + 1) * size)

            def write(p, value):
                o_ref[at, p * LANES : (p + 1) * LANES] = value

            l_ref[at, :] = finish_heads(at, top, tot, acc, write)


def whole(a):
    return pl.BlockSpec(a.shape, lambda *_: (0,) * a.ndim)


def part(weights, index, columns, half):
    return pl.BlockSpec((1, weights.shape[1], columns), lambda *_: (index, 0, half))


def params(us, vmem):
    return dict(
        compiler_params=pltpu.CompilerParams(vmem_limit_bytes=vmem * 2**20),
        cost_estimate=pl.CostEstimate(flops=us * 10**9, bytes_accessed=2**20, transcendentals=0),
    )


apart = pl.BlockSpec(memory_space=pl.ANY)


def out_array(shape, dtype):
    return pltpu.HBM(shape, dtype)


def placed(*arrays):
    return [pltpu.with_memory_space_constraint(a, pltpu.HBM) for a in arrays]


def self_forward(items, x, weights, idr, after, turns=2, block=QROWS, tile=256):
    total, width = x.shape
    heads = width // HD
    rows = total // turns
    early = lambda w: pl.BlockSpec((rows, w), lambda i, *_: (jnp.minimum(i, turns - 1), 0))
    fixed = lambda w: pl.BlockSpec((total, w), lambda i, *_: (0, 0))
    sds = out_array
    full = sds((total, width), bf16)
    return pl.pallas_call(
        functools.partial(self_forward_kernel, tile, block),
        grid_spec=pltpu.PrefetchScalarGridSpec(
            num_scalar_prefetch=1,
            grid=(turns + 1,),
            in_specs=[early(width)] + [part(weights, i, width, 0) for i in range(3)] + [whole(idr)] + [apart] * len(after),
            out_specs=[early(width)] * 3 + [fixed(width), fixed(LANES)],
            scratch_shapes=[
                pltpu.VMEM((total, width), bf16), pltpu.VMEM((total, width), bf16), pltpu.VMEM((total, 2 * width), bf16),
                pltpu.VMEM((total, LANES), jnp.int32),
                pltpu.VMEM((heads, total, LANES), f32), pltpu.VMEM((heads // 2, total, LANES), f32), pltpu.VMEM((heads // 2, total, LANES), f32),
            ],
        ),
        out_shape=[full] * 4 + [sds((total, LANES), f32)],
        name="self_forward",
        **params(13, 32),
    )(items, *placed(x), weights, weights, weights, idr, *after)


def cross_forward_kernel(
    tile, block, items_ref, memory_ref, wk_ref, wv_ref, x_ref, o1_ref, wso_ref, wcq_ref, norms_ref, idr_ref, idk_ref,
    k2_ref, v2_ref, r1_ref, h1b_ref, q2_ref, h1_ref, o_ref, l_ref, k_all, vx_all, q_all, ids_all, top, tot, acc,
):
    step = pl.program_id(0)
    rows, width = x_ref.shape
    keys = k_all.shape[0]
    turns = pl.num_programs(0) - 1

    @pl.when(step < turns)
    def _():
        per = memory_ref.shape[0]
        memory = memory_ref[...]
        r1 = x_ref[...].astype(f32) + mm(o1_ref[...], wso_ref[0])
        k2 = mm(memory, wk_ref[0]).astype(bf16)
        r1_ref[...] = r1.astype(bf16)
        n1, _ = norm_rows(r1)
        v2 = mm(memory, wv_ref[0]).astype(bf16)
        h1 = n1 * norms_ref[0:1, :] + norms_ref[1:2, :]
        h1b = h1.astype(bf16)
        h1b_ref[...] = h1b
        q2 = mm(h1b, wcq_ref[0]).astype(bf16)
        q2_ref[...] = q2
        k2_ref[...] = k2
        v2_ref[...] = v2
        here = pl.ds(pl.multiple_of(step * rows, rows), rows)
        q_all[here, :] = q2 * jnp.asarray(HD ** -0.5, bf16)
        h1_ref[...] = h1
        ids_all[here, :] = column_of(idr_ref[:, here])
        there = pl.ds(pl.multiple_of(step * per, per), per)
        k_all[there, :] = k2
        vx_all[there, :] = values_with_ones(v2)

    @pl.when(step == turns)
    def _():
        attend(items_ref, idk_ref, ids_all, q_all, k_all, vx_all, top, tot, acc, tile, block, False)

        size = 2 * block
        for j in range(q_all.shape[0] // size):
            at = slice(j * size, (j + 1) * size)

            def write(p, value):
                o_ref[at, p * LANES : (p + 1) * LANES] = value

            l_ref[at, :] = finish_heads(at, top, tot, acc, write)


def cross_forward(items, memory, x, o1, weights, norms, idr, idk, turns=2, block=QROWS, tile=256):
    total, width = x.shape
    keys = memory.shape[0]
    heads = width // HD
    rows, per = total // turns, keys // turns
    early = lambda r, w: pl.BlockSpec((r, w), lambda i, *_: (jnp.minimum(i, turns - 1), 0))
    fixed = lambda w: pl.BlockSpec((total, w), lambda i, *_: (0, 0))
    sds = out_array
    return pl.pallas_call(
        functools.partial(cross_forward_kernel, tile, block),
        grid_spec=pltpu.PrefetchScalarGridSpec(
            num_scalar_prefetch=1,
            grid=(turns + 1,),
            in_specs=[early(per, width), part(weights, 2, width, 0), part(weights, 3, width, 0)]
            + [early(rows, width), early(rows, width), part(weights, 0, width, 0), part(weights, 1, width, 0)]
            + [whole(norms), whole(idr), whole(idk)],
            out_specs=[early(per, width)] * 2 + [early(rows, width)] * 4 + [fixed(width), fixed(LANES)],
            scratch_shapes=[
                pltpu.VMEM((keys, width), bf16),
                pltpu.VMEM((keys, 2 * width), bf16),
                pltpu.VMEM((total, width), bf16),
                pltpu.VMEM((total, LANES), jnp.int32),
                pltpu.VMEM((heads, total, LANES), f32),
                pltpu.VMEM((heads // 2, total, LANES), f32),
                pltpu.VMEM((heads // 2, total, LANES), f32),
            ],
        ),
        out_shape=[
            sds((keys, width), bf16), sds((keys, width), bf16), sds((total, width), bf16), sds((total, width), bf16),
            sds((total, width), bf16), sds((total, width), f32), sds((total, width), bf16), sds((total, LANES), f32),
        ],
        name="cross_forward",
        **params(19, 44),
    )(items, *placed(memory), weights, weights, *placed(x, o1), weights, weights, norms, idr, idk)


def norm_back(incoming, normal, rstd, gain):
    m = incoming * gain
    return rstd * (
        m - jnp.mean(m, axis=-1, keepdims=True) - normal * jnp.mean(m * normal, axis=-1, keepdims=True)
    )


def head_columns(left, right):
    width = left.shape[1]
    prod = left.astype(f32) * right.astype(f32)
    lane = lax.broadcasted_iota(jnp.int32, (width, LANES), 1)
    own = lax.broadcasted_iota(jnp.int32, (width, LANES), 0) // HD == 2 * (lane % HD) + lane // HD
    own = own.astype(bf16)
    high = prod.astype(bf16)
    low = (prod - high.astype(f32)).astype(bf16)
    return mm(high, own) + mm(low, own)


def column_sums(a):
    return jnp.sum(a, axis=0, keepdims=True)


def spread(keep_ref, send_ref, core, write):
    def one(j, _):
        write(2 * j + core, keep_ref, j)
        write(2 * j + 1 - core, send_ref, j)
        return 0

    lax.fori_loop(0, keep_ref.shape[0], one, 0)


def ffn_kernel(
    core_ref, h1_ref, x_ref, cot_ref, o2_ref, w_ref, norms_ref,
    out_ref, dr3_ref, dr2_ref, do2_ref, delta_ref, keep_ref, send_ref, gn_ref, gin, gout, gco,
):
    step = pl.program_id(0)
    last = pl.num_programs(0) - 1
    width = x_ref.shape[1]
    blocks = w_ref.shape[1] // 2

    @pl.when(step == 0)
    def _():
        gin[...] = jnp.zeros_like(gin)
        gout[...] = jnp.zeros_like(gout)
        gco[...] = jnp.zeros_like(gco)
        gn_ref[...] = jnp.zeros_like(gn_ref)

    win = [w_ref[:, c].reshape(width, width) for c in range(blocks)]
    wout = w_ref[:, blocks : 2 * blocks].reshape(blocks * width, width)
    wco = w_ref[:, 2 * blocks].reshape(width, width)
    n2, rstd2 = norm_rows(h1_ref[...] + mm(o2_ref[...], wco))
    h2 = n2 * norms_ref[2:3, :] + norms_ref[3:4, :]
    h2b = h2.astype(bf16)
    chunk = min(FFN_CHUNK, width)
    parts = blocks * width // chunk
    per = width // chunk

    def win_part(c):
        return win[c // per][:, (c % per) * chunk : (c % per + 1) * chunk]

    acts, slopes, hidden = [], [], [mm(h2b, win_part(0))]
    ff = jnp.zeros(h2.shape, f32)
    for c in range(parts):
        if c + 1 < parts:
            hidden.append(mm(h2b, win_part(c + 1)))
        u = hidden[c]
        square = u * u
        t = jnp.tanh(u * (0.7978845608028654 + (0.7978845608028654 * 0.044715) * square))
        half = 0.5 + 0.5 * t
        acts.append((u * half).astype(bf16))
        rise = u * (0.5 * 0.7978845608028654 + (0.5 * 0.7978845608028654 * 3 * 0.044715) * square)
        slopes.append(half + (1.0 - t * t) * rise)
        if c:
            ff += mm(acts[c - 1], wout[(c - 1) * chunk : c * chunk, :])
    ff += mm(acts[-1], wout[(parts - 1) * chunk :, :])
    r3 = h2 + ff + x_ref[...].astype(f32)
    n3, rstd3 = norm_rows(r3)
    gain3 = norms_ref[4:5, :]
    out_ref[...] = (n3 * gain3 + norms_ref[5:6, :]).astype(bf16)
    e = cot_ref[...].astype(f32)
    gn_ref[2:3, :] += column_sums(e * n3)
    gn_ref[3:4, :] += column_sums(e)
    dr3 = norm_back(e, n3, rstd3, gain3)
    dr3_ref[...] = dr3.astype(bf16)
    dfb = dr3.astype(bf16)
    dh2 = dr3
    raw, made = [mm(dfb, wout[:chunk, :], NT)], []
    for c in range(parts + 1):
        if c + 1 < parts:
            raw.append(mm(dfb, wout[(c + 1) * chunk : (c + 2) * chunk, :], NT))
        if c < parts:
            gout[c * chunk : (c + 1) * chunk, :] += mm(acts[c], dfb, TN)
            made.append((raw[c] * slopes[c]).astype(bf16))
        if c:
            gin[:, (c - 1) * chunk : c * chunk] += mm(h2b, made[c - 1], TN)
            dh2 += mm(made[c - 1], win_part(c - 1), NT)
    gn_ref[0:1, :] += column_sums(dh2 * n2)
    gn_ref[1:2, :] += column_sums(dh2)
    dr2 = norm_back(dh2, n2, rstd2, norms_ref[2:3, :])
    da2 = dr2.astype(bf16)
    dr2_ref[...] = da2
    o2 = o2_ref[...]
    gco[...] += mm(o2, da2, TN)
    do2 = mm(da2, wco, NT).astype(bf16)
    do2_ref[...] = do2
    delta_ref[...] = head_columns(do2, o2)

    @pl.when(step == last)
    def _():
        r = keep_ref.shape[2]

        def write(device, ref, j):
            here = pl.ds(pl.multiple_of(device * r, r), r)
            for c in range(blocks):
                ref[j, c] = gin[here, c * width : (c + 1) * width].astype(bf16)
            ref[j, blocks] = gco[here, :].astype(bf16)
            there = pl.ds(pl.multiple_of(device * blocks * r, blocks * r), blocks * r)
            ref[j, blocks + 1 :] = gout[there, :].astype(bf16).reshape(blocks, r, width)

        spread(keep_ref, send_ref, core_ref[0], write)


def ffn(core, pairs, h1, x, cot, o2, w, norms, rows=512):
    total, width = x.shape
    blocks = w.shape[1] // 2
    rowspec = lambda w: pl.BlockSpec((rows, w), lambda i: (i, 0))
    sds = jax.ShapeDtypeStruct
    side = jax.ShapeDtypeStruct((pairs, 2 * blocks + 1, width // (2 * pairs), width), bf16)
    return pl.pallas_call(
        ffn_kernel,
        grid=(total // rows,),
        in_specs=[pl.BlockSpec(memory_space=pltpu.SMEM)] + [rowspec(width)] * 4 + [whole(w), whole(norms)],
        out_specs=[rowspec(width)] * 4
        + [rowspec(LANES), whole(side), whole(side), pl.BlockSpec((4, width), lambda i: (0, 0))],
        out_shape=[
            sds((total, width), bf16), sds((total, width), bf16), sds((total, width), bf16), sds((total, width), bf16),
            sds((total, LANES), f32), side, side, sds((4, width), f32),
        ],
        scratch_shapes=[pltpu.VMEM((width, blocks * width), f32), pltpu.VMEM((blocks * width, width), f32), pltpu.VMEM((width, width), f32)],
        name="ffn",
        **params(32, 51),
    )(core, *placed(h1, x, cot, o2, w), norms)


def cross_backward_kernel(
    tile, block, half, items_ref, q2_ref, k2_ref, v2_ref, do_ref, l_ref, delta_ref, idr_ref, idk_ref, memory_ref, *rest
):
    dq_ref, dk_ref, dv_ref, grads_ref, q_all, ids_all, dq, dk, dv, grads = rest[-10:]
    step = pl.program_id(0)
    total, width = q2_ref.shape

    @pl.when(step == 0)
    def _():
        dq[...] = jnp.zeros_like(dq)
        dk[...] = jnp.zeros_like(dk)
        dv[...] = jnp.zeros_like(dv)
        grads[...] = jnp.zeros_like(grads)
        q_all[...] = q2_ref[...] * jnp.asarray(HD ** -0.5, bf16)
        for j in range(total // block):
            ids_all[j * block : (j + 1) * block, :] = column_of(idr_ref[:, j * block : (j + 1) * block])
        attend_back(
            items_ref, idk_ref, ids_all, q_all, do_ref, k2_ref, v2_ref, l_ref, delta_ref, dq, dk, dv, tile, block,
            2 * half * (width // LANES), False,
        )

    memory = memory_ref[...]
    per = memory.shape[0]
    here = pl.ds(pl.multiple_of(step * per, per), per)
    for i, (ref, out_ref) in enumerate(((dk, dk_ref), (dv, dv_ref))):
        grad = ref[here, :].astype(bf16)
        out_ref[...] = grad
        grads[i] += mm(memory, grad, TN)
    rows = dq_ref.shape[0]
    dq_ref[...] = (dq[pl.ds(pl.multiple_of(step * rows, rows), rows), :] * HD ** -0.5).astype(bf16)

    @pl.when(step == pl.num_programs(0) - 1)
    def _():
        grads_ref[...] = grads[...].astype(bf16)


def cross_backward(items, q2, k2, v2, do, l, delta, idr, idk, memory, half, after, turns=2, block=QROWS, tile=256):
    total, width = q2.shape
    keys = k2.shape[0]
    columns = width // 2
    cols = lambda r: pl.BlockSpec((r, columns), lambda i, *_: (0, half))
    rowspec = lambda r, w: pl.BlockSpec((r, w), lambda i, *_: (i, 0))
    sds = jax.ShapeDtypeStruct
    grad = jax.ShapeDtypeStruct((2, width, columns), bf16)
    return pl.pallas_call(
        functools.partial(cross_backward_kernel, tile, block, half),
        grid_spec=pltpu.PrefetchScalarGridSpec(
            num_scalar_prefetch=1,
            grid=(turns,),
            in_specs=[cols(total), cols(keys), cols(keys), cols(total)]
            + [whole(l), whole(delta), whole(idr), whole(idk), rowspec(keys // turns, width)] + [apart] * len(after),
            out_specs=[rowspec(total // turns, columns), rowspec(keys // turns, columns), rowspec(keys // turns, columns), whole(grad)],
            scratch_shapes=[
                pltpu.VMEM((total, columns), bf16), pltpu.VMEM((total, LANES), jnp.int32), pltpu.VMEM((total, columns), f32),
                pltpu.VMEM((keys, columns), f32), pltpu.VMEM((keys, columns), f32), pltpu.VMEM((2, width, columns), f32),
            ],
        ),
        out_shape=[sds((total, columns), bf16), sds((keys, columns), bf16), sds((keys, columns), bf16), grad],
        name="cross_backward",
        **params(12, 21),
    )(items, *placed(q2, k2, v2, do, l, delta), idr, idk, *placed(memory), *after)


def memory_grad_kernel(ka_ref, kb_ref, va_ref, vb_ref, wk_ref, wv_ref, *rest):
    half = ka_ref.shape[1]
    total = mm(ka_ref[...], wk_ref[0, :, :half], NT) + mm(kb_ref[...], wk_ref[0, :, half:], NT)
    total += mm(va_ref[...], wv_ref[0, :, :half], NT) + mm(vb_ref[...], wv_ref[0, :, half:], NT)
    rest[-1][...] = total.astype(bf16)


def memory_grad(ka, kb, va, vb, weights, index, after, rows=512):
    keys, width = ka.shape[0], weights.shape[2]
    rowspec = lambda w: pl.BlockSpec((rows, w), lambda i: (i, 0))
    return pl.pallas_call(
        memory_grad_kernel,
        grid=(keys // rows,),
        in_specs=[rowspec(width // 2)] * 4 + [part(weights, index, width, 0), part(weights, index + 1, width, 0)] + [apart] * len(after),
        out_specs=rowspec(width),
        out_shape=out_array((keys, width), bf16),
        name="memory_grad",
        **params(4, 9),
    )(ka, kb, va, vb, weights, weights, *after)


def between_kernel(
    core_ref, ga_ref, gb_ref, gn23_ref, r1_ref, dr2_ref, dr3_ref, dqa_ref, dqb_ref, h1b_ref, o1_ref, wso_ref, wcq_ref, norms_ref, *rest
):
    dsum_ref, do1_ref, delta_ref, keep_ref, send_ref, gn_ref, total = rest[-7:]
    step = pl.program_id(0)

    @pl.when(step == 0)
    def _():
        total[...] = jnp.zeros_like(total)
        gn_ref[...] = jnp.zeros_like(gn_ref)

    dq2 = jnp.concatenate([dqa_ref[...], dqb_ref[...]], axis=1)
    dh1 = dr2_ref[...].astype(f32) + mm(dq2, wcq_ref[0], NT)
    n1, rstd1 = norm_rows(r1_ref[...].astype(f32))
    gn_ref[0:1, :] += column_sums(dh1 * n1)
    gn_ref[1:2, :] += column_sums(dh1)
    dr1 = norm_back(dh1, n1, rstd1, norms_ref[0:1, :])
    dsum_ref[...] = (dr1 + dr3_ref[...].astype(f32)).astype(bf16)
    da1 = dr1.astype(bf16)
    o1 = o1_ref[...]
    do1 = mm(da1, wso_ref[0], NT).astype(bf16)
    do1_ref[...] = do1
    delta_ref[...] = head_columns(do1, o1)
    total[0] += mm(h1b_ref[...], dq2, TN)
    total[1] += mm(o1, da1, TN)

    @pl.when(step == pl.num_programs(0) - 1)
    def _():
        gn_ref[2:6, :] = gn23_ref[...]
        r, width = keep_ref.shape[2:]
        norm_part = jnp.concatenate([gn_ref[...], jnp.zeros((r - 8, width), f32)]).astype(bf16)

        def write(device, ref, j):
            here = pl.ds(pl.multiple_of(device * r, r), r)
            for i in range(2):
                ref[j, i, :, : width // 2] = ga_ref[i, here, :]
                ref[j, i, :, width // 2 :] = gb_ref[i, here, :]
                ref[j, 2 + i] = total[i, here, :].astype(bf16)
            ref[j, 4] = norm_part

        spread(keep_ref, send_ref, core_ref[0], write)


def between(core, pairs, ga, gb, gn23, r1, dr2, dr3, dqa, dqb, h1b, o1, weights, norms, after, rows=256):
    total, width = r1.shape
    rowspec = lambda w: pl.BlockSpec((rows, w), lambda i: (i, 0))
    sds = jax.ShapeDtypeStruct
    side = jax.ShapeDtypeStruct((pairs, 5, width // (2 * pairs), width), bf16)
    return pl.pallas_call(
        between_kernel,
        grid=(total // rows,),
        in_specs=[pl.BlockSpec(memory_space=pltpu.SMEM), whole(ga), whole(gb), whole(gn23)]
        + [rowspec(width)] * 3 + [rowspec(width // 2)] * 2 + [rowspec(width)] * 2
        + [part(weights, 0, width, 0), part(weights, 1, width, 0), whole(norms)] + [apart] * len(after),
        out_specs=[rowspec(width)] * 2
        + [rowspec(LANES), whole(side), whole(side), pl.BlockSpec((8, width), lambda i: (0, 0))],
        out_shape=[sds((total, width), bf16), sds((total, width), bf16), sds((total, LANES), f32), side, side, sds((8, width), f32)],
        scratch_shapes=[pltpu.VMEM((2, width, width), f32)],
        name="between",
        **params(7, 13),
    )(core, ga, gb, gn23, *placed(r1), dr2, dr3, dqa, dqb, *placed(h1b, o1), weights, weights, norms, *after)


def self_backward_kernel(
    tile, block, half, items_ref, q_ref, k_ref, v_ref, do_ref, l_ref, delta_ref, idr_ref, x_ref, wq_ref, wk_ref, wv_ref, sofar_ref, *rest
):
    if half:
        core_ref, before_ref = rest[:2]
        gx_ref, keep_ref, send_ref, q_all, ids_all, dq, dk, dv, grads = rest[-9:]
    else:
        gx_ref, grads_ref, q_all, ids_all, dq, dk, dv, grads = rest[-8:]
    step = pl.program_id(0)
    total, width = q_ref.shape

    @pl.when(step == 0)
    def _():
        dq[...] = jnp.zeros_like(dq)
        dk[...] = jnp.zeros_like(dk)
        dv[...] = jnp.zeros_like(dv)
        grads[...] = jnp.zeros_like(grads)
        q_all[...] = q_ref[...] * jnp.asarray(HD ** -0.5, bf16)
        for j in range(total // block):
            ids_all[j * block : (j + 1) * block, :] = column_of(idr_ref[:, j * block : (j + 1) * block])
        attend_back(
            items_ref, idr_ref, ids_all, q_all, do_ref, k_ref, v_ref, l_ref, delta_ref, dq, dk, dv, tile, block,
            2 * half * (width // LANES), True,
        )

    x = x_ref[...]
    rows = x.shape[0]
    here = pl.ds(pl.multiple_of(step * rows, rows), rows)
    gx = sofar_ref[...].astype(f32)
    parts = (dq[here, :] * HD ** -0.5).astype(bf16), dk[here, :].astype(bf16), dv[here, :].astype(bf16)
    for i, (grad, w_ref) in enumerate(zip(parts, (wq_ref, wk_ref, wv_ref))):
        gx += mm(grad, w_ref[0], NT)
        grads[i] += mm(x, grad, TN)
    gx_ref[...] = gx.astype(bf16)

    @pl.when(step == pl.num_programs(0) - 1)
    def _():
        if not half:
            grads_ref[...] = grads[...].astype(bf16)
            return
        r = keep_ref.shape[2]

        def write(device, ref, j):
            place = pl.ds(pl.multiple_of(device * r, r), r)
            for i in range(3):
                ref[j, i, :, :width] = before_ref[i, place, :]
                ref[j, i, :, width:] = grads[i, place, :].astype(bf16)

        spread(keep_ref, send_ref, core_ref[0], write)


def self_backward(
    items, q, k, v, do, l, delta, idr, x, weights, sofar, half, after, core=None, before=None, pairs=1, turns=2, block=QROWS, tile=256
):
    total, width = x.shape
    columns = width // 2
    sds = jax.ShapeDtypeStruct
    sides = [jax.ShapeDtypeStruct((pairs, 3, width // (2 * pairs), width), bf16)] * 2 if half else [jax.ShapeDtypeStruct((3, width, columns), bf16)]
    more = [core, before] if half else []
    rowspec = lambda w: pl.BlockSpec((total // turns, w), lambda i, *_: (i, 0))
    return pl.pallas_call(
        functools.partial(self_backward_kernel, tile, block, half),
        grid_spec=pltpu.PrefetchScalarGridSpec(
            num_scalar_prefetch=1,
            grid=(turns,),
            in_specs=[pl.BlockSpec((total, columns), lambda i, *_: (0, half))] * 4 + [whole(l), whole(delta), whole(idr)]
            + [rowspec(width)] + [part(weights, i, columns, half) for i in range(3)] + [rowspec(width)]
            + ([pl.BlockSpec(memory_space=pltpu.SMEM), whole(before)] if half else []) + [apart] * len(after),
            out_specs=[rowspec(width)] + [whole(side) for side in sides],
            scratch_shapes=[
                pltpu.VMEM((total, columns), bf16), pltpu.VMEM((total, LANES), jnp.int32),
                pltpu.VMEM((total, columns), f32), pltpu.VMEM((total, columns), f32), pltpu.VMEM((total, columns), f32),
                pltpu.VMEM((3, width, columns), f32),
            ],
        ),
        out_shape=[sds((total, width), bf16)] + sides,
        name="self_backward",
        **params(10, 19),
    )(items, *placed(q, k, v), do, *placed(l), delta, idr, *placed(x), weights, weights, weights, sofar, *more, *after)


def add_split_kernel(count, here_ref, *refs):
    places = refs[0].shape[1]
    for m in range(places):
        at = here_ref[0] ^ m
        total = refs[0][:, at].astype(f32)
        for ref in refs[1:count]:
            total += ref[:, at].astype(f32)
        refs[count + m][...] = total.astype(bf16)


def add_split(here, parts, outer, places):
    tail = parts[0].shape[1:]
    parts = [p.reshape((outer, places) + tail) for p in parts]
    out = pl.pallas_call(
        functools.partial(add_split_kernel, len(parts)),
        grid=(outer,),
        in_specs=[pl.BlockSpec(memory_space=pltpu.SMEM)] + [pl.BlockSpec((1, places) + tail, lambda i: (i, 0, 0, 0, 0))] * len(parts),
        out_specs=[pl.BlockSpec((1,) + tail, lambda i: (i, 0, 0, 0))] * places,
        out_shape=[jax.ShapeDtypeStruct((outer,) + tail, bf16)] * places,
        name="add_split",
        **params(3, 24),
    )(here, *parts)
    return list(out)


def own_block(shape):
    return pl.BlockSpec(shape, lambda *_: (0,) * len(shape))


def pack_kernel(moves, count, *refs):
    ins, out_ref, wide = refs[:count], refs[count], refs[count + 1 :]
    rows = out_ref.shape[1]
    for ref, w in zip(ins, wide):
        w[...] = ref[...].astype(f32)
    for source, begin, step, square, block in moves:
        value = wide[source][pl.ds(begin, rows, stride=step), :]
        out_ref[square, :, block * LANES : (block + 1) * LANES] = value.astype(bf16)


def pack(arrays, moves, squares, rows, width, name):
    arrays = [a.reshape(-1, LANES) for a in arrays]
    return pl.pallas_call(
        functools.partial(pack_kernel, moves, len(arrays)),
        in_specs=[own_block(a.shape) for a in arrays],
        out_specs=own_block((squares, rows, width)),
        out_shape=jax.ShapeDtypeStruct((squares, rows, width), bf16),
        scratch_shapes=[pltpu.VMEM(a.shape, f32) for a in arrays],
        name=name,
        **params(1, 16),
    )(*arrays)


def square_moves(source, square, width):
    blocks = width // LANES
    return [(source, b, blocks, square, b) for b in range(blocks)]


def finish_kernel(moves, count, *refs):
    ins, outs = refs[:count], refs[count:]
    rows = ins[0].shape[1]
    for square, block, out, begin, step in moves:
        cols = slice(block * LANES, (block + 1) * LANES)
        total = ins[0][square, :, cols].astype(f32)
        for ref in ins[1:]:
            total += ref[square, :, cols].astype(f32)
        if step:
            outs[out][pl.ds(begin, rows, stride=step), :] = total
        else:
            outs[out][:, cols] = total


def finish(parts, moves, shapes, name):
    return pl.pallas_call(
        functools.partial(finish_kernel, moves, len(parts)),
        in_specs=[own_block(p.shape) for p in parts],
        out_specs=[own_block(s) for s in shapes],
        out_shape=[jax.ShapeDtypeStruct(s, f32) for s in shapes],
        name=name,
        **params(1, 16),
    )(*parts)


def fill_items(ref, first, high, keys, block, tile):
    filled = jnp.int32(0)
    for b in range(len(first)):
        count = (high[b] - first[b] * LANES + tile - 1) // tile

        def put(j, at, b=b):
            ref[0, at] = b
            ref[1, at] = first[b] + j * (tile // LANES)
            return at + 1

        filled = lax.fori_loop(0, count, put, filled)
    for j in range(FORWARD_ITEMS * BACKWARD_ITEMS):
        ref[0, filled + j] = len(first) - 1
        ref[1, filled + j] = keys // LANES
    for i, n in enumerate((FORWARD_ITEMS, BACKWARD_ITEMS)):
        ref[2, i] = (filled + n - 1) // n


def plan_kernel(block, tile, seg_ref, mem_ref, qid_ref, mid_ref, own_ref, cross_ref):
    def ends_of(ref):
        ends, total = [], jnp.int32(0)
        for i in range(ref.shape[1]):
            total += ref[0, i]
            ends.append(total)
        return ends

    ends, mem_ends = ends_of(seg_ref), ends_of(mem_ref)
    for ref, marks in ((qid_ref, ends), (mid_ref, mem_ends)):
        places = lax.broadcasted_iota(jnp.int32, ref.shape, 1)
        ids = jnp.zeros(ref.shape, jnp.int32)
        for mark in marks:
            ids += (places >= mark).astype(jnp.int32)
        ref[...] = ids
    total, keys = qid_ref.shape[1], mid_ref.shape[1]
    own, low, high = [], [], []
    for begin in range(0, total, block):
        own_first, first, last = jnp.int32(0), jnp.int32(0), mem_ref[0, 0]
        for i in range(seg_ref.shape[1]):
            passed = (ends[i] <= begin).astype(jnp.int32)
            own_first += passed * seg_ref[0, i]
            first += passed * mem_ref[0, i]
            if i + 1 < seg_ref.shape[1]:
                last += (ends[i] <= begin + block - 1).astype(jnp.int32) * mem_ref[0, i + 1]
        own.append(own_first // LANES)
        low.append(first // LANES)
        high.append(last)
    fill_items(own_ref, own, [begin + block for begin in range(0, total, block)], total, block, tile)
    fill_items(cross_ref, low, high, keys, block, tile)


def plan(seg, mem, total, keys, block=QROWS, tile=256):
    smem = pl.BlockSpec(memory_space=pltpu.SMEM)
    sds = jax.ShapeDtypeStruct
    more = FORWARD_ITEMS * BACKWARD_ITEMS
    return pl.pallas_call(
        functools.partial(plan_kernel, block, tile),
        in_specs=[smem, smem],
        out_specs=[own_block((1, total)), own_block((1, keys)), smem, smem],
        out_shape=[
            sds((1, total), jnp.int32), sds((1, keys), jnp.int32),
            sds((3, total // block * (total // tile) + more), jnp.int32), sds((3, total // block * (keys // tile) + more), jnp.int32),
        ],
        name="plan",
        **params(1, 16),
    )(seg, mem)


def mesh_size():
    return lax.axis_size("dp") * lax.axis_size("fsdp")


def position():
    return lax.axis_index("dp") * lax.axis_size("fsdp") + lax.axis_index("fsdp")


def bit_groups():
    count = mesh_size().bit_length() - 1
    groups = [(0, 1)]
    while groups[-1][0] + groups[-1][1] < count:
        low = groups[-1][0] + groups[-1][1]
        groups.append((low, min(2, count - low)))
    return groups


def swap(x, mask):
    return lax.ppermute(x, ("dp", "fsdp"), [(i, i ^ mask) for i in range(mesh_size())])


def place_in(group):
    return (position() >> group[0]) & ((1 << group[1]) - 1)


def tie(x, *after):
    return lax.optimization_barrier((x, *after))[0] if after else x


def gather_step(x, group, after=()):
    low, width = group
    here = place_in(group)
    blocks = [x] + tie([swap(x, m << low) for m in range(1, 1 << width)], *after)
    for j in range(width):
        flip = (here >> j) & 1 == 1
        blocks = [jnp.where(flip, blocks[p ^ (1 << j)], blocks[p]) for p in range(1 << width)]
    return jnp.stack(blocks, axis=x.ndim - 2)


def gathered(x):
    return x.reshape(x.shape[:1] + (-1, x.shape[-1]))


def swap_pieces(parts, group, after=()):
    return [parts[0]] + tie([swap(parts[m], m << group[0]) for m in range(1, len(parts))], *after)


def next_pieces(parts, groups, done):
    group = groups[done]
    outer = 1 << sum(g[1] for g in groups[done + 1 :])
    return add_split(place_in(group).reshape(1).astype(jnp.int32), parts, outer, 1 << group[1])


def norm_parts(norm_params, size):
    parts, left = [], norm_params
    for _ in range(3):
        part = left.astype(bf16)
        parts.append(jnp.pad(part, (0, LANES - part.size)))
        left = left - part.astype(f32)
    flat = jnp.concatenate(parts)
    return jnp.pad(flat, (0, size - flat.size))


def resplit(keep, send, devices, core, squares):
    halves = jnp.concatenate([keep, send])
    width = halves.shape[-1]
    first = halves[:, :squares].transpose(1, 0, 2, 3).reshape(squares, devices, -1, width).transpose(1, 0, 2, 3)
    rows = first.shape[2]
    if halves.shape[1] > squares:
        rest = halves[:, squares:].reshape(devices, halves.shape[1] - squares, rows, width)
        first = jnp.concatenate([first, rest], axis=1)
    both = first.reshape(devices // 2, 2, -1, rows, width)
    return [lax.dynamic_index_in_dim(both, core ^ m, 1, keepdims=False) for m in range(2)]


def body(
    inputs, memory, seg_lengths, mem_lengths, self_query, self_key, self_value, self_out,
    cross_query, cross_key, cross_value, cross_out, ffn_in, ffn_out, norm_params, cotangent,
):
    total, width = inputs.shape
    keys = memory.shape[0]
    devices = mesh_size()
    groups = bit_groups()
    down = groups[::-1]
    shard = norm_params.shape[0]
    size = self_query.shape[0]
    own_rows = size // width
    blocks = ffn_in.shape[0] // size
    whole_tiles = own_rows % 16 == 0
    core = place_in(groups[0]).reshape(1).astype(jnp.int32)

    firsts = (self_query, self_key, self_value)
    seconds = (self_out, cross_query, cross_key, cross_value, norm_parts(norm_params, size))
    if whole_tiles:
        lane_blocks = width // LANES
        three = [m for i in range(3) for m in square_moves(i, i, width)]
        five = three + [m for i in range(3, 5) for m in square_moves(i, i, width)]
        wide = [(0, c * lane_blocks + b, blocks * lane_blocks, c, b) for c in range(blocks) for b in range(lane_blocks)]
        tall = [(1, j * own_rows * lane_blocks + b, lane_blocks, blocks + j, b) for j in range(blocks) for b in range(lane_blocks)]
        first = pack(firsts, three, 3, own_rows, width, "pack_self")
        second = pack(tie(seconds, first), five, 5, own_rows, width, "pack_cross")
        last = square_moves(2, 2 * blocks, width)
        ffn_own = pack(tie((ffn_in, ffn_out, cross_out), first), wide + tall + last, 2 * blocks + 1, own_rows, width, "pack_ffn")
    else:
        first = jnp.concatenate(firsts).reshape(3, own_rows, width)
        second = jnp.concatenate(seconds).reshape(5, own_rows, width)
        fi = ffn_in.reshape(own_rows, blocks, width).transpose(1, 0, 2)
        ffn_own = jnp.concatenate([fi, ffn_out.reshape(blocks, own_rows, width), cross_out.reshape(1, own_rows, width)])
    for i, g in enumerate(down[:-1]):
        first = gather_step(first, g, [second] if i else [])
        begun = begun if i else first
        if i < len(down) - 2:
            second = gather_step(second, g)
    early = second
    first = gathered(gather_step(first, down[-1]))
    ffn_all = lax.all_gather(ffn_own.reshape(-1, width), ("dp", "fsdp"), axis=0, tiled=True)
    ffn_all = ffn_all.reshape(devices, 2 * blocks + 1, own_rows, width)
    if not whole_tiles:
        squares = [ffn_all[:, i].reshape(width, width) for i in range(blocks)]
        squares += list(ffn_all[:, blocks : 2 * blocks].reshape(blocks, width, width))
        ffn_all = jnp.stack(squares + [ffn_all[:, 2 * blocks].reshape(width, width)])[None]
    pairs = devices // 2 if whole_tiles else 1
    part_of = core if whole_tiles else jnp.zeros_like(core)

    qid, mid, own_items, items = plan(*tie((seg_lengths, mem_lengths), begun), total, keys)
    q1, k1, v1, o1, l1 = self_forward(own_items, inputs, first, qid, [early])
    second = gather_step(second, down[-2], [l1])
    second = gathered(gather_step(second, down[-1]))
    norm_all = second[4].reshape(devices, -1)[:, : 3 * LANES].reshape(devices, 3, LANES)[:, :, :shard].astype(f32)
    norms = jnp.sum(norm_all, axis=1).reshape(6, width)
    k2, v2, r1, h1b, q2, h1, o2, l2 = cross_forward(items, memory, inputs, o1, second, norms, qid, mid)
    out, dr3, dr2, do2, delta2, keep, send, gn23 = ffn(part_of, pairs, h1, inputs, cotangent, o2, ffn_all, norms)

    one = [keep, send] if whole_tiles else resplit(keep, send, devices, core[0], blocks + 1)
    dq2a, dk2a, dv2a, gckva = cross_backward(items, q2, k2, v2, do2, l2, delta2, qid, mid, memory, 0, [])
    one = next_pieces(swap_pieces(one, groups[0], [dq2a]), groups, 1)
    dq2b, dk2b, dv2b, gckvb = cross_backward(items, q2, k2, v2, do2, l2, delta2, qid, mid, memory, 1, one[1:])
    gm = memory_grad(dk2a, dk2b, dv2a, dv2b, second, 2, [])
    dsum, do1, delta1, keep, send, gn = between(
        part_of, pairs, gckva, gckvb, gn23, r1, dr2, dr3, dq2a, dq2b, h1b, o1, second, norms, [gm]
    )
    two = [keep, send]
    if not whole_tiles:
        two = resplit(keep, send, devices, core[0], 5)
        own_norms = jnp.pad(gn[:6].astype(bf16).reshape(devices, -1), ((0, 0), (0, size - shard)))
        own_norms = own_norms.reshape(devices // 2, 2, own_rows, width)
        two = [two[m].at[:, 4].set(lax.dynamic_index_in_dim(own_norms, core[0] ^ m, 1, keepdims=False)) for m in range(2)]
    one = next_pieces(swap_pieces(one, groups[1], [do1]), groups, 2)
    gxa, gsa = self_backward(own_items, q1, k1, v1, do1, l1, delta1, qid, inputs, first, dsum, 0, one[1:])
    for i in range(3, len(groups)):
        one = next_pieces(swap_pieces(one, groups[i - 1]), groups, i)
    one = swap_pieces(one, groups[-1], [gsa])
    two = next_pieces(swap_pieces(two, groups[0], [gsa]), groups, 1)
    gx, keep, send = self_backward(
        own_items, q1, k1, v1, do1, l1, delta1, qid, inputs, first, gxa, 1, two[1:] + one[1:2], core=part_of, before=gsa, pairs=pairs
    )
    two = next_pieces(swap_pieces(two, groups[1], [gx]), groups, 2)
    keep, send = tie((keep, send), two[1])
    three = [keep, send] if whole_tiles else resplit(keep, send, devices, core[0], 3)
    three = next_pieces(swap_pieces(three, groups[0]), groups, 1)
    for i in range(2, len(groups)):
        three = next_pieces(swap_pieces(three, groups[i - 1]), groups, i)
        if i > 2:
            two = next_pieces(swap_pieces(two, groups[i - 1]), groups, i)

    def flat(g):
        return g.reshape(-1)

    chains = [one, swap_pieces(two, groups[-1]), swap_pieces(three, groups[-1])]
    chains = [[p.reshape(-1, own_rows, width) for p in chain] for chain in chains]
    if whole_tiles:
        lane_rows = size // LANES
        square, long = (lane_rows, LANES), (blocks * lane_rows, LANES)

        moves = [(c, b, 0, c * lane_blocks + b, blocks * lane_blocks) for c in range(blocks) for b in range(lane_blocks)]
        moves += [(blocks, b, 1, b, lane_blocks) for b in range(lane_blocks)]
        moves += [
            (blocks + 1 + j, b, 2, j * own_rows * lane_blocks + b, lane_blocks) for j in range(blocks) for b in range(lane_blocks)
        ]
        gfi, gco, gfo = finish(chains[0], moves, [long, square, long], "finish_ffn")
        moves = [(i, b, i, b, lane_blocks) for i in range(4) for b in range(lane_blocks)] + [(4, b, 4, 0, 0) for b in range(lane_blocks)]
        gck, gcv, gcq, gso, gn = finish(chains[1], moves, [square] * 4 + [(own_rows, width)], "finish_cross")
        gn = lax.dynamic_slice_in_dim(flat(gn[:6]), position() * shard, shard)
        moves = [(i, b, i, b, lane_blocks) for i in range(3) for b in range(lane_blocks)]
        gsq, gsk, gsv = finish(chains[2], moves, [square] * 3, "finish_self")
    else:
        one, two, three = (sum(p.astype(f32) for p in chain) for chain in chains)
        gfi, gco, gfo = one[:blocks].transpose(1, 0, 2), one[blocks], one[blocks + 1 :]
        gck, gcv, gcq, gso, gn = two[0], two[1], two[2], two[3], flat(two[4])[:shard]
        gsq, gsk, gsv = three[0], three[1], three[2]
    return (out, gx, gm) + tuple(flat(g) for g in (gsq, gsk, gsv, gso, gcq, gck, gcv, gco, gfi, gfo, gn))


def solution(mesh):
    rows, flat = P(("dp", "fsdp"), None), P(("dp", "fsdp"))
    return jax.shard_map(
        body,
        mesh=mesh,
        in_specs=(rows,) * 4 + (flat,) * 11 + (rows,),
        out_specs=(rows,) * 3 + (flat,) * 11,
        check_vma=False,
    )
```

```python
import functools
import jax
import jax.numpy as jnp
from jax import lax
from jax.experimental import pallas as pl
from jax.experimental.pallas import tpu as pltpu
from jax.sharding import PartitionSpec as P

HD = 64
LANES = 128
MOST = 256
QROWS = 128
EACH = (2, 3, 6)
PADDING = 6
FFN_CHUNK = 256
masked_score = -1e30
norm_eps = 1e-05
bf16, f32 = jnp.bfloat16, jnp.float32
NT = (((1,), (1,)), ((), ()))
TN = (((0,), (0,)), ((), ()))
NN = (((1,), (0,)), ((), ()))


def mm(left, right, dims=NN):
    return lax.dot_general(left, right, dims, preferred_element_type=f32)


def norm_rows(source):
    mean = jnp.mean(source, axis=-1, keepdims=True)
    centered = source - mean
    variance = jnp.mean(centered * centered, axis=-1, keepdims=True)
    rstd = lax.rsqrt(variance + norm_eps)
    return centered * rstd, rstd


def lane_below(rows):
    return lax.broadcasted_iota(jnp.int32, (rows, LANES), 1) < HD


def column_of(row):
    return jnp.broadcast_to(row, (LANES, row.shape[1])).T


def head_part(pair, which, low):
    return jnp.where(low == (which == 0), pair, jnp.zeros_like(pair))


def values_with_ones(values):
    parts = []
    for p in range(values.shape[1] // LANES):
        pair = values[:, p * LANES : (p + 1) * LANES]
        parts += [pair, jnp.ones_like(pair)]
    return jnp.concatenate(parts, axis=1)


def finish_heads(at, top, tot, acc, write):
    shape = acc.shape[0], at.size if hasattr(at, "size") else at.stop - at.start, LANES
    lane = lax.broadcasted_iota(jnp.int32, shape[1:], 1)
    sums, tops = jnp.ones(shape[1:], f32), jnp.zeros(shape[1:], f32)
    for p in range(shape[0]):
        total = tot[p, at, :]
        write(p, (acc[p, at, :] / total).astype(bf16))
        sums = jnp.where(lane % HD == p, total, sums)
        tops = jnp.where(lane == p, top[2 * p, at, :], jnp.where(lane == HD + p, top[2 * p + 1, at, :], tops))
    return tops + jnp.log(sums)


def column_at(head):
    return head % 2 * HD + head // 2


def item_at(items_ref, n, idk_ref, ids_q, keys, tile, block, causal):
    begin = pl.multiple_of(items_ref[0, n] * block, block)
    wanted = items_ref[1, n] * LANES
    start = pl.multiple_of(jnp.minimum(wanted, keys - tile), LANES)
    at = pl.ds(begin, block)
    pos = start + lax.broadcasted_iota(jnp.int32, (1, tile), 1)
    ids_k = jnp.where(pos >= wanted, idk_ref[:, pl.ds(start, tile)], -1)
    allowed = ids_q[at, :1] == ids_k
    if causal:
        allowed &= pos <= begin + lax.broadcasted_iota(jnp.int32, (block, 1), 0)
    return at, pl.ds(start, tile), jnp.where(allowed, 0.0, masked_score).astype(f32)


def attend(items_ref, idk_ref, ids_q, q_all, k_all, vx_all, top, tot, acc, tile, block, causal):
    keys, width = k_all.shape
    pairs = width // LANES
    heads = 2 * pairs
    low = lane_below(block)
    top[...] = jnp.full(top.shape, masked_score, f32)
    tot[...] = jnp.zeros(tot.shape, f32)
    acc[...] = jnp.zeros(acc.shape, f32)

    def some(i, _):
        loads, made = [], []
        for t in range(EACH[0]):
            at, there, bias = item_at(items_ref, EACH[0] * i + t, idk_ref, ids_q, keys, tile, block, causal)
            loads.append((at, there, bias))
            for p in range(pairs):
                cols = slice(p * LANES, (p + 1) * LANES)
                part = q_all[at, cols]
                both = jnp.concatenate([head_part(part, h, low) for h in range(2)])
                made.append(mm(both, k_all[there, cols], NT))
        weights, scales = [], []
        for t, (at, there, bias) in enumerate(loads):
            for head in range(heads):
                s = made[t * pairs + head // 2][head % 2 * block : (head % 2 + 1) * block] + bias
                old = top[head, at, :]
                new = jnp.maximum(old, jnp.max(s, axis=1, keepdims=True))
                top[head, at, :] = new
                scales.append(jnp.exp(old - new))
                weights.append(jnp.exp(s - jnp.concatenate([new] * (tile // LANES), axis=1)).astype(bf16))
        mixed = [
            mm(jnp.concatenate(weights[t * heads + 2 * p : t * heads + 2 * p + 2]), vx_all[there, 2 * p * LANES : 2 * (p + 1) * LANES])
            for t, (_, there, _) in enumerate(loads) for p in range(pairs)
        ]
        for t, (at, _, _) in enumerate(loads):
            for p in range(pairs):
                n = t * pairs + p
                scale = jnp.where(low, scales[2 * n], scales[2 * n + 1])
                o = mixed[n]
                acc[p, at, :] = acc[p, at, :] * scale + jnp.where(low, o[:block, :LANES], o[block:, :LANES])
                tot[p, at, :] = tot[p, at, :] * scale + jnp.where(low, o[:block, LANES:], o[block:, LANES:])
        return 0

    lax.fori_loop(0, items_ref[2, 0], some, 0)


def attend_back(items_ref, idk_ref, ids_q, q_all, do_ref, k_ref, v_ref, l_ref, delta_ref, dq, dk, dv, tile, block, first_head, causal, each):
    keys, width = k_ref.shape
    pairs = width // LANES
    low = lane_below(block)

    def some(i, _):
        loads, scores, grads = [], [], []
        for t in range(each):
            at, there, bias = item_at(items_ref, each * i + t, idk_ref, ids_q, keys, tile, block, causal)
            loads.append((at, there, bias))
            for p in range(pairs):
                cols = slice(p * LANES, (p + 1) * LANES)
                q, do = q_all[at, cols], do_ref[at, cols]
                qs = jnp.concatenate([head_part(q, h, low) for h in range(2)])
                dos = jnp.concatenate([head_part(do, h, low) for h in range(2)])
                scores.append((mm(qs, k_ref[there, cols], NT), qs))
                grads.append((mm(dos, v_ref[there, cols], NT), dos))
        weights, slopes = [], []
        for t, (at, there, bias) in enumerate(loads):
            logs, deltas = l_ref[at, :], delta_ref[at, :]
            for p in range(pairs):
                es, ds = [], []
                for h in range(2):
                    lane = column_at(first_head + 2 * p + h)
                    rows = slice(h * block, (h + 1) * block)
                    e = jnp.exp(scores[t * pairs + p][0][rows] + bias - logs[:, lane : lane + 1])
                    es.append(e.astype(bf16))
                    ds.append((e * (grads[t * pairs + p][0][rows] - deltas[:, lane : lane + 1])).astype(bf16))
                weights.append(jnp.concatenate(es))
                slopes.append(jnp.concatenate(ds))
        for t, (at, there, _) in enumerate(loads):
            for p in range(pairs):
                cols = slice(p * LANES, (p + 1) * LANES)
                n = t * pairs + p
                gq = mm(slopes[n], k_ref[there, cols])
                gk = mm(slopes[n], scores[n][1], TN)
                gv = mm(weights[n], grads[n][1], TN)
                dq[at, cols] += jnp.where(low, gq[:block], gq[block:])
                dk[there, cols] += gk
                dv[there, cols] += gv
        return 0

    lax.fori_loop(0, items_ref[2, EACH.index(each)], some, 0)


def self_forward_kernel(tile, block, items_ref, x_ref, wq_ref, wk_ref, wv_ref, idr_ref, *rest):
    q_ref, k_ref, v_ref, o_ref, l_ref, q_all, k_all, vx_all, ids_all, top, tot, acc = rest[-12:]
    step = pl.program_id(0)
    rows = x_ref.shape[0]
    total, width = k_all.shape
    turns = total // rows

    @pl.when(step < turns)
    def _():
        x = x_ref[...]
        q = mm(x, wq_ref[0]).astype(bf16)
        k = mm(x, wk_ref[0]).astype(bf16)
        v = mm(x, wv_ref[0]).astype(bf16)
        q_ref[...] = q
        k_ref[...] = k
        v_ref[...] = v
        here = pl.ds(pl.multiple_of(step * rows, rows), rows)
        q_all[here, :] = q * jnp.asarray(HD ** -0.5, bf16)
        k_all[here, :] = k
        vx_all[here, :] = values_with_ones(v)
        ids_all[here, :] = column_of(idr_ref[:, here])

    @pl.when(step == turns)
    def _():
        attend(items_ref, idr_ref, ids_all, q_all, k_all, vx_all, top, tot, acc, tile, block, True)
        size = 2 * block
        for j in range(total // size):
            at = slice(j * size, (j + 1) * size)

            def write(p, value):
                o_ref[at, p * LANES : (p + 1) * LANES] = value

            l_ref[at, :] = finish_heads(at, top, tot, acc, write)


def whole(a):
    return pl.BlockSpec(a.shape, lambda *_: (0,) * a.ndim)


def part(weights, index, columns, half):
    return pl.BlockSpec((1, weights.shape[1], columns), lambda *_: (index, 0, half))


def params(us, vmem):
    return dict(
        compiler_params=pltpu.CompilerParams(vmem_limit_bytes=vmem * 2**20),
        cost_estimate=pl.CostEstimate(flops=us * 10**9, bytes_accessed=2**20, transcendentals=0),
    )


apart = pl.BlockSpec(memory_space=pl.ANY)


def out_array(shape, dtype):
    return pltpu.HBM(shape, dtype)


def placed(*arrays):
    return [pltpu.with_memory_space_constraint(a, pltpu.HBM) for a in arrays]


def self_forward(items, x, weights, idr, after, turns=2, block=QROWS, tile=256):
    total, width = x.shape
    heads = width // HD
    rows = total // turns
    early = lambda w: pl.BlockSpec((rows, w), lambda i, *_: (jnp.minimum(i, turns - 1), 0))
    fixed = lambda w: pl.BlockSpec((total, w), lambda i, *_: (0, 0))
    sds = out_array
    full = sds((total, width), bf16)
    return pl.pallas_call(
        functools.partial(self_forward_kernel, tile, block),
        grid_spec=pltpu.PrefetchScalarGridSpec(
            num_scalar_prefetch=1,
            grid=(turns + 1,),
            in_specs=[early(width)] + [part(weights, i, width, 0) for i in range(3)] + [whole(idr)] + [apart] * len(after),
            out_specs=[early(width)] * 3 + [fixed(width), fixed(LANES)],
            scratch_shapes=[
                pltpu.VMEM((total, width), bf16), pltpu.VMEM((total, width), bf16), pltpu.VMEM((total, 2 * width), bf16),
                pltpu.VMEM((total, LANES), jnp.int32),
                pltpu.VMEM((heads, total, LANES), f32), pltpu.VMEM((heads // 2, total, LANES), f32), pltpu.VMEM((heads // 2, total, LANES), f32),
            ],
        ),
        out_shape=[full] * 4 + [sds((total, LANES), f32)],
        name="self_forward",
        **params(13, 32),
    )(items, *placed(x), weights, weights, weights, idr, *after)


def cross_forward_kernel(
    tile, block, items_ref, memory_ref, wk_ref, wv_ref, x_ref, o1_ref, wso_ref, wcq_ref, norms_ref, idr_ref, idk_ref,
    k2_ref, v2_ref, r1_ref, h1b_ref, q2_ref, h1_ref, o_ref, l_ref, k_all, vx_all, q_all, ids_all, top, tot, acc,
):
    step = pl.program_id(0)
    rows, width = x_ref.shape
    keys = k_all.shape[0]
    turns = pl.num_programs(0) - 1

    @pl.when(step < turns)
    def _():
        per = memory_ref.shape[0]
        memory = memory_ref[...]
        r1 = x_ref[...].astype(f32) + mm(o1_ref[...], wso_ref[0])
        k2 = mm(memory, wk_ref[0]).astype(bf16)
        r1_ref[...] = r1.astype(bf16)
        n1, _ = norm_rows(r1)
        v2 = mm(memory, wv_ref[0]).astype(bf16)
        h1 = n1 * norms_ref[0:1, :] + norms_ref[1:2, :]
        h1b = h1.astype(bf16)
        h1b_ref[...] = h1b
        q2 = mm(h1b, wcq_ref[0]).astype(bf16)
        q2_ref[...] = q2
        k2_ref[...] = k2
        v2_ref[...] = v2
        here = pl.ds(pl.multiple_of(step * rows, rows), rows)
        q_all[here, :] = q2 * jnp.asarray(HD ** -0.5, bf16)
        h1_ref[...] = h1
        ids_all[here, :] = column_of(idr_ref[:, here])
        there = pl.ds(pl.multiple_of(step * per, per), per)
        k_all[there, :] = k2
        vx_all[there, :] = values_with_ones(v2)

    @pl.when(step == turns)
    def _():
        attend(items_ref, idk_ref, ids_all, q_all, k_all, vx_all, top, tot, acc, tile, block, False)

        size = 2 * block
        for j in range(q_all.shape[0] // size):
            at = slice(j * size, (j + 1) * size)

            def write(p, value):
                o_ref[at, p * LANES : (p + 1) * LANES] = value

            l_ref[at, :] = finish_heads(at, top, tot, acc, write)


def cross_forward(items, memory, x, o1, weights, norms, idr, idk, turns=2, block=QROWS, tile=256):
    total, width = x.shape
    keys = memory.shape[0]
    heads = width // HD
    rows, per = total // turns, keys // turns
    early = lambda r, w: pl.BlockSpec((r, w), lambda i, *_: (jnp.minimum(i, turns - 1), 0))
    fixed = lambda w: pl.BlockSpec((total, w), lambda i, *_: (0, 0))
    sds = out_array
    return pl.pallas_call(
        functools.partial(cross_forward_kernel, tile, block),
        grid_spec=pltpu.PrefetchScalarGridSpec(
            num_scalar_prefetch=1,
            grid=(turns + 1,),
            in_specs=[early(per, width), part(weights, 2, width, 0), part(weights, 3, width, 0)]
            + [early(rows, width), early(rows, width), part(weights, 0, width, 0), part(weights, 1, width, 0)]
            + [whole(norms), whole(idr), whole(idk)],
            out_specs=[early(per, width)] * 2 + [early(rows, width)] * 4 + [fixed(width), fixed(LANES)],
            scratch_shapes=[
                pltpu.VMEM((keys, width), bf16),
                pltpu.VMEM((keys, 2 * width), bf16),
                pltpu.VMEM((total, width), bf16),
                pltpu.VMEM((total, LANES), jnp.int32),
                pltpu.VMEM((heads, total, LANES), f32),
                pltpu.VMEM((heads // 2, total, LANES), f32),
                pltpu.VMEM((heads // 2, total, LANES), f32),
            ],
        ),
        out_shape=[
            sds((keys, width), bf16), sds((keys, width), bf16), sds((total, width), bf16), sds((total, width), bf16),
            sds((total, width), bf16), sds((total, width), f32), sds((total, width), bf16), sds((total, LANES), f32),
        ],
        name="cross_forward",
        **params(19, 44),
    )(items, *placed(memory), weights, weights, *placed(x, o1), weights, weights, norms, idr, idk)


def norm_back(incoming, normal, rstd, gain):
    m = incoming * gain
    return rstd * (
        m - jnp.mean(m, axis=-1, keepdims=True) - normal * jnp.mean(m * normal, axis=-1, keepdims=True)
    )


def head_columns(left, right):
    width = left.shape[1]
    prod = left.astype(f32) * right.astype(f32)
    lane = lax.broadcasted_iota(jnp.int32, (width, LANES), 1)
    own = lax.broadcasted_iota(jnp.int32, (width, LANES), 0) // HD == 2 * (lane % HD) + lane // HD
    own = own.astype(bf16)
    high = prod.astype(bf16)
    low = (prod - high.astype(f32)).astype(bf16)
    return mm(high, own) + mm(low, own)


def column_sums(a):
    return jnp.sum(a, axis=0, keepdims=True)


def spread(keep_ref, send_ref, core, write):
    def one(j, _):
        write(2 * j + core, keep_ref, j)
        write(2 * j + 1 - core, send_ref, j)
        return 0

    lax.fori_loop(0, keep_ref.shape[0], one, 0)


def ffn_kernel(
    core_ref, h1_ref, x_ref, cot_ref, o2_ref, w_ref, norms_ref,
    out_ref, dr3_ref, dr2_ref, do2_ref, delta_ref, keep_ref, send_ref, gn_ref, gin, gout, gco,
):
    step = pl.program_id(0)
    last = pl.num_programs(0) - 1
    width = x_ref.shape[1]
    blocks = w_ref.shape[1] // 2

    @pl.when(step == 0)
    def _():
        gin[...] = jnp.zeros_like(gin)
        gout[...] = jnp.zeros_like(gout)
        gco[...] = jnp.zeros_like(gco)
        gn_ref[...] = jnp.zeros_like(gn_ref)

    win = [w_ref[:, c].reshape(width, width) for c in range(blocks)]
    wout = w_ref[:, blocks : 2 * blocks].reshape(blocks * width, width)
    wco = w_ref[:, 2 * blocks].reshape(width, width)
    n2, rstd2 = norm_rows(h1_ref[...] + mm(o2_ref[...], wco))
    h2 = n2 * norms_ref[2:3, :] + norms_ref[3:4, :]
    h2b = h2.astype(bf16)
    chunk = min(FFN_CHUNK, width)
    parts = blocks * width // chunk
    per = width // chunk

    def win_part(c):
        return win[c // per][:, (c % per) * chunk : (c % per + 1) * chunk]

    acts, slopes, hidden = [], [], [mm(h2b, win_part(0))]
    ff = jnp.zeros(h2.shape, f32)
    for c in range(parts):
        if c + 1 < parts:
            hidden.append(mm(h2b, win_part(c + 1)))
        u = hidden[c]
        square = u * u
        t = jnp.tanh(u * (0.7978845608028654 + (0.7978845608028654 * 0.044715) * square))
        half = 0.5 + 0.5 * t
        acts.append((u * half).astype(bf16))
        rise = u * (0.5 * 0.7978845608028654 + (0.5 * 0.7978845608028654 * 3 * 0.044715) * square)
        slopes.append(half + (1.0 - t * t) * rise)
        if c:
            ff += mm(acts[c - 1], wout[(c - 1) * chunk : c * chunk, :])
    ff += mm(acts[-1], wout[(parts - 1) * chunk :, :])
    r3 = h2 + ff + x_ref[...].astype(f32)
    n3, rstd3 = norm_rows(r3)
    gain3 = norms_ref[4:5, :]
    out_ref[...] = (n3 * gain3 + norms_ref[5:6, :]).astype(bf16)
    e = cot_ref[...].astype(f32)
    gn_ref[2:3, :] += column_sums(e * n3)
    gn_ref[3:4, :] += column_sums(e)
    dr3 = norm_back(e, n3, rstd3, gain3)
    dr3_ref[...] = dr3.astype(bf16)
    dfb = dr3.astype(bf16)
    dh2 = dr3
    raw, made = [mm(dfb, wout[:chunk, :], NT)], []
    for c in range(parts + 1):
        if c + 1 < parts:
            raw.append(mm(dfb, wout[(c + 1) * chunk : (c + 2) * chunk, :], NT))
        if c < parts:
            gout[c * chunk : (c + 1) * chunk, :] += mm(acts[c], dfb, TN)
            made.append((raw[c] * slopes[c]).astype(bf16))
        if c:
            gin[:, (c - 1) * chunk : c * chunk] += mm(h2b, made[c - 1], TN)
            dh2 += mm(made[c - 1], win_part(c - 1), NT)
    gn_ref[0:1, :] += column_sums(dh2 * n2)
    gn_ref[1:2, :] += column_sums(dh2)
    dr2 = norm_back(dh2, n2, rstd2, norms_ref[2:3, :])
    da2 = dr2.astype(bf16)
    dr2_ref[...] = da2
    o2 = o2_ref[...]
    gco[...] += mm(o2, da2, TN)
    do2 = mm(da2, wco, NT).astype(bf16)
    do2_ref[...] = do2
    delta_ref[...] = head_columns(do2, o2)

    @pl.when(step == last)
    def _():
        r = keep_ref.shape[2]

        def write(device, ref, j):
            here = pl.ds(pl.multiple_of(device * r, r), r)
            for c in range(blocks):
                ref[j, c] = gin[here, c * width : (c + 1) * width].astype(bf16)
            ref[j, blocks] = gco[here, :].astype(bf16)
            there = pl.ds(pl.multiple_of(device * blocks * r, blocks * r), blocks * r)
            ref[j, blocks + 1 :] = gout[there, :].astype(bf16).reshape(blocks, r, width)

        spread(keep_ref, send_ref, core_ref[0], write)


def ffn(core, pairs, h1, x, cot, o2, w, norms, rows=512):
    total, width = x.shape
    blocks = w.shape[1] // 2
    rowspec = lambda w: pl.BlockSpec((rows, w), lambda i: (i, 0))
    sds = out_array
    side = jax.ShapeDtypeStruct((pairs, 2 * blocks + 1, width // (2 * pairs), width), bf16)
    return pl.pallas_call(
        ffn_kernel,
        grid=(total // rows,),
        in_specs=[pl.BlockSpec(memory_space=pltpu.SMEM)] + [rowspec(width)] * 4 + [whole(w), whole(norms)],
        out_specs=[rowspec(width)] * 4
        + [rowspec(LANES), whole(side), whole(side), pl.BlockSpec((4, width), lambda i: (0, 0))],
        out_shape=[
            sds((total, width), bf16), sds((total, width), bf16), sds((total, width), bf16), sds((total, width), bf16),
            sds((total, LANES), f32), side, side, sds((4, width), f32),
        ],
        scratch_shapes=[pltpu.VMEM((width, blocks * width), f32), pltpu.VMEM((blocks * width, width), f32), pltpu.VMEM((width, width), f32)],
        name="ffn",
        **params(32, 51),
    )(core, *placed(h1, x, cot, o2, w), norms)


def cross_backward_kernel(
    tile, block, first, count, each, items_ref, q2_ref, k2_ref, v2_ref, do_ref, l_ref, delta_ref, idr_ref, idk_ref, memory_ref, *rest
):
    dq_ref, dk_ref, dv_ref, grads_ref, q_all, ids_all, dq, dk, dv, grads = rest[-10:]
    step = pl.program_id(0)
    total = q2_ref.shape[0]
    begin = first * LANES if q2_ref.shape[1] > count * LANES else 0
    cols = slice(begin, begin + count * LANES)

    @pl.when(step == 0)
    def _():
        dq[...] = jnp.zeros_like(dq)
        dk[...] = jnp.zeros_like(dk)
        dv[...] = jnp.zeros_like(dv)
        grads[...] = jnp.zeros_like(grads)
        q_all[...] = q2_ref[:, cols] * jnp.asarray(HD ** -0.5, bf16)
        for j in range(total // block):
            ids_all[j * block : (j + 1) * block, :] = column_of(idr_ref[:, j * block : (j + 1) * block])
        attend_back(
            items_ref, idk_ref, ids_all, q_all, do_ref.at[:, cols], k2_ref.at[:, cols], v2_ref.at[:, cols], l_ref, delta_ref,
            dq, dk, dv, tile, block, 2 * first, False, each,
        )

    memory = memory_ref[...]
    per = memory.shape[0]
    here = pl.ds(pl.multiple_of(step * per, per), per)
    for i, (ref, out_ref) in enumerate(((dk, dk_ref), (dv, dv_ref))):
        grad = ref[here, :].astype(bf16)
        out_ref[...] = grad
        grads[i] += mm(memory, grad, TN)
    rows = dq_ref.shape[0]
    dq_ref[...] = (dq[pl.ds(pl.multiple_of(step * rows, rows), rows), :] * HD ** -0.5).astype(bf16)

    @pl.when(step == pl.num_programs(0) - 1)
    def _():
        grads_ref[...] = grads[...].astype(bf16)


def cross_backward(items, q2, k2, v2, do, l, delta, idr, idk, memory, first, count, each, after, turns=2, block=QROWS, tile=256):
    total, width = q2.shape
    keys = k2.shape[0]
    columns = count * LANES
    alone = first % count == 0
    cols = lambda r: pl.BlockSpec((r, columns if alone else width), lambda i, *_: (0, first // count if alone else 0))
    rowspec = lambda r, w: pl.BlockSpec((r, w), lambda i, *_: (i, 0))
    sds = jax.ShapeDtypeStruct
    grad = sds((2, width, columns), bf16)
    return pl.pallas_call(
        functools.partial(cross_backward_kernel, tile, block, first, count, each),
        grid_spec=pltpu.PrefetchScalarGridSpec(
            num_scalar_prefetch=1,
            grid=(turns,),
            in_specs=[cols(total), cols(keys), cols(keys), cols(total)]
            + [whole(l), whole(delta), whole(idr), whole(idk), rowspec(keys // turns, width)] + [apart] * len(after),
            out_specs=[rowspec(total // turns, columns), rowspec(keys // turns, columns), rowspec(keys // turns, columns), whole(grad)],
            scratch_shapes=[
                pltpu.VMEM((total, columns), bf16), pltpu.VMEM((total, LANES), jnp.int32), pltpu.VMEM((total, columns), f32),
                pltpu.VMEM((keys, columns), f32), pltpu.VMEM((keys, columns), f32), pltpu.VMEM((2, width, columns), f32),
            ],
        ),
        out_shape=[sds((total, columns), bf16), sds((keys, columns), bf16), sds((keys, columns), bf16), grad],
        name="cross_backward",
        **params(5 * count + 4, 10 * count + 4),
    )(items, *placed(q2, k2, v2, do, l, delta), idr, idk, *placed(memory), *after)


def memory_grad_kernel(ka_ref, kb_ref, va_ref, vb_ref, wk_ref, wv_ref, *rest):
    total = mm(jnp.concatenate([ka_ref[...], kb_ref[...]], axis=1), wk_ref[0], NT)
    total += mm(jnp.concatenate([va_ref[...], vb_ref[...]], axis=1), wv_ref[0], NT)
    rest[-1][...] = total.astype(bf16)


def memory_grad(ka, kb, va, vb, weights, index, after, rows=1024):
    keys, width = ka.shape[0], weights.shape[2]
    rowspec = lambda w: pl.BlockSpec((rows, w), lambda i: (i, 0))
    return pl.pallas_call(
        memory_grad_kernel,
        grid=(keys // rows,),
        in_specs=[rowspec(a.shape[1]) for a in (ka, kb, va, vb)] + [part(weights, index, width, 0), part(weights, index + 1, width, 0)] + [apart] * len(after),
        out_specs=rowspec(width),
        out_shape=out_array((keys, width), bf16),
        name="memory_grad",
        **params(4, 16),
    )(ka, kb, va, vb, weights, weights, *after)


def between_kernel(
    core_ref, ga_ref, gb_ref, gn23_ref, r1_ref, dr2_ref, dr3_ref, dqa_ref, dqb_ref, h1b_ref, o1_ref, wso_ref, wcq_ref, norms_ref, *rest
):
    dsum_ref, do1_ref, delta_ref, keep_ref, send_ref, gn_ref, total = rest[-7:]
    step = pl.program_id(0)

    @pl.when(step == 0)
    def _():
        total[...] = jnp.zeros_like(total)
        gn_ref[...] = jnp.zeros_like(gn_ref)

    dq2 = jnp.concatenate([dqa_ref[...], dqb_ref[...]], axis=1)
    dh1 = dr2_ref[...].astype(f32) + mm(dq2, wcq_ref[0], NT)
    n1, rstd1 = norm_rows(r1_ref[...].astype(f32))
    gn_ref[0:1, :] += column_sums(dh1 * n1)
    gn_ref[1:2, :] += column_sums(dh1)
    dr1 = norm_back(dh1, n1, rstd1, norms_ref[0:1, :])
    dsum_ref[...] = (dr1 + dr3_ref[...].astype(f32)).astype(bf16)
    da1 = dr1.astype(bf16)
    o1 = o1_ref[...]
    do1 = mm(da1, wso_ref[0], NT).astype(bf16)
    do1_ref[...] = do1
    delta_ref[...] = head_columns(do1, o1)
    total[0] += mm(h1b_ref[...], dq2, TN)
    total[1] += mm(o1, da1, TN)

    @pl.when(step == pl.num_programs(0) - 1)
    def _():
        gn_ref[2:6, :] = gn23_ref[...]
        r, width = keep_ref.shape[2:]
        norm_part = jnp.concatenate([gn_ref[...], jnp.zeros((r - 8, width), f32)]).astype(bf16)

        def write(device, ref, j):
            here = pl.ds(pl.multiple_of(device * r, r), r)
            for i in range(2):
                ref[j, i, :, : ga_ref.shape[2]] = ga_ref[i, here, :]
                ref[j, i, :, ga_ref.shape[2] :] = gb_ref[i, here, :]
                ref[j, 2 + i] = total[i, here, :].astype(bf16)
            ref[j, 4] = norm_part

        spread(keep_ref, send_ref, core_ref[0], write)


def between(core, pairs, ga, gb, gn23, r1, dr2, dr3, dqa, dqb, h1b, o1, weights, norms, after, rows=512):
    total, width = r1.shape
    rowspec = lambda w: pl.BlockSpec((rows, w), lambda i: (i, 0))
    sds = jax.ShapeDtypeStruct
    side = jax.ShapeDtypeStruct((pairs, 5, width // (2 * pairs), width), bf16)
    return pl.pallas_call(
        between_kernel,
        grid=(total // rows,),
        in_specs=[pl.BlockSpec(memory_space=pltpu.SMEM), whole(ga), whole(gb), whole(gn23)]
        + [rowspec(width)] * 3 + [rowspec(dqa.shape[1]), rowspec(dqb.shape[1])] + [rowspec(width)] * 2
        + [part(weights, 0, width, 0), part(weights, 1, width, 0), whole(norms)] + [apart] * len(after),
        out_specs=[rowspec(width)] * 2
        + [rowspec(LANES), whole(side), whole(side), pl.BlockSpec((8, width), lambda i: (0, 0))],
        out_shape=[sds((total, width), bf16), sds((total, width), bf16), sds((total, LANES), f32), side, side, sds((8, width), f32)],
        scratch_shapes=[pltpu.VMEM((2, width, width), f32)],
        name="between",
        **params(7, 24),
    )(core, ga, gb, gn23, *placed(r1), dr2, dr3, dqa, dqb, *placed(h1b, o1), weights, weights, norms, *after)


def self_backward_kernel(
    tile, block, core_ref, items_ref, q_ref, k_ref, v_ref, do_ref, l_ref, delta_ref, idr_ref, x_ref, wq_ref, wk_ref, wv_ref, sofar_ref, *rest
):
    gx_ref, keep_ref, send_ref, q_all, ids_all, dq, dk, dv, grads = rest[-9:]
    step = pl.program_id(0)
    total, width = q_ref.shape

    @pl.when(step == 0)
    def _():
        dq[...] = jnp.zeros_like(dq)
        dk[...] = jnp.zeros_like(dk)
        dv[...] = jnp.zeros_like(dv)
        grads[...] = jnp.zeros_like(grads)
        q_all[...] = q_ref[...] * jnp.asarray(HD ** -0.5, bf16)
        for j in range(total // block):
            ids_all[j * block : (j + 1) * block, :] = column_of(idr_ref[:, j * block : (j + 1) * block])
        attend_back(
            items_ref, idr_ref, ids_all, q_all, do_ref, k_ref, v_ref, l_ref, delta_ref, dq, dk, dv, tile, block, 0, True, 2
        )

    x = x_ref[...]
    rows = x.shape[0]
    here = pl.ds(pl.multiple_of(step * rows, rows), rows)
    gx = sofar_ref[...].astype(f32)
    parts = (dq[here, :] * HD ** -0.5).astype(bf16), dk[here, :].astype(bf16), dv[here, :].astype(bf16)
    for i, (grad, w_ref) in enumerate(zip(parts, (wq_ref, wk_ref, wv_ref))):
        gx += mm(grad, w_ref[0], NT)
        grads[i] += mm(x, grad, TN)
    gx_ref[...] = gx.astype(bf16)

    @pl.when(step == pl.num_programs(0) - 1)
    def _():
        r = keep_ref.shape[2]

        def write(device, ref, j):
            place = pl.ds(pl.multiple_of(device * r, r), r)
            for i in range(3):
                ref[j, i] = grads[i, place, :].astype(bf16)

        spread(keep_ref, send_ref, core_ref[0], write)


def self_backward(core, pairs, items, q, k, v, do, l, delta, idr, x, weights, sofar, after, turns=2, block=QROWS, tile=256):
    total, width = x.shape
    sds = jax.ShapeDtypeStruct
    side = sds((pairs, 3, width // (2 * pairs), width), bf16)
    rowspec = lambda w: pl.BlockSpec((total // turns, w), lambda i, *_: (i, 0))
    return pl.pallas_call(
        functools.partial(self_backward_kernel, tile, block),
        grid_spec=pltpu.PrefetchScalarGridSpec(
            num_scalar_prefetch=2,
            grid=(turns,),
            in_specs=[whole(a) for a in (q, k, v, do, l, delta, idr)]
            + [rowspec(width)] + [part(weights, i, width, 0) for i in range(3)] + [rowspec(width)] + [apart] * len(after),
            out_specs=[rowspec(width), whole(side), whole(side)],
            scratch_shapes=[
                pltpu.VMEM((total, width), bf16), pltpu.VMEM((total, LANES), jnp.int32),
                pltpu.VMEM((total, width), f32), pltpu.VMEM((total, width), f32), pltpu.VMEM((total, width), f32),
                pltpu.VMEM((3, width, width), f32),
            ],
        ),
        out_shape=[sds((total, width), bf16), side, side],
        name="self_backward",
        **params(17, 34),
    )(core, items, q, k, v, do, l, delta, idr, x, weights, weights, weights, sofar, *after)


def add_split_kernel(count, here_ref, *refs):
    places = refs[0].shape[1]
    for m in range(places):
        at = here_ref[0] ^ m
        total = refs[0][:, at].astype(f32)
        for ref in refs[1:count]:
            total += ref[:, at].astype(f32)
        refs[count + m][...] = total.astype(bf16)


def add_split(here, parts, outer, places):
    tail = parts[0].shape[1:]
    parts = [p.reshape((outer, places) + tail) for p in parts]
    out = pl.pallas_call(
        functools.partial(add_split_kernel, len(parts)),
        grid=(outer,),
        in_specs=[pl.BlockSpec(memory_space=pltpu.SMEM)] + [pl.BlockSpec((1, places) + tail, lambda i: (i, 0, 0, 0, 0))] * len(parts),
        out_specs=[pl.BlockSpec((1,) + tail, lambda i: (i, 0, 0, 0))] * places,
        out_shape=[jax.ShapeDtypeStruct((outer,) + tail, bf16)] * places,
        name="add_split",
        **params(3, 24),
    )(here, *parts)
    return list(out)


def first_pair_kernel(cut, here_ref, keep, came, *outs):
    for m in range(2):
        at = here_ref[0] ^ m
        outs[m][0] = (keep[0, :, at, :cut].astype(f32) + came[0, :, at, :cut].astype(f32)).astype(bf16)
        at = here_ref[1] ^ m
        outs[2 + m][0] = (keep[0, at, :, cut:].astype(f32) + came[0, at, :, cut:].astype(f32)).astype(bf16)


def first_pair(here, keep, came, outer, cut):
    squares, rows, width = keep.shape[1:]
    parts = [p.reshape(outer, 2, 2, squares, rows, width) for p in (keep, came)]
    shapes = [(outer, 2, n, rows, width) for n in (cut, cut, squares - cut, squares - cut)]
    out = pl.pallas_call(
        functools.partial(first_pair_kernel, cut),
        grid=(outer,),
        in_specs=[pl.BlockSpec(memory_space=pltpu.SMEM)] + [pl.BlockSpec((1,) + p.shape[1:], lambda i: (i, 0, 0, 0, 0, 0)) for p in parts],
        out_specs=[pl.BlockSpec((1,) + s[1:], lambda i: (i, 0, 0, 0, 0)) for s in shapes],
        out_shape=[jax.ShapeDtypeStruct(s, bf16) for s in shapes],
        name="first_pair",
        **params(2, 24),
    )(here, *parts)
    return list(out)


def second_pair_kernel(here_ref, keep_a, came_a, keep_b, came_b, *outs):
    for m in range(2):
        at = here_ref[1] ^ m
        outs[m][0] = (keep_a[0, at].astype(f32) + came_a[0, at].astype(f32)).astype(bf16)
        at = here_ref[0] ^ m
        outs[2 + m][0] = (keep_b[0, at].astype(f32) + came_b[0, at].astype(f32)).astype(bf16)


def second_pair(here, parts):
    outer = parts[0].shape[0]
    shapes = [(p.shape[0],) + p.shape[2:] for p in parts]
    out = pl.pallas_call(
        second_pair_kernel,
        grid=(outer,),
        in_specs=[pl.BlockSpec(memory_space=pltpu.SMEM)] + [pl.BlockSpec((1,) + p.shape[1:], lambda i: (i, 0, 0, 0, 0)) for p in parts],
        out_specs=[pl.BlockSpec((1,) + s[1:], lambda i: (i, 0, 0, 0)) for s in shapes],
        out_shape=[jax.ShapeDtypeStruct(s, bf16) for s in shapes],
        name="second_pair",
        **params(1, 24),
    )(here, *parts)
    return list(out)


def join_split_kernel(here_ref, keep_a, came_a, keep_b, came_b, *outs):
    cut = keep_a.shape[2]
    for m, out in enumerate(outs):
        at = here_ref[0] ^ m
        out[:, :cut] = (keep_a[:, at].astype(f32) + came_a[:, at].astype(f32)).astype(bf16)
        out[:, cut:] = (keep_b[:, at].astype(f32) + came_b[:, at].astype(f32)).astype(bf16)


def join_split(here, parts, outer, places):
    parts = [p.reshape((outer, places) + p.shape[1:]) for p in parts]
    tail = (parts[0].shape[2] + parts[2].shape[2],) + parts[0].shape[3:]
    out = pl.pallas_call(
        join_split_kernel,
        grid=(outer,),
        in_specs=[pl.BlockSpec(memory_space=pltpu.SMEM)] + [pl.BlockSpec((1,) + p.shape[1:], lambda i: (i, 0, 0, 0, 0)) for p in parts],
        out_specs=[pl.BlockSpec((1,) + tail, lambda i: (i, 0, 0, 0))] * places,
        out_shape=[jax.ShapeDtypeStruct((outer,) + tail, bf16)] * places,
        name="join_split",
        **params(1, 24),
    )(here, *parts)
    return list(out)


def own_block(shape):
    return pl.BlockSpec(shape, lambda *_: (0,) * len(shape))


def pack_kernel(moves, count, *refs):
    ins, out_ref, wide = refs[:count], refs[count], refs[count + 1 :]
    rows = out_ref.shape[1]
    for ref, w in zip(ins, wide):
        w[...] = ref[...].astype(f32)
    for source, begin, step, square, block in moves:
        value = wide[source][pl.ds(begin, rows, stride=step), :]
        out_ref[square, :, block * LANES : (block + 1) * LANES] = value.astype(bf16)


def pack(arrays, moves, squares, rows, width, name):
    arrays = [a.reshape(-1, LANES) for a in arrays]
    return pl.pallas_call(
        functools.partial(pack_kernel, moves, len(arrays)),
        in_specs=[own_block(a.shape) for a in arrays],
        out_specs=own_block((squares, rows, width)),
        out_shape=jax.ShapeDtypeStruct((squares, rows, width), bf16),
        scratch_shapes=[pltpu.VMEM(a.shape, f32) for a in arrays],
        name=name,
        **params(1, 16),
    )(*placed(*arrays))


def square_moves(source, square, width):
    blocks = width // LANES
    return [(source, b, blocks, square, b) for b in range(blocks)]


def finish_kernel(moves, count, *refs):
    ins, outs = refs[:count], refs[count:]
    rows = ins[0].shape[1]
    for square, block, out, begin, step in moves:
        cols = slice(block * LANES, (block + 1) * LANES)
        total = ins[0][square, :, cols].astype(f32)
        for ref in ins[1:]:
            total += ref[square, :, cols].astype(f32)
        if step:
            outs[out][pl.ds(begin, rows, stride=step), :] = total
        else:
            outs[out][:, cols] = total


def finish(parts, moves, shapes, name):
    return pl.pallas_call(
        functools.partial(finish_kernel, moves, len(parts)),
        in_specs=[own_block(p.shape) for p in parts],
        out_specs=[own_block(s) for s in shapes],
        out_shape=[jax.ShapeDtypeStruct(s, f32) for s in shapes],
        name=name,
        **params(1, 16),
    )(*parts)


def fill_items(ref, first, high, keys, block, tile):
    filled = jnp.int32(0)
    for b in range(len(first)):
        count = (high[b] - first[b] * LANES + tile - 1) // tile

        def put(j, at, b=b):
            ref[0, at] = b
            ref[1, at] = first[b] + j * (tile // LANES)
            return at + 1

        filled = lax.fori_loop(0, count, put, filled)
    for j in range(PADDING):
        ref[0, filled + j] = len(first) - 1
        ref[1, filled + j] = keys // LANES
    for i, n in enumerate(EACH):
        ref[2, i] = (filled + n - 1) // n


def plan_kernel(block, tile, seg_ref, mem_ref, qid_ref, mid_ref, own_ref, cross_ref):
    def ends_of(ref):
        ends, total = [], jnp.int32(0)
        for i in range(ref.shape[1]):
            total += ref[0, i]
            ends.append(total)
        return ends

    ends, mem_ends = ends_of(seg_ref), ends_of(mem_ref)
    for ref, marks in ((qid_ref, ends), (mid_ref, mem_ends)):
        places = lax.broadcasted_iota(jnp.int32, ref.shape, 1)
        ids = jnp.zeros(ref.shape, jnp.int32)
        for mark in marks:
            ids += (places >= mark).astype(jnp.int32)
        ref[...] = ids
    total, keys = qid_ref.shape[1], mid_ref.shape[1]
    own, low, high = [], [], []
    for begin in range(0, total, block):
        own_first, first, last = jnp.int32(0), jnp.int32(0), mem_ref[0, 0]
        for i in range(seg_ref.shape[1]):
            passed = (ends[i] <= begin).astype(jnp.int32)
            own_first += passed * seg_ref[0, i]
            first += passed * mem_ref[0, i]
            if i + 1 < seg_ref.shape[1]:
                last += (ends[i] <= begin + block - 1).astype(jnp.int32) * mem_ref[0, i + 1]
        own.append(own_first // LANES)
        low.append(first // LANES)
        high.append(last)
    fill_items(own_ref, own, [begin + block for begin in range(0, total, block)], total, block, tile)
    fill_items(cross_ref, low, high, keys, block, tile)


def plan(seg, mem, total, keys, block=QROWS, tile=256):
    smem = pl.BlockSpec(memory_space=pltpu.SMEM)
    sds = jax.ShapeDtypeStruct
    more = PADDING
    return pl.pallas_call(
        functools.partial(plan_kernel, block, tile),
        in_specs=[smem, smem],
        out_specs=[own_block((1, total)), own_block((1, keys)), smem, smem],
        out_shape=[
            sds((1, total), jnp.int32), sds((1, keys), jnp.int32),
            sds((3, total // block * (total // tile) + more), jnp.int32), sds((3, total // block * (keys // tile) + more), jnp.int32),
        ],
        name="plan",
        **params(1, 16),
    )(seg, mem)

HEAD_START = 1


def mesh_size():
    return lax.axis_size("dp") * lax.axis_size("fsdp")


def position():
    return lax.axis_index("dp") * lax.axis_size("fsdp") + lax.axis_index("fsdp")


def bit_groups(wide):
    count = mesh_size().bit_length() - 1
    groups = [(0, 1)]
    while groups[-1][0] + groups[-1][1] < count:
        low = groups[-1][0] + groups[-1][1]
        groups.append((low, min(2 if len(groups) <= wide else 1, count - low)))
    return groups


def swap(x, mask):
    return lax.ppermute(x, ("dp", "fsdp"), [(i, i ^ mask) for i in range(mesh_size())])


def place_in(group):
    return (position() >> group[0]) & ((1 << group[1]) - 1)


def tie(x, *after):
    return lax.optimization_barrier((x, *after))[0] if after else x


def gather_step(x, group, after=()):
    low, width = group
    here = place_in(group)
    blocks = [x] + tie([swap(x, m << low) for m in range(1, 1 << width)], *after)
    for j in range(width):
        flip = (here >> j) & 1 == 1
        blocks = [jnp.where(flip, blocks[p ^ (1 << j)], blocks[p]) for p in range(1 << width)]
    return jnp.stack(blocks, axis=x.ndim - 2)


def gathered(x):
    return x.reshape(x.shape[:1] + (-1, x.shape[-1]))


def swap_pieces(parts, group, after=()):
    return [parts[0]] + tie([swap(parts[m], m << group[0]) for m in range(1, len(parts))], *after)


def next_pieces(parts, groups, done):
    group = groups[done]
    outer = 1 << sum(g[1] for g in groups[done + 1 :])
    return add_split(place_in(group).reshape(1).astype(jnp.int32), parts, outer, 1 << group[1])


def norm_parts(norm_params, size):
    parts, left = [], norm_params
    for _ in range(3):
        part = left.astype(bf16)
        parts.append(jnp.pad(part, (0, LANES - part.size)))
        left = left - part.astype(f32)
    flat = jnp.concatenate(parts)
    return jnp.pad(flat, (0, size - flat.size))


def resplit(keep, send, devices, core, squares):
    halves = jnp.concatenate([keep, send])
    width = halves.shape[-1]
    first = halves[:, :squares].transpose(1, 0, 2, 3).reshape(squares, devices, -1, width).transpose(1, 0, 2, 3)
    rows = first.shape[2]
    if halves.shape[1] > squares:
        rest = halves[:, squares:].reshape(devices, halves.shape[1] - squares, rows, width)
        first = jnp.concatenate([first, rest], axis=1)
    both = first.reshape(devices // 2, 2, -1, rows, width)
    return [lax.dynamic_index_in_dim(both, core ^ m, 1, keepdims=False) for m in range(2)]


def body(
    inputs, memory, seg_lengths, mem_lengths, self_query, self_key, self_value, self_out,
    cross_query, cross_key, cross_value, cross_out, ffn_in, ffn_out, norm_params, cotangent,
):
    total, width = inputs.shape
    keys = memory.shape[0]
    devices = mesh_size()
    groups, single = bit_groups(8), bit_groups(1)
    down = groups[::-1]
    shard = norm_params.shape[0]
    size = self_query.shape[0]
    own_rows = size // width
    blocks = ffn_in.shape[0] // size
    whole_tiles = own_rows % 16 == 0
    core = place_in(groups[0]).reshape(1).astype(jnp.int32)

    firsts = (self_query, self_key, self_value)
    seconds = (self_out, cross_query, cross_key, cross_value, norm_parts(norm_params, size))
    if whole_tiles:
        lane_blocks = width // LANES
        three = [m for i in range(3) for m in square_moves(i, i, width)]
        five = three + [m for i in range(3, 5) for m in square_moves(i, i, width)]
        wide = [(0, c * lane_blocks + b, blocks * lane_blocks, c, b) for c in range(blocks) for b in range(lane_blocks)]
        tall = [(1, j * own_rows * lane_blocks + b, lane_blocks, blocks + j, b) for j in range(blocks) for b in range(lane_blocks)]
        first = pack(firsts, three, 3, own_rows, width, "pack_self")
        second = pack(tie(seconds, first), five, 5, own_rows, width, "pack_cross")
        last = square_moves(2, 2 * blocks, width)
        ffn_own = pack(tie((ffn_in, ffn_out, cross_out), first), wide + tall + last, 2 * blocks + 1, own_rows, width, "pack_ffn")
    else:
        first = jnp.concatenate(firsts).reshape(3, own_rows, width)
        second = jnp.concatenate(seconds).reshape(5, own_rows, width)
        fi = ffn_in.reshape(own_rows, blocks, width).transpose(1, 0, 2)
        ffn_own = jnp.concatenate([fi, ffn_out.reshape(blocks, own_rows, width), cross_out.reshape(1, own_rows, width)])
    for i, g in enumerate(down[:-1]):
        first = gather_step(first, g, [second, own_items] if i else [])
        if not i:
            qid, mid, own_items, items = plan(*tie((seg_lengths, mem_lengths), first), total, keys)
        if i < len(down) - 2:
            second = gather_step(second, g)
    early = second
    first = gathered(gather_step(first, down[-1]))
    ffn_all = lax.all_gather(ffn_own.reshape(-1, width), ("dp", "fsdp"), axis=0, tiled=True)
    ffn_all = ffn_all.reshape(devices, 2 * blocks + 1, own_rows, width)
    if not whole_tiles:
        squares = [ffn_all[:, i].reshape(width, width) for i in range(blocks)]
        squares += list(ffn_all[:, blocks : 2 * blocks].reshape(blocks, width, width))
        ffn_all = jnp.stack(squares + [ffn_all[:, 2 * blocks].reshape(width, width)])[None]
    pairs = devices // 2 if whole_tiles else 1
    part_of = core if whole_tiles else jnp.zeros_like(core)

    q1, k1, v1, o1, l1 = self_forward(own_items, inputs, first, qid, [early])
    second = gather_step(second, down[-2], [l1])
    second = gathered(gather_step(second, down[-1]))
    norm_all = second[4].reshape(devices, -1)[:, : 3 * LANES].reshape(devices, 3, LANES)[:, :, :shard].astype(f32)
    norms = jnp.sum(norm_all, axis=1).reshape(6, width)
    k2, v2, r1, h1b, q2, h1, o2, l2 = cross_forward(items, memory, inputs, o1, second, norms, qid, mid)
    out, dr3, dr2, do2, delta2, keep, send, gn23 = ffn(part_of, pairs, h1, inputs, cotangent, o2, ffn_all, norms)

    one = [keep, send] if whole_tiles else resplit(keep, send, devices, core[0], blocks + 1)
    dq2a, dk2a, dv2a, gckva = cross_backward(items, q2, k2, v2, do2, l2, delta2, qid, mid, memory, 0, HEAD_START, 6, [])
    low, high = 1 << groups[1][0], 2 << groups[1][0]
    both = jnp.stack([(position() >> (groups[1][0] + j)) & 1 for j in range(2)]).astype(jnp.int32)
    one = swap_pieces(one, groups[0], [dq2a])
    one = first_pair(both, one[0], one[1], devices // 8, blocks + 1)
    more = width // LANES - HEAD_START
    dq2b, dk2b, dv2b, gckvb = cross_backward(
        items, q2, k2, v2, do2, l2, delta2, qid, mid, memory, HEAD_START, more, 2, [one[1], one[3]]
    )
    came = tie([swap(one[1], low), swap(one[3], high)], dq2b)
    one = second_pair(both, [one[0], came[0], one[2], came[1]])
    gm = memory_grad(dk2a, dk2b, dv2a, dv2b, second, 2, [one[1], one[3]])
    dsum, do1, delta1, keep, send, gn = between(
        part_of, pairs, gckva, gckvb, gn23, r1, dr2, dr3, dq2a, dq2b, h1b, o1, second, norms, placed(gm)
    )
    came = tie([swap(one[1], high), swap(one[3], low)], do1)
    one = join_split(
        place_in(single[2]).reshape(1).astype(jnp.int32), [one[0], came[0], one[2], came[1]],
        1 << sum(g[1] for g in single[3:]), 1 << single[2][1],
    )
    two = [keep, send]
    if not whole_tiles:
        two = resplit(keep, send, devices, core[0], 5)
        own_norms = jnp.pad(gn[:6].astype(bf16).reshape(devices, -1), ((0, 0), (0, size - shard)))
        own_norms = own_norms.reshape(devices // 2, 2, own_rows, width)
        two = [two[m].at[:, 4].set(lax.dynamic_index_in_dim(own_norms, core[0] ^ m, 1, keepdims=False)) for m in range(2)]
    two = next_pieces(swap_pieces(tie(two, one[1]), groups[0]), groups, 1)
    gx, keep, send = self_backward(part_of, pairs, own_items, q1, k1, v1, do1, l1, delta1, qid, inputs, first, dsum, one[1:] + two[1:])
    two = next_pieces(swap_pieces(two, groups[1], [gx]), single, 2)
    one = next_pieces(swap_pieces(one, single[2], [gx]), single, 3)
    keep, send = tie((keep, send), two[1], one[1])
    three = [keep, send] if whole_tiles else resplit(keep, send, devices, core[0], 3)
    three = next_pieces(swap_pieces(three, groups[0]), groups, 1)
    for i in range(2, len(groups)):
        three = next_pieces(swap_pieces(three, groups[i - 1]), groups, i)
    for i in range(3, len(single)):
        two = next_pieces(swap_pieces(two, single[i - 1]), single, i)
        if i > 3:
            one = next_pieces(swap_pieces(one, single[i - 1]), single, i)

    def flat(g):
        return g.reshape(-1)

    chains = [swap_pieces(one, single[-1], [three[1]]), swap_pieces(two, single[-1], [three[1]]), swap_pieces(three, groups[-1])]
    chains = [[p.reshape(-1, own_rows, width) for p in chain] for chain in chains]
    if whole_tiles:
        lane_rows = size // LANES
        square, long = (lane_rows, LANES), (blocks * lane_rows, LANES)

        moves = [(c, b, 0, c * lane_blocks + b, blocks * lane_blocks) for c in range(blocks) for b in range(lane_blocks)]
        moves += [(blocks, b, 1, b, lane_blocks) for b in range(lane_blocks)]
        moves += [
            (blocks + 1 + j, b, 2, j * own_rows * lane_blocks + b, lane_blocks) for j in range(blocks) for b in range(lane_blocks)
        ]
        gfi, gco, gfo = finish(chains[0], moves, [long, square, long], "finish_ffn")
        moves = [(i, b, i, b, lane_blocks) for i in range(4) for b in range(lane_blocks)] + [(4, b, 4, 0, 0) for b in range(lane_blocks)]
        gck, gcv, gcq, gso, gn = finish(chains[1], moves, [square] * 4 + [(own_rows, width)], "finish_cross")
        gn = lax.dynamic_slice_in_dim(flat(gn[:6]), position() * shard, shard)
        moves = [(i, b, i, b, lane_blocks) for i in range(3) for b in range(lane_blocks)]
        gsq, gsk, gsv = finish(chains[2], moves, [square] * 3, "finish_self")
    else:
        one, two, three = (sum(p.astype(f32) for p in chain) for chain in chains)
        gfi, gco, gfo = one[:blocks].transpose(1, 0, 2), one[blocks], one[blocks + 1 :]
        gck, gcv, gcq, gso, gn = two[0], two[1], two[2], two[3], flat(two[4])[:shard]
        gsq, gsk, gsv = three[0], three[1], three[2]
    return (out, gx, gm) + tuple(flat(g) for g in (gsq, gsk, gsv, gso, gcq, gck, gcv, gco, gfi, gfo, gn))


def solution(mesh):
    rows, flat = P(("dp", "fsdp"), None), P(("dp", "fsdp"))
    return jax.shard_map(
        body,
        mesh=mesh,
        in_specs=(rows,) * 4 + (flat,) * 11 + (rows,),
        out_specs=(rows,) * 3 + (flat,) * 11,
        check_vma=False,
    )
```

```python
import functools
import jax
import jax.numpy as jnp
from jax import lax
from jax.experimental import pallas as pl
from jax.experimental.pallas import tpu as pltpu
from jax.sharding import PartitionSpec as P

HD = 64
LANES = 128
MOST = 256
QROWS = 128
EACH = (2, 3, 6)
PADDING = 6
FFN_CHUNK = 256
masked_score = -1e30
norm_eps = 1e-05
bf16, f32 = jnp.bfloat16, jnp.float32
NT = (((1,), (1,)), ((), ()))
TN = (((0,), (0,)), ((), ()))
NN = (((1,), (0,)), ((), ()))


def mm(left, right, dims=NN):
    return lax.dot_general(left, right, dims, preferred_element_type=f32)


def norm_rows(source):
    mean = jnp.mean(source, axis=-1, keepdims=True)
    centered = source - mean
    variance = jnp.mean(centered * centered, axis=-1, keepdims=True)
    rstd = lax.rsqrt(variance + norm_eps)
    return centered * rstd, rstd


def lane_below(rows):
    return lax.broadcasted_iota(jnp.int32, (rows, LANES), 1) < HD


def column_of(row):
    return jnp.broadcast_to(row, (LANES, row.shape[1])).T


def head_part(pair, which, low):
    return jnp.where(low == (which == 0), pair, jnp.zeros_like(pair))


def values_with_ones(values):
    parts = []
    for p in range(values.shape[1] // LANES):
        pair = values[:, p * LANES : (p + 1) * LANES]
        parts += [pair, jnp.ones_like(pair)]
    return jnp.concatenate(parts, axis=1)


def finish_heads(at, top, tot, acc, write):
    shape = acc.shape[0], at.size if hasattr(at, "size") else at.stop - at.start, LANES
    lane = lax.broadcasted_iota(jnp.int32, shape[1:], 1)
    sums, tops = jnp.ones(shape[1:], f32), jnp.zeros(shape[1:], f32)
    for p in range(shape[0]):
        total = tot[p, at, :]
        write(p, (acc[p, at, :] / total).astype(bf16))
        sums = jnp.where(lane % HD == p, total, sums)
        tops = jnp.where(lane == p, top[2 * p, at, :], jnp.where(lane == HD + p, top[2 * p + 1, at, :], tops))
    return tops + jnp.log(sums)


def column_at(head):
    return head % 2 * HD + head // 2


def item_at(items_ref, n, idk_ref, ids_q, keys, tile, block, causal):
    begin = pl.multiple_of(items_ref[0, n] * block, block)
    wanted = items_ref[1, n] * LANES
    start = pl.multiple_of(jnp.minimum(wanted, keys - tile), LANES)
    at = pl.ds(begin, block)
    pos = start + lax.broadcasted_iota(jnp.int32, (1, tile), 1)
    ids_k = jnp.where(pos >= wanted, idk_ref[:, pl.ds(start, tile)], -1)
    allowed = ids_q[at, :1] == ids_k
    if causal:
        allowed &= pos <= begin + lax.broadcasted_iota(jnp.int32, (block, 1), 0)
    return at, pl.ds(start, tile), jnp.where(allowed, 0.0, masked_score).astype(f32)


def attend(items_ref, idk_ref, ids_q, q_all, k_all, vx_all, top, tot, acc, tile, block, causal):
    keys, width = k_all.shape
    pairs = width // LANES
    heads = 2 * pairs
    low = lane_below(block)
    top[...] = jnp.full(top.shape, masked_score, f32)
    tot[...] = jnp.zeros(tot.shape, f32)
    acc[...] = jnp.zeros(acc.shape, f32)

    def some(i, _):
        loads, made = [], []
        for t in range(EACH[0]):
            at, there, bias = item_at(items_ref, EACH[0] * i + t, idk_ref, ids_q, keys, tile, block, causal)
            loads.append((at, there, bias))
            for p in range(pairs):
                cols = slice(p * LANES, (p + 1) * LANES)
                part = q_all[at, cols]
                both = jnp.concatenate([head_part(part, h, low) for h in range(2)])
                made.append(mm(both, k_all[there, cols], NT))
        weights, scales = [], []
        for t, (at, there, bias) in enumerate(loads):
            for head in range(heads):
                s = made[t * pairs + head // 2][head % 2 * block : (head % 2 + 1) * block] + bias
                old = top[head, at, :]
                new = jnp.maximum(old, jnp.max(s, axis=1, keepdims=True))
                top[head, at, :] = new
                scales.append(jnp.exp(old - new))
                weights.append(jnp.exp(s - jnp.concatenate([new] * (tile // LANES), axis=1)).astype(bf16))
        mixed = [
            mm(jnp.concatenate(weights[t * heads + 2 * p : t * heads + 2 * p + 2]), vx_all[there, 2 * p * LANES : 2 * (p + 1) * LANES])
            for t, (_, there, _) in enumerate(loads) for p in range(pairs)
        ]
        for t, (at, _, _) in enumerate(loads):
            for p in range(pairs):
                n = t * pairs + p
                scale = jnp.where(low, scales[2 * n], scales[2 * n + 1])
                o = mixed[n]
                acc[p, at, :] = acc[p, at, :] * scale + jnp.where(low, o[:block, :LANES], o[block:, :LANES])
                tot[p, at, :] = tot[p, at, :] * scale + jnp.where(low, o[:block, LANES:], o[block:, LANES:])
        return 0

    lax.fori_loop(0, items_ref[2, 0], some, 0)


def attend_back(items_ref, idk_ref, ids_q, q_all, do_ref, k_ref, v_ref, l_ref, delta_ref, dq, dk, dv, tile, block, first_head, causal, each):
    keys, width = k_ref.shape
    pairs = width // LANES
    low = lane_below(block)

    def some(i, _):
        loads, scores, grads = [], [], []
        for t in range(each):
            at, there, bias = item_at(items_ref, each * i + t, idk_ref, ids_q, keys, tile, block, causal)
            loads.append((at, there, bias))
            for p in range(pairs):
                cols = slice(p * LANES, (p + 1) * LANES)
                q, do = q_all[at, cols], do_ref[at, cols]
                qs = jnp.concatenate([head_part(q, h, low) for h in range(2)])
                dos = jnp.concatenate([head_part(do, h, low) for h in range(2)])
                scores.append((mm(qs, k_ref[there, cols], NT), qs))
                grads.append((mm(dos, v_ref[there, cols], NT), dos))
        weights, slopes = [], []
        for t, (at, there, bias) in enumerate(loads):
            logs, deltas = l_ref[at, :], delta_ref[at, :]
            for p in range(pairs):
                es, ds = [], []
                for h in range(2):
                    lane = column_at(first_head + 2 * p + h)
                    rows = slice(h * block, (h + 1) * block)
                    e = jnp.exp(scores[t * pairs + p][0][rows] + bias - logs[:, lane : lane + 1])
                    es.append(e.astype(bf16))
                    ds.append((e * (grads[t * pairs + p][0][rows] - deltas[:, lane : lane + 1])).astype(bf16))
                weights.append(jnp.concatenate(es))
                slopes.append(jnp.concatenate(ds))
        for t, (at, there, _) in enumerate(loads):
            for p in range(pairs):
                cols = slice(p * LANES, (p + 1) * LANES)
                n = t * pairs + p
                gq = mm(slopes[n], k_ref[there, cols])
                gk = mm(slopes[n], scores[n][1], TN)
                gv = mm(weights[n], grads[n][1], TN)
                dq[at, cols] += jnp.where(low, gq[:block], gq[block:])
                dk[there, cols] += gk
                dv[there, cols] += gv
        return 0

    lax.fori_loop(0, items_ref[2, EACH.index(each)], some, 0)


def self_forward_kernel(tile, block, items_ref, x_ref, wq_ref, wk_ref, wv_ref, idr_ref, *rest):
    q_ref, k_ref, v_ref, o_ref, l_ref, q_all, k_all, vx_all, ids_all, top, tot, acc = rest[-12:]
    step = pl.program_id(0)
    rows = x_ref.shape[0]
    total, width = k_all.shape
    turns = total // rows

    @pl.when(step < turns)
    def _():
        x = x_ref[...]
        q = mm(x, wq_ref[0]).astype(bf16)
        k = mm(x, wk_ref[0]).astype(bf16)
        v = mm(x, wv_ref[0]).astype(bf16)
        q_ref[...] = q
        k_ref[...] = k
        v_ref[...] = v
        here = pl.ds(pl.multiple_of(step * rows, rows), rows)
        q_all[here, :] = q * jnp.asarray(HD ** -0.5, bf16)
        k_all[here, :] = k
        vx_all[here, :] = values_with_ones(v)
        ids_all[here, :] = column_of(idr_ref[:, here])

    @pl.when(step == turns)
    def _():
        attend(items_ref, idr_ref, ids_all, q_all, k_all, vx_all, top, tot, acc, tile, block, True)
        size = 2 * block
        for j in range(total // size):
            at = slice(j * size, (j + 1) * size)

            def write(p, value):
                o_ref[at, p * LANES : (p + 1) * LANES] = value

            l_ref[at, :] = finish_heads(at, top, tot, acc, write)


def whole(a):
    return pl.BlockSpec(a.shape, lambda *_: (0,) * a.ndim)


def part(weights, index, columns, half):
    return pl.BlockSpec((1, weights.shape[1], columns), lambda *_: (index, 0, half))


def params(us, vmem):
    return dict(
        compiler_params=pltpu.CompilerParams(vmem_limit_bytes=vmem * 2**20),
        cost_estimate=pl.CostEstimate(flops=us * 10**9, bytes_accessed=2**20, transcendentals=0),
    )


apart = pl.BlockSpec(memory_space=pl.ANY)


def out_array(shape, dtype):
    return pltpu.HBM(shape, dtype)


def placed(*arrays):
    return [pltpu.with_memory_space_constraint(a, pltpu.HBM) for a in arrays]


def self_forward(items, x, weights, idr, after, turns=2, block=QROWS, tile=256):
    total, width = x.shape
    heads = width // HD
    rows = total // turns
    early = lambda w: pl.BlockSpec((rows, w), lambda i, *_: (jnp.minimum(i, turns - 1), 0))
    fixed = lambda w: pl.BlockSpec((total, w), lambda i, *_: (0, 0))
    sds = out_array
    full = sds((total, width), bf16)
    return pl.pallas_call(
        functools.partial(self_forward_kernel, tile, block),
        grid_spec=pltpu.PrefetchScalarGridSpec(
            num_scalar_prefetch=1,
            grid=(turns + 1,),
            in_specs=[early(width)] + [part(weights, i, width, 0) for i in range(3)] + [whole(idr)] + [apart] * len(after),
            out_specs=[early(width)] * 3 + [fixed(width), fixed(LANES)],
            scratch_shapes=[
                pltpu.VMEM((total, width), bf16), pltpu.VMEM((total, width), bf16), pltpu.VMEM((total, 2 * width), bf16),
                pltpu.VMEM((total, LANES), jnp.int32),
                pltpu.VMEM((heads, total, LANES), f32), pltpu.VMEM((heads // 2, total, LANES), f32), pltpu.VMEM((heads // 2, total, LANES), f32),
            ],
        ),
        out_shape=[full] * 4 + [sds((total, LANES), f32)],
        name="self_forward",
        **params(13, 32),
    )(items, *placed(x), weights, weights, weights, idr, *after)


def cross_forward_kernel(
    tile, block, items_ref, memory_ref, wk_ref, wv_ref, x_ref, o1_ref, wso_ref, wcq_ref, norms_ref, idr_ref, idk_ref, *rest
):
    k2_ref, v2_ref, r1_ref, h1b_ref, q2_ref, h1_ref, o_ref, l_ref, k_all, vx_all, q_all, ids_all, top, tot, acc = rest[-15:]
    step = pl.program_id(0)
    rows, width = x_ref.shape
    keys = k_all.shape[0]
    turns = pl.num_programs(0) - 1

    @pl.when(step < turns)
    def _():
        per = memory_ref.shape[0]
        memory = memory_ref[...]
        r1 = x_ref[...].astype(f32) + mm(o1_ref[...], wso_ref[0])
        k2 = mm(memory, wk_ref[0]).astype(bf16)
        r1_ref[...] = r1.astype(bf16)
        n1, _ = norm_rows(r1)
        v2 = mm(memory, wv_ref[0]).astype(bf16)
        h1 = n1 * norms_ref[0:1, :] + norms_ref[1:2, :]
        h1b = h1.astype(bf16)
        h1b_ref[...] = h1b
        q2 = mm(h1b, wcq_ref[0]).astype(bf16)
        q2_ref[...] = q2
        k2_ref[...] = k2
        v2_ref[...] = v2
        here = pl.ds(pl.multiple_of(step * rows, rows), rows)
        q_all[here, :] = q2 * jnp.asarray(HD ** -0.5, bf16)
        h1_ref[...] = h1
        ids_all[here, :] = column_of(idr_ref[:, here])
        there = pl.ds(pl.multiple_of(step * per, per), per)
        k_all[there, :] = k2
        vx_all[there, :] = values_with_ones(v2)

    @pl.when(step == turns)
    def _():
        attend(items_ref, idk_ref, ids_all, q_all, k_all, vx_all, top, tot, acc, tile, block, False)

        size = 2 * block
        for j in range(q_all.shape[0] // size):
            at = slice(j * size, (j + 1) * size)

            def write(p, value):
                o_ref[at, p * LANES : (p + 1) * LANES] = value

            l_ref[at, :] = finish_heads(at, top, tot, acc, write)


def cross_forward(items, memory, x, o1, weights, norms, idr, idk, after, turns=2, block=QROWS, tile=256):
    total, width = x.shape
    keys = memory.shape[0]
    heads = width // HD
    rows, per = total // turns, keys // turns
    early = lambda r, w: pl.BlockSpec((r, w), lambda i, *_: (jnp.minimum(i, turns - 1), 0))
    fixed = lambda w: pl.BlockSpec((total, w), lambda i, *_: (0, 0))
    sds = out_array
    return pl.pallas_call(
        functools.partial(cross_forward_kernel, tile, block),
        grid_spec=pltpu.PrefetchScalarGridSpec(
            num_scalar_prefetch=1,
            grid=(turns + 1,),
            in_specs=[early(per, width), part(weights, 2, width, 0), part(weights, 3, width, 0)]
            + [early(rows, width), early(rows, width), part(weights, 0, width, 0), part(weights, 1, width, 0)]
            + [whole(norms), whole(idr), whole(idk)] + [apart] * len(after),
            out_specs=[early(per, width)] * 2 + [early(rows, width)] * 4 + [fixed(width), fixed(LANES)],
            scratch_shapes=[
                pltpu.VMEM((keys, width), bf16),
                pltpu.VMEM((keys, 2 * width), bf16),
                pltpu.VMEM((total, width), bf16),
                pltpu.VMEM((total, LANES), jnp.int32),
                pltpu.VMEM((heads, total, LANES), f32),
                pltpu.VMEM((heads // 2, total, LANES), f32),
                pltpu.VMEM((heads // 2, total, LANES), f32),
            ],
        ),
        out_shape=[
            sds((keys, width), bf16), sds((keys, width), bf16), sds((total, width), bf16), sds((total, width), bf16),
            sds((total, width), bf16), sds((total, width), f32), sds((total, width), bf16), sds((total, LANES), f32),
        ],
        name="cross_forward",
        **params(19, 44),
    )(items, *placed(memory), weights, weights, *placed(x, o1), weights, weights, norms, idr, idk, *after)


def norm_back(incoming, normal, rstd, gain):
    m = incoming * gain
    return rstd * (
        m - jnp.mean(m, axis=-1, keepdims=True) - normal * jnp.mean(m * normal, axis=-1, keepdims=True)
    )


def head_columns(left, right):
    width = left.shape[1]
    prod = left.astype(f32) * right.astype(f32)
    lane = lax.broadcasted_iota(jnp.int32, (width, LANES), 1)
    own = lax.broadcasted_iota(jnp.int32, (width, LANES), 0) // HD == 2 * (lane % HD) + lane // HD
    own = own.astype(bf16)
    high = prod.astype(bf16)
    low = (prod - high.astype(f32)).astype(bf16)
    return mm(high, own) + mm(low, own)


def column_sums(a):
    return jnp.sum(a, axis=0, keepdims=True)


def spread(keep_ref, send_ref, core, write):
    def one(j, _):
        write(2 * j + core, keep_ref, j)
        write(2 * j + 1 - core, send_ref, j)
        return 0

    lax.fori_loop(0, keep_ref.shape[0], one, 0)


def ffn_kernel(
    core_ref, h1_ref, x_ref, cot_ref, o2_ref, wa_ref, wb_ref, norms_ref,
    out_ref, dr3_ref, dr2_ref, do2_ref, delta_ref, keep_ref, send_ref, gn_ref, gin, gout, gco,
):
    step = pl.program_id(0)
    last = pl.num_programs(0) - 1
    width = x_ref.shape[1]
    blocks = wb_ref.shape[1]

    @pl.when(step == 0)
    def _():
        gin[...] = jnp.zeros_like(gin)
        gout[...] = jnp.zeros_like(gout)
        gco[...] = jnp.zeros_like(gco)
        gn_ref[...] = jnp.zeros_like(gn_ref)

    win = [wa_ref[:, c].reshape(width, width) for c in range(blocks)]
    wout = wb_ref[...].reshape(blocks * width, width)
    wco = wa_ref[:, blocks].reshape(width, width)
    n2, rstd2 = norm_rows(h1_ref[...] + mm(o2_ref[...], wco))
    h2 = n2 * norms_ref[2:3, :] + norms_ref[3:4, :]
    h2b = h2.astype(bf16)
    chunk = min(FFN_CHUNK, width)
    parts = blocks * width // chunk
    per = width // chunk

    def win_part(c):
        return win[c // per][:, (c % per) * chunk : (c % per + 1) * chunk]

    acts, slopes, hidden = [], [], [mm(h2b, win_part(0))]
    ff = jnp.zeros(h2.shape, f32)
    for c in range(parts):
        if c + 1 < parts:
            hidden.append(mm(h2b, win_part(c + 1)))
        u = hidden[c]
        square = u * u
        t = jnp.tanh(u * (0.7978845608028654 + (0.7978845608028654 * 0.044715) * square))
        half = 0.5 + 0.5 * t
        acts.append((u * half).astype(bf16))
        rise = u * (0.5 * 0.7978845608028654 + (0.5 * 0.7978845608028654 * 3 * 0.044715) * square)
        slopes.append(half + (1.0 - t * t) * rise)
        if c:
            ff += mm(acts[c - 1], wout[(c - 1) * chunk : c * chunk, :])
    ff += mm(acts[-1], wout[(parts - 1) * chunk :, :])
    r3 = h2 + ff + x_ref[...].astype(f32)
    n3, rstd3 = norm_rows(r3)
    gain3 = norms_ref[4:5, :]
    out_ref[...] = (n3 * gain3 + norms_ref[5:6, :]).astype(bf16)
    e = cot_ref[...].astype(f32)
    gn_ref[2:3, :] += column_sums(e * n3)
    gn_ref[3:4, :] += column_sums(e)
    dr3 = norm_back(e, n3, rstd3, gain3)
    dr3_ref[...] = dr3.astype(bf16)
    dfb = dr3.astype(bf16)
    dh2 = dr3
    raw, made = [mm(dfb, wout[:chunk, :], NT)], []
    for c in range(parts + 1):
        if c + 1 < parts:
            raw.append(mm(dfb, wout[(c + 1) * chunk : (c + 2) * chunk, :], NT))
        if c < parts:
            gout[c * chunk : (c + 1) * chunk, :] += mm(acts[c], dfb, TN)
            made.append((raw[c] * slopes[c]).astype(bf16))
        if c:
            gin[:, (c - 1) * chunk : c * chunk] += mm(h2b, made[c - 1], TN)
            dh2 += mm(made[c - 1], win_part(c - 1), NT)
    gn_ref[0:1, :] += column_sums(dh2 * n2)
    gn_ref[1:2, :] += column_sums(dh2)
    dr2 = norm_back(dh2, n2, rstd2, norms_ref[2:3, :])
    da2 = dr2.astype(bf16)
    dr2_ref[...] = da2
    o2 = o2_ref[...]
    gco[...] += mm(o2, da2, TN)
    do2 = mm(da2, wco, NT).astype(bf16)
    do2_ref[...] = do2
    delta_ref[...] = head_columns(do2, o2)

    @pl.when(step == last)
    def _():
        r = keep_ref.shape[2]

        def write(device, ref, j):
            here = pl.ds(pl.multiple_of(device * r, r), r)
            for c in range(blocks):
                ref[j, c] = gin[here, c * width : (c + 1) * width].astype(bf16)
            ref[j, blocks] = gco[here, :].astype(bf16)
            there = pl.ds(pl.multiple_of(device * blocks * r, blocks * r), blocks * r)
            ref[j, blocks + 1 :] = gout[there, :].astype(bf16).reshape(blocks, r, width)

        spread(keep_ref, send_ref, core_ref[0], write)


def ffn(core, pairs, h1, x, cot, o2, wa, wb, norms, rows=512):
    total, width = x.shape
    blocks = wb.shape[1]
    rowspec = lambda w: pl.BlockSpec((rows, w), lambda i: (i, 0))
    sds = out_array
    side = jax.ShapeDtypeStruct((pairs, 2 * blocks + 1, width // (2 * pairs), width), bf16)
    return pl.pallas_call(
        ffn_kernel,
        grid=(total // rows,),
        in_specs=[pl.BlockSpec(memory_space=pltpu.SMEM)] + [rowspec(width)] * 4 + [whole(wa), whole(wb), whole(norms)],
        out_specs=[rowspec(width)] * 4
        + [rowspec(LANES), whole(side), whole(side), pl.BlockSpec((4, width), lambda i: (0, 0))],
        out_shape=[
            sds((total, width), bf16), sds((total, width), bf16), sds((total, width), bf16), sds((total, width), bf16),
            sds((total, LANES), f32), side, side, sds((4, width), f32),
        ],
        scratch_shapes=[pltpu.VMEM((width, blocks * width), f32), pltpu.VMEM((blocks * width, width), f32), pltpu.VMEM((width, width), f32)],
        name="ffn",
        **params(32, 51),
    )(core, *placed(h1, x, cot, o2), wa, wb, norms)


def cross_backward_kernel(
    tile, block, first, count, each, items_ref, q2_ref, k2_ref, v2_ref, do_ref, l_ref, delta_ref, idr_ref, idk_ref, memory_ref, *rest
):
    dq_ref, dk_ref, dv_ref, grads_ref, q_all, ids_all, dq, dk, dv, grads = rest[-10:]
    step = pl.program_id(0)
    total = q2_ref.shape[0]
    begin = first * LANES if q2_ref.shape[1] > count * LANES else 0
    cols = slice(begin, begin + count * LANES)

    @pl.when(step == 0)
    def _():
        dq[...] = jnp.zeros_like(dq)
        dk[...] = jnp.zeros_like(dk)
        dv[...] = jnp.zeros_like(dv)
        grads[...] = jnp.zeros_like(grads)
        q_all[...] = q2_ref[:, cols] * jnp.asarray(HD ** -0.5, bf16)
        for j in range(total // block):
            ids_all[j * block : (j + 1) * block, :] = column_of(idr_ref[:, j * block : (j + 1) * block])
        attend_back(
            items_ref, idk_ref, ids_all, q_all, do_ref.at[:, cols], k2_ref.at[:, cols], v2_ref.at[:, cols], l_ref, delta_ref,
            dq, dk, dv, tile, block, 2 * first, False, each,
        )

    memory = memory_ref[...]
    per = memory.shape[0]
    here = pl.ds(pl.multiple_of(step * per, per), per)
    for i, (ref, out_ref) in enumerate(((dk, dk_ref), (dv, dv_ref))):
        grad = ref[here, :].astype(bf16)
        out_ref[...] = grad
        grads[i] += mm(memory, grad, TN)
    rows = dq_ref.shape[0]
    dq_ref[...] = (dq[pl.ds(pl.multiple_of(step * rows, rows), rows), :] * HD ** -0.5).astype(bf16)

    @pl.when(step == pl.num_programs(0) - 1)
    def _():
        grads_ref[...] = grads[...].astype(bf16)


def cross_backward(items, q2, k2, v2, do, l, delta, idr, idk, memory, first, count, each, after, turns=2, block=QROWS, tile=256):
    total, width = q2.shape
    keys = k2.shape[0]
    columns = count * LANES
    alone = first % count == 0
    cols = lambda r: pl.BlockSpec((r, columns if alone else width), lambda i, *_: (0, first // count if alone else 0))
    rowspec = lambda r, w: pl.BlockSpec((r, w), lambda i, *_: (i, 0))
    sds = jax.ShapeDtypeStruct
    grad = sds((2, width, columns), bf16)
    return pl.pallas_call(
        functools.partial(cross_backward_kernel, tile, block, first, count, each),
        grid_spec=pltpu.PrefetchScalarGridSpec(
            num_scalar_prefetch=1,
            grid=(turns,),
            in_specs=[cols(total), cols(keys), cols(keys), cols(total)]
            + [whole(l), whole(delta), whole(idr), whole(idk), rowspec(keys // turns, width)] + [apart] * len(after),
            out_specs=[rowspec(total // turns, columns), rowspec(keys // turns, columns), rowspec(keys // turns, columns), whole(grad)],
            scratch_shapes=[
                pltpu.VMEM((total, columns), bf16), pltpu.VMEM((total, LANES), jnp.int32), pltpu.VMEM((total, columns), f32),
                pltpu.VMEM((keys, columns), f32), pltpu.VMEM((keys, columns), f32), pltpu.VMEM((2, width, columns), f32),
            ],
        ),
        out_shape=[sds((total, columns), bf16), sds((keys, columns), bf16), sds((keys, columns), bf16), grad],
        name="cross_backward",
        **params(5 * count + 4, 10 * count + 4),
    )(items, *placed(q2, k2, v2, do, l, delta), idr, idk, *placed(memory), *after)


def memory_grad_kernel(ka_ref, kb_ref, va_ref, vb_ref, wk_ref, wv_ref, *rest):
    total = mm(jnp.concatenate([ka_ref[...], kb_ref[...]], axis=1), wk_ref[0], NT)
    total += mm(jnp.concatenate([va_ref[...], vb_ref[...]], axis=1), wv_ref[0], NT)
    rest[-1][...] = total.astype(bf16)


def memory_grad(ka, kb, va, vb, weights, index, after, rows=1024):
    keys, width = ka.shape[0], weights.shape[2]
    rowspec = lambda w: pl.BlockSpec((rows, w), lambda i: (i, 0))
    return pl.pallas_call(
        memory_grad_kernel,
        grid=(keys // rows,),
        in_specs=[rowspec(a.shape[1]) for a in (ka, kb, va, vb)] + [part(weights, index, width, 0), part(weights, index + 1, width, 0)] + [apart] * len(after),
        out_specs=rowspec(width),
        out_shape=out_array((keys, width), bf16),
        name="memory_grad",
        **params(4, 16),
    )(ka, kb, va, vb, weights, weights, *after)


def between_kernel(
    core_ref, ga_ref, gb_ref, gn23_ref, r1_ref, dr2_ref, dr3_ref, dqa_ref, dqb_ref, h1b_ref, o1_ref, wso_ref, wcq_ref, norms_ref, *rest
):
    dsum_ref, do1_ref, delta_ref, keep_ref, send_ref, gn_ref, total = rest[-7:]
    step = pl.program_id(0)

    @pl.when(step == 0)
    def _():
        total[...] = jnp.zeros_like(total)
        gn_ref[...] = jnp.zeros_like(gn_ref)

    dq2 = jnp.concatenate([dqa_ref[...], dqb_ref[...]], axis=1)
    dh1 = dr2_ref[...].astype(f32) + mm(dq2, wcq_ref[0], NT)
    n1, rstd1 = norm_rows(r1_ref[...].astype(f32))
    gn_ref[0:1, :] += column_sums(dh1 * n1)
    gn_ref[1:2, :] += column_sums(dh1)
    dr1 = norm_back(dh1, n1, rstd1, norms_ref[0:1, :])
    dsum_ref[...] = (dr1 + dr3_ref[...].astype(f32)).astype(bf16)
    da1 = dr1.astype(bf16)
    o1 = o1_ref[...]
    do1 = mm(da1, wso_ref[0], NT).astype(bf16)
    do1_ref[...] = do1
    delta_ref[...] = head_columns(do1, o1)
    total[0] += mm(h1b_ref[...], dq2, TN)
    total[1] += mm(o1, da1, TN)

    @pl.when(step == pl.num_programs(0) - 1)
    def _():
        gn_ref[2:6, :] = gn23_ref[...]
        r, width = keep_ref.shape[2:]
        norm_part = jnp.concatenate([gn_ref[...], jnp.zeros((r - 8, width), f32)]).astype(bf16)

        def write(device, ref, j):
            here = pl.ds(pl.multiple_of(device * r, r), r)
            for i in range(2):
                ref[j, i, :, : ga_ref.shape[2]] = ga_ref[i, here, :]
                ref[j, i, :, ga_ref.shape[2] :] = gb_ref[i, here, :]
                ref[j, 2 + i] = total[i, here, :].astype(bf16)
            ref[j, 4] = norm_part

        spread(keep_ref, send_ref, core_ref[0], write)


def between(core, pairs, ga, gb, gn23, r1, dr2, dr3, dqa, dqb, h1b, o1, weights, norms, after, rows=512):
    total, width = r1.shape
    rowspec = lambda w: pl.BlockSpec((rows, w), lambda i: (i, 0))
    sds = jax.ShapeDtypeStruct
    side = jax.ShapeDtypeStruct((pairs, 5, width // (2 * pairs), width), bf16)
    return pl.pallas_call(
        between_kernel,
        grid=(total // rows,),
        in_specs=[pl.BlockSpec(memory_space=pltpu.SMEM), whole(ga), whole(gb), whole(gn23)]
        + [rowspec(width)] * 3 + [rowspec(dqa.shape[1]), rowspec(dqb.shape[1])] + [rowspec(width)] * 2
        + [part(weights, 0, width, 0), part(weights, 1, width, 0), whole(norms)] + [apart] * len(after),
        out_specs=[rowspec(width)] * 2
        + [rowspec(LANES), whole(side), whole(side), pl.BlockSpec((8, width), lambda i: (0, 0))],
        out_shape=[sds((total, width), bf16), sds((total, width), bf16), sds((total, LANES), f32), side, side, sds((8, width), f32)],
        scratch_shapes=[pltpu.VMEM((2, width, width), f32)],
        name="between",
        **params(7, 24),
    )(core, ga, gb, gn23, *placed(r1), dr2, dr3, dqa, dqb, *placed(h1b, o1), weights, weights, norms, *after)


def self_backward_kernel(
    tile, block, core_ref, items_ref, q_ref, k_ref, v_ref, do_ref, l_ref, delta_ref, idr_ref, x_ref, wq_ref, wk_ref, wv_ref, sofar_ref, *rest
):
    gx_ref, keep_ref, send_ref, q_all, ids_all, dq, dk, dv, grads = rest[-9:]
    step = pl.program_id(0)
    total, width = q_ref.shape

    @pl.when(step == 0)
    def _():
        dq[...] = jnp.zeros_like(dq)
        dk[...] = jnp.zeros_like(dk)
        dv[...] = jnp.zeros_like(dv)
        grads[...] = jnp.zeros_like(grads)
        q_all[...] = q_ref[...] * jnp.asarray(HD ** -0.5, bf16)
        for j in range(total // block):
            ids_all[j * block : (j + 1) * block, :] = column_of(idr_ref[:, j * block : (j + 1) * block])
        attend_back(
            items_ref, idr_ref, ids_all, q_all, do_ref, k_ref, v_ref, l_ref, delta_ref, dq, dk, dv, tile, block, 0, True, 2
        )

    x = x_ref[...]
    rows = x.shape[0]
    here = pl.ds(pl.multiple_of(step * rows, rows), rows)
    gx = sofar_ref[...].astype(f32)
    parts = (dq[here, :] * HD ** -0.5).astype(bf16), dk[here, :].astype(bf16), dv[here, :].astype(bf16)
    for i, (grad, w_ref) in enumerate(zip(parts, (wq_ref, wk_ref, wv_ref))):
        gx += mm(grad, w_ref[0], NT)
        grads[i] += mm(x, grad, TN)
    gx_ref[...] = gx.astype(bf16)

    @pl.when(step == pl.num_programs(0) - 1)
    def _():
        r = keep_ref.shape[2]

        def write(device, ref, j):
            place = pl.ds(pl.multiple_of(device * r, r), r)
            for i in range(3):
                ref[j, i] = grads[i, place, :].astype(bf16)

        spread(keep_ref, send_ref, core_ref[0], write)


def self_backward(core, pairs, items, q, k, v, do, l, delta, idr, x, weights, sofar, after, turns=2, block=QROWS, tile=256):
    total, width = x.shape
    sds = jax.ShapeDtypeStruct
    side = sds((pairs, 3, width // (2 * pairs), width), bf16)
    rowspec = lambda w: pl.BlockSpec((total // turns, w), lambda i, *_: (i, 0))
    return pl.pallas_call(
        functools.partial(self_backward_kernel, tile, block),
        grid_spec=pltpu.PrefetchScalarGridSpec(
            num_scalar_prefetch=2,
            grid=(turns,),
            in_specs=[whole(a) for a in (q, k, v, do, l, delta, idr)]
            + [rowspec(width)] + [part(weights, i, width, 0) for i in range(3)] + [rowspec(width)] + [apart] * len(after),
            out_specs=[rowspec(width), whole(side), whole(side)],
            scratch_shapes=[
                pltpu.VMEM((total, width), bf16), pltpu.VMEM((total, LANES), jnp.int32),
                pltpu.VMEM((total, width), f32), pltpu.VMEM((total, width), f32), pltpu.VMEM((total, width), f32),
                pltpu.VMEM((3, width, width), f32),
            ],
        ),
        out_shape=[sds((total, width), bf16), side, side],
        name="self_backward",
        **params(17, 34),
    )(core, items, q, k, v, do, l, delta, idr, x, weights, weights, weights, sofar, *after)


def add_split_kernel(count, here_ref, *refs):
    places = refs[0].shape[1]
    for m in range(places):
        at = here_ref[0] ^ m
        total = refs[0][:, at].astype(f32)
        for ref in refs[1:count]:
            total += ref[:, at].astype(f32)
        refs[count + m][...] = total.astype(bf16)


def add_split(here, parts, outer, places):
    tail = parts[0].shape[1:]
    parts = [p.reshape((outer, places) + tail) for p in parts]
    out = pl.pallas_call(
        functools.partial(add_split_kernel, len(parts)),
        grid=(outer,),
        in_specs=[pl.BlockSpec(memory_space=pltpu.SMEM)] + [pl.BlockSpec((1, places) + tail, lambda i: (i, 0, 0, 0, 0))] * len(parts),
        out_specs=[pl.BlockSpec((1,) + tail, lambda i: (i, 0, 0, 0))] * places,
        out_shape=[jax.ShapeDtypeStruct((outer,) + tail, bf16)] * places,
        name="add_split",
        **params(3, 24),
    )(here, *parts)
    return list(out)


def first_pair_kernel(cut, here_ref, keep, came, *outs):
    for m in range(2):
        at = here_ref[0] ^ m
        outs[m][0] = (keep[0, :, at, :cut].astype(f32) + came[0, :, at, :cut].astype(f32)).astype(bf16)
        at = here_ref[1] ^ m
        outs[2 + m][0] = (keep[0, at, :, cut:].astype(f32) + came[0, at, :, cut:].astype(f32)).astype(bf16)


def first_pair(here, keep, came, outer, cut):
    squares, rows, width = keep.shape[1:]
    parts = [p.reshape(outer, 2, 2, squares, rows, width) for p in (keep, came)]
    shapes = [(outer, 2, n, rows, width) for n in (cut, cut, squares - cut, squares - cut)]
    out = pl.pallas_call(
        functools.partial(first_pair_kernel, cut),
        grid=(outer,),
        in_specs=[pl.BlockSpec(memory_space=pltpu.SMEM)] + [pl.BlockSpec((1,) + p.shape[1:], lambda i: (i, 0, 0, 0, 0, 0)) for p in parts],
        out_specs=[pl.BlockSpec((1,) + s[1:], lambda i: (i, 0, 0, 0, 0)) for s in shapes],
        out_shape=[jax.ShapeDtypeStruct(s, bf16) for s in shapes],
        name="first_pair",
        **params(2, 24),
    )(here, *parts)
    return list(out)


def second_pair_kernel(here_ref, keep_a, came_a, keep_b, came_b, *outs):
    for m in range(2):
        at = here_ref[1] ^ m
        outs[m][0] = (keep_a[0, at].astype(f32) + came_a[0, at].astype(f32)).astype(bf16)
        at = here_ref[0] ^ m
        outs[2 + m][0] = (keep_b[0, at].astype(f32) + came_b[0, at].astype(f32)).astype(bf16)


def second_pair(here, parts):
    outer = parts[0].shape[0]
    shapes = [(p.shape[0],) + p.shape[2:] for p in parts]
    out = pl.pallas_call(
        second_pair_kernel,
        grid=(outer,),
        in_specs=[pl.BlockSpec(memory_space=pltpu.SMEM)] + [pl.BlockSpec((1,) + p.shape[1:], lambda i: (i, 0, 0, 0, 0)) for p in parts],
        out_specs=[pl.BlockSpec((1,) + s[1:], lambda i: (i, 0, 0, 0)) for s in shapes],
        out_shape=[jax.ShapeDtypeStruct(s, bf16) for s in shapes],
        name="second_pair",
        **params(1, 24),
    )(here, *parts)
    return list(out)


def join_split_kernel(here_ref, keep_a, came_a, keep_b, came_b, *outs):
    cut = keep_a.shape[2]
    for m, out in enumerate(outs):
        at = here_ref[0] ^ m
        out[:, :cut] = (keep_a[:, at].astype(f32) + came_a[:, at].astype(f32)).astype(bf16)
        out[:, cut:] = (keep_b[:, at].astype(f32) + came_b[:, at].astype(f32)).astype(bf16)


def join_split(here, parts, outer, places):
    parts = [p.reshape((outer, places) + p.shape[1:]) for p in parts]
    tail = (parts[0].shape[2] + parts[2].shape[2],) + parts[0].shape[3:]
    out = pl.pallas_call(
        join_split_kernel,
        grid=(outer,),
        in_specs=[pl.BlockSpec(memory_space=pltpu.SMEM)] + [pl.BlockSpec((1,) + p.shape[1:], lambda i: (i, 0, 0, 0, 0)) for p in parts],
        out_specs=[pl.BlockSpec((1,) + tail, lambda i: (i, 0, 0, 0))] * places,
        out_shape=[jax.ShapeDtypeStruct((outer,) + tail, bf16)] * places,
        name="join_split",
        **params(1, 24),
    )(here, *parts)
    return list(out)


def own_block(shape):
    return pl.BlockSpec(shape, lambda *_: (0,) * len(shape))


def pack_kernel(moves, count, *refs):
    ins, out_ref, wide = refs[:count], refs[count], refs[count + 1 :]
    rows = out_ref.shape[1]
    for ref, w in zip(ins, wide):
        w[...] = ref[...].astype(f32)
    for source, begin, step, square, block in moves:
        value = wide[source][pl.ds(begin, rows, stride=step), :]
        out_ref[square, :, block * LANES : (block + 1) * LANES] = value.astype(bf16)


def pack(arrays, moves, squares, rows, width, name):
    arrays = [a.reshape(-1, LANES) for a in arrays]
    return pl.pallas_call(
        functools.partial(pack_kernel, moves, len(arrays)),
        in_specs=[own_block(a.shape) for a in arrays],
        out_specs=own_block((squares, rows, width)),
        out_shape=jax.ShapeDtypeStruct((squares, rows, width), bf16),
        scratch_shapes=[pltpu.VMEM(a.shape, f32) for a in arrays],
        name=name,
        **params(1, 16),
    )(*placed(*arrays))


def square_moves(source, square, width):
    blocks = width // LANES
    return [(source, b, blocks, square, b) for b in range(blocks)]


def finish_kernel(moves, count, *refs):
    ins, outs = refs[:count], refs[count:]
    rows = ins[0].shape[1]
    for square, block, out, begin, step in moves:
        cols = slice(block * LANES, (block + 1) * LANES)
        total = ins[0][square, :, cols].astype(f32)
        for ref in ins[1:]:
            total += ref[square, :, cols].astype(f32)
        if step:
            outs[out][pl.ds(begin, rows, stride=step), :] = total
        else:
            outs[out][:, cols] = total


def finish(parts, moves, shapes, name):
    return pl.pallas_call(
        functools.partial(finish_kernel, moves, len(parts)),
        in_specs=[own_block(p.shape) for p in parts],
        out_specs=[own_block(s) for s in shapes],
        out_shape=[jax.ShapeDtypeStruct(s, f32) for s in shapes],
        name=name,
        **params(1, 16),
    )(*parts)


def fill_items(ref, first, high, keys, block, tile):
    filled = jnp.int32(0)
    for b in range(len(first)):
        count = (high[b] - first[b] * LANES + tile - 1) // tile

        def put(j, at, b=b):
            ref[0, at] = b
            ref[1, at] = first[b] + j * (tile // LANES)
            return at + 1

        filled = lax.fori_loop(0, count, put, filled)
    for j in range(PADDING):
        ref[0, filled + j] = len(first) - 1
        ref[1, filled + j] = keys // LANES
    for i, n in enumerate(EACH):
        ref[2, i] = (filled + n - 1) // n


def plan_kernel(block, tile, seg_ref, mem_ref, qid_ref, mid_ref, own_ref, cross_ref):
    def ends_of(ref):
        ends, total = [], jnp.int32(0)
        for i in range(ref.shape[1]):
            total += ref[0, i]
            ends.append(total)
        return ends

    ends, mem_ends = ends_of(seg_ref), ends_of(mem_ref)
    for ref, marks in ((qid_ref, ends), (mid_ref, mem_ends)):
        places = lax.broadcasted_iota(jnp.int32, ref.shape, 1)
        ids = jnp.zeros(ref.shape, jnp.int32)
        for mark in marks:
            ids += (places >= mark).astype(jnp.int32)
        ref[...] = ids
    total, keys = qid_ref.shape[1], mid_ref.shape[1]
    own, low, high = [], [], []
    for begin in range(0, total, block):
        own_first, first, last = jnp.int32(0), jnp.int32(0), mem_ref[0, 0]
        for i in range(seg_ref.shape[1]):
            passed = (ends[i] <= begin).astype(jnp.int32)
            own_first += passed * seg_ref[0, i]
            first += passed * mem_ref[0, i]
            if i + 1 < seg_ref.shape[1]:
                last += (ends[i] <= begin + block - 1).astype(jnp.int32) * mem_ref[0, i + 1]
        own.append(own_first // LANES)
        low.append(first // LANES)
        high.append(last)
    fill_items(own_ref, own, [begin + block for begin in range(0, total, block)], total, block, tile)
    fill_items(cross_ref, low, high, keys, block, tile)


def plan(seg, mem, total, keys, block=QROWS, tile=256):
    smem = pl.BlockSpec(memory_space=pltpu.SMEM)
    sds = jax.ShapeDtypeStruct
    more = PADDING
    return pl.pallas_call(
        functools.partial(plan_kernel, block, tile),
        in_specs=[smem, smem],
        out_specs=[own_block((1, total)), own_block((1, keys)), smem, smem],
        out_shape=[
            sds((1, total), jnp.int32), sds((1, keys), jnp.int32),
            sds((3, total // block * (total // tile) + more), jnp.int32), sds((3, total // block * (keys // tile) + more), jnp.int32),
        ],
        name="plan",
        **params(1, 16),
    )(seg, mem)

HEAD_START = 1


def mesh_size():
    return lax.axis_size("dp") * lax.axis_size("fsdp")


def position():
    return lax.axis_index("dp") * lax.axis_size("fsdp") + lax.axis_index("fsdp")


def bit_groups(wide):
    count = mesh_size().bit_length() - 1
    groups = [(0, 1)]
    while groups[-1][0] + groups[-1][1] < count:
        low = groups[-1][0] + groups[-1][1]
        groups.append((low, min(2 if len(groups) <= wide else 1, count - low)))
    return groups


def swap(x, mask):
    return lax.ppermute(x, ("dp", "fsdp"), [(i, i ^ mask) for i in range(mesh_size())])


def place_in(group):
    return (position() >> group[0]) & ((1 << group[1]) - 1)


def tie(x, *after):
    return lax.optimization_barrier((x, *after))[0] if after else x


def gather_step(x, group, after=(), lower=0, came=None):
    low, width = group
    here = place_in(group)
    if came is None:
        came = tie([swap(x, m << low) for m in range(1, 1 << width)], *after)
    blocks = [x] + came
    for j in range(width):
        flip = (here >> j) & 1 == 1
        blocks = [jnp.where(flip, blocks[p ^ (1 << j)], blocks[p]) for p in range(1 << width)]
    return jnp.stack(blocks, axis=x.ndim - 2 - lower)


def gathered(x):
    return x.reshape(x.shape[:1] + (-1, x.shape[-1]))


def swap_pieces(parts, group, after=()):
    return [parts[0]] + tie([swap(parts[m], m << group[0]) for m in range(1, len(parts))], *after)


def next_pieces(parts, groups, done):
    group = groups[done]
    outer = 1 << sum(g[1] for g in groups[done + 1 :])
    return add_split(place_in(group).reshape(1).astype(jnp.int32), parts, outer, 1 << group[1])


def norm_parts(norm_params, size):
    parts, left = [], norm_params
    for _ in range(3):
        part = left.astype(bf16)
        parts.append(jnp.pad(part, (0, LANES - part.size)))
        left = left - part.astype(f32)
    flat = jnp.concatenate(parts)
    return jnp.pad(flat, (0, size - flat.size))


def resplit(keep, send, devices, core, squares):
    halves = jnp.concatenate([keep, send])
    width = halves.shape[-1]
    first = halves[:, :squares].transpose(1, 0, 2, 3).reshape(squares, devices, -1, width).transpose(1, 0, 2, 3)
    rows = first.shape[2]
    if halves.shape[1] > squares:
        rest = halves[:, squares:].reshape(devices, halves.shape[1] - squares, rows, width)
        first = jnp.concatenate([first, rest], axis=1)
    both = first.reshape(devices // 2, 2, -1, rows, width)
    return [lax.dynamic_index_in_dim(both, core ^ m, 1, keepdims=False) for m in range(2)]


def body(
    inputs, memory, seg_lengths, mem_lengths, self_query, self_key, self_value, self_out,
    cross_query, cross_key, cross_value, cross_out, ffn_in, ffn_out, norm_params, cotangent,
):
    total, width = inputs.shape
    keys = memory.shape[0]
    devices = mesh_size()
    groups, single = bit_groups(8), bit_groups(1)
    down = groups[::-1]
    shard = norm_params.shape[0]
    size = self_query.shape[0]
    own_rows = size // width
    blocks = ffn_in.shape[0] // size
    whole_tiles = own_rows % 16 == 0
    core = place_in(groups[0]).reshape(1).astype(jnp.int32)

    firsts = (self_query, self_key, self_value)
    seconds = (self_out, cross_query, cross_key, cross_value, norm_parts(norm_params, size))
    if whole_tiles:
        lane_blocks = width // LANES
        three = [m for i in range(3) for m in square_moves(i, i, width)]
        five = three + [m for i in range(3, 5) for m in square_moves(i, i, width)]
        wide = [(0, c * lane_blocks + b, blocks * lane_blocks, c, b) for c in range(blocks) for b in range(lane_blocks)]
        tall = [(1, j * own_rows * lane_blocks + b, lane_blocks, blocks + 1 + j, b) for j in range(blocks) for b in range(lane_blocks)]
        first = pack(firsts, three, 3, own_rows, width, "pack_self")
        second = pack(tie(seconds, first), five, 5, own_rows, width, "pack_cross")
        last = square_moves(2, blocks, width)
        third = pack(tie((ffn_in, ffn_out, cross_out), first), wide + tall + last, 2 * blocks + 1, own_rows, width, "pack_ffn")
    else:
        first = jnp.concatenate(firsts).reshape(3, own_rows, width)
        second = jnp.concatenate(seconds).reshape(5, own_rows, width)
        fi = ffn_in.reshape(own_rows, blocks, width).transpose(1, 0, 2)
        third = jnp.concatenate([fi, cross_out.reshape(1, own_rows, width), ffn_out.reshape(blocks, own_rows, width)])
    third = third.reshape(-1, width)
    plane = groups[1]
    high_bits = [(b, 1) for b in reversed(range(plane[0] + plane[1], devices.bit_length() - 1))]
    for g in down[:-2]:
        first = gather_step(first, g)
    second = gather_step(second, high_bits[0])
    qid, mid, own_items, items = plan(*tie((seg_lengths, mem_lengths), first), total, keys)
    first = gather_step(first, plane, [second, own_items])
    for g in high_bits[1:]:
        second = gather_step(second, g)
    third = gather_step(third, high_bits[0])
    first = gathered(gather_step(first, down[-1], [second, third]))
    for g in high_bits[1:]:
        third = gather_step(third, g)
    low, high = (plane[0], 1), (plane[0] + 1, 1)
    cut = (blocks + 1) * own_rows
    part_a, part_b = tie((third[..., :cut, :], third[..., cut:, :]), first)
    early = [second, part_a, part_b]
    pairs = devices // 2 if whole_tiles else 1
    part_of = core if whole_tiles else jnp.zeros_like(core)

    q1, k1, v1, o1, l1 = self_forward(own_items, inputs, first, qid, early)
    second = gather_step(second, plane, [l1])
    came_a, came_b = tie((swap(part_a, 1 << low[0]), swap(part_b, 1 << high[0])), l1)
    second = tie(second, came_a, came_b)
    part_a, part_b = gather_step(part_a, low, came=[came_a]), gather_step(part_b, high, came=[came_b])
    second = gathered(gather_step(second, down[-1]))
    norm_all = second[4].reshape(devices, -1)[:, : 3 * LANES].reshape(devices, 3, LANES)[:, :, :shard].astype(f32)
    norms = jnp.sum(norm_all, axis=1).reshape(6, width)
    k2, v2, r1, h1b, q2, h1, o2, l2 = cross_forward(items, memory, inputs, o1, second, norms, qid, mid, [])
    part_a, part_b = gather_step(part_a, high, [l2], 1), gather_step(part_b, low, [l2])
    ffn_a, ffn_b = (gather_step(p, down[-1]).reshape(devices, -1, own_rows, width) for p in (part_a, part_b))
    if not whole_tiles:
        ffn_a = jnp.stack([ffn_a[:, i].reshape(width, width) for i in range(blocks + 1)])[None]
        ffn_b = ffn_b.reshape(1, blocks, width, width)
    out, dr3, dr2, do2, delta2, keep, send, gn23 = ffn(part_of, pairs, h1, inputs, cotangent, o2, ffn_a, ffn_b, norms)

    one = [keep, send] if whole_tiles else resplit(keep, send, devices, core[0], blocks + 1)
    dq2a, dk2a, dv2a, gckva = cross_backward(items, q2, k2, v2, do2, l2, delta2, qid, mid, memory, 0, HEAD_START, 6, [])
    low, high = 1 << groups[1][0], 2 << groups[1][0]
    both = jnp.stack([(position() >> (groups[1][0] + j)) & 1 for j in range(2)]).astype(jnp.int32)
    one = swap_pieces(one, groups[0], [dq2a])
    one = first_pair(both, one[0], one[1], devices // 8, blocks + 1)
    more = width // LANES - HEAD_START
    dq2b, dk2b, dv2b, gckvb = cross_backward(
        items, q2, k2, v2, do2, l2, delta2, qid, mid, memory, HEAD_START, more, 2, [one[1], one[3]]
    )
    came = tie([swap(one[1], low), swap(one[3], high)], dq2b)
    one = second_pair(both, [one[0], came[0], one[2], came[1]])
    gm = memory_grad(dk2a, dk2b, dv2a, dv2b, second, 2, [one[1], one[3]])
    dsum, do1, delta1, keep, send, gn = between(
        part_of, pairs, gckva, gckvb, gn23, r1, dr2, dr3, dq2a, dq2b, h1b, o1, second, norms, placed(gm)
    )
    came = tie([swap(one[1], high), swap(one[3], low)], do1)
    one = join_split(
        place_in(single[2]).reshape(1).astype(jnp.int32), [one[0], came[0], one[2], came[1]],
        1 << sum(g[1] for g in single[3:]), 1 << single[2][1],
    )
    two = [keep, send]
    if not whole_tiles:
        two = resplit(keep, send, devices, core[0], 5)
        own_norms = jnp.pad(gn[:6].astype(bf16).reshape(devices, -1), ((0, 0), (0, size - shard)))
        own_norms = own_norms.reshape(devices // 2, 2, own_rows, width)
        two = [two[m].at[:, 4].set(lax.dynamic_index_in_dim(own_norms, core[0] ^ m, 1, keepdims=False)) for m in range(2)]
    two = next_pieces(swap_pieces(tie(two, one[1]), groups[0]), groups, 1)
    gx, keep, send = self_backward(part_of, pairs, own_items, q1, k1, v1, do1, l1, delta1, qid, inputs, first, dsum, one[1:] + two[1:])
    two = next_pieces(swap_pieces(two, groups[1], [gx]), single, 2)
    one = next_pieces(swap_pieces(one, single[2], [gx]), single, 3)
    keep, send = tie((keep, send), two[1], one[1])
    three = [keep, send] if whole_tiles else resplit(keep, send, devices, core[0], 3)
    three = next_pieces(swap_pieces(three, groups[0]), groups, 1)
    for i in range(2, len(groups)):
        three = next_pieces(swap_pieces(three, groups[i - 1]), groups, i)
    for i in range(3, len(single)):
        two = next_pieces(swap_pieces(two, single[i - 1]), single, i)
        if i > 3:
            one = next_pieces(swap_pieces(one, single[i - 1]), single, i)

    def flat(g):
        return g.reshape(-1)

    chains = [swap_pieces(one, single[-1], [three[1]]), swap_pieces(two, single[-1], [three[1]]), swap_pieces(three, groups[-1])]
    chains = [[p.reshape(-1, own_rows, width) for p in chain] for chain in chains]
    if whole_tiles:
        lane_rows = size // LANES
        square, long = (lane_rows, LANES), (blocks * lane_rows, LANES)

        moves = [(c, b, 0, c * lane_blocks + b, blocks * lane_blocks) for c in range(blocks) for b in range(lane_blocks)]
        moves += [(blocks, b, 1, b, lane_blocks) for b in range(lane_blocks)]
        moves += [
            (blocks + 1 + j, b, 2, j * own_rows * lane_blocks + b, lane_blocks) for j in range(blocks) for b in range(lane_blocks)
        ]
        gfi, gco, gfo = finish(chains[0], moves, [long, square, long], "finish_ffn")
        moves = [(i, b, i, b, lane_blocks) for i in range(4) for b in range(lane_blocks)] + [(4, b, 4, 0, 0) for b in range(lane_blocks)]
        gck, gcv, gcq, gso, gn = finish(chains[1], moves, [square] * 4 + [(own_rows, width)], "finish_cross")
        gn = lax.dynamic_slice_in_dim(flat(gn[:6]), position() * shard, shard)
        moves = [(i, b, i, b, lane_blocks) for i in range(3) for b in range(lane_blocks)]
        gsq, gsk, gsv = finish(chains[2], moves, [square] * 3, "finish_self")
    else:
        one, two, three = (sum(p.astype(f32) for p in chain) for chain in chains)
        gfi, gco, gfo = one[:blocks].transpose(1, 0, 2), one[blocks], one[blocks + 1 :]
        gck, gcv, gcq, gso, gn = two[0], two[1], two[2], two[3], flat(two[4])[:shard]
        gsq, gsk, gsv = three[0], three[1], three[2]
    return (out, gx, gm) + tuple(flat(g) for g in (gsq, gsk, gsv, gso, gcq, gck, gcv, gco, gfi, gfo, gn))


def solution(mesh):
    rows, flat = P(("dp", "fsdp"), None), P(("dp", "fsdp"))
    return jax.shard_map(
        body,
        mesh=mesh,
        in_specs=(rows,) * 4 + (flat,) * 11 + (rows,),
        out_specs=(rows,) * 3 + (flat,) * 11,
        check_vma=False,
    )
```

```python
import functools
import jax
import jax.numpy as jnp
from jax import lax
from jax.experimental import pallas as pl
from jax.experimental.pallas import tpu as pltpu
from jax.sharding import PartitionSpec as P

HD = 64
LANES = 128
MOST = 256
QROWS = 128
EACH = (2, 3, 6)
PADDING = 6
FFN_CHUNK = 256
masked_score = -1e30
norm_eps = 1e-05
bf16, f32 = jnp.bfloat16, jnp.float32
NT = (((1,), (1,)), ((), ()))
TN = (((0,), (0,)), ((), ()))
NN = (((1,), (0,)), ((), ()))


def mm(left, right, dims=NN):
    return lax.dot_general(left, right, dims, preferred_element_type=f32)


def norm_rows(source):
    mean = jnp.mean(source, axis=-1, keepdims=True)
    centered = source - mean
    variance = jnp.mean(centered * centered, axis=-1, keepdims=True)
    rstd = lax.rsqrt(variance + norm_eps)
    return centered * rstd, rstd


def lane_below(rows):
    return lax.broadcasted_iota(jnp.int32, (rows, LANES), 1) < HD


def column_of(row):
    return jnp.broadcast_to(row, (LANES, row.shape[1])).T


def head_part(pair, which, low):
    return jnp.where(low == (which == 0), pair, jnp.zeros_like(pair))


def values_with_ones(values):
    parts = []
    for p in range(values.shape[1] // LANES):
        pair = values[:, p * LANES : (p + 1) * LANES]
        parts += [pair, jnp.ones_like(pair)]
    return jnp.concatenate(parts, axis=1)


def finish_heads(at, top, tot, acc, write):
    shape = acc.shape[0], at.size if hasattr(at, "size") else at.stop - at.start, LANES
    lane = lax.broadcasted_iota(jnp.int32, shape[1:], 1)
    sums, tops = jnp.ones(shape[1:], f32), jnp.zeros(shape[1:], f32)
    for p in range(shape[0]):
        total = tot[p, at, :]
        write(p, (acc[p, at, :] / total).astype(bf16))
        sums = jnp.where(lane % HD == p, total, sums)
        tops = jnp.where(lane == p, top[2 * p, at, :], jnp.where(lane == HD + p, top[2 * p + 1, at, :], tops))
    return tops + jnp.log(sums)


def column_at(head):
    return head % 2 * HD + head // 2


def item_at(items_ref, n, idk_ref, ids_q, keys, tile, block, causal):
    begin = pl.multiple_of(items_ref[0, n] * block, block)
    wanted = items_ref[1, n] * LANES
    start = pl.multiple_of(jnp.minimum(wanted, keys - tile), LANES)
    at = pl.ds(begin, block)
    pos = start + lax.broadcasted_iota(jnp.int32, (1, tile), 1)
    ids_k = jnp.where(pos >= wanted, idk_ref[:, pl.ds(start, tile)], -1)
    allowed = ids_q[at, :1] == ids_k
    if causal:
        allowed &= pos <= begin + lax.broadcasted_iota(jnp.int32, (block, 1), 0)
    return at, pl.ds(start, tile), jnp.where(allowed, 0.0, masked_score).astype(f32)


def attend(items_ref, idk_ref, ids_q, q_all, k_all, vx_all, top, tot, acc, tile, block, causal):
    keys, width = k_all.shape
    pairs = width // LANES
    heads = 2 * pairs
    low = lane_below(block)
    top[...] = jnp.full(top.shape, masked_score, f32)
    tot[...] = jnp.zeros(tot.shape, f32)
    acc[...] = jnp.zeros(acc.shape, f32)

    def some(i, _):
        loads, made = [], []
        for t in range(EACH[0]):
            at, there, bias = item_at(items_ref, EACH[0] * i + t, idk_ref, ids_q, keys, tile, block, causal)
            loads.append((at, there, bias))
            for p in range(pairs):
                cols = slice(p * LANES, (p + 1) * LANES)
                part = q_all[at, cols]
                both = jnp.concatenate([head_part(part, h, low) for h in range(2)])
                made.append(mm(both, k_all[there, cols], NT))
        weights, scales = [], []
        for t, (at, there, bias) in enumerate(loads):
            for head in range(heads):
                s = made[t * pairs + head // 2][head % 2 * block : (head % 2 + 1) * block] + bias
                old = top[head, at, :]
                new = jnp.maximum(old, jnp.max(s, axis=1, keepdims=True))
                top[head, at, :] = new
                scales.append(jnp.exp(old - new))
                weights.append(jnp.exp(s - jnp.concatenate([new] * (tile // LANES), axis=1)).astype(bf16))
        mixed = [
            mm(jnp.concatenate(weights[t * heads + 2 * p : t * heads + 2 * p + 2]), vx_all[there, 2 * p * LANES : 2 * (p + 1) * LANES])
            for t, (_, there, _) in enumerate(loads) for p in range(pairs)
        ]
        for t, (at, _, _) in enumerate(loads):
            for p in range(pairs):
                n = t * pairs + p
                scale = jnp.where(low, scales[2 * n], scales[2 * n + 1])
                o = mixed[n]
                acc[p, at, :] = acc[p, at, :] * scale + jnp.where(low, o[:block, :LANES], o[block:, :LANES])
                tot[p, at, :] = tot[p, at, :] * scale + jnp.where(low, o[:block, LANES:], o[block:, LANES:])
        return 0

    lax.fori_loop(0, items_ref[2, 0], some, 0)


def attend_back(items_ref, idk_ref, ids_q, q_all, do_ref, k_ref, v_ref, l_ref, delta_ref, dq, dk, dv, tile, block, first_head, causal, each):
    keys, width = k_ref.shape
    pairs = width // LANES
    low = lane_below(block)

    def some(i, _):
        loads, scores, grads = [], [], []
        for t in range(each):
            at, there, bias = item_at(items_ref, each * i + t, idk_ref, ids_q, keys, tile, block, causal)
            loads.append((at, there, bias))
            for p in range(pairs):
                cols = slice(p * LANES, (p + 1) * LANES)
                q, do = q_all[at, cols], do_ref[at, cols]
                qs = jnp.concatenate([head_part(q, h, low) for h in range(2)])
                dos = jnp.concatenate([head_part(do, h, low) for h in range(2)])
                scores.append((mm(qs, k_ref[there, cols], NT), qs))
                grads.append((mm(dos, v_ref[there, cols], NT), dos))
        weights, slopes = [], []
        for t, (at, there, bias) in enumerate(loads):
            logs, deltas = l_ref[at, :], delta_ref[at, :]
            for p in range(pairs):
                es, ds = [], []
                for h in range(2):
                    lane = column_at(first_head + 2 * p + h)
                    rows = slice(h * block, (h + 1) * block)
                    e = jnp.exp(scores[t * pairs + p][0][rows] + bias - logs[:, lane : lane + 1])
                    es.append(e.astype(bf16))
                    ds.append((e * (grads[t * pairs + p][0][rows] - deltas[:, lane : lane + 1])).astype(bf16))
                weights.append(jnp.concatenate(es))
                slopes.append(jnp.concatenate(ds))
        for t, (at, there, _) in enumerate(loads):
            for p in range(pairs):
                cols = slice(p * LANES, (p + 1) * LANES)
                n = t * pairs + p
                gq = mm(slopes[n], k_ref[there, cols])
                gk = mm(slopes[n], scores[n][1], TN)
                gv = mm(weights[n], grads[n][1], TN)
                dq[at, cols] += jnp.where(low, gq[:block], gq[block:])
                dk[there, cols] += gk
                dv[there, cols] += gv
        return 0

    lax.fori_loop(0, items_ref[2, EACH.index(each)], some, 0)


def self_forward_kernel(tile, block, items_ref, x_ref, wq_ref, wk_ref, wv_ref, idr_ref, *rest):
    q_ref, k_ref, v_ref, o_ref, l_ref, q_all, k_all, vx_all, ids_all, top, tot, acc = rest[-12:]
    step = pl.program_id(0)
    rows = x_ref.shape[0]
    total, width = k_all.shape
    turns = total // rows

    @pl.when(step < turns)
    def _():
        x = x_ref[...]
        q = mm(x, wq_ref[0]).astype(bf16)
        k = mm(x, wk_ref[0]).astype(bf16)
        v = mm(x, wv_ref[0]).astype(bf16)
        q_ref[...] = q
        k_ref[...] = k
        v_ref[...] = v
        here = pl.ds(pl.multiple_of(step * rows, rows), rows)
        q_all[here, :] = q * jnp.asarray(HD ** -0.5, bf16)
        k_all[here, :] = k
        vx_all[here, :] = values_with_ones(v)
        ids_all[here, :] = column_of(idr_ref[:, here])

    @pl.when(step == turns)
    def _():
        attend(items_ref, idr_ref, ids_all, q_all, k_all, vx_all, top, tot, acc, tile, block, True)
        size = 2 * block
        for j in range(total // size):
            at = slice(j * size, (j + 1) * size)

            def write(p, value):
                o_ref[at, p * LANES : (p + 1) * LANES] = value

            l_ref[at, :] = finish_heads(at, top, tot, acc, write)


def whole(a):
    return pl.BlockSpec(a.shape, lambda *_: (0,) * a.ndim)


def once(a):
    return pl.BlockSpec(a.shape, lambda *_: (0,) * a.ndim, pipeline_mode=pl.Buffered(1))


def part(weights, index, columns, half):
    return pl.BlockSpec((1, weights.shape[1], columns), lambda *_: (index, 0, half))


def params(us, vmem):
    return dict(
        compiler_params=pltpu.CompilerParams(vmem_limit_bytes=vmem * 2**20),
        cost_estimate=pl.CostEstimate(flops=us * 10**9, bytes_accessed=2**20, transcendentals=0),
    )


apart = pl.BlockSpec(memory_space=pl.ANY)


def out_array(shape, dtype):
    return pltpu.HBM(shape, dtype)


def placed(*arrays):
    return [pltpu.with_memory_space_constraint(a, pltpu.HBM) for a in arrays]


def self_forward(items, x, weights, idr, after, turns=2, block=QROWS, tile=256):
    total, width = x.shape
    heads = width // HD
    rows = total // turns
    early = lambda w: pl.BlockSpec((rows, w), lambda i, *_: (jnp.minimum(i, turns - 1), 0))
    fixed = lambda w: pl.BlockSpec((total, w), lambda i, *_: (0, 0))
    sds = out_array
    full = sds((total, width), bf16)
    return pl.pallas_call(
        functools.partial(self_forward_kernel, tile, block),
        grid_spec=pltpu.PrefetchScalarGridSpec(
            num_scalar_prefetch=1,
            grid=(turns + 1,),
            in_specs=[early(width)] + [part(weights, i, width, 0) for i in range(3)] + [whole(idr)] + [apart] * len(after),
            out_specs=[early(width)] * 3 + [fixed(width), fixed(LANES)],
            scratch_shapes=[
                pltpu.VMEM((total, width), bf16), pltpu.VMEM((total, width), bf16), pltpu.VMEM((total, 2 * width), bf16),
                pltpu.VMEM((total, LANES), jnp.int32),
                pltpu.VMEM((heads, total, LANES), f32), pltpu.VMEM((heads // 2, total, LANES), f32), pltpu.VMEM((heads // 2, total, LANES), f32),
            ],
        ),
        out_shape=[full] * 4 + [sds((total, LANES), f32)],
        name="self_forward",
        **params(13, 32),
    )(items, *placed(x), weights, weights, weights, idr, *after)


def cross_forward_kernel(
    tile, block, items_ref, memory_ref, wk_ref, wv_ref, x_ref, o1_ref, wso_ref, wcq_ref, norms_ref, idr_ref, idk_ref, *rest
):
    k2_ref, v2_ref, r1_ref, h1b_ref, q2_ref, h1_ref, o_ref, l_ref, k_all, vx_all, q_all, ids_all, top, tot, acc = rest[-15:]
    step = pl.program_id(0)
    rows, width = x_ref.shape
    keys = k_all.shape[0]
    turns = pl.num_programs(0) - 1

    @pl.when(step < turns)
    def _():
        per = memory_ref.shape[0]
        memory = memory_ref[...]
        r1 = x_ref[...].astype(f32) + mm(o1_ref[...], wso_ref[0])
        k2 = mm(memory, wk_ref[0]).astype(bf16)
        r1_ref[...] = r1.astype(bf16)
        n1, _ = norm_rows(r1)
        v2 = mm(memory, wv_ref[0]).astype(bf16)
        h1 = n1 * norms_ref[0:1, :] + norms_ref[1:2, :]
        h1b = h1.astype(bf16)
        h1b_ref[...] = h1b
        q2 = mm(h1b, wcq_ref[0]).astype(bf16)
        q2_ref[...] = q2
        k2_ref[...] = k2
        v2_ref[...] = v2
        here = pl.ds(pl.multiple_of(step * rows, rows), rows)
        q_all[here, :] = q2 * jnp.asarray(HD ** -0.5, bf16)
        h1_ref[...] = h1
        ids_all[here, :] = column_of(idr_ref[:, here])
        there = pl.ds(pl.multiple_of(step * per, per), per)
        k_all[there, :] = k2
        vx_all[there, :] = values_with_ones(v2)

    @pl.when(step == turns)
    def _():
        attend(items_ref, idk_ref, ids_all, q_all, k_all, vx_all, top, tot, acc, tile, block, False)

        size = 2 * block
        for j in range(q_all.shape[0] // size):
            at = slice(j * size, (j + 1) * size)

            def write(p, value):
                o_ref[at, p * LANES : (p + 1) * LANES] = value

            l_ref[at, :] = finish_heads(at, top, tot, acc, write)


def cross_forward(items, memory, x, o1, weights, norms, idr, idk, after, turns=2, block=QROWS, tile=256):
    total, width = x.shape
    keys = memory.shape[0]
    heads = width // HD
    rows, per = total // turns, keys // turns
    early = lambda r, w: pl.BlockSpec((r, w), lambda i, *_: (jnp.minimum(i, turns - 1), 0))
    fixed = lambda w: pl.BlockSpec((total, w), lambda i, *_: (0, 0))
    sds = out_array
    return pl.pallas_call(
        functools.partial(cross_forward_kernel, tile, block),
        grid_spec=pltpu.PrefetchScalarGridSpec(
            num_scalar_prefetch=1,
            grid=(turns + 1,),
            in_specs=[early(per, width), part(weights, 2, width, 0), part(weights, 3, width, 0)]
            + [early(rows, width), early(rows, width), part(weights, 0, width, 0), part(weights, 1, width, 0)]
            + [whole(norms), whole(idr), whole(idk)] + [apart] * len(after),
            out_specs=[early(per, width)] * 2 + [early(rows, width)] * 4 + [fixed(width), fixed(LANES)],
            scratch_shapes=[
                pltpu.VMEM((keys, width), bf16),
                pltpu.VMEM((keys, 2 * width), bf16),
                pltpu.VMEM((total, width), bf16),
                pltpu.VMEM((total, LANES), jnp.int32),
                pltpu.VMEM((heads, total, LANES), f32),
                pltpu.VMEM((heads // 2, total, LANES), f32),
                pltpu.VMEM((heads // 2, total, LANES), f32),
            ],
        ),
        out_shape=[
            sds((keys, width), bf16), sds((keys, width), bf16), sds((total, width), bf16), sds((total, width), bf16),
            sds((total, width), bf16), sds((total, width), f32), sds((total, width), bf16), sds((total, LANES), f32),
        ],
        name="cross_forward",
        **params(19, 44),
    )(items, *placed(memory), weights, weights, *placed(x, o1), weights, weights, norms, idr, idk, *after)


def norm_back(incoming, normal, rstd, gain):
    m = incoming * gain
    return rstd * (
        m - jnp.mean(m, axis=-1, keepdims=True) - normal * jnp.mean(m * normal, axis=-1, keepdims=True)
    )


def head_columns(left, right):
    width = left.shape[1]
    prod = left.astype(f32) * right.astype(f32)
    lane = lax.broadcasted_iota(jnp.int32, (width, LANES), 1)
    own = lax.broadcasted_iota(jnp.int32, (width, LANES), 0) // HD == 2 * (lane % HD) + lane // HD
    own = own.astype(bf16)
    high = prod.astype(bf16)
    low = (prod - high.astype(f32)).astype(bf16)
    return mm(high, own) + mm(low, own)


def column_sums(a):
    return jnp.sum(a, axis=0, keepdims=True)


def spread(keep_ref, send_ref, core, write):
    def one(j, _):
        write(2 * j + core, keep_ref, j)
        write(2 * j + 1 - core, send_ref, j)
        return 0

    lax.fori_loop(0, keep_ref.shape[0], one, 0)


def ffn_kernel(
    core_ref, here_ref, h1_ref, x_ref, cot_ref, o2_ref, norms_ref, *rest
):
    count = len(rest) - 11
    pieces = 8 if count >= 8 else 2
    weights, rest = rest[:pieces], rest[pieces:]
    out_ref, dr3_ref, dr2_ref, do2_ref, delta_ref, keep_ref, send_ref, gn_ref, gin, gout, gco = rest[:11]
    wa_ref, wb_ref = rest[11:] if pieces == 8 else weights
    step = pl.program_id(0)
    last = pl.num_programs(0) - 1
    width = x_ref.shape[1]
    share = width // wb_ref.shape[0]
    blocks = wb_ref.shape[1] // share

    @pl.when(step == 0)
    def _():
        if pieces == 8:
            bits = here_ref[0], here_ref[1]
            for n, (ref, axis) in enumerate(((wa_ref, 1), (wb_ref, 0))):
                for m in range(4):
                    across, core = bits[axis] ^ (m % 2), here_ref[2] ^ (m // 2)
                    piece = weights[4 * n + m]
                    for z in range(piece.shape[0]):
                        for other in range(2):
                            planes = (across, other) if axis else (other, across)
                            ref[z * 8 + planes[0] * 4 + planes[1] * 2 + core] = piece[z, other]
        gin[...] = jnp.zeros_like(gin)
        gout[...] = jnp.zeros_like(gout)
        gco[...] = jnp.zeros_like(gco)
        gn_ref[...] = jnp.zeros_like(gn_ref)

    win = [wa_ref[:, c * share : (c + 1) * share].reshape(width, width) for c in range(blocks)]
    wout = wb_ref[...].reshape(blocks * width, width)
    wco = wa_ref[:, blocks * share :].reshape(width, width)
    n2, rstd2 = norm_rows(h1_ref[...] + mm(o2_ref[...], wco))
    h2 = n2 * norms_ref[2:3, :] + norms_ref[3:4, :]
    h2b = h2.astype(bf16)
    chunk = min(FFN_CHUNK, width)
    parts = blocks * width // chunk
    per = width // chunk

    def win_part(c):
        return win[c // per][:, (c % per) * chunk : (c % per + 1) * chunk]

    acts, slopes, hidden = [], [], [mm(h2b, win_part(0))]
    ff = jnp.zeros(h2.shape, f32)
    for c in range(parts):
        if c + 1 < parts:
            hidden.append(mm(h2b, win_part(c + 1)))
        u = hidden[c]
        square = u * u
        t = jnp.tanh(u * (0.7978845608028654 + (0.7978845608028654 * 0.044715) * square))
        half = 0.5 + 0.5 * t
        acts.append((u * half).astype(bf16))
        rise = u * (0.5 * 0.7978845608028654 + (0.5 * 0.7978845608028654 * 3 * 0.044715) * square)
        slopes.append(half + (1.0 - t * t) * rise)
        if c:
            ff += mm(acts[c - 1], wout[(c - 1) * chunk : c * chunk, :])
    ff += mm(acts[-1], wout[(parts - 1) * chunk :, :])
    r3 = h2 + ff + x_ref[...].astype(f32)
    n3, rstd3 = norm_rows(r3)
    gain3 = norms_ref[4:5, :]
    out_ref[...] = (n3 * gain3 + norms_ref[5:6, :]).astype(bf16)
    e = cot_ref[...].astype(f32)
    gn_ref[2:3, :] += column_sums(e * n3)
    gn_ref[3:4, :] += column_sums(e)
    dr3 = norm_back(e, n3, rstd3, gain3)
    dr3_ref[...] = dr3.astype(bf16)
    dfb = dr3.astype(bf16)
    dh2 = dr3
    raw, made = [mm(dfb, wout[:chunk, :], NT)], []
    for c in range(parts + 1):
        if c + 1 < parts:
            raw.append(mm(dfb, wout[(c + 1) * chunk : (c + 2) * chunk, :], NT))
        if c < parts:
            gout[c * chunk : (c + 1) * chunk, :] += mm(acts[c], dfb, TN)
            made.append((raw[c] * slopes[c]).astype(bf16))
        if c:
            gin[:, (c - 1) * chunk : c * chunk] += mm(h2b, made[c - 1], TN)
            dh2 += mm(made[c - 1], win_part(c - 1), NT)
    gn_ref[0:1, :] += column_sums(dh2 * n2)
    gn_ref[1:2, :] += column_sums(dh2)
    dr2 = norm_back(dh2, n2, rstd2, norms_ref[2:3, :])
    da2 = dr2.astype(bf16)
    dr2_ref[...] = da2
    o2 = o2_ref[...]
    gco[...] += mm(o2, da2, TN)
    do2 = mm(da2, wco, NT).astype(bf16)
    do2_ref[...] = do2
    delta_ref[...] = head_columns(do2, o2)

    @pl.when(step == last)
    def _():
        r = keep_ref.shape[2]

        def write(device, ref, j):
            here = pl.ds(pl.multiple_of(device * r, r), r)
            for c in range(blocks):
                ref[j, c] = gin[here, c * width : (c + 1) * width].astype(bf16)
            ref[j, blocks] = gco[here, :].astype(bf16)
            there = pl.ds(pl.multiple_of(device * blocks * r, blocks * r), blocks * r)
            ref[j, blocks + 1 :] = gout[there, :].astype(bf16).reshape(blocks, r, width)

        spread(keep_ref, send_ref, core_ref[0], write)


def ffn(core, here, pairs, h1, x, cot, o2, weights, norms, rows=512):
    total, width = x.shape
    devices = 1 if len(weights) == 2 else 2 * pairs
    blocks = weights[-1].size // width**2 if devices == 1 else 8 * weights[-1].size // (2 * width**2)
    held = [(devices, (blocks + 1) * width // devices, width), (devices, blocks * width // devices, width)]
    rowspec = lambda w: pl.BlockSpec((rows, w), lambda i: (i, 0))
    smem = pl.BlockSpec(memory_space=pltpu.SMEM)
    sds = out_array
    side = jax.ShapeDtypeStruct((pairs, 2 * blocks + 1, width // (2 * pairs), width), bf16)
    return pl.pallas_call(
        ffn_kernel,
        grid=(total // rows,),
        in_specs=[smem, smem] + [rowspec(width)] * 4 + [whole(norms)] + [once(w) for w in weights],
        out_specs=[rowspec(width)] * 4 + [rowspec(LANES), whole(side), whole(side), pl.BlockSpec((4, width), lambda i: (0, 0))],
        out_shape=[
            sds((total, width), bf16), sds((total, width), bf16), sds((total, width), bf16), sds((total, width), bf16),
            sds((total, LANES), f32), side, side, sds((4, width), f32),
        ],
        scratch_shapes=[pltpu.VMEM((width, blocks * width), f32), pltpu.VMEM((blocks * width, width), f32), pltpu.VMEM((width, width), f32)]
        + ([pltpu.VMEM(h, bf16) for h in held] if devices > 1 else []),
        name="ffn",
        **params(32, 56),
    )(core, here, *placed(h1, x, cot, o2), norms, *weights)


def cross_backward_kernel(
    tile, block, first, count, each, items_ref, q2_ref, k2_ref, v2_ref, do_ref, l_ref, delta_ref, idr_ref, idk_ref, memory_ref, *rest
):
    dq_ref, dk_ref, dv_ref, grads_ref, q_all, ids_all, dq, dk, dv, grads = rest[-10:]
    step = pl.program_id(0)
    total = q2_ref.shape[0]
    begin = first * LANES if q2_ref.shape[1] > count * LANES else 0
    cols = slice(begin, begin + count * LANES)

    @pl.when(step == 0)
    def _():
        dq[...] = jnp.zeros_like(dq)
        dk[...] = jnp.zeros_like(dk)
        dv[...] = jnp.zeros_like(dv)
        grads[...] = jnp.zeros_like(grads)
        q_all[...] = q2_ref[:, cols] * jnp.asarray(HD ** -0.5, bf16)
        for j in range(total // block):
            ids_all[j * block : (j + 1) * block, :] = column_of(idr_ref[:, j * block : (j + 1) * block])
        attend_back(
            items_ref, idk_ref, ids_all, q_all, do_ref.at[:, cols], k2_ref.at[:, cols], v2_ref.at[:, cols], l_ref, delta_ref,
            dq, dk, dv, tile, block, 2 * first, False, each,
        )

    memory = memory_ref[...]
    per = memory.shape[0]
    here = pl.ds(pl.multiple_of(step * per, per), per)
    for i, (ref, out_ref) in enumerate(((dk, dk_ref), (dv, dv_ref))):
        grad = ref[here, :].astype(bf16)
        out_ref[...] = grad
        grads[i] += mm(memory, grad, TN)
    rows = dq_ref.shape[0]
    dq_ref[...] = (dq[pl.ds(pl.multiple_of(step * rows, rows), rows), :] * HD ** -0.5).astype(bf16)

    @pl.when(step == pl.num_programs(0) - 1)
    def _():
        grads_ref[...] = grads[...].astype(bf16)


def cross_backward(items, q2, k2, v2, do, l, delta, idr, idk, memory, first, count, each, after, turns=2, block=QROWS, tile=256):
    total, width = q2.shape
    keys = k2.shape[0]
    columns = count * LANES
    alone = first % count == 0
    cols = lambda r: pl.BlockSpec((r, columns if alone else width), lambda i, *_: (0, first // count if alone else 0))
    rowspec = lambda r, w: pl.BlockSpec((r, w), lambda i, *_: (i, 0))
    sds = jax.ShapeDtypeStruct
    grad = sds((2, width, columns), bf16)
    return pl.pallas_call(
        functools.partial(cross_backward_kernel, tile, block, first, count, each),
        grid_spec=pltpu.PrefetchScalarGridSpec(
            num_scalar_prefetch=1,
            grid=(turns,),
            in_specs=[cols(total), cols(keys), cols(keys), cols(total)]
            + [whole(l), whole(delta), whole(idr), whole(idk), rowspec(keys // turns, width)] + [apart] * len(after),
            out_specs=[rowspec(total // turns, columns), rowspec(keys // turns, columns), rowspec(keys // turns, columns), whole(grad)],
            scratch_shapes=[
                pltpu.VMEM((total, columns), bf16), pltpu.VMEM((total, LANES), jnp.int32), pltpu.VMEM((total, columns), f32),
                pltpu.VMEM((keys, columns), f32), pltpu.VMEM((keys, columns), f32), pltpu.VMEM((2, width, columns), f32),
            ],
        ),
        out_shape=[sds((total, columns), bf16), sds((keys, columns), bf16), sds((keys, columns), bf16), grad],
        name="cross_backward",
        **params(5 * count + 4, 10 * count + 4),
    )(items, *placed(q2, k2, v2, do, l, delta), idr, idk, *placed(memory), *after)


def memory_grad_kernel(ka_ref, kb_ref, va_ref, vb_ref, wk_ref, wv_ref, *rest):
    total = mm(jnp.concatenate([ka_ref[...], kb_ref[...]], axis=1), wk_ref[0], NT)
    total += mm(jnp.concatenate([va_ref[...], vb_ref[...]], axis=1), wv_ref[0], NT)
    rest[-1][...] = total.astype(bf16)


def memory_grad(ka, kb, va, vb, weights, index, after, rows=1024):
    keys, width = ka.shape[0], weights.shape[2]
    rowspec = lambda w: pl.BlockSpec((rows, w), lambda i: (i, 0))
    return pl.pallas_call(
        memory_grad_kernel,
        grid=(keys // rows,),
        in_specs=[rowspec(a.shape[1]) for a in (ka, kb, va, vb)] + [part(weights, index, width, 0), part(weights, index + 1, width, 0)] + [apart] * len(after),
        out_specs=rowspec(width),
        out_shape=out_array((keys, width), bf16),
        name="memory_grad",
        **params(4, 16),
    )(ka, kb, va, vb, weights, weights, *after)


def between_kernel(
    core_ref, ga_ref, gb_ref, gn23_ref, r1_ref, dr2_ref, dr3_ref, dqa_ref, dqb_ref, h1b_ref, o1_ref, wso_ref, wcq_ref, norms_ref, *rest
):
    dsum_ref, do1_ref, delta_ref, keep_ref, send_ref, gn_ref, total = rest[-7:]
    step = pl.program_id(0)

    @pl.when(step == 0)
    def _():
        total[...] = jnp.zeros_like(total)
        gn_ref[...] = jnp.zeros_like(gn_ref)

    dq2 = jnp.concatenate([dqa_ref[...], dqb_ref[...]], axis=1)
    dh1 = dr2_ref[...].astype(f32) + mm(dq2, wcq_ref[0], NT)
    n1, rstd1 = norm_rows(r1_ref[...].astype(f32))
    gn_ref[0:1, :] += column_sums(dh1 * n1)
    gn_ref[1:2, :] += column_sums(dh1)
    dr1 = norm_back(dh1, n1, rstd1, norms_ref[0:1, :])
    dsum_ref[...] = (dr1 + dr3_ref[...].astype(f32)).astype(bf16)
    da1 = dr1.astype(bf16)
    o1 = o1_ref[...]
    do1 = mm(da1, wso_ref[0], NT).astype(bf16)
    do1_ref[...] = do1
    delta_ref[...] = head_columns(do1, o1)
    total[0] += mm(h1b_ref[...], dq2, TN)
    total[1] += mm(o1, da1, TN)

    @pl.when(step == pl.num_programs(0) - 1)
    def _():
        gn_ref[2:6, :] = gn23_ref[...]
        r, width = keep_ref.shape[2:]
        norm_part = jnp.concatenate([gn_ref[...], jnp.zeros((r - 8, width), f32)]).astype(bf16)

        def write(device, ref, j):
            here = pl.ds(pl.multiple_of(device * r, r), r)
            for i in range(2):
                ref[j, i, :, : ga_ref.shape[2]] = ga_ref[i, here, :]
                ref[j, i, :, ga_ref.shape[2] :] = gb_ref[i, here, :]
                ref[j, 2 + i] = total[i, here, :].astype(bf16)
            ref[j, 4] = norm_part

        spread(keep_ref, send_ref, core_ref[0], write)


def between(core, pairs, ga, gb, gn23, r1, dr2, dr3, dqa, dqb, h1b, o1, weights, norms, after, rows=512):
    total, width = r1.shape
    rowspec = lambda w: pl.BlockSpec((rows, w), lambda i: (i, 0))
    sds = jax.ShapeDtypeStruct
    side = jax.ShapeDtypeStruct((pairs, 5, width // (2 * pairs), width), bf16)
    return pl.pallas_call(
        between_kernel,
        grid=(total // rows,),
        in_specs=[pl.BlockSpec(memory_space=pltpu.SMEM), whole(ga), whole(gb), whole(gn23)]
        + [rowspec(width)] * 3 + [rowspec(dqa.shape[1]), rowspec(dqb.shape[1])] + [rowspec(width)] * 2
        + [part(weights, 0, width, 0), part(weights, 1, width, 0), whole(norms)] + [apart] * len(after),
        out_specs=[rowspec(width)] * 2
        + [rowspec(LANES), whole(side), whole(side), pl.BlockSpec((8, width), lambda i: (0, 0))],
        out_shape=[sds((total, width), bf16), sds((total, width), bf16), sds((total, LANES), f32), side, side, sds((8, width), f32)],
        scratch_shapes=[pltpu.VMEM((2, width, width), f32)],
        name="between",
        **params(7, 24),
    )(core, ga, gb, gn23, *placed(r1), dr2, dr3, dqa, dqb, *placed(h1b, o1), weights, weights, norms, *after)


def self_backward_kernel(
    tile, block, core_ref, items_ref, q_ref, k_ref, v_ref, do_ref, l_ref, delta_ref, idr_ref, x_ref, wq_ref, wk_ref, wv_ref, sofar_ref, *rest
):
    gx_ref, keep_ref, send_ref, q_all, ids_all, dq, dk, dv, grads = rest[-9:]
    step = pl.program_id(0)
    total, width = q_ref.shape

    @pl.when(step == 0)
    def _():
        dq[...] = jnp.zeros_like(dq)
        dk[...] = jnp.zeros_like(dk)
        dv[...] = jnp.zeros_like(dv)
        grads[...] = jnp.zeros_like(grads)
        q_all[...] = q_ref[...] * jnp.asarray(HD ** -0.5, bf16)
        for j in range(total // block):
            ids_all[j * block : (j + 1) * block, :] = column_of(idr_ref[:, j * block : (j + 1) * block])
        attend_back(
            items_ref, idr_ref, ids_all, q_all, do_ref, k_ref, v_ref, l_ref, delta_ref, dq, dk, dv, tile, block, 0, True, 2
        )

    x = x_ref[...]
    rows = x.shape[0]
    here = pl.ds(pl.multiple_of(step * rows, rows), rows)
    gx = sofar_ref[...].astype(f32)
    parts = (dq[here, :] * HD ** -0.5).astype(bf16), dk[here, :].astype(bf16), dv[here, :].astype(bf16)
    for i, (grad, w_ref) in enumerate(zip(parts, (wq_ref, wk_ref, wv_ref))):
        gx += mm(grad, w_ref[0], NT)
        grads[i] += mm(x, grad, TN)
    gx_ref[...] = gx.astype(bf16)

    @pl.when(step == pl.num_programs(0) - 1)
    def _():
        r = keep_ref.shape[2]

        def write(device, ref, j):
            place = pl.ds(pl.multiple_of(device * r, r), r)
            for i in range(3):
                ref[j, i] = grads[i, place, :].astype(bf16)

        spread(keep_ref, send_ref, core_ref[0], write)


def self_backward(core, pairs, items, q, k, v, do, l, delta, idr, x, weights, sofar, after, turns=2, block=QROWS, tile=256):
    total, width = x.shape
    sds = jax.ShapeDtypeStruct
    side = sds((pairs, 3, width // (2 * pairs), width), bf16)
    rowspec = lambda w: pl.BlockSpec((total // turns, w), lambda i, *_: (i, 0))
    return pl.pallas_call(
        functools.partial(self_backward_kernel, tile, block),
        grid_spec=pltpu.PrefetchScalarGridSpec(
            num_scalar_prefetch=2,
            grid=(turns,),
            in_specs=[whole(a) for a in (q, k, v, do, l, delta, idr)]
            + [rowspec(width)] + [part(weights, i, width, 0) for i in range(3)] + [rowspec(width)] + [apart] * len(after),
            out_specs=[rowspec(width), whole(side), whole(side)],
            scratch_shapes=[
                pltpu.VMEM((total, width), bf16), pltpu.VMEM((total, LANES), jnp.int32),
                pltpu.VMEM((total, width), f32), pltpu.VMEM((total, width), f32), pltpu.VMEM((total, width), f32),
                pltpu.VMEM((3, width, width), f32),
            ],
        ),
        out_shape=[sds((total, width), bf16), side, side],
        name="self_backward",
        **params(17, 34),
    )(core, items, q, k, v, do, l, delta, idr, x, weights, weights, weights, sofar, *after)


def add_split_kernel(count, here_ref, *refs):
    places = refs[0].shape[1]
    for m in range(places):
        at = here_ref[0] ^ m
        total = refs[0][:, at].astype(f32)
        for ref in refs[1:count]:
            total += ref[:, at].astype(f32)
        refs[count + m][...] = total.astype(bf16)


def add_split(here, parts, outer, places):
    tail = parts[0].shape[1:]
    parts = [p.reshape((outer, places) + tail) for p in parts]
    out = pl.pallas_call(
        functools.partial(add_split_kernel, len(parts)),
        grid=(outer,),
        in_specs=[pl.BlockSpec(memory_space=pltpu.SMEM)] + [pl.BlockSpec((1, places) + tail, lambda i: (i, 0, 0, 0, 0))] * len(parts),
        out_specs=[pl.BlockSpec((1,) + tail, lambda i: (i, 0, 0, 0))] * places,
        out_shape=[jax.ShapeDtypeStruct((outer,) + tail, bf16)] * places,
        name="add_split",
        **params(3, 24),
    )(here, *parts)
    return list(out)


def first_pair_kernel(cut, here_ref, keep, came, *outs):
    for m in range(2):
        at = here_ref[0] ^ m
        outs[m][0] = (keep[0, :, at, :cut].astype(f32) + came[0, :, at, :cut].astype(f32)).astype(bf16)
        at = here_ref[1] ^ m
        outs[2 + m][0] = (keep[0, at, :, cut:].astype(f32) + came[0, at, :, cut:].astype(f32)).astype(bf16)


def first_pair(here, keep, came, outer, cut):
    squares, rows, width = keep.shape[1:]
    parts = [p.reshape(outer, 2, 2, squares, rows, width) for p in (keep, came)]
    shapes = [(outer, 2, n, rows, width) for n in (cut, cut, squares - cut, squares - cut)]
    out = pl.pallas_call(
        functools.partial(first_pair_kernel, cut),
        grid=(outer,),
        in_specs=[pl.BlockSpec(memory_space=pltpu.SMEM)] + [pl.BlockSpec((1,) + p.shape[1:], lambda i: (i, 0, 0, 0, 0, 0)) for p in parts],
        out_specs=[pl.BlockSpec((1,) + s[1:], lambda i: (i, 0, 0, 0, 0)) for s in shapes],
        out_shape=[jax.ShapeDtypeStruct(s, bf16) for s in shapes],
        name="first_pair",
        **params(2, 24),
    )(here, *parts)
    return list(out)


def second_pair_kernel(here_ref, keep_a, came_a, keep_b, came_b, *outs):
    for m in range(2):
        at = here_ref[1] ^ m
        outs[m][0] = (keep_a[0, at].astype(f32) + came_a[0, at].astype(f32)).astype(bf16)
        at = here_ref[0] ^ m
        outs[2 + m][0] = (keep_b[0, at].astype(f32) + came_b[0, at].astype(f32)).astype(bf16)


def second_pair(here, parts):
    outer = parts[0].shape[0]
    shapes = [(p.shape[0],) + p.shape[2:] for p in parts]
    out = pl.pallas_call(
        second_pair_kernel,
        grid=(outer,),
        in_specs=[pl.BlockSpec(memory_space=pltpu.SMEM)] + [pl.BlockSpec((1,) + p.shape[1:], lambda i: (i, 0, 0, 0, 0)) for p in parts],
        out_specs=[pl.BlockSpec((1,) + s[1:], lambda i: (i, 0, 0, 0)) for s in shapes],
        out_shape=[jax.ShapeDtypeStruct(s, bf16) for s in shapes],
        name="second_pair",
        **params(1, 24),
    )(here, *parts)
    return list(out)


def join_split_kernel(here_ref, keep_a, came_a, keep_b, came_b, *outs):
    cut = keep_a.shape[2]
    for m, out in enumerate(outs):
        at = here_ref[0] ^ m
        out[:, :cut] = (keep_a[:, at].astype(f32) + came_a[:, at].astype(f32)).astype(bf16)
        out[:, cut:] = (keep_b[:, at].astype(f32) + came_b[:, at].astype(f32)).astype(bf16)


def join_split(here, parts, outer, places):
    parts = [p.reshape((outer, places) + p.shape[1:]) for p in parts]
    tail = (parts[0].shape[2] + parts[2].shape[2],) + parts[0].shape[3:]
    out = pl.pallas_call(
        join_split_kernel,
        grid=(outer,),
        in_specs=[pl.BlockSpec(memory_space=pltpu.SMEM)] + [pl.BlockSpec((1,) + p.shape[1:], lambda i: (i, 0, 0, 0, 0)) for p in parts],
        out_specs=[pl.BlockSpec((1,) + tail, lambda i: (i, 0, 0, 0))] * places,
        out_shape=[jax.ShapeDtypeStruct((outer,) + tail, bf16)] * places,
        name="join_split",
        **params(1, 24),
    )(here, *parts)
    return list(out)


def place_kernel(here_ref, *refs):
    out_ref = refs[-1]
    for m, ref in enumerate(refs[:-1]):
        out_ref[0, :, here_ref[0] ^ m] = ref[0]


def place(here, pieces):
    shape = pieces[0].shape
    pieces = [p.reshape((shape[0], -1) + shape[-2:]) for p in pieces]
    count, tail = len(pieces), pieces[0].shape[2:]
    inner = pieces[0].shape[1]
    out = pl.pallas_call(
        place_kernel,
        grid=(shape[0],),
        in_specs=[pl.BlockSpec(memory_space=pltpu.SMEM)] + [pl.BlockSpec((1, inner) + tail, lambda i: (i, 0, 0, 0))] * count,
        out_specs=pl.BlockSpec((1, inner, count) + tail, lambda i: (i, 0, 0, 0, 0)),
        out_shape=jax.ShapeDtypeStruct((shape[0], inner, count) + tail, bf16),
        name="place",
        **params(1, 16),
    )(here, *pieces)
    return out.reshape(shape[:-2] + (count,) + tail)


def own_block(shape):
    return pl.BlockSpec(shape, lambda *_: (0,) * len(shape))


def pack_kernel(moves, count, *refs):
    ins, out_ref, wide = refs[:count], refs[count], refs[count + 1 :]
    rows = out_ref.shape[1]
    for ref, w in zip(ins, wide):
        w[...] = ref[...].astype(f32)
    for source, begin, step, square, block in moves:
        value = wide[source][pl.ds(begin, rows, stride=step), :]
        out_ref[square, :, block * LANES : (block + 1) * LANES] = value.astype(bf16)


def pack(arrays, moves, squares, rows, width, name):
    arrays = [a.reshape(-1, LANES) for a in arrays]
    return pl.pallas_call(
        functools.partial(pack_kernel, moves, len(arrays)),
        in_specs=[own_block(a.shape) for a in arrays],
        out_specs=own_block((squares, rows, width)),
        out_shape=jax.ShapeDtypeStruct((squares, rows, width), bf16),
        scratch_shapes=[pltpu.VMEM(a.shape, f32) for a in arrays],
        name=name,
        **params(1, 16),
    )(*placed(*arrays))


def square_moves(source, square, width):
    blocks = width // LANES
    return [(source, b, blocks, square, b) for b in range(blocks)]


def finish_kernel(moves, count, *refs):
    ins, outs = refs[:count], refs[count:]
    rows = ins[0].shape[1]
    for square, block, out, begin, step in moves:
        cols = slice(block * LANES, (block + 1) * LANES)
        total = ins[0][square, :, cols].astype(f32)
        for ref in ins[1:]:
            total += ref[square, :, cols].astype(f32)
        if step:
            outs[out][pl.ds(begin, rows, stride=step), :] = total
        else:
            outs[out][:, cols] = total


def finish(parts, moves, shapes, name):
    return pl.pallas_call(
        functools.partial(finish_kernel, moves, len(parts)),
        in_specs=[own_block(p.shape) for p in parts],
        out_specs=[own_block(s) for s in shapes],
        out_shape=[jax.ShapeDtypeStruct(s, f32) for s in shapes],
        name=name,
        **params(1, 16),
    )(*parts)


def fill_items(ref, first, high, keys, block, tile):
    filled = jnp.int32(0)
    for b in range(len(first)):
        count = (high[b] - first[b] * LANES + tile - 1) // tile

        def put(j, at, b=b):
            ref[0, at] = b
            ref[1, at] = first[b] + j * (tile // LANES)
            return at + 1

        filled = lax.fori_loop(0, count, put, filled)
    for j in range(PADDING):
        ref[0, filled + j] = len(first) - 1
        ref[1, filled + j] = keys // LANES
    for i, n in enumerate(EACH):
        ref[2, i] = (filled + n - 1) // n


def plan_kernel(block, tile, seg_ref, mem_ref, qid_ref, mid_ref, own_ref, cross_ref):
    def ends_of(ref):
        ends, total = [], jnp.int32(0)
        for i in range(ref.shape[1]):
            total += ref[0, i]
            ends.append(total)
        return ends

    ends, mem_ends = ends_of(seg_ref), ends_of(mem_ref)
    for ref, marks in ((qid_ref, ends), (mid_ref, mem_ends)):
        places = lax.broadcasted_iota(jnp.int32, ref.shape, 1)
        ids = jnp.zeros(ref.shape, jnp.int32)
        for mark in marks:
            ids += (places >= mark).astype(jnp.int32)
        ref[...] = ids
    total, keys = qid_ref.shape[1], mid_ref.shape[1]
    own, low, high = [], [], []
    for begin in range(0, total, block):
        own_first, first, last = jnp.int32(0), jnp.int32(0), mem_ref[0, 0]
        for i in range(seg_ref.shape[1]):
            passed = (ends[i] <= begin).astype(jnp.int32)
            own_first += passed * seg_ref[0, i]
            first += passed * mem_ref[0, i]
            if i + 1 < seg_ref.shape[1]:
                last += (ends[i] <= begin + block - 1).astype(jnp.int32) * mem_ref[0, i + 1]
        own.append(own_first // LANES)
        low.append(first // LANES)
        high.append(last)
    fill_items(own_ref, own, [begin + block for begin in range(0, total, block)], total, block, tile)
    fill_items(cross_ref, low, high, keys, block, tile)


def plan(seg, mem, total, keys, block=QROWS, tile=256):
    smem = pl.BlockSpec(memory_space=pltpu.SMEM)
    sds = jax.ShapeDtypeStruct
    more = PADDING
    return pl.pallas_call(
        functools.partial(plan_kernel, block, tile),
        in_specs=[smem, smem],
        out_specs=[own_block((1, total)), own_block((1, keys)), smem, smem],
        out_shape=[
            sds((1, total), jnp.int32), sds((1, keys), jnp.int32),
            sds((3, total // block * (total // tile) + more), jnp.int32), sds((3, total // block * (keys // tile) + more), jnp.int32),
        ],
        name="plan",
        **params(1, 16),
    )(seg, mem)

HEAD_START = 1


def mesh_size():
    return lax.axis_size("dp") * lax.axis_size("fsdp")


def position():
    return lax.axis_index("dp") * lax.axis_size("fsdp") + lax.axis_index("fsdp")


def bit_groups(wide):
    count = mesh_size().bit_length() - 1
    groups = [(0, 1)]
    while groups[-1][0] + groups[-1][1] < count:
        low = groups[-1][0] + groups[-1][1]
        groups.append((low, min(2 if len(groups) <= wide else 1, count - low)))
    return groups


def swap(x, mask):
    return lax.ppermute(x, ("dp", "fsdp"), [(i, i ^ mask) for i in range(mesh_size())])


def place_in(group):
    return (position() >> group[0]) & ((1 << group[1]) - 1)


def tie(x, *after):
    return lax.optimization_barrier((x, *after))[0] if after else x


def gather_step(x, group, after=(), lower=0, came=None):
    low, width = group
    here = place_in(group)
    if came is None:
        came = tie([swap(x, m << low) for m in range(1, 1 << width)], *after)
    blocks = [x] + came
    for j in range(width):
        flip = (here >> j) & 1 == 1
        blocks = [jnp.where(flip, blocks[p ^ (1 << j)], blocks[p]) for p in range(1 << width)]
    return jnp.stack(blocks, axis=x.ndim - 2 - lower)


def gathered(x):
    return x.reshape(x.shape[:1] + (-1, x.shape[-1]))


def swap_pieces(parts, group, after=()):
    return [parts[0]] + tie([swap(parts[m], m << group[0]) for m in range(1, len(parts))], *after)


def next_pieces(parts, groups, done):
    group = groups[done]
    outer = 1 << sum(g[1] for g in groups[done + 1 :])
    return add_split(place_in(group).reshape(1).astype(jnp.int32), parts, outer, 1 << group[1])


def norm_parts(norm_params, size):
    parts, left = [], norm_params
    for _ in range(3):
        part = left.astype(bf16)
        parts.append(jnp.pad(part, (0, LANES - part.size)))
        left = left - part.astype(f32)
    flat = jnp.concatenate(parts)
    return jnp.pad(flat, (0, size - flat.size))


def resplit(keep, send, devices, core, squares):
    halves = jnp.concatenate([keep, send])
    width = halves.shape[-1]
    first = halves[:, :squares].transpose(1, 0, 2, 3).reshape(squares, devices, -1, width).transpose(1, 0, 2, 3)
    rows = first.shape[2]
    if halves.shape[1] > squares:
        rest = halves[:, squares:].reshape(devices, halves.shape[1] - squares, rows, width)
        first = jnp.concatenate([first, rest], axis=1)
    both = first.reshape(devices // 2, 2, -1, rows, width)
    return [lax.dynamic_index_in_dim(both, core ^ m, 1, keepdims=False) for m in range(2)]


def body(
    inputs, memory, seg_lengths, mem_lengths, self_query, self_key, self_value, self_out,
    cross_query, cross_key, cross_value, cross_out, ffn_in, ffn_out, norm_params, cotangent,
):
    total, width = inputs.shape
    keys = memory.shape[0]
    devices = mesh_size()
    groups, single = bit_groups(8), bit_groups(1)
    down = groups[::-1]
    shard = norm_params.shape[0]
    size = self_query.shape[0]
    own_rows = size // width
    blocks = ffn_in.shape[0] // size
    whole_tiles = own_rows % 16 == 0
    core = place_in(groups[0]).reshape(1).astype(jnp.int32)

    firsts = (self_query, self_key, self_value)
    seconds = (self_out, cross_query, cross_key, cross_value, norm_parts(norm_params, size))
    if whole_tiles:
        lane_blocks = width // LANES
        three = [m for i in range(3) for m in square_moves(i, i, width)]
        five = three + [m for i in range(3, 5) for m in square_moves(i, i, width)]
        wide = [(0, c * lane_blocks + b, blocks * lane_blocks, c, b) for c in range(blocks) for b in range(lane_blocks)]
        tall = [(1, j * own_rows * lane_blocks + b, lane_blocks, blocks + 1 + j, b) for j in range(blocks) for b in range(lane_blocks)]
        first = pack(firsts, three, 3, own_rows, width, "pack_self")
        second = pack(tie(seconds, first), five, 5, own_rows, width, "pack_cross")
        last = square_moves(2, blocks, width)
        third = pack(tie((ffn_in, ffn_out, cross_out), first), wide + tall + last, 2 * blocks + 1, own_rows, width, "pack_ffn")
    else:
        first = jnp.concatenate(firsts).reshape(3, own_rows, width)
        second = jnp.concatenate(seconds).reshape(5, own_rows, width)
        fi = ffn_in.reshape(own_rows, blocks, width).transpose(1, 0, 2)
        third = jnp.concatenate([fi, cross_out.reshape(1, own_rows, width), ffn_out.reshape(blocks, own_rows, width)])
    third = third.reshape(-1, width)
    plane = groups[1]
    high_bits = [(b, 1) for b in reversed(range(plane[0] + plane[1], devices.bit_length() - 1))]
    for g in down[:-2]:
        first = gather_step(first, g)
    second = gather_step(second, high_bits[0])
    qid, mid, own_items, items = plan(*tie((seg_lengths, mem_lengths), first), total, keys)
    first = gather_step(first, plane, [second, own_items])
    for g in high_bits[1:]:
        second = gather_step(second, g)
    third = gather_step(third, high_bits[0])
    first = gathered(gather_step(first, down[-1], [second, third]))
    for g in high_bits[1:]:
        third = gather_step(third, g)
    low, high = (plane[0], 1), (plane[0] + 1, 1)
    cut = (blocks + 1) * own_rows
    part_a, part_b = tie((third[..., :cut, :], third[..., cut:, :]), first)
    early = [second, part_a, part_b]
    pairs = devices // 2 if whole_tiles else 1
    part_of = core if whole_tiles else jnp.zeros_like(core)

    q1, k1, v1, o1, l1 = self_forward(own_items, inputs, first, qid, early)
    def at(group):
        return place_in(group).reshape(1).astype(jnp.int32)

    second = gather_step(second, plane, [l1])
    came_a, came_b = tie((swap(part_a, 1 << low[0]), swap(part_b, 1 << high[0])), l1)
    second = tie(second, came_a, came_b)
    part_a, part_b = place(at(low), [part_a, came_a]), place(at(high), [part_b, came_b])
    second = gathered(gather_step(second, down[-1]))
    norm_all = second[4].reshape(devices, -1)[:, : 3 * LANES].reshape(devices, 3, LANES)[:, :, :shard].astype(f32)
    norms = jnp.sum(norm_all, axis=1).reshape(6, width)
    k2, v2, r1, h1b, q2, h1, o2, l2 = cross_forward(items, memory, inputs, o1, second, norms, qid, mid, [])
    part_a, part_b = [part_a, swap(part_a, 1 << high[0])], [part_b, swap(part_b, 1 << low[0])]
    came = [swap(part_a[0], 1), swap(part_b[0], 1)]
    part_a[1], part_b[1], came[0], came[1] = tie((part_a[1], part_b[1], came[0], came[1]), l2)
    part_a += [came[0], swap(part_a[1], 1)]
    part_b += [came[1], swap(part_b[1], 1)]
    bits = jnp.stack([(position() >> b) & 1 for b in (low[0], high[0], 0)]).astype(jnp.int32)
    if whole_tiles:
        pieces = [p.reshape((-1, 2) + p.shape[-2:]) for p in part_a + part_b]
    else:
        pieces = []
        for parts, group, lower in ((part_a, high, 1), (part_b, low, 0)):
            halves = [gather_step(parts[j], group, lower=lower, came=[parts[j + 1]]) for j in (0, 2)]
            both = gather_step(halves[0], down[-1], came=[halves[1]]).reshape(devices, -1, own_rows, width)
            pieces.append(both)
        pieces[0] = jnp.concatenate([pieces[0][:, i].reshape(width, width) for i in range(blocks + 1)])[None]
        pieces[1] = pieces[1].reshape(1, -1, width)
    out, dr3, dr2, do2, delta2, keep, send, gn23 = ffn(part_of, bits, pairs, h1, inputs, cotangent, o2, pieces, norms)

    one = [keep, send] if whole_tiles else resplit(keep, send, devices, core[0], blocks + 1)
    dq2a, dk2a, dv2a, gckva = cross_backward(items, q2, k2, v2, do2, l2, delta2, qid, mid, memory, 0, HEAD_START, 6, [])
    low, high = 1 << groups[1][0], 2 << groups[1][0]
    both = jnp.stack([(position() >> (groups[1][0] + j)) & 1 for j in range(2)]).astype(jnp.int32)
    one = swap_pieces(one, groups[0], [dq2a])
    one = first_pair(both, one[0], one[1], devices // 8, blocks + 1)
    more = width // LANES - HEAD_START
    dq2b, dk2b, dv2b, gckvb = cross_backward(
        items, q2, k2, v2, do2, l2, delta2, qid, mid, memory, HEAD_START, more, 2, [one[1], one[3]]
    )
    came = tie([swap(one[1], low), swap(one[3], high)], dq2b)
    one = second_pair(both, [one[0], came[0], one[2], came[1]])
    gm = memory_grad(dk2a, dk2b, dv2a, dv2b, second, 2, [one[1], one[3]])
    dsum, do1, delta1, keep, send, gn = between(
        part_of, pairs, gckva, gckvb, gn23, r1, dr2, dr3, dq2a, dq2b, h1b, o1, second, norms, placed(gm)
    )
    came = tie([swap(one[1], high), swap(one[3], low)], do1)
    one = join_split(
        place_in(single[2]).reshape(1).astype(jnp.int32), [one[0], came[0], one[2], came[1]],
        1 << sum(g[1] for g in single[3:]), 1 << single[2][1],
    )
    two = [keep, send]
    if not whole_tiles:
        two = resplit(keep, send, devices, core[0], 5)
        own_norms = jnp.pad(gn[:6].astype(bf16).reshape(devices, -1), ((0, 0), (0, size - shard)))
        own_norms = own_norms.reshape(devices // 2, 2, own_rows, width)
        two = [two[m].at[:, 4].set(lax.dynamic_index_in_dim(own_norms, core[0] ^ m, 1, keepdims=False)) for m in range(2)]
    two = next_pieces(swap_pieces(tie(two, one[1]), groups[0]), groups, 1)
    gx, keep, send = self_backward(part_of, pairs, own_items, q1, k1, v1, do1, l1, delta1, qid, inputs, first, dsum, one[1:] + two[1:])
    two = next_pieces(swap_pieces(two, groups[1], [gx]), single, 2)
    one = next_pieces(swap_pieces(one, single[2], [gx]), single, 3)
    keep, send = tie((keep, send), two[1], one[1])
    three = [keep, send] if whole_tiles else resplit(keep, send, devices, core[0], 3)
    three = next_pieces(swap_pieces(three, groups[0]), groups, 1)
    for i in range(2, len(groups)):
        three = next_pieces(swap_pieces(three, groups[i - 1]), groups, i)
    for i in range(3, len(single)):
        two = next_pieces(swap_pieces(two, single[i - 1]), single, i)
        if i > 3:
            one = next_pieces(swap_pieces(one, single[i - 1]), single, i)

    def flat(g):
        return g.reshape(-1)

    chains = [swap_pieces(one, single[-1], [three[1]]), swap_pieces(two, single[-1], [three[1]]), swap_pieces(three, groups[-1])]
    chains = [[p.reshape(-1, own_rows, width) for p in chain] for chain in chains]
    if whole_tiles:
        lane_rows = size // LANES
        square, long = (lane_rows, LANES), (blocks * lane_rows, LANES)

        moves = [(c, b, 0, c * lane_blocks + b, blocks * lane_blocks) for c in range(blocks) for b in range(lane_blocks)]
        moves += [(blocks, b, 1, b, lane_blocks) for b in range(lane_blocks)]
        moves += [
            (blocks + 1 + j, b, 2, j * own_rows * lane_blocks + b, lane_blocks) for j in range(blocks) for b in range(lane_blocks)
        ]
        gfi, gco, gfo = finish(chains[0], moves, [long, square, long], "finish_ffn")
        moves = [(i, b, i, b, lane_blocks) for i in range(4) for b in range(lane_blocks)] + [(4, b, 4, 0, 0) for b in range(lane_blocks)]
        gck, gcv, gcq, gso, gn = finish(chains[1], moves, [square] * 4 + [(own_rows, width)], "finish_cross")
        gn = lax.dynamic_slice_in_dim(flat(gn[:6]), position() * shard, shard)
        moves = [(i, b, i, b, lane_blocks) for i in range(3) for b in range(lane_blocks)]
        gsq, gsk, gsv = finish(chains[2], moves, [square] * 3, "finish_self")
    else:
        one, two, three = (sum(p.astype(f32) for p in chain) for chain in chains)
        gfi, gco, gfo = one[:blocks].transpose(1, 0, 2), one[blocks], one[blocks + 1 :]
        gck, gcv, gcq, gso, gn = two[0], two[1], two[2], two[3], flat(two[4])[:shard]
        gsq, gsk, gsv = three[0], three[1], three[2]
    return (out, gx, gm) + tuple(flat(g) for g in (gsq, gsk, gsv, gso, gcq, gck, gcv, gco, gfi, gfo, gn))


def solution(mesh):
    rows, flat = P(("dp", "fsdp"), None), P(("dp", "fsdp"))
    return jax.shard_map(
        body,
        mesh=mesh,
        in_specs=(rows,) * 4 + (flat,) * 11 + (rows,),
        out_specs=(rows,) * 3 + (flat,) * 11,
        check_vma=False,
    )
```

```python
import functools
import jax
import jax.numpy as jnp
from jax import lax
from jax.experimental import pallas as pl
from jax.experimental.pallas import tpu as pltpu
from jax.sharding import PartitionSpec as P

HD = 64
LANES = 128
MOST = 256
QROWS = 128
EACH = (2, 4)
PADDING = 4
FFN_CHUNK = 256
masked_score = -1e30
norm_eps = 1e-05
bf16, f32 = jnp.bfloat16, jnp.float32
NT = (((1,), (1,)), ((), ()))
TN = (((0,), (0,)), ((), ()))
NN = (((1,), (0,)), ((), ()))


def mm(left, right, dims=NN):
    return lax.dot_general(left, right, dims, preferred_element_type=f32)


def norm_rows(source):
    mean = jnp.mean(source, axis=-1, keepdims=True)
    centered = source - mean
    variance = jnp.mean(centered * centered, axis=-1, keepdims=True)
    rstd = lax.rsqrt(variance + norm_eps)
    return centered * rstd, rstd


def lane_below(rows):
    return lax.broadcasted_iota(jnp.int32, (rows, LANES), 1) < HD


def column_of(row):
    return jnp.broadcast_to(row, (LANES, row.shape[1])).T


def head_part(pair, which, low):
    return jnp.where(low == (which == 0), pair, jnp.zeros_like(pair))


def values_with_ones(values):
    parts = []
    for p in range(values.shape[1] // LANES):
        pair = values[:, p * LANES : (p + 1) * LANES]
        parts += [pair, jnp.ones_like(pair)]
    return jnp.concatenate(parts, axis=1)


def finish_heads(at, top, tot, acc, write):
    shape = acc.shape[0], at.size if hasattr(at, "size") else at.stop - at.start, LANES
    lane = lax.broadcasted_iota(jnp.int32, shape[1:], 1)
    sums, tops = jnp.ones(shape[1:], f32), jnp.zeros(shape[1:], f32)
    for p in range(shape[0]):
        total = tot[p, at, :]
        write(p, (acc[p, at, :] / total).astype(bf16))
        sums = jnp.where(lane % HD == p, total, sums)
        tops = jnp.where(lane == p, top[2 * p, at, :], jnp.where(lane == HD + p, top[2 * p + 1, at, :], tops))
    return tops + jnp.log(sums)


def column_at(head):
    return head % 2 * HD + head // 2


def item_at(items_ref, n, idk_ref, ids_q, keys, tile, block, causal):
    begin = pl.multiple_of(items_ref[0, n] * block, block)
    wanted = items_ref[1, n] * LANES
    start = pl.multiple_of(jnp.minimum(wanted, keys - tile), LANES)
    at = pl.ds(begin, block)
    pos = start + lax.broadcasted_iota(jnp.int32, (1, tile), 1)
    ids_k = jnp.where(pos >= wanted, idk_ref[:, pl.ds(start, tile)], -1)
    allowed = ids_q[at, :1] == ids_k
    if causal:
        allowed &= pos <= begin + lax.broadcasted_iota(jnp.int32, (block, 1), 0)
    return at, pl.ds(start, tile), jnp.where(allowed, 0.0, masked_score).astype(f32)


def attend(items_ref, idk_ref, ids_q, q_all, k_all, vx_all, top, tot, acc, tile, block, causal):
    keys, width = k_all.shape
    pairs = width // LANES
    heads = 2 * pairs
    low = lane_below(block)
    top[...] = jnp.full(top.shape, masked_score, f32)
    tot[...] = jnp.zeros(tot.shape, f32)
    acc[...] = jnp.zeros(acc.shape, f32)

    def some(i, _):
        loads, made = [], []
        for t in range(EACH[0]):
            at, there, bias = item_at(items_ref, EACH[0] * i + t, idk_ref, ids_q, keys, tile, block, causal)
            loads.append((at, there, bias))
            for p in range(pairs):
                cols = slice(p * LANES, (p + 1) * LANES)
                part = q_all[at, cols]
                both = jnp.concatenate([head_part(part, h, low) for h in range(2)])
                made.append(mm(both, k_all[there, cols], NT))
        weights, scales = [], []
        for t, (at, there, bias) in enumerate(loads):
            for head in range(heads):
                s = made[t * pairs + head // 2][head % 2 * block : (head % 2 + 1) * block] + bias
                old = top[head, at, :]
                new = jnp.maximum(old, jnp.max(s, axis=1, keepdims=True))
                top[head, at, :] = new
                scales.append(jnp.exp(old - new))
                weights.append(jnp.exp(s - jnp.concatenate([new] * (tile // LANES), axis=1)).astype(bf16))
        mixed = [
            mm(jnp.concatenate(weights[t * heads + 2 * p : t * heads + 2 * p + 2]), vx_all[there, 2 * p * LANES : 2 * (p + 1) * LANES])
            for t, (_, there, _) in enumerate(loads) for p in range(pairs)
        ]
        for t, (at, _, _) in enumerate(loads):
            for p in range(pairs):
                n = t * pairs + p
                scale = jnp.where(low, scales[2 * n], scales[2 * n + 1])
                o = mixed[n]
                acc[p, at, :] = acc[p, at, :] * scale + jnp.where(low, o[:block, :LANES], o[block:, :LANES])
                tot[p, at, :] = tot[p, at, :] * scale + jnp.where(low, o[:block, LANES:], o[block:, LANES:])
        return 0

    lax.fori_loop(0, items_ref[2, 0], some, 0)


def attend_back(items_ref, idk_ref, ids_q, q_all, do_ref, k_ref, v_ref, l_ref, delta_ref, dq, dk, dv, tile, block, first_head, causal, each):
    keys, width = k_ref.shape
    pairs = width // LANES
    low = lane_below(block)

    def some(i, _):
        loads, scores, grads = [], [], []
        for t in range(each):
            at, there, bias = item_at(items_ref, each * i + t, idk_ref, ids_q, keys, tile, block, causal)
            loads.append((at, there, bias))
            for p in range(pairs):
                cols = slice(p * LANES, (p + 1) * LANES)
                q, do = q_all[at, cols], do_ref[at, cols]
                qs = jnp.concatenate([head_part(q, h, low) for h in range(2)])
                dos = jnp.concatenate([head_part(do, h, low) for h in range(2)])
                scores.append((mm(qs, k_ref[there, cols], NT), qs))
                grads.append((mm(dos, v_ref[there, cols], NT), dos))
        weights, slopes = [], []
        for t, (at, there, bias) in enumerate(loads):
            logs, deltas = l_ref[at, :], delta_ref[at, :]
            for p in range(pairs):
                es, ds = [], []
                for h in range(2):
                    lane = column_at(first_head + 2 * p + h)
                    rows = slice(h * block, (h + 1) * block)
                    e = jnp.exp(scores[t * pairs + p][0][rows] + bias - logs[:, lane : lane + 1])
                    es.append(e.astype(bf16))
                    ds.append((e * (grads[t * pairs + p][0][rows] - deltas[:, lane : lane + 1])).astype(bf16))
                weights.append(jnp.concatenate(es))
                slopes.append(jnp.concatenate(ds))
        for t, (at, there, _) in enumerate(loads):
            for p in range(pairs):
                cols = slice(p * LANES, (p + 1) * LANES)
                n = t * pairs + p
                gq = mm(slopes[n], k_ref[there, cols])
                gk = mm(slopes[n], scores[n][1], TN)
                gv = mm(weights[n], grads[n][1], TN)
                dq[at, cols] += jnp.where(low, gq[:block], gq[block:])
                dk[there, cols] += gk
                dv[there, cols] += gv
        return 0

    lax.fori_loop(0, items_ref[2, EACH.index(each)], some, 0)


def self_forward_kernel(tile, block, items_ref, x_ref, wq_ref, wk_ref, wv_ref, idr_ref, *rest):
    q_ref, k_ref, v_ref, o_ref, l_ref, q_all, k_all, vx_all, ids_all, top, tot, acc = rest[-12:]
    step = pl.program_id(0)
    rows = x_ref.shape[0]
    total, width = k_all.shape
    turns = total // rows

    @pl.when(step < turns)
    def _():
        x = x_ref[...]
        q = mm(x, wq_ref[0]).astype(bf16)
        k = mm(x, wk_ref[0]).astype(bf16)
        v = mm(x, wv_ref[0]).astype(bf16)
        q_ref[...] = q
        k_ref[...] = k
        v_ref[...] = v
        here = pl.ds(pl.multiple_of(step * rows, rows), rows)
        q_all[here, :] = q * jnp.asarray(HD ** -0.5, bf16)
        k_all[here, :] = k
        vx_all[here, :] = values_with_ones(v)
        ids_all[here, :] = column_of(idr_ref[:, here])

    @pl.when(step == turns)
    def _():
        attend(items_ref, idr_ref, ids_all, q_all, k_all, vx_all, top, tot, acc, tile, block, True)
        size = 2 * block
        for j in range(total // size):
            at = slice(j * size, (j + 1) * size)

            def write(p, value):
                o_ref[at, p * LANES : (p + 1) * LANES] = value

            l_ref[at, :] = finish_heads(at, top, tot, acc, write)


def whole(a):
    return pl.BlockSpec(a.shape, lambda *_: (0,) * a.ndim)


def once(a):
    return pl.BlockSpec(a.shape, lambda *_: (0,) * a.ndim, pipeline_mode=pl.Buffered(1))


def part(weights, index, columns, half):
    return pl.BlockSpec((1, weights.shape[1], columns), lambda *_: (index, 0, half))


def params(us, vmem):
    return dict(
        compiler_params=pltpu.CompilerParams(vmem_limit_bytes=vmem * 2**20),
        cost_estimate=pl.CostEstimate(flops=us * 10**9, bytes_accessed=2**20, transcendentals=0),
    )


apart = pl.BlockSpec(memory_space=pl.ANY)


def out_array(shape, dtype):
    return pltpu.HBM(shape, dtype)


def placed(*arrays):
    return [pltpu.with_memory_space_constraint(a, pltpu.HBM) for a in arrays]


def self_forward(items, x, weights, idr, after, turns=2, block=QROWS, tile=256):
    total, width = x.shape
    heads = width // HD
    rows = total // turns
    early = lambda w: pl.BlockSpec((rows, w), lambda i, *_: (jnp.minimum(i, turns - 1), 0))
    fixed = lambda w: pl.BlockSpec((total, w), lambda i, *_: (0, 0))
    sds = out_array
    full = sds((total, width), bf16)
    return pl.pallas_call(
        functools.partial(self_forward_kernel, tile, block),
        grid_spec=pltpu.PrefetchScalarGridSpec(
            num_scalar_prefetch=1,
            grid=(turns + 1,),
            in_specs=[early(width)] + [part(weights, i, width, 0) for i in range(3)] + [whole(idr)] + [apart] * len(after),
            out_specs=[early(width)] * 3 + [fixed(width), fixed(LANES)],
            scratch_shapes=[
                pltpu.VMEM((total, width), bf16), pltpu.VMEM((total, width), bf16), pltpu.VMEM((total, 2 * width), bf16),
                pltpu.VMEM((total, LANES), jnp.int32),
                pltpu.VMEM((heads, total, LANES), f32), pltpu.VMEM((heads // 2, total, LANES), f32), pltpu.VMEM((heads // 2, total, LANES), f32),
            ],
        ),
        out_shape=[full] * 4 + [sds((total, LANES), f32)],
        name="self_forward",
        **params(13, 32),
    )(items, *placed(x), weights, weights, weights, idr, *after)


def cross_forward_kernel(
    tile, block, items_ref, memory_ref, wk_ref, wv_ref, x_ref, o1_ref, wso_ref, wcq_ref, norms_ref, idr_ref, idk_ref, *rest
):
    k2_ref, v2_ref, r1_ref, h1b_ref, q2_ref, h1_ref, o_ref, l_ref, k_all, vx_all, q_all, ids_all, top, tot, acc = rest[-15:]
    step = pl.program_id(0)
    rows, width = x_ref.shape
    keys = k_all.shape[0]
    turns = pl.num_programs(0) - 1

    @pl.when(step < turns)
    def _():
        per = memory_ref.shape[0]
        memory = memory_ref[...]
        r1 = x_ref[...].astype(f32) + mm(o1_ref[...], wso_ref[0])
        k2 = mm(memory, wk_ref[0]).astype(bf16)
        r1_ref[...] = r1.astype(bf16)
        n1, _ = norm_rows(r1)
        v2 = mm(memory, wv_ref[0]).astype(bf16)
        h1 = n1 * norms_ref[0:1, :] + norms_ref[1:2, :]
        h1b = h1.astype(bf16)
        h1b_ref[...] = h1b
        q2 = mm(h1b, wcq_ref[0]).astype(bf16)
        q2_ref[...] = q2
        k2_ref[...] = k2
        v2_ref[...] = v2
        here = pl.ds(pl.multiple_of(step * rows, rows), rows)
        q_all[here, :] = q2 * jnp.asarray(HD ** -0.5, bf16)
        h1_ref[...] = h1
        ids_all[here, :] = column_of(idr_ref[:, here])
        there = pl.ds(pl.multiple_of(step * per, per), per)
        k_all[there, :] = k2
        vx_all[there, :] = values_with_ones(v2)

    @pl.when(step == turns)
    def _():
        attend(items_ref, idk_ref, ids_all, q_all, k_all, vx_all, top, tot, acc, tile, block, False)

        size = 2 * block
        for j in range(q_all.shape[0] // size):
            at = slice(j * size, (j + 1) * size)

            def write(p, value):
                o_ref[at, p * LANES : (p + 1) * LANES] = value

            l_ref[at, :] = finish_heads(at, top, tot, acc, write)


def cross_forward(items, memory, x, o1, weights, norms, idr, idk, after, turns=2, block=QROWS, tile=256):
    total, width = x.shape
    keys = memory.shape[0]
    heads = width // HD
    rows, per = total // turns, keys // turns
    early = lambda r, w: pl.BlockSpec((r, w), lambda i, *_: (jnp.minimum(i, turns - 1), 0))
    fixed = lambda w: pl.BlockSpec((total, w), lambda i, *_: (0, 0))
    sds = out_array
    return pl.pallas_call(
        functools.partial(cross_forward_kernel, tile, block),
        grid_spec=pltpu.PrefetchScalarGridSpec(
            num_scalar_prefetch=1,
            grid=(turns + 1,),
            in_specs=[early(per, width), part(weights, 2, width, 0), part(weights, 3, width, 0)]
            + [early(rows, width), early(rows, width), part(weights, 0, width, 0), part(weights, 1, width, 0)]
            + [whole(norms), whole(idr), whole(idk)] + [apart] * len(after),
            out_specs=[early(per, width)] * 2 + [early(rows, width)] * 4 + [fixed(width), fixed(LANES)],
            scratch_shapes=[
                pltpu.VMEM((keys, width), bf16),
                pltpu.VMEM((keys, 2 * width), bf16),
                pltpu.VMEM((total, width), bf16),
                pltpu.VMEM((total, LANES), jnp.int32),
                pltpu.VMEM((heads, total, LANES), f32),
                pltpu.VMEM((heads // 2, total, LANES), f32),
                pltpu.VMEM((heads // 2, total, LANES), f32),
            ],
        ),
        out_shape=[
            sds((keys, width), bf16), sds((keys, width), bf16), sds((total, width), bf16), sds((total, width), bf16),
            sds((total, width), bf16), sds((total, width), f32), sds((total, width), bf16), sds((total, LANES), f32),
        ],
        name="cross_forward",
        **params(19, 44),
    )(items, *placed(memory), weights, weights, *placed(x, o1), weights, weights, norms, idr, idk, *after)


def norm_back(incoming, normal, rstd, gain):
    m = incoming * gain
    return rstd * (
        m - jnp.mean(m, axis=-1, keepdims=True) - normal * jnp.mean(m * normal, axis=-1, keepdims=True)
    )


def head_columns(left, right):
    width = left.shape[1]
    prod = left.astype(f32) * right.astype(f32)
    lane = lax.broadcasted_iota(jnp.int32, (width, LANES), 1)
    own = lax.broadcasted_iota(jnp.int32, (width, LANES), 0) // HD == 2 * (lane % HD) + lane // HD
    own = own.astype(bf16)
    high = prod.astype(bf16)
    low = (prod - high.astype(f32)).astype(bf16)
    return mm(high, own) + mm(low, own)


def column_sums(a):
    return jnp.sum(a, axis=0, keepdims=True)


def spread(keep_ref, send_ref, core, write):
    def one(j, _):
        write(2 * j + core, keep_ref, j)
        write(2 * j + 1 - core, send_ref, j)
        return 0

    lax.fori_loop(0, keep_ref.shape[0], one, 0)


def ffn_kernel(
    core_ref, here_ref, h1_ref, x_ref, cot_ref, o2_ref, norms_ref, *rest
):
    count = len(rest) - 11
    pieces = 8 if count >= 8 else 2
    weights, rest = rest[:pieces], rest[pieces:]
    out_ref, dr3_ref, dr2_ref, do2_ref, delta_ref, keep_ref, send_ref, gn_ref, gin, gout, gco = rest[:11]
    wa_ref, wb_ref = rest[11:] if pieces == 8 else weights
    step = pl.program_id(0)
    last = pl.num_programs(0) - 1
    width = x_ref.shape[1]
    share = width // wb_ref.shape[0]
    blocks = wb_ref.shape[1] // share

    @pl.when(step == 0)
    def _():
        if pieces == 8:
            bits = here_ref[0], here_ref[1]
            for n, (ref, axis) in enumerate(((wa_ref, 1), (wb_ref, 0))):
                for m in range(4):
                    across, core = bits[axis] ^ (m % 2), here_ref[2] ^ (m // 2)
                    piece = weights[4 * n + m]
                    for z in range(piece.shape[0]):
                        for other in range(2):
                            planes = (across, other) if axis else (other, across)
                            ref[z * 8 + planes[0] * 4 + planes[1] * 2 + core] = piece[z, other]
        gin[...] = jnp.zeros_like(gin)
        gout[...] = jnp.zeros_like(gout)
        gco[...] = jnp.zeros_like(gco)
        gn_ref[...] = jnp.zeros_like(gn_ref)

    win = [wa_ref[:, c * share : (c + 1) * share].reshape(width, width) for c in range(blocks)]
    wout = wb_ref[...].reshape(blocks * width, width)
    wco = wa_ref[:, blocks * share :].reshape(width, width)
    n2, rstd2 = norm_rows(h1_ref[...] + mm(o2_ref[...], wco))
    h2 = n2 * norms_ref[2:3, :] + norms_ref[3:4, :]
    h2b = h2.astype(bf16)
    chunk = min(FFN_CHUNK, width)
    parts = blocks * width // chunk
    per = width // chunk

    def win_part(c):
        return win[c // per][:, (c % per) * chunk : (c % per + 1) * chunk]

    acts, slopes, hidden = [], [], [mm(h2b, win_part(0))]
    ff = jnp.zeros(h2.shape, f32)
    for c in range(parts):
        if c + 1 < parts:
            hidden.append(mm(h2b, win_part(c + 1)))
        u = hidden[c]
        square = u * u
        t = jnp.tanh(u * (0.7978845608028654 + (0.7978845608028654 * 0.044715) * square))
        half = 0.5 + 0.5 * t
        acts.append((u * half).astype(bf16))
        rise = u * (0.5 * 0.7978845608028654 + (0.5 * 0.7978845608028654 * 3 * 0.044715) * square)
        slopes.append(half + (1.0 - t * t) * rise)
        if c:
            ff += mm(acts[c - 1], wout[(c - 1) * chunk : c * chunk, :])
    ff += mm(acts[-1], wout[(parts - 1) * chunk :, :])
    r3 = h2 + ff + x_ref[...].astype(f32)
    n3, rstd3 = norm_rows(r3)
    gain3 = norms_ref[4:5, :]
    out_ref[...] = (n3 * gain3 + norms_ref[5:6, :]).astype(bf16)
    e = cot_ref[...].astype(f32)
    gn_ref[2:3, :] += column_sums(e * n3)
    gn_ref[3:4, :] += column_sums(e)
    dr3 = norm_back(e, n3, rstd3, gain3)
    dr3_ref[...] = dr3.astype(bf16)
    dfb = dr3.astype(bf16)
    dh2 = dr3
    raw, made = [mm(dfb, wout[:chunk, :], NT)], []
    for c in range(parts + 1):
        if c + 1 < parts:
            raw.append(mm(dfb, wout[(c + 1) * chunk : (c + 2) * chunk, :], NT))
        if c < parts:
            gout[c * chunk : (c + 1) * chunk, :] += mm(acts[c], dfb, TN)
            made.append((raw[c] * slopes[c]).astype(bf16))
        if c:
            gin[:, (c - 1) * chunk : c * chunk] += mm(h2b, made[c - 1], TN)
            dh2 += mm(made[c - 1], win_part(c - 1), NT)
    gn_ref[0:1, :] += column_sums(dh2 * n2)
    gn_ref[1:2, :] += column_sums(dh2)
    dr2 = norm_back(dh2, n2, rstd2, norms_ref[2:3, :])
    da2 = dr2.astype(bf16)
    dr2_ref[...] = da2
    o2 = o2_ref[...]
    gco[...] += mm(o2, da2, TN)
    do2 = mm(da2, wco, NT).astype(bf16)
    do2_ref[...] = do2
    delta_ref[...] = head_columns(do2, o2)

    @pl.when(step == last)
    def _():
        r = keep_ref.shape[2]

        def write(device, ref, j):
            here = pl.ds(pl.multiple_of(device * r, r), r)
            for c in range(blocks):
                ref[j, c] = gin[here, c * width : (c + 1) * width].astype(bf16)
            ref[j, blocks] = gco[here, :].astype(bf16)
            there = pl.ds(pl.multiple_of(device * blocks * r, blocks * r), blocks * r)
            ref[j, blocks + 1 :] = gout[there, :].astype(bf16).reshape(blocks, r, width)

        spread(keep_ref, send_ref, core_ref[0], write)


def ffn(core, here, pairs, h1, x, cot, o2, weights, norms, rows=256):
    total, width = x.shape
    devices = 1 if len(weights) == 2 else 2 * pairs
    blocks = weights[-1].size // width**2 if devices == 1 else 8 * weights[-1].size // (2 * width**2)
    held = [(devices, (blocks + 1) * width // devices, width), (devices, blocks * width // devices, width)]
    rowspec = lambda w: pl.BlockSpec((rows, w), lambda i: (i, 0))
    smem = pl.BlockSpec(memory_space=pltpu.SMEM)
    sds = out_array
    side = jax.ShapeDtypeStruct((pairs, 2 * blocks + 1, width // (2 * pairs), width), bf16)
    return pl.pallas_call(
        ffn_kernel,
        grid=(total // rows,),
        in_specs=[smem, smem] + [rowspec(width)] * 4 + [whole(norms)] + [once(w) for w in weights],
        out_specs=[rowspec(width)] * 4 + [rowspec(LANES), whole(side), whole(side), pl.BlockSpec((4, width), lambda i: (0, 0))],
        out_shape=[
            sds((total, width), bf16), sds((total, width), bf16), sds((total, width), bf16), sds((total, width), bf16),
            sds((total, LANES), f32), side, side, sds((4, width), f32),
        ],
        scratch_shapes=[pltpu.VMEM((width, blocks * width), f32), pltpu.VMEM((blocks * width, width), f32), pltpu.VMEM((width, width), f32)]
        + ([pltpu.VMEM(h, bf16) for h in held] if devices > 1 else []),
        name="ffn",
        **params(32, 56),
    )(core, here, *placed(h1, x, cot, o2), norms, *weights)


def cross_backward_kernel(
    tile, block, first, count, each, items_ref, q2_ref, k2_ref, v2_ref, do_ref, l_ref, delta_ref, idr_ref, idk_ref, memory_ref, *rest
):
    dq_ref, dk_ref, dv_ref, grads_ref, q_all, ids_all, dq, dk, dv, grads = rest[-10:]
    step = pl.program_id(0)
    total = q2_ref.shape[0]
    begin = first * LANES if q2_ref.shape[1] > count * LANES else 0
    cols = slice(begin, begin + count * LANES)

    @pl.when(step == 0)
    def _():
        dq[...] = jnp.zeros_like(dq)
        dk[...] = jnp.zeros_like(dk)
        dv[...] = jnp.zeros_like(dv)
        grads[...] = jnp.zeros_like(grads)
        q_all[...] = q2_ref[:, cols] * jnp.asarray(HD ** -0.5, bf16)
        for j in range(total // block):
            ids_all[j * block : (j + 1) * block, :] = column_of(idr_ref[:, j * block : (j + 1) * block])
        attend_back(
            items_ref, idk_ref, ids_all, q_all, do_ref.at[:, cols], k2_ref.at[:, cols], v2_ref.at[:, cols], l_ref, delta_ref,
            dq, dk, dv, tile, block, 2 * first, False, each,
        )

    memory = memory_ref[...]
    per = memory.shape[0]
    here = pl.ds(pl.multiple_of(step * per, per), per)
    for i, (ref, out_ref) in enumerate(((dk, dk_ref), (dv, dv_ref))):
        grad = ref[here, :].astype(bf16)
        out_ref[...] = grad
        grads[i] += mm(memory, grad, TN)
    rows = dq_ref.shape[0]
    dq_ref[...] = (dq[pl.ds(pl.multiple_of(step * rows, rows), rows), :] * HD ** -0.5).astype(bf16)

    @pl.when(step == pl.num_programs(0) - 1)
    def _():
        grads_ref[...] = grads[...].astype(bf16)


def cross_backward(items, q2, k2, v2, do, l, delta, idr, idk, memory, first, count, each, after, turns=2, block=QROWS, tile=256):
    total, width = q2.shape
    keys = k2.shape[0]
    columns = count * LANES
    alone = first % count == 0
    cols = lambda r: pl.BlockSpec((r, columns if alone else width), lambda i, *_: (0, first // count if alone else 0))
    rowspec = lambda r, w: pl.BlockSpec((r, w), lambda i, *_: (i, 0))
    sds = jax.ShapeDtypeStruct
    grad = sds((2, width, columns), bf16)
    return pl.pallas_call(
        functools.partial(cross_backward_kernel, tile, block, first, count, each),
        grid_spec=pltpu.PrefetchScalarGridSpec(
            num_scalar_prefetch=1,
            grid=(turns,),
            in_specs=[cols(total), cols(keys), cols(keys), cols(total)]
            + [whole(l), whole(delta), whole(idr), whole(idk), rowspec(keys // turns, width)] + [apart] * len(after),
            out_specs=[rowspec(total // turns, columns), rowspec(keys // turns, columns), rowspec(keys // turns, columns), whole(grad)],
            scratch_shapes=[
                pltpu.VMEM((total, columns), bf16), pltpu.VMEM((total, LANES), jnp.int32), pltpu.VMEM((total, columns), f32),
                pltpu.VMEM((keys, columns), f32), pltpu.VMEM((keys, columns), f32), pltpu.VMEM((2, width, columns), f32),
            ],
        ),
        out_shape=[sds((total, columns), bf16), sds((keys, columns), bf16), sds((keys, columns), bf16), grad],
        name="cross_backward",
        **params(5 * count + 4, 10 * count + 4),
    )(items, *placed(q2, k2, v2, do, l, delta), idr, idk, *placed(memory), *after)


def memory_grad_kernel(ka_ref, kb_ref, va_ref, vb_ref, wk_ref, wv_ref, *rest):
    total = mm(jnp.concatenate([ka_ref[...], kb_ref[...]], axis=1), wk_ref[0], NT)
    total += mm(jnp.concatenate([va_ref[...], vb_ref[...]], axis=1), wv_ref[0], NT)
    rest[-1][...] = total.astype(bf16)


def memory_grad(ka, kb, va, vb, weights, index, after, rows=1024):
    keys, width = ka.shape[0], weights.shape[2]
    rowspec = lambda w: pl.BlockSpec((rows, w), lambda i: (i, 0))
    return pl.pallas_call(
        memory_grad_kernel,
        grid=(keys // rows,),
        in_specs=[rowspec(a.shape[1]) for a in (ka, kb, va, vb)] + [part(weights, index, width, 0), part(weights, index + 1, width, 0)] + [apart] * len(after),
        out_specs=rowspec(width),
        out_shape=out_array((keys, width), bf16),
        name="memory_grad",
        **params(4, 16),
    )(ka, kb, va, vb, weights, weights, *after)


def between_kernel(
    core_ref, ga_ref, gb_ref, gn23_ref, r1_ref, dr2_ref, dr3_ref, dqa_ref, dqb_ref, h1b_ref, o1_ref, wso_ref, wcq_ref, norms_ref, *rest
):
    dsum_ref, do1_ref, delta_ref, keep_ref, send_ref, gn_ref, total = rest[-7:]
    step = pl.program_id(0)

    @pl.when(step == 0)
    def _():
        total[...] = jnp.zeros_like(total)
        gn_ref[...] = jnp.zeros_like(gn_ref)

    dq2 = jnp.concatenate([dqa_ref[...], dqb_ref[...]], axis=1)
    dh1 = dr2_ref[...].astype(f32) + mm(dq2, wcq_ref[0], NT)
    n1, rstd1 = norm_rows(r1_ref[...].astype(f32))
    gn_ref[0:1, :] += column_sums(dh1 * n1)
    gn_ref[1:2, :] += column_sums(dh1)
    dr1 = norm_back(dh1, n1, rstd1, norms_ref[0:1, :])
    dsum_ref[...] = (dr1 + dr3_ref[...].astype(f32)).astype(bf16)
    da1 = dr1.astype(bf16)
    o1 = o1_ref[...]
    do1 = mm(da1, wso_ref[0], NT).astype(bf16)
    do1_ref[...] = do1
    delta_ref[...] = head_columns(do1, o1)
    total[0] += mm(h1b_ref[...], dq2, TN)
    total[1] += mm(o1, da1, TN)

    @pl.when(step == pl.num_programs(0) - 1)
    def _():
        gn_ref[2:6, :] = gn23_ref[...]
        r, width = keep_ref.shape[2:]
        norm_part = jnp.concatenate([gn_ref[...], jnp.zeros((r - 8, width), f32)]).astype(bf16)

        def write(device, ref, j):
            here = pl.ds(pl.multiple_of(device * r, r), r)
            for i in range(2):
                ref[j, i, :, : ga_ref.shape[2]] = ga_ref[i, here, :]
                ref[j, i, :, ga_ref.shape[2] :] = gb_ref[i, here, :]
                ref[j, 2 + i] = total[i, here, :].astype(bf16)
            ref[j, 4] = norm_part

        spread(keep_ref, send_ref, core_ref[0], write)


def between(core, pairs, ga, gb, gn23, r1, dr2, dr3, dqa, dqb, h1b, o1, weights, norms, after, rows=512):
    total, width = r1.shape
    rowspec = lambda w: pl.BlockSpec((rows, w), lambda i: (i, 0))
    sds = jax.ShapeDtypeStruct
    side = jax.ShapeDtypeStruct((pairs, 5, width // (2 * pairs), width), bf16)
    return pl.pallas_call(
        between_kernel,
        grid=(total // rows,),
        in_specs=[pl.BlockSpec(memory_space=pltpu.SMEM), whole(ga), whole(gb), whole(gn23)]
        + [rowspec(width)] * 3 + [rowspec(dqa.shape[1]), rowspec(dqb.shape[1])] + [rowspec(width)] * 2
        + [part(weights, 0, width, 0), part(weights, 1, width, 0), whole(norms)] + [apart] * len(after),
        out_specs=[rowspec(width)] * 2
        + [rowspec(LANES), whole(side), whole(side), pl.BlockSpec((8, width), lambda i: (0, 0))],
        out_shape=[sds((total, width), bf16), sds((total, width), bf16), sds((total, LANES), f32), side, side, sds((8, width), f32)],
        scratch_shapes=[pltpu.VMEM((2, width, width), f32)],
        name="between",
        **params(7, 24),
    )(core, ga, gb, gn23, *placed(r1), dr2, dr3, dqa, dqb, *placed(h1b, o1), weights, weights, norms, *after)


def self_backward_kernel(
    tile, block, core_ref, items_ref, q_ref, k_ref, v_ref, do_ref, l_ref, delta_ref, idr_ref, x_ref, wq_ref, wk_ref, wv_ref, sofar_ref, *rest
):
    gx_ref, keep_ref, send_ref, q_all, ids_all, dq, dk, dv, grads = rest[-9:]
    step = pl.program_id(0)
    total, width = q_ref.shape

    @pl.when(step == 0)
    def _():
        dq[...] = jnp.zeros_like(dq)
        dk[...] = jnp.zeros_like(dk)
        dv[...] = jnp.zeros_like(dv)
        grads[...] = jnp.zeros_like(grads)
        q_all[...] = q_ref[...] * jnp.asarray(HD ** -0.5, bf16)
        for j in range(total // block):
            ids_all[j * block : (j + 1) * block, :] = column_of(idr_ref[:, j * block : (j + 1) * block])
        attend_back(
            items_ref, idr_ref, ids_all, q_all, do_ref, k_ref, v_ref, l_ref, delta_ref, dq, dk, dv, tile, block, 0, True, 2
        )

    x = x_ref[...]
    rows = x.shape[0]
    here = pl.ds(pl.multiple_of(step * rows, rows), rows)
    gx = sofar_ref[...].astype(f32)
    parts = (dq[here, :] * HD ** -0.5).astype(bf16), dk[here, :].astype(bf16), dv[here, :].astype(bf16)
    for i, (grad, w_ref) in enumerate(zip(parts, (wq_ref, wk_ref, wv_ref))):
        gx += mm(grad, w_ref[0], NT)
        grads[i] += mm(x, grad, TN)
    gx_ref[...] = gx.astype(bf16)

    @pl.when(step == pl.num_programs(0) - 1)
    def _():
        r = keep_ref.shape[2]

        def write(device, ref, j):
            place = pl.ds(pl.multiple_of(device * r, r), r)
            for i in range(3):
                ref[j, i] = grads[i, place, :].astype(bf16)

        spread(keep_ref, send_ref, core_ref[0], write)


def self_backward(core, pairs, items, q, k, v, do, l, delta, idr, x, weights, sofar, after, turns=2, block=QROWS, tile=256):
    total, width = x.shape
    sds = jax.ShapeDtypeStruct
    side = sds((pairs, 3, width // (2 * pairs), width), bf16)
    rowspec = lambda w: pl.BlockSpec((total // turns, w), lambda i, *_: (i, 0))
    return pl.pallas_call(
        functools.partial(self_backward_kernel, tile, block),
        grid_spec=pltpu.PrefetchScalarGridSpec(
            num_scalar_prefetch=2,
            grid=(turns,),
            in_specs=[whole(a) for a in (q, k, v, do, l, delta, idr)]
            + [rowspec(width)] + [part(weights, i, width, 0) for i in range(3)] + [rowspec(width)] + [apart] * len(after),
            out_specs=[rowspec(width), whole(side), whole(side)],
            scratch_shapes=[
                pltpu.VMEM((total, width), bf16), pltpu.VMEM((total, LANES), jnp.int32),
                pltpu.VMEM((total, width), f32), pltpu.VMEM((total, width), f32), pltpu.VMEM((total, width), f32),
                pltpu.VMEM((3, width, width), f32),
            ],
        ),
        out_shape=[sds((total, width), bf16), side, side],
        name="self_backward",
        **params(17, 34),
    )(core, items, q, k, v, do, l, delta, idr, x, weights, weights, weights, sofar, *after)


def add_split_kernel(count, here_ref, *refs):
    places = refs[0].shape[1]
    for m in range(places):
        at = here_ref[0] ^ m
        total = refs[0][:, at].astype(f32)
        for ref in refs[1:count]:
            total += ref[:, at].astype(f32)
        refs[count + m][...] = total.astype(bf16)


def add_split(here, parts, outer, places):
    tail = parts[0].shape[1:]
    parts = [p.reshape((outer, places) + tail) for p in parts]
    out = pl.pallas_call(
        functools.partial(add_split_kernel, len(parts)),
        grid=(outer,),
        in_specs=[pl.BlockSpec(memory_space=pltpu.SMEM)] + [pl.BlockSpec((1, places) + tail, lambda i: (i, 0, 0, 0, 0))] * len(parts),
        out_specs=[pl.BlockSpec((1,) + tail, lambda i: (i, 0, 0, 0))] * places,
        out_shape=[jax.ShapeDtypeStruct((outer,) + tail, bf16)] * places,
        name="add_split",
        **params(3, 24),
    )(here, *parts)
    return list(out)


def first_pair_kernel(cut, here_ref, keep, came, *outs):
    for m in range(2):
        at = here_ref[0] ^ m
        outs[m][0] = (keep[0, :, at, :cut].astype(f32) + came[0, :, at, :cut].astype(f32)).astype(bf16)
        at = here_ref[1] ^ m
        outs[2 + m][0] = (keep[0, at, :, cut:].astype(f32) + came[0, at, :, cut:].astype(f32)).astype(bf16)


def first_pair(here, keep, came, outer, cut):
    squares, rows, width = keep.shape[1:]
    parts = [p.reshape(outer, 2, 2, squares, rows, width) for p in (keep, came)]
    shapes = [(outer, 2, n, rows, width) for n in (cut, cut, squares - cut, squares - cut)]
    out = pl.pallas_call(
        functools.partial(first_pair_kernel, cut),
        grid=(outer,),
        in_specs=[pl.BlockSpec(memory_space=pltpu.SMEM)] + [pl.BlockSpec((1,) + p.shape[1:], lambda i: (i, 0, 0, 0, 0, 0)) for p in parts],
        out_specs=[pl.BlockSpec((1,) + s[1:], lambda i: (i, 0, 0, 0, 0)) for s in shapes],
        out_shape=[jax.ShapeDtypeStruct(s, bf16) for s in shapes],
        name="first_pair",
        **params(2, 24),
    )(here, *parts)
    return list(out)


def second_pair_kernel(here_ref, keep_a, came_a, keep_b, came_b, *outs):
    for m in range(2):
        at = here_ref[1] ^ m
        outs[m][0] = (keep_a[0, at].astype(f32) + came_a[0, at].astype(f32)).astype(bf16)
        at = here_ref[0] ^ m
        outs[2 + m][0] = (keep_b[0, at].astype(f32) + came_b[0, at].astype(f32)).astype(bf16)


def second_pair(here, parts):
    outer = parts[0].shape[0]
    shapes = [(p.shape[0],) + p.shape[2:] for p in parts]
    out = pl.pallas_call(
        second_pair_kernel,
        grid=(outer,),
        in_specs=[pl.BlockSpec(memory_space=pltpu.SMEM)] + [pl.BlockSpec((1,) + p.shape[1:], lambda i: (i, 0, 0, 0, 0)) for p in parts],
        out_specs=[pl.BlockSpec((1,) + s[1:], lambda i: (i, 0, 0, 0)) for s in shapes],
        out_shape=[jax.ShapeDtypeStruct(s, bf16) for s in shapes],
        name="second_pair",
        **params(1, 24),
    )(here, *parts)
    return list(out)


def join_split_kernel(here_ref, keep_a, came_a, keep_b, came_b, *outs):
    cut = keep_a.shape[2]
    for m, out in enumerate(outs):
        at = here_ref[0] ^ m
        out[:, :cut] = (keep_a[:, at].astype(f32) + came_a[:, at].astype(f32)).astype(bf16)
        out[:, cut:] = (keep_b[:, at].astype(f32) + came_b[:, at].astype(f32)).astype(bf16)


def join_split(here, parts, outer, places):
    parts = [p.reshape((outer, places) + p.shape[1:]) for p in parts]
    tail = (parts[0].shape[2] + parts[2].shape[2],) + parts[0].shape[3:]
    out = pl.pallas_call(
        join_split_kernel,
        grid=(outer,),
        in_specs=[pl.BlockSpec(memory_space=pltpu.SMEM)] + [pl.BlockSpec((1,) + p.shape[1:], lambda i: (i, 0, 0, 0, 0)) for p in parts],
        out_specs=[pl.BlockSpec((1,) + tail, lambda i: (i, 0, 0, 0))] * places,
        out_shape=[jax.ShapeDtypeStruct((outer,) + tail, bf16)] * places,
        name="join_split",
        **params(1, 24),
    )(here, *parts)
    return list(out)


def place_kernel(here_ref, *refs):
    out_ref = refs[-1]
    for m, ref in enumerate(refs[:-1]):
        out_ref[0, :, here_ref[0] ^ m] = ref[0]


def place(here, pieces):
    shape = pieces[0].shape
    pieces = [p.reshape((shape[0], -1) + shape[-2:]) for p in pieces]
    count, tail = len(pieces), pieces[0].shape[2:]
    inner = pieces[0].shape[1]
    out = pl.pallas_call(
        place_kernel,
        grid=(shape[0],),
        in_specs=[pl.BlockSpec(memory_space=pltpu.SMEM)] + [pl.BlockSpec((1, inner) + tail, lambda i: (i, 0, 0, 0))] * count,
        out_specs=pl.BlockSpec((1, inner, count) + tail, lambda i: (i, 0, 0, 0, 0)),
        out_shape=jax.ShapeDtypeStruct((shape[0], inner, count) + tail, bf16),
        name="place",
        **params(1, 16),
    )(here, *pieces)
    return out.reshape(shape[:-2] + (count,) + tail)


def own_block(shape):
    return pl.BlockSpec(shape, lambda *_: (0,) * len(shape))


def pack_kernel(moves, count, *refs):
    ins, out_ref, wide = refs[:count], refs[count], refs[count + 1 :]
    rows = out_ref.shape[1]
    for ref, w in zip(ins, wide):
        w[...] = ref[...].astype(f32)
    for source, begin, step, square, block in moves:
        value = wide[source][pl.ds(begin, rows, stride=step), :]
        out_ref[square, :, block * LANES : (block + 1) * LANES] = value.astype(bf16)


def pack(arrays, moves, squares, rows, width, name):
    arrays = [a.reshape(-1, LANES) for a in arrays]
    return pl.pallas_call(
        functools.partial(pack_kernel, moves, len(arrays)),
        in_specs=[own_block(a.shape) for a in arrays],
        out_specs=own_block((squares, rows, width)),
        out_shape=jax.ShapeDtypeStruct((squares, rows, width), bf16),
        scratch_shapes=[pltpu.VMEM(a.shape, f32) for a in arrays],
        name=name,
        **params(1, 16),
    )(*placed(*arrays))


def square_moves(source, square, width):
    blocks = width // LANES
    return [(source, b, blocks, square, b) for b in range(blocks)]


def finish_kernel(moves, count, *refs):
    ins, outs = refs[:count], refs[count:]
    rows = ins[0].shape[1]
    for square, block, out, begin, step in moves:
        cols = slice(block * LANES, (block + 1) * LANES)
        total = ins[0][square, :, cols].astype(f32)
        for ref in ins[1:]:
            total += ref[square, :, cols].astype(f32)
        if step:
            outs[out][pl.ds(begin, rows, stride=step), :] = total
        else:
            outs[out][:, cols] = total


def finish(parts, moves, shapes, name):
    return pl.pallas_call(
        functools.partial(finish_kernel, moves, len(parts)),
        in_specs=[own_block(p.shape) for p in parts],
        out_specs=[own_block(s) for s in shapes],
        out_shape=[jax.ShapeDtypeStruct(s, f32) for s in shapes],
        name=name,
        **params(1, 16),
    )(*parts)


def fill_items(ref, first, high, keys, block, tile):
    filled = jnp.int32(0)
    for b in range(len(first)):
        count = (high[b] - first[b] * LANES + tile - 1) // tile

        def put(j, at, b=b):
            ref[0, at] = b
            ref[1, at] = first[b] + j * (tile // LANES)
            return at + 1

        filled = lax.fori_loop(0, count, put, filled)
    for j in range(PADDING):
        ref[0, filled + j] = len(first) - 1
        ref[1, filled + j] = keys // LANES
    for i, n in enumerate(EACH):
        ref[2, i] = (filled + n - 1) // n


def plan_kernel(block, tile, seg_ref, mem_ref, qid_ref, mid_ref, own_ref, cross_ref):
    def ends_of(ref):
        ends, total = [], jnp.int32(0)
        for i in range(ref.shape[1]):
            total += ref[0, i]
            ends.append(total)
        return ends

    ends, mem_ends = ends_of(seg_ref), ends_of(mem_ref)
    for ref, marks in ((qid_ref, ends), (mid_ref, mem_ends)):
        places = lax.broadcasted_iota(jnp.int32, ref.shape, 1)
        ids = jnp.zeros(ref.shape, jnp.int32)
        for mark in marks:
            ids += (places >= mark).astype(jnp.int32)
        ref[...] = ids
    total, keys = qid_ref.shape[1], mid_ref.shape[1]
    own, low, high = [], [], []
    for begin in range(0, total, block):
        own_first, first, last = jnp.int32(0), jnp.int32(0), mem_ref[0, 0]
        for i in range(seg_ref.shape[1]):
            passed = (ends[i] <= begin).astype(jnp.int32)
            own_first += passed * seg_ref[0, i]
            first += passed * mem_ref[0, i]
            if i + 1 < seg_ref.shape[1]:
                last += (ends[i] <= begin + block - 1).astype(jnp.int32) * mem_ref[0, i + 1]
        own.append(own_first // LANES)
        low.append(first // LANES)
        high.append(last)
    fill_items(own_ref, own, [begin + block for begin in range(0, total, block)], total, block, tile)
    fill_items(cross_ref, low, high, keys, block, tile)


def plan(seg, mem, total, keys, block=QROWS, tile=256):
    smem = pl.BlockSpec(memory_space=pltpu.SMEM)
    sds = jax.ShapeDtypeStruct
    more = PADDING
    return pl.pallas_call(
        functools.partial(plan_kernel, block, tile),
        in_specs=[smem, smem],
        out_specs=[own_block((1, total)), own_block((1, keys)), smem, smem],
        out_shape=[
            sds((1, total), jnp.int32), sds((1, keys), jnp.int32),
            sds((3, total // block * (total // tile) + more), jnp.int32), sds((3, total // block * (keys // tile) + more), jnp.int32),
        ],
        name="plan",
        **params(1, 16),
    )(seg, mem)

HEAD_START = 1


def mesh_size():
    return lax.axis_size("dp") * lax.axis_size("fsdp")


def position():
    return lax.axis_index("dp") * lax.axis_size("fsdp") + lax.axis_index("fsdp")


def bit_groups(wide):
    count = mesh_size().bit_length() - 1
    groups = [(0, 1)]
    while groups[-1][0] + groups[-1][1] < count:
        low = groups[-1][0] + groups[-1][1]
        groups.append((low, min(2 if len(groups) <= wide else 1, count - low)))
    return groups


def swap(x, mask):
    return lax.ppermute(x, ("dp", "fsdp"), [(i, i ^ mask) for i in range(mesh_size())])


def place_in(group):
    return (position() >> group[0]) & ((1 << group[1]) - 1)


def tie(x, *after):
    return lax.optimization_barrier((x, *after))[0] if after else x


def gather_step(x, group, after=(), lower=0, came=None):
    low, width = group
    here = place_in(group)
    if came is None:
        came = tie([swap(x, m << low) for m in range(1, 1 << width)], *after)
    blocks = [x] + came
    for j in range(width):
        flip = (here >> j) & 1 == 1
        blocks = [jnp.where(flip, blocks[p ^ (1 << j)], blocks[p]) for p in range(1 << width)]
    return jnp.stack(blocks, axis=x.ndim - 2 - lower)


def gathered(x):
    return x.reshape(x.shape[:1] + (-1, x.shape[-1]))


def swap_pieces(parts, group, after=()):
    return [parts[0]] + tie([swap(parts[m], m << group[0]) for m in range(1, len(parts))], *after)


def next_pieces(parts, groups, done):
    group = groups[done]
    outer = 1 << sum(g[1] for g in groups[done + 1 :])
    return add_split(place_in(group).reshape(1).astype(jnp.int32), parts, outer, 1 << group[1])


def norm_parts(norm_params, size):
    parts, left = [], norm_params
    for _ in range(3):
        part = left.astype(bf16)
        parts.append(jnp.pad(part, (0, LANES - part.size)))
        left = left - part.astype(f32)
    flat = jnp.concatenate(parts)
    return jnp.pad(flat, (0, size - flat.size))


def resplit(keep, send, devices, core, squares):
    halves = jnp.concatenate([keep, send])
    width = halves.shape[-1]
    first = halves[:, :squares].transpose(1, 0, 2, 3).reshape(squares, devices, -1, width).transpose(1, 0, 2, 3)
    rows = first.shape[2]
    if halves.shape[1] > squares:
        rest = halves[:, squares:].reshape(devices, halves.shape[1] - squares, rows, width)
        first = jnp.concatenate([first, rest], axis=1)
    both = first.reshape(devices // 2, 2, -1, rows, width)
    return [lax.dynamic_index_in_dim(both, core ^ m, 1, keepdims=False) for m in range(2)]


def body(
    inputs, memory, seg_lengths, mem_lengths, self_query, self_key, self_value, self_out,
    cross_query, cross_key, cross_value, cross_out, ffn_in, ffn_out, norm_params, cotangent,
):
    total, width = inputs.shape
    keys = memory.shape[0]
    devices = mesh_size()
    groups, single = bit_groups(8), bit_groups(1)
    down = groups[::-1]
    shard = norm_params.shape[0]
    size = self_query.shape[0]
    own_rows = size // width
    blocks = ffn_in.shape[0] // size
    whole_tiles = own_rows % 16 == 0
    core = place_in(groups[0]).reshape(1).astype(jnp.int32)

    firsts = (self_query, self_key, self_value)
    seconds = (self_out, cross_query, cross_key, cross_value, norm_parts(norm_params, size))
    if whole_tiles:
        lane_blocks = width // LANES
        three = [m for i in range(3) for m in square_moves(i, i, width)]
        five = three + [m for i in range(3, 5) for m in square_moves(i, i, width)]
        wide = [(0, c * lane_blocks + b, blocks * lane_blocks, c, b) for c in range(blocks) for b in range(lane_blocks)]
        tall = [(1, j * own_rows * lane_blocks + b, lane_blocks, blocks + 1 + j, b) for j in range(blocks) for b in range(lane_blocks)]
        first = pack(firsts, three, 3, own_rows, width, "pack_self")
        second = pack(tie(seconds, first), five, 5, own_rows, width, "pack_cross")
        last = square_moves(2, blocks, width)
        third = pack(tie((ffn_in, ffn_out, cross_out), first), wide + tall + last, 2 * blocks + 1, own_rows, width, "pack_ffn")
    else:
        first = jnp.concatenate(firsts).reshape(3, own_rows, width)
        second = jnp.concatenate(seconds).reshape(5, own_rows, width)
        fi = ffn_in.reshape(own_rows, blocks, width).transpose(1, 0, 2)
        third = jnp.concatenate([fi, cross_out.reshape(1, own_rows, width), ffn_out.reshape(blocks, own_rows, width)])
    third = third.reshape(-1, width)
    plane = groups[1]
    high_bits = [(b, 1) for b in reversed(range(plane[0] + plane[1], devices.bit_length() - 1))]
    for g in down[:-2]:
        first = gather_step(first, g)
    second = gather_step(second, high_bits[0])
    qid, mid, own_items, items = plan(*tie((seg_lengths, mem_lengths), first), total, keys)
    first = gather_step(first, plane, [second, own_items])
    for g in high_bits[1:]:
        second = gather_step(second, g)
    third = gather_step(third, high_bits[0])
    first = gathered(gather_step(first, down[-1], [second, third]))
    for g in high_bits[1:]:
        third = gather_step(third, g)
    low, high = (plane[0], 1), (plane[0] + 1, 1)
    cut = (blocks + 1) * own_rows
    part_a, part_b = tie((third[..., :cut, :], third[..., cut:, :]), first)
    early = [second, part_a, part_b]
    bits = jnp.stack([(position() >> b) & 1 for b in (low[0], high[0], 0)]).astype(jnp.int32)
    pairs = devices // 2 if whole_tiles else 1
    part_of = core if whole_tiles else jnp.zeros_like(core)

    q1, k1, v1, o1, l1 = self_forward(own_items, inputs, first, qid, early)
    def at(group):
        return place_in(group).reshape(1).astype(jnp.int32)

    second = gather_step(second, plane, [l1])
    came_a, came_b = tie((swap(part_a, 1 << low[0]), swap(part_b, 1 << high[0])), l1)
    second = tie(second, came_a, came_b)
    part_a, part_b = place(at(low), [part_a, came_a]), place(at(high), [part_b, came_b])
    second = gathered(gather_step(second, down[-1]))
    norm_all = second[4].reshape(devices, -1)[:, : 3 * LANES].reshape(devices, 3, LANES)[:, :, :shard].astype(f32)
    norms = jnp.sum(norm_all, axis=1).reshape(6, width)
    k2, v2, r1, h1b, q2, h1, o2, l2 = cross_forward(items, memory, inputs, o1, second, norms, qid, mid, [bits])
    part_a, part_b = [part_a, swap(part_a, 1 << high[0])], [part_b, swap(part_b, 1 << low[0])]
    came = [swap(part_a[0], 1), swap(part_b[0], 1)]
    part_a[1], part_b[1], came[0], came[1] = tie((part_a[1], part_b[1], came[0], came[1]), l2)
    part_a += [came[0], swap(part_a[1], 1)]
    part_b += [came[1], swap(part_b[1], 1)]
    if whole_tiles:
        pieces = [p.reshape((-1, 2) + p.shape[-2:]) for p in part_a + part_b]
    else:
        pieces = []
        for parts, group, lower in ((part_a, high, 1), (part_b, low, 0)):
            halves = [gather_step(parts[j], group, lower=lower, came=[parts[j + 1]]) for j in (0, 2)]
            both = gather_step(halves[0], down[-1], came=[halves[1]]).reshape(devices, -1, own_rows, width)
            pieces.append(both)
        pieces[0] = jnp.concatenate([pieces[0][:, i].reshape(width, width) for i in range(blocks + 1)])[None]
        pieces[1] = pieces[1].reshape(1, -1, width)
    out, dr3, dr2, do2, delta2, keep, send, gn23 = ffn(part_of, bits, pairs, h1, inputs, cotangent, o2, pieces, norms)

    one = [keep, send] if whole_tiles else resplit(keep, send, devices, core[0], blocks + 1)
    dq2a, dk2a, dv2a, gckva = cross_backward(items, q2, k2, v2, do2, l2, delta2, qid, mid, memory, 0, HEAD_START, 4, [])
    low, high = 1 << groups[1][0], 2 << groups[1][0]
    both = jnp.stack([(position() >> (groups[1][0] + j)) & 1 for j in range(2)]).astype(jnp.int32)
    one = swap_pieces(one, groups[0], [dq2a])
    one = first_pair(both, one[0], one[1], devices // 8, blocks + 1)
    more = width // LANES - HEAD_START
    dq2b, dk2b, dv2b, gckvb = cross_backward(
        items, q2, k2, v2, do2, l2, delta2, qid, mid, memory, HEAD_START, more, 2, [one[1], one[3]]
    )
    came = tie([swap(one[1], low), swap(one[3], high)], dq2b)
    one = second_pair(both, [one[0], came[0], one[2], came[1]])
    gm = memory_grad(dk2a, dk2b, dv2a, dv2b, second, 2, [one[1], one[3]])
    dsum, do1, delta1, keep, send, gn = between(
        part_of, pairs, gckva, gckvb, gn23, r1, dr2, dr3, dq2a, dq2b, h1b, o1, second, norms, placed(gm)
    )
    came = tie([swap(one[1], high), swap(one[3], low)], do1)
    one = join_split(
        place_in(single[2]).reshape(1).astype(jnp.int32), [one[0], came[0], one[2], came[1]],
        1 << sum(g[1] for g in single[3:]), 1 << single[2][1],
    )
    two = [keep, send]
    if not whole_tiles:
        two = resplit(keep, send, devices, core[0], 5)
        own_norms = jnp.pad(gn[:6].astype(bf16).reshape(devices, -1), ((0, 0), (0, size - shard)))
        own_norms = own_norms.reshape(devices // 2, 2, own_rows, width)
        two = [two[m].at[:, 4].set(lax.dynamic_index_in_dim(own_norms, core[0] ^ m, 1, keepdims=False)) for m in range(2)]
    two = next_pieces(swap_pieces(tie(two, one[1]), groups[0]), groups, 1)
    gx, keep, send = self_backward(part_of, pairs, own_items, q1, k1, v1, do1, l1, delta1, qid, inputs, first, dsum, one[1:] + two[1:])
    two = next_pieces(swap_pieces(two, groups[1], [gx]), single, 2)
    one = next_pieces(swap_pieces(one, single[2], [gx]), single, 3)
    keep, send = tie((keep, send), two[1], one[1])
    three = [keep, send] if whole_tiles else resplit(keep, send, devices, core[0], 3)
    three = next_pieces(swap_pieces(three, groups[0]), groups, 1)
    for i in range(2, len(groups)):
        three = next_pieces(swap_pieces(three, groups[i - 1]), groups, i)
    for i in range(3, len(single)):
        two = next_pieces(swap_pieces(two, single[i - 1]), single, i)
        if i > 3:
            one = next_pieces(swap_pieces(one, single[i - 1]), single, i)

    def flat(g):
        return g.reshape(-1)

    chains = [swap_pieces(one, single[-1], [three[1]]), swap_pieces(two, single[-1], [three[1]]), swap_pieces(three, groups[-1])]
    chains = [[p.reshape(-1, own_rows, width) for p in chain] for chain in chains]
    if whole_tiles:
        lane_rows = size // LANES
        square, long = (lane_rows, LANES), (blocks * lane_rows, LANES)

        moves = [(c, b, 0, c * lane_blocks + b, blocks * lane_blocks) for c in range(blocks) for b in range(lane_blocks)]
        moves += [(blocks, b, 1, b, lane_blocks) for b in range(lane_blocks)]
        moves += [
            (blocks + 1 + j, b, 2, j * own_rows * lane_blocks + b, lane_blocks) for j in range(blocks) for b in range(lane_blocks)
        ]
        gfi, gco, gfo = finish(chains[0], moves, [long, square, long], "finish_ffn")
        moves = [(i, b, i, b, lane_blocks) for i in range(4) for b in range(lane_blocks)] + [(4, b, 4, 0, 0) for b in range(lane_blocks)]
        gck, gcv, gcq, gso, gn = finish(chains[1], moves, [square] * 4 + [(own_rows, width)], "finish_cross")
        gn = lax.dynamic_slice_in_dim(flat(gn[:6]), position() * shard, shard)
        moves = [(i, b, i, b, lane_blocks) for i in range(3) for b in range(lane_blocks)]
        gsq, gsk, gsv = finish(chains[2], moves, [square] * 3, "finish_self")
    else:
        one, two, three = (sum(p.astype(f32) for p in chain) for chain in chains)
        gfi, gco, gfo = one[:blocks].transpose(1, 0, 2), one[blocks], one[blocks + 1 :]
        gck, gcv, gcq, gso, gn = two[0], two[1], two[2], two[3], flat(two[4])[:shard]
        gsq, gsk, gsv = three[0], three[1], three[2]
    return (out, gx, gm) + tuple(flat(g) for g in (gsq, gsk, gsv, gso, gcq, gck, gcv, gco, gfi, gfo, gn))


def solution(mesh):
    rows, flat = P(("dp", "fsdp"), None), P(("dp", "fsdp"))
    return jax.shard_map(
        body,
        mesh=mesh,
        in_specs=(rows,) * 4 + (flat,) * 11 + (rows,),
        out_specs=(rows,) * 3 + (flat,) * 11,
        check_vma=False,
    )
```

```python
import functools
import jax
import jax.numpy as jnp
from jax import lax
from jax.experimental import pallas as pl
from jax.experimental.pallas import tpu as pltpu
from jax.sharding import PartitionSpec as P

HD = 64
LANES = 128
MOST = 256
QROWS = 128
EACH = (2, 4)
PADDING = 4
FFN_CHUNK = 256
masked_score = -1e30
norm_eps = 1e-05
bf16, f32 = jnp.bfloat16, jnp.float32
NT = (((1,), (1,)), ((), ()))
TN = (((0,), (0,)), ((), ()))
NN = (((1,), (0,)), ((), ()))


def mm(left, right, dims=NN):
    return lax.dot_general(left, right, dims, preferred_element_type=f32)


def norm_rows(source):
    mean = jnp.mean(source, axis=-1, keepdims=True)
    centered = source - mean
    variance = jnp.mean(centered * centered, axis=-1, keepdims=True)
    rstd = lax.rsqrt(variance + norm_eps)
    return centered * rstd, rstd


def lane_below(rows):
    return lax.broadcasted_iota(jnp.int32, (rows, LANES), 1) < HD


def column_of(row):
    return jnp.broadcast_to(row, (LANES, row.shape[1])).T


def head_part(pair, which, low):
    return jnp.where(low == (which == 0), pair, jnp.zeros_like(pair))


def values_with_ones(values):
    parts = []
    for p in range(values.shape[1] // LANES):
        pair = values[:, p * LANES : (p + 1) * LANES]
        parts += [pair, jnp.ones_like(pair)]
    return jnp.concatenate(parts, axis=1)


def finish_heads(at, top, tot, acc, write):
    shape = acc.shape[0], at.size if hasattr(at, "size") else at.stop - at.start, LANES
    lane = lax.broadcasted_iota(jnp.int32, shape[1:], 1)
    sums, tops = jnp.ones(shape[1:], f32), jnp.zeros(shape[1:], f32)
    for p in range(shape[0]):
        total = tot[p, at, :]
        write(p, (acc[p, at, :] / total).astype(bf16))
        sums = jnp.where(lane % HD == p, total, sums)
        tops = jnp.where(lane == p, top[2 * p, at, :], jnp.where(lane == HD + p, top[2 * p + 1, at, :], tops))
    return tops + jnp.log(sums)


def column_at(head):
    return head % 2 * HD + head // 2


def item_at(items_ref, n, idk_ref, ids_q, keys, tile, block, causal):
    begin = pl.multiple_of(items_ref[0, n] * block, block)
    wanted = items_ref[1, n] * LANES
    start = pl.multiple_of(jnp.minimum(wanted, keys - tile), LANES)
    at = pl.ds(begin, block)
    pos = start + lax.broadcasted_iota(jnp.int32, (1, tile), 1)
    ids_k = jnp.where(pos >= wanted, idk_ref[:, pl.ds(start, tile)], -1)
    allowed = ids_q[at, :1] == ids_k
    if causal:
        allowed &= pos <= begin + lax.broadcasted_iota(jnp.int32, (block, 1), 0)
    return at, pl.ds(start, tile), jnp.where(allowed, 0.0, masked_score).astype(f32)


def attend(items_ref, idk_ref, ids_q, q_all, k_all, vx_all, top, tot, acc, tile, block, causal):
    keys, width = k_all.shape
    pairs = width // LANES
    heads = 2 * pairs
    low = lane_below(block)
    top[...] = jnp.full(top.shape, masked_score, f32)
    tot[...] = jnp.zeros(tot.shape, f32)
    acc[...] = jnp.zeros(acc.shape, f32)

    def some(i, _):
        loads, made = [], []
        for t in range(EACH[0]):
            at, there, bias = item_at(items_ref, EACH[0] * i + t, idk_ref, ids_q, keys, tile, block, causal)
            loads.append((at, there, bias))
            for p in range(pairs):
                cols = slice(p * LANES, (p + 1) * LANES)
                part = q_all[at, cols]
                both = jnp.concatenate([head_part(part, h, low) for h in range(2)])
                made.append(mm(both, k_all[there, cols], NT))
        weights, scales = [], []
        for t, (at, there, bias) in enumerate(loads):
            for head in range(heads):
                s = made[t * pairs + head // 2][head % 2 * block : (head % 2 + 1) * block] + bias
                old = top[head, at, :]
                new = jnp.maximum(old, jnp.max(s, axis=1, keepdims=True))
                top[head, at, :] = new
                scales.append(jnp.exp(old - new))
                weights.append(jnp.exp(s - jnp.concatenate([new] * (tile // LANES), axis=1)).astype(bf16))
        mixed = [
            mm(jnp.concatenate(weights[t * heads + 2 * p : t * heads + 2 * p + 2]), vx_all[there, 2 * p * LANES : 2 * (p + 1) * LANES])
            for t, (_, there, _) in enumerate(loads) for p in range(pairs)
        ]
        for t, (at, _, _) in enumerate(loads):
            for p in range(pairs):
                n = t * pairs + p
                scale = jnp.where(low, scales[2 * n], scales[2 * n + 1])
                o = mixed[n]
                acc[p, at, :] = acc[p, at, :] * scale + jnp.where(low, o[:block, :LANES], o[block:, :LANES])
                tot[p, at, :] = tot[p, at, :] * scale + jnp.where(low, o[:block, LANES:], o[block:, LANES:])
        return 0

    lax.fori_loop(0, items_ref[2, 0], some, 0)


def attend_back(items_ref, idk_ref, ids_q, q_all, do_ref, k_ref, v_ref, l_ref, delta_ref, dq, dk, dv, tile, block, first_head, causal, each):
    keys, width = k_ref.shape
    pairs = width // LANES
    low = lane_below(block)

    def some(i, _):
        loads, scores, grads = [], [], []
        for t in range(each):
            at, there, bias = item_at(items_ref, each * i + t, idk_ref, ids_q, keys, tile, block, causal)
            loads.append((at, there, bias))
            for p in range(pairs):
                cols = slice(p * LANES, (p + 1) * LANES)
                q, do = q_all[at, cols], do_ref[at, cols]
                qs = jnp.concatenate([head_part(q, h, low) for h in range(2)])
                dos = jnp.concatenate([head_part(do, h, low) for h in range(2)])
                scores.append((mm(qs, k_ref[there, cols], NT), qs))
                grads.append((mm(dos, v_ref[there, cols], NT), dos))
        weights, slopes = [], []
        for t, (at, there, bias) in enumerate(loads):
            logs, deltas = l_ref[at, :], delta_ref[at, :]
            for p in range(pairs):
                es, ds = [], []
                for h in range(2):
                    lane = column_at(first_head + 2 * p + h)
                    rows = slice(h * block, (h + 1) * block)
                    e = jnp.exp(scores[t * pairs + p][0][rows] + bias - logs[:, lane : lane + 1])
                    es.append(e.astype(bf16))
                    ds.append((e * (grads[t * pairs + p][0][rows] - deltas[:, lane : lane + 1])).astype(bf16))
                weights.append(jnp.concatenate(es))
                slopes.append(jnp.concatenate(ds))
        for t, (at, there, _) in enumerate(loads):
            for p in range(pairs):
                cols = slice(p * LANES, (p + 1) * LANES)
                n = t * pairs + p
                gq = mm(slopes[n], k_ref[there, cols])
                gk = mm(slopes[n], scores[n][1], TN)
                gv = mm(weights[n], grads[n][1], TN)
                dq[at, cols] += jnp.where(low, gq[:block], gq[block:])
                dk[there, cols] += gk
                dv[there, cols] += gv
        return 0

    lax.fori_loop(0, items_ref[2, EACH.index(each)], some, 0)


def self_forward_kernel(tile, block, items_ref, x_ref, wq_ref, wk_ref, wv_ref, idr_ref, *rest):
    q_ref, k_ref, v_ref, o_ref, l_ref, q_all, k_all, vx_all, ids_all, top, tot, acc = rest[-12:]
    step = pl.program_id(0)
    rows = x_ref.shape[0]
    total, width = k_all.shape
    turns = total // rows

    @pl.when(step < turns)
    def _():
        x = x_ref[...]
        q = mm(x, wq_ref[0]).astype(bf16)
        k = mm(x, wk_ref[0]).astype(bf16)
        v = mm(x, wv_ref[0]).astype(bf16)
        q_ref[...] = q
        k_ref[...] = k
        v_ref[...] = v
        here = pl.ds(pl.multiple_of(step * rows, rows), rows)
        q_all[here, :] = q * jnp.asarray(HD ** -0.5, bf16)
        k_all[here, :] = k
        vx_all[here, :] = values_with_ones(v)
        ids_all[here, :] = column_of(idr_ref[:, here])

    @pl.when(step == turns)
    def _():
        attend(items_ref, idr_ref, ids_all, q_all, k_all, vx_all, top, tot, acc, tile, block, True)
        size = 2 * block
        for j in range(total // size):
            at = slice(j * size, (j + 1) * size)

            def write(p, value):
                o_ref[at, p * LANES : (p + 1) * LANES] = value

            l_ref[at, :] = finish_heads(at, top, tot, acc, write)


def whole(a):
    return pl.BlockSpec(a.shape, lambda *_: (0,) * a.ndim)


def once(a):
    return pl.BlockSpec(a.shape, lambda *_: (0,) * a.ndim, pipeline_mode=pl.Buffered(1))


def part(weights, index, columns, half):
    return pl.BlockSpec((1, weights.shape[1], columns), lambda *_: (index, 0, half))


def params(us, vmem):
    return dict(
        compiler_params=pltpu.CompilerParams(vmem_limit_bytes=vmem * 2**20),
        cost_estimate=pl.CostEstimate(flops=us * 10**9, bytes_accessed=2**20, transcendentals=0),
    )


apart = pl.BlockSpec(memory_space=pl.ANY)


def out_array(shape, dtype):
    return pltpu.HBM(shape, dtype)


def placed(*arrays):
    return [pltpu.with_memory_space_constraint(a, pltpu.HBM) for a in arrays]


def self_forward(items, x, weights, idr, after, turns=2, block=QROWS, tile=256):
    total, width = x.shape
    heads = width // HD
    rows = total // turns
    early = lambda w: pl.BlockSpec((rows, w), lambda i, *_: (jnp.minimum(i, turns - 1), 0))
    fixed = lambda w: pl.BlockSpec((total, w), lambda i, *_: (0, 0))
    sds = out_array
    full = sds((total, width), bf16)
    return pl.pallas_call(
        functools.partial(self_forward_kernel, tile, block),
        grid_spec=pltpu.PrefetchScalarGridSpec(
            num_scalar_prefetch=1,
            grid=(turns + 1,),
            in_specs=[early(width)] + [part(weights, i, width, 0) for i in range(3)] + [whole(idr)] + [apart] * len(after),
            out_specs=[early(width)] * 3 + [fixed(width), fixed(LANES)],
            scratch_shapes=[
                pltpu.VMEM((total, width), bf16), pltpu.VMEM((total, width), bf16), pltpu.VMEM((total, 2 * width), bf16),
                pltpu.VMEM((total, LANES), jnp.int32),
                pltpu.VMEM((heads, total, LANES), f32), pltpu.VMEM((heads // 2, total, LANES), f32), pltpu.VMEM((heads // 2, total, LANES), f32),
            ],
        ),
        out_shape=[full] * 4 + [sds((total, LANES), f32)],
        name="self_forward",
        **params(13, 26),
    )(items, *placed(x), weights, weights, weights, idr, *after)


def cross_forward_kernel(
    tile, block, items_ref, memory_ref, wk_ref, wv_ref, x_ref, o1_ref, wso_ref, wcq_ref, norms_ref, idr_ref, idk_ref, *rest
):
    k2_ref, v2_ref, r1_ref, h1b_ref, q2_ref, h1_ref, o_ref, l_ref, k_all, vx_all, q_all, ids_all, top, tot, acc = rest[-15:]
    step = pl.program_id(0)
    rows, width = x_ref.shape
    keys = k_all.shape[0]
    turns = pl.num_programs(0) - 1

    @pl.when(step < turns)
    def _():
        per = memory_ref.shape[0]
        memory = memory_ref[...]
        r1 = x_ref[...].astype(f32) + mm(o1_ref[...], wso_ref[0])
        k2 = mm(memory, wk_ref[0]).astype(bf16)
        r1_ref[...] = r1.astype(bf16)
        n1, _ = norm_rows(r1)
        v2 = mm(memory, wv_ref[0]).astype(bf16)
        h1 = n1 * norms_ref[0:1, :] + norms_ref[1:2, :]
        h1b = h1.astype(bf16)
        h1b_ref[...] = h1b
        q2 = mm(h1b, wcq_ref[0]).astype(bf16)
        q2_ref[...] = q2
        k2_ref[...] = k2
        v2_ref[...] = v2
        here = pl.ds(pl.multiple_of(step * rows, rows), rows)
        q_all[here, :] = q2 * jnp.asarray(HD ** -0.5, bf16)
        h1_ref[...] = h1
        ids_all[here, :] = column_of(idr_ref[:, here])
        there = pl.ds(pl.multiple_of(step * per, per), per)
        k_all[there, :] = k2
        vx_all[there, :] = values_with_ones(v2)

    @pl.when(step == turns)
    def _():
        attend(items_ref, idk_ref, ids_all, q_all, k_all, vx_all, top, tot, acc, tile, block, False)

        size = 2 * block
        for j in range(q_all.shape[0] // size):
            at = slice(j * size, (j + 1) * size)

            def write(p, value):
                o_ref[at, p * LANES : (p + 1) * LANES] = value

            l_ref[at, :] = finish_heads(at, top, tot, acc, write)


def cross_forward(items, memory, x, o1, weights, norms, idr, idk, after, turns=2, block=QROWS, tile=256):
    total, width = x.shape
    keys = memory.shape[0]
    heads = width // HD
    rows, per = total // turns, keys // turns
    early = lambda r, w: pl.BlockSpec((r, w), lambda i, *_: (jnp.minimum(i, turns - 1), 0))
    fixed = lambda w: pl.BlockSpec((total, w), lambda i, *_: (0, 0))
    sds = out_array
    return pl.pallas_call(
        functools.partial(cross_forward_kernel, tile, block),
        grid_spec=pltpu.PrefetchScalarGridSpec(
            num_scalar_prefetch=1,
            grid=(turns + 1,),
            in_specs=[early(per, width), part(weights, 2, width, 0), part(weights, 3, width, 0)]
            + [early(rows, width), early(rows, width), part(weights, 0, width, 0), part(weights, 1, width, 0)]
            + [whole(norms), whole(idr), whole(idk)] + [apart] * len(after),
            out_specs=[early(per, width)] * 2 + [early(rows, width)] * 4 + [fixed(width), fixed(LANES)],
            scratch_shapes=[
                pltpu.VMEM((keys, width), bf16),
                pltpu.VMEM((keys, 2 * width), bf16),
                pltpu.VMEM((total, width), bf16),
                pltpu.VMEM((total, LANES), jnp.int32),
                pltpu.VMEM((heads, total, LANES), f32),
                pltpu.VMEM((heads // 2, total, LANES), f32),
                pltpu.VMEM((heads // 2, total, LANES), f32),
            ],
        ),
        out_shape=[
            sds((keys, width), bf16), sds((keys, width), bf16), sds((total, width), bf16), sds((total, width), bf16),
            sds((total, width), bf16), sds((total, width), f32), sds((total, width), bf16), sds((total, LANES), f32),
        ],
        name="cross_forward",
        **params(19, 38),
    )(items, *placed(memory), weights, weights, *placed(x, o1), weights, weights, norms, idr, idk, *after)


def norm_back(incoming, normal, rstd, gain):
    m = incoming * gain
    return rstd * (
        m - jnp.mean(m, axis=-1, keepdims=True) - normal * jnp.mean(m * normal, axis=-1, keepdims=True)
    )


def head_columns(left, right):
    width = left.shape[1]
    prod = left.astype(f32) * right.astype(f32)
    lane = lax.broadcasted_iota(jnp.int32, (width, LANES), 1)
    own = lax.broadcasted_iota(jnp.int32, (width, LANES), 0) // HD == 2 * (lane % HD) + lane // HD
    own = own.astype(bf16)
    high = prod.astype(bf16)
    low = (prod - high.astype(f32)).astype(bf16)
    return mm(high, own) + mm(low, own)


def column_sums(a):
    return jnp.sum(a, axis=0, keepdims=True)


def spread(keep_ref, send_ref, core, write):
    def one(j, _):
        write(2 * j + core, keep_ref, j)
        write(2 * j + 1 - core, send_ref, j)
        return 0

    lax.fori_loop(0, keep_ref.shape[0], one, 0)


def ffn_kernel(
    core_ref, here_ref, h1_ref, x_ref, cot_ref, o2_ref, norms_ref, *rest
):
    count = len(rest) - 11
    pieces = 8 if count >= 8 else 2
    weights, rest = rest[:pieces], rest[pieces:]
    out_ref, dr3_ref, dr2_ref, do2_ref, delta_ref, keep_ref, send_ref, gn_ref, gin, gout, gco = rest[:11]
    wa_ref, wb_ref = rest[11:] if pieces == 8 else weights
    step = pl.program_id(0)
    last = pl.num_programs(0) - 1
    width = x_ref.shape[1]
    share = width // wb_ref.shape[0]
    blocks = wb_ref.shape[1] // share

    @pl.when(step == 0)
    def _():
        if pieces == 8:
            bits = here_ref[0], here_ref[1]
            for n, (ref, axis) in enumerate(((wa_ref, 1), (wb_ref, 0))):
                for m in range(4):
                    across, core = bits[axis] ^ (m % 2), here_ref[2] ^ (m // 2)
                    piece = weights[4 * n + m]
                    for z in range(piece.shape[0]):
                        for other in range(2):
                            planes = (across, other) if axis else (other, across)
                            ref[z * 8 + planes[0] * 4 + planes[1] * 2 + core] = piece[z, other]
        gin[...] = jnp.zeros_like(gin)
        gout[...] = jnp.zeros_like(gout)
        gco[...] = jnp.zeros_like(gco)
        gn_ref[...] = jnp.zeros_like(gn_ref)

    win = [wa_ref[:, c * share : (c + 1) * share].reshape(width, width) for c in range(blocks)]
    wout = wb_ref[...].reshape(blocks * width, width)
    wco = wa_ref[:, blocks * share :].reshape(width, width)
    n2, rstd2 = norm_rows(h1_ref[...] + mm(o2_ref[...], wco))
    h2 = n2 * norms_ref[2:3, :] + norms_ref[3:4, :]
    h2b = h2.astype(bf16)
    chunk = min(FFN_CHUNK, width)
    parts = blocks * width // chunk
    per = width // chunk

    def win_part(c):
        return win[c // per][:, (c % per) * chunk : (c % per + 1) * chunk]

    acts, slopes, hidden = [], [], [mm(h2b, win_part(0))]
    ff = jnp.zeros(h2.shape, f32)
    for c in range(parts):
        if c + 1 < parts:
            hidden.append(mm(h2b, win_part(c + 1)))
        u = hidden[c]
        square = u * u
        t = jnp.tanh(u * (0.7978845608028654 + (0.7978845608028654 * 0.044715) * square))
        half = 0.5 + 0.5 * t
        acts.append((u * half).astype(bf16))
        rise = u * (0.5 * 0.7978845608028654 + (0.5 * 0.7978845608028654 * 3 * 0.044715) * square)
        slopes.append(half + (1.0 - t * t) * rise)
        if c:
            ff += mm(acts[c - 1], wout[(c - 1) * chunk : c * chunk, :])
    ff += mm(acts[-1], wout[(parts - 1) * chunk :, :])
    r3 = h2 + ff + x_ref[...].astype(f32)
    n3, rstd3 = norm_rows(r3)
    gain3 = norms_ref[4:5, :]
    out_ref[...] = (n3 * gain3 + norms_ref[5:6, :]).astype(bf16)
    e = cot_ref[...].astype(f32)
    gn_ref[2:3, :] += column_sums(e * n3)
    gn_ref[3:4, :] += column_sums(e)
    dr3 = norm_back(e, n3, rstd3, gain3)
    dr3_ref[...] = dr3.astype(bf16)
    dfb = dr3.astype(bf16)
    dh2 = dr3
    raw, made = [mm(dfb, wout[:chunk, :], NT)], []
    for c in range(parts + 1):
        if c + 1 < parts:
            raw.append(mm(dfb, wout[(c + 1) * chunk : (c + 2) * chunk, :], NT))
        if c < parts:
            gout[c * chunk : (c + 1) * chunk, :] += mm(acts[c], dfb, TN)
            made.append((raw[c] * slopes[c]).astype(bf16))
        if c:
            gin[:, (c - 1) * chunk : c * chunk] += mm(h2b, made[c - 1], TN)
            dh2 += mm(made[c - 1], win_part(c - 1), NT)
    gn_ref[0:1, :] += column_sums(dh2 * n2)
    gn_ref[1:2, :] += column_sums(dh2)
    dr2 = norm_back(dh2, n2, rstd2, norms_ref[2:3, :])
    da2 = dr2.astype(bf16)
    dr2_ref[...] = da2
    o2 = o2_ref[...]
    gco[...] += mm(o2, da2, TN)
    do2 = mm(da2, wco, NT).astype(bf16)
    do2_ref[...] = do2
    delta_ref[...] = head_columns(do2, o2)

    @pl.when(step == last)
    def _():
        r = keep_ref.shape[2]

        def write(device, ref, j):
            here = pl.ds(pl.multiple_of(device * r, r), r)
            for c in range(blocks):
                ref[j, c] = gin[here, c * width : (c + 1) * width].astype(bf16)
            ref[j, blocks] = gco[here, :].astype(bf16)
            there = pl.ds(pl.multiple_of(device * blocks * r, blocks * r), blocks * r)
            ref[j, blocks + 1 :] = gout[there, :].astype(bf16).reshape(blocks, r, width)

        spread(keep_ref, send_ref, core_ref[0], write)


def ffn(core, here, pairs, h1, x, cot, o2, weights, norms, rows=256):
    total, width = x.shape
    devices = 1 if len(weights) == 2 else 2 * pairs
    blocks = weights[-1].size // width**2 if devices == 1 else 8 * weights[-1].size // (2 * width**2)
    held = [(devices, (blocks + 1) * width // devices, width), (devices, blocks * width // devices, width)]
    rowspec = lambda w: pl.BlockSpec((rows, w), lambda i: (i, 0))
    smem = pl.BlockSpec(memory_space=pltpu.SMEM)
    sds = out_array
    side = jax.ShapeDtypeStruct((pairs, 2 * blocks + 1, width // (2 * pairs), width), bf16)
    return pl.pallas_call(
        ffn_kernel,
        grid=(total // rows,),
        in_specs=[smem, smem] + [rowspec(width)] * 4 + [whole(norms)] + [once(w) for w in weights],
        out_specs=[rowspec(width)] * 4 + [rowspec(LANES), whole(side), whole(side), pl.BlockSpec((4, width), lambda i: (0, 0))],
        out_shape=[
            sds((total, width), bf16), sds((total, width), bf16), sds((total, width), bf16), sds((total, width), bf16),
            sds((total, LANES), f32), side, side, sds((4, width), f32),
        ],
        scratch_shapes=[pltpu.VMEM((width, blocks * width), f32), pltpu.VMEM((blocks * width, width), f32), pltpu.VMEM((width, width), f32)]
        + ([pltpu.VMEM(h, bf16) for h in held] if devices > 1 else []),
        name="ffn",
        **params(32, 43),
    )(core, here, *placed(h1, x, cot, o2), norms, *weights)


def cross_backward_kernel(
    tile, block, first, count, each, items_ref, q2_ref, k2_ref, v2_ref, do_ref, l_ref, delta_ref, idr_ref, idk_ref, memory_ref, *rest
):
    dq_ref, dk_ref, dv_ref, grads_ref, q_all, ids_all, dq, dk, dv, grads = rest[-10:]
    step = pl.program_id(0)
    total = q2_ref.shape[0]
    begin = first * LANES if q2_ref.shape[1] > count * LANES else 0
    cols = slice(begin, begin + count * LANES)

    @pl.when(step == 0)
    def _():
        dq[...] = jnp.zeros_like(dq)
        dk[...] = jnp.zeros_like(dk)
        dv[...] = jnp.zeros_like(dv)
        grads[...] = jnp.zeros_like(grads)
        q_all[...] = q2_ref[:, cols] * jnp.asarray(HD ** -0.5, bf16)
        for j in range(total // block):
            ids_all[j * block : (j + 1) * block, :] = column_of(idr_ref[:, j * block : (j + 1) * block])
        attend_back(
            items_ref, idk_ref, ids_all, q_all, do_ref.at[:, cols], k2_ref.at[:, cols], v2_ref.at[:, cols], l_ref, delta_ref,
            dq, dk, dv, tile, block, 2 * first, False, each,
        )

    memory = memory_ref[...]
    per = memory.shape[0]
    here = pl.ds(pl.multiple_of(step * per, per), per)
    for i, (ref, out_ref) in enumerate(((dk, dk_ref), (dv, dv_ref))):
        grad = ref[here, :].astype(bf16)
        out_ref[...] = grad
        grads[i] += mm(memory, grad, TN)
    rows = dq_ref.shape[0]
    dq_ref[...] = (dq[pl.ds(pl.multiple_of(step * rows, rows), rows), :] * HD ** -0.5).astype(bf16)

    @pl.when(step == pl.num_programs(0) - 1)
    def _():
        grads_ref[...] = grads[...].astype(bf16)


def cross_backward(items, q2, k2, v2, do, l, delta, idr, idk, memory, first, count, each, after, turns=2, block=QROWS, tile=256):
    total, width = q2.shape
    keys = k2.shape[0]
    columns = count * LANES
    alone = first % count == 0
    cols = lambda r: pl.BlockSpec((r, columns if alone else width), lambda i, *_: (0, first // count if alone else 0))
    rowspec = lambda r, w: pl.BlockSpec((r, w), lambda i, *_: (i, 0))
    sds = jax.ShapeDtypeStruct
    grad = sds((2, width, columns), bf16)
    return pl.pallas_call(
        functools.partial(cross_backward_kernel, tile, block, first, count, each),
        grid_spec=pltpu.PrefetchScalarGridSpec(
            num_scalar_prefetch=1,
            grid=(turns,),
            in_specs=[cols(total), cols(keys), cols(keys), cols(total)]
            + [whole(l), whole(delta), whole(idr), whole(idk), rowspec(keys // turns, width)] + [apart] * len(after),
            out_specs=[rowspec(total // turns, columns), rowspec(keys // turns, columns), rowspec(keys // turns, columns), whole(grad)],
            scratch_shapes=[
                pltpu.VMEM((total, columns), bf16), pltpu.VMEM((total, LANES), jnp.int32), pltpu.VMEM((total, columns), f32),
                pltpu.VMEM((keys, columns), f32), pltpu.VMEM((keys, columns), f32), pltpu.VMEM((2, width, columns), f32),
            ],
        ),
        out_shape=[sds((total, columns), bf16), sds((keys, columns), bf16), sds((keys, columns), bf16), grad],
        name="cross_backward",
        **params(5 * count + 4, 10 * count + 4),
    )(items, *placed(q2, k2, v2, do, l, delta), idr, idk, *placed(memory), *after)


def memory_grad_kernel(ka_ref, kb_ref, va_ref, vb_ref, wk_ref, wv_ref, *rest):
    total = mm(jnp.concatenate([ka_ref[...], kb_ref[...]], axis=1), wk_ref[0], NT)
    total += mm(jnp.concatenate([va_ref[...], vb_ref[...]], axis=1), wv_ref[0], NT)
    rest[-1][...] = total.astype(bf16)


def memory_grad(ka, kb, va, vb, weights, index, after, rows=1024):
    keys, width = ka.shape[0], weights.shape[2]
    rowspec = lambda w: pl.BlockSpec((rows, w), lambda i: (i, 0))
    return pl.pallas_call(
        memory_grad_kernel,
        grid=(keys // rows,),
        in_specs=[rowspec(a.shape[1]) for a in (ka, kb, va, vb)] + [part(weights, index, width, 0), part(weights, index + 1, width, 0)] + [apart] * len(after),
        out_specs=rowspec(width),
        out_shape=out_array((keys, width), bf16),
        name="memory_grad",
        **params(4, 16),
    )(ka, kb, va, vb, weights, weights, *after)


def between_kernel(
    core_ref, ga_ref, gb_ref, gn23_ref, r1_ref, dr2_ref, dr3_ref, dqa_ref, dqb_ref, h1b_ref, o1_ref, wso_ref, wcq_ref, norms_ref, *rest
):
    dsum_ref, do1_ref, delta_ref, keep_ref, send_ref, gn_ref, total = rest[-7:]
    step = pl.program_id(0)

    @pl.when(step == 0)
    def _():
        total[...] = jnp.zeros_like(total)
        gn_ref[...] = jnp.zeros_like(gn_ref)

    dq2 = jnp.concatenate([dqa_ref[...], dqb_ref[...]], axis=1)
    dh1 = dr2_ref[...].astype(f32) + mm(dq2, wcq_ref[0], NT)
    n1, rstd1 = norm_rows(r1_ref[...].astype(f32))
    gn_ref[0:1, :] += column_sums(dh1 * n1)
    gn_ref[1:2, :] += column_sums(dh1)
    dr1 = norm_back(dh1, n1, rstd1, norms_ref[0:1, :])
    dsum_ref[...] = (dr1 + dr3_ref[...].astype(f32)).astype(bf16)
    da1 = dr1.astype(bf16)
    o1 = o1_ref[...]
    do1 = mm(da1, wso_ref[0], NT).astype(bf16)
    do1_ref[...] = do1
    delta_ref[...] = head_columns(do1, o1)
    total[0] += mm(h1b_ref[...], dq2, TN)
    total[1] += mm(o1, da1, TN)

    @pl.when(step == pl.num_programs(0) - 1)
    def _():
        gn_ref[2:6, :] = gn23_ref[...]
        r, width = keep_ref.shape[2:]
        norm_part = jnp.concatenate([gn_ref[...], jnp.zeros((r - 8, width), f32)]).astype(bf16)

        def write(device, ref, j):
            here = pl.ds(pl.multiple_of(device * r, r), r)
            for i in range(2):
                ref[j, i, :, : ga_ref.shape[2]] = ga_ref[i, here, :]
                ref[j, i, :, ga_ref.shape[2] :] = gb_ref[i, here, :]
                ref[j, 2 + i] = total[i, here, :].astype(bf16)
            ref[j, 4] = norm_part

        spread(keep_ref, send_ref, core_ref[0], write)


def between(core, pairs, ga, gb, gn23, r1, dr2, dr3, dqa, dqb, h1b, o1, weights, norms, after, rows=512):
    total, width = r1.shape
    rowspec = lambda w: pl.BlockSpec((rows, w), lambda i: (i, 0))
    sds = jax.ShapeDtypeStruct
    side = jax.ShapeDtypeStruct((pairs, 5, width // (2 * pairs), width), bf16)
    return pl.pallas_call(
        between_kernel,
        grid=(total // rows,),
        in_specs=[pl.BlockSpec(memory_space=pltpu.SMEM), whole(ga), whole(gb), whole(gn23)]
        + [rowspec(width)] * 3 + [rowspec(dqa.shape[1]), rowspec(dqb.shape[1])] + [rowspec(width)] * 2
        + [part(weights, 0, width, 0), part(weights, 1, width, 0), whole(norms)] + [apart] * len(after),
        out_specs=[rowspec(width)] * 2
        + [rowspec(LANES), whole(side), whole(side), pl.BlockSpec((8, width), lambda i: (0, 0))],
        out_shape=[sds((total, width), bf16), sds((total, width), bf16), sds((total, LANES), f32), side, side, sds((8, width), f32)],
        scratch_shapes=[pltpu.VMEM((2, width, width), f32)],
        name="between",
        **params(7, 24),
    )(core, ga, gb, gn23, *placed(r1), dr2, dr3, dqa, dqb, *placed(h1b, o1), weights, weights, norms, *after)


def self_backward_kernel(
    tile, block, core_ref, items_ref, q_ref, k_ref, v_ref, do_ref, l_ref, delta_ref, idr_ref, x_ref, wq_ref, wk_ref, wv_ref, sofar_ref, *rest
):
    gx_ref, keep_ref, send_ref, q_all, ids_all, dq, dk, dv, grads = rest[-9:]
    step = pl.program_id(0)
    total, width = q_ref.shape

    @pl.when(step == 0)
    def _():
        dq[...] = jnp.zeros_like(dq)
        dk[...] = jnp.zeros_like(dk)
        dv[...] = jnp.zeros_like(dv)
        grads[...] = jnp.zeros_like(grads)
        q_all[...] = q_ref[...] * jnp.asarray(HD ** -0.5, bf16)
        for j in range(total // block):
            ids_all[j * block : (j + 1) * block, :] = column_of(idr_ref[:, j * block : (j + 1) * block])
        attend_back(
            items_ref, idr_ref, ids_all, q_all, do_ref, k_ref, v_ref, l_ref, delta_ref, dq, dk, dv, tile, block, 0, True, 2
        )

    x = x_ref[...]
    rows = x.shape[0]
    here = pl.ds(pl.multiple_of(step * rows, rows), rows)
    gx = sofar_ref[...].astype(f32)
    parts = (dq[here, :] * HD ** -0.5).astype(bf16), dk[here, :].astype(bf16), dv[here, :].astype(bf16)
    for i, (grad, w_ref) in enumerate(zip(parts, (wq_ref, wk_ref, wv_ref))):
        gx += mm(grad, w_ref[0], NT)
        grads[i] += mm(x, grad, TN)
    gx_ref[...] = gx.astype(bf16)

    @pl.when(step == pl.num_programs(0) - 1)
    def _():
        r = keep_ref.shape[2]

        def write(device, ref, j):
            place = pl.ds(pl.multiple_of(device * r, r), r)
            for i in range(3):
                ref[j, i] = grads[i, place, :].astype(bf16)

        spread(keep_ref, send_ref, core_ref[0], write)


def self_backward(core, pairs, items, q, k, v, do, l, delta, idr, x, weights, sofar, after, turns=2, block=QROWS, tile=256):
    total, width = x.shape
    sds = jax.ShapeDtypeStruct
    side = sds((pairs, 3, width // (2 * pairs), width), bf16)
    rowspec = lambda w: pl.BlockSpec((total // turns, w), lambda i, *_: (i, 0))
    return pl.pallas_call(
        functools.partial(self_backward_kernel, tile, block),
        grid_spec=pltpu.PrefetchScalarGridSpec(
            num_scalar_prefetch=2,
            grid=(turns,),
            in_specs=[whole(a) for a in (q, k, v, do, l, delta, idr)]
            + [rowspec(width)] + [part(weights, i, width, 0) for i in range(3)] + [rowspec(width)] + [apart] * len(after),
            out_specs=[rowspec(width), whole(side), whole(side)],
            scratch_shapes=[
                pltpu.VMEM((total, width), bf16), pltpu.VMEM((total, LANES), jnp.int32),
                pltpu.VMEM((total, width), f32), pltpu.VMEM((total, width), f32), pltpu.VMEM((total, width), f32),
                pltpu.VMEM((3, width, width), f32),
            ],
        ),
        out_shape=[sds((total, width), bf16), side, side],
        name="self_backward",
        **params(17, 26),
    )(core, items, q, k, v, do, l, delta, idr, x, weights, weights, weights, sofar, *after)


def add_split_kernel(count, here_ref, *refs):
    places = refs[0].shape[1]
    for m in range(places):
        at = here_ref[0] ^ m
        total = refs[0][:, at].astype(f32)
        for ref in refs[1:count]:
            total += ref[:, at].astype(f32)
        refs[count + m][...] = total.astype(bf16)


def add_split(here, parts, outer, places):
    tail = parts[0].shape[1:]
    parts = [p.reshape((outer, places) + tail) for p in parts]
    out = pl.pallas_call(
        functools.partial(add_split_kernel, len(parts)),
        grid=(outer,),
        in_specs=[pl.BlockSpec(memory_space=pltpu.SMEM)] + [pl.BlockSpec((1, places) + tail, lambda i: (i, 0, 0, 0, 0))] * len(parts),
        out_specs=[pl.BlockSpec((1,) + tail, lambda i: (i, 0, 0, 0))] * places,
        out_shape=[jax.ShapeDtypeStruct((outer,) + tail, bf16)] * places,
        name="add_split",
        **params(3, 24),
    )(here, *parts)
    return list(out)


def first_pair_kernel(cut, here_ref, keep, came, *outs):
    for m in range(2):
        at = here_ref[0] ^ m
        outs[m][0] = (keep[0, :, at, :cut].astype(f32) + came[0, :, at, :cut].astype(f32)).astype(bf16)
        at = here_ref[1] ^ m
        outs[2 + m][0] = (keep[0, at, :, cut:].astype(f32) + came[0, at, :, cut:].astype(f32)).astype(bf16)


def first_pair(here, keep, came, outer, cut):
    squares, rows, width = keep.shape[1:]
    parts = [p.reshape(outer, 2, 2, squares, rows, width) for p in (keep, came)]
    shapes = [(outer, 2, n, rows, width) for n in (cut, cut, squares - cut, squares - cut)]
    out = pl.pallas_call(
        functools.partial(first_pair_kernel, cut),
        grid=(outer,),
        in_specs=[pl.BlockSpec(memory_space=pltpu.SMEM)] + [pl.BlockSpec((1,) + p.shape[1:], lambda i: (i, 0, 0, 0, 0, 0)) for p in parts],
        out_specs=[pl.BlockSpec((1,) + s[1:], lambda i: (i, 0, 0, 0, 0)) for s in shapes],
        out_shape=[jax.ShapeDtypeStruct(s, bf16) for s in shapes],
        name="first_pair",
        **params(2, 24),
    )(here, *parts)
    return list(out)


def second_pair_kernel(here_ref, keep_a, came_a, keep_b, came_b, *outs):
    for m in range(2):
        at = here_ref[1] ^ m
        outs[m][0] = (keep_a[0, at].astype(f32) + came_a[0, at].astype(f32)).astype(bf16)
        at = here_ref[0] ^ m
        outs[2 + m][0] = (keep_b[0, at].astype(f32) + came_b[0, at].astype(f32)).astype(bf16)


def second_pair(here, parts):
    outer = parts[0].shape[0]
    shapes = [(p.shape[0],) + p.shape[2:] for p in parts]
    out = pl.pallas_call(
        second_pair_kernel,
        grid=(outer,),
        in_specs=[pl.BlockSpec(memory_space=pltpu.SMEM)] + [pl.BlockSpec((1,) + p.shape[1:], lambda i: (i, 0, 0, 0, 0)) for p in parts],
        out_specs=[pl.BlockSpec((1,) + s[1:], lambda i: (i, 0, 0, 0)) for s in shapes],
        out_shape=[jax.ShapeDtypeStruct(s, bf16) for s in shapes],
        name="second_pair",
        **params(1, 24),
    )(here, *parts)
    return list(out)


def join_split_kernel(here_ref, keep_a, came_a, keep_b, came_b, *outs):
    cut = keep_a.shape[2]
    for m, out in enumerate(outs):
        at = here_ref[0] ^ m
        out[:, :cut] = (keep_a[:, at].astype(f32) + came_a[:, at].astype(f32)).astype(bf16)
        out[:, cut:] = (keep_b[:, at].astype(f32) + came_b[:, at].astype(f32)).astype(bf16)


def join_split(here, parts, outer, places):
    parts = [p.reshape((outer, places) + p.shape[1:]) for p in parts]
    tail = (parts[0].shape[2] + parts[2].shape[2],) + parts[0].shape[3:]
    out = pl.pallas_call(
        join_split_kernel,
        grid=(outer,),
        in_specs=[pl.BlockSpec(memory_space=pltpu.SMEM)] + [pl.BlockSpec((1,) + p.shape[1:], lambda i: (i, 0, 0, 0, 0)) for p in parts],
        out_specs=[pl.BlockSpec((1,) + tail, lambda i: (i, 0, 0, 0))] * places,
        out_shape=[jax.ShapeDtypeStruct((outer,) + tail, bf16)] * places,
        name="join_split",
        **params(1, 24),
    )(here, *parts)
    return list(out)


def place_kernel(here_ref, *refs):
    out_ref = refs[-1]
    for m, ref in enumerate(refs[:-1]):
        out_ref[0, :, here_ref[0] ^ m] = ref[0]


def place(here, pieces):
    shape = pieces[0].shape
    pieces = [p.reshape((shape[0], -1) + shape[-2:]) for p in pieces]
    count, tail = len(pieces), pieces[0].shape[2:]
    inner = pieces[0].shape[1]
    out = pl.pallas_call(
        place_kernel,
        grid=(shape[0],),
        in_specs=[pl.BlockSpec(memory_space=pltpu.SMEM)] + [pl.BlockSpec((1, inner) + tail, lambda i: (i, 0, 0, 0))] * count,
        out_specs=pl.BlockSpec((1, inner, count) + tail, lambda i: (i, 0, 0, 0, 0)),
        out_shape=jax.ShapeDtypeStruct((shape[0], inner, count) + tail, bf16),
        name="place",
        **params(1, 16),
    )(here, *pieces)
    return out.reshape(shape[:-2] + (count,) + tail)


def own_block(shape):
    return pl.BlockSpec(shape, lambda *_: (0,) * len(shape))


def pack_kernel(moves, count, *refs):
    ins, out_ref, wide = refs[:count], refs[count], refs[count + 1 :]
    rows = out_ref.shape[1]
    for ref, w in zip(ins, wide):
        w[...] = ref[...].astype(f32)
    for source, begin, step, square, block in moves:
        value = wide[source][pl.ds(begin, rows, stride=step), :]
        out_ref[square, :, block * LANES : (block + 1) * LANES] = value.astype(bf16)


def pack(arrays, moves, squares, rows, width, name):
    arrays = [a.reshape(-1, LANES) for a in arrays]
    return pl.pallas_call(
        functools.partial(pack_kernel, moves, len(arrays)),
        in_specs=[own_block(a.shape) for a in arrays],
        out_specs=own_block((squares, rows, width)),
        out_shape=jax.ShapeDtypeStruct((squares, rows, width), bf16),
        scratch_shapes=[pltpu.VMEM(a.shape, f32) for a in arrays],
        name=name,
        **params(1, 16),
    )(*placed(*arrays))


def square_moves(source, square, width):
    blocks = width // LANES
    return [(source, b, blocks, square, b) for b in range(blocks)]


def finish_kernel(moves, count, *refs):
    ins, outs = refs[:count], refs[count:]
    rows = ins[0].shape[1]
    for square, block, out, begin, step in moves:
        cols = slice(block * LANES, (block + 1) * LANES)
        total = ins[0][square, :, cols].astype(f32)
        for ref in ins[1:]:
            total += ref[square, :, cols].astype(f32)
        if step:
            outs[out][pl.ds(begin, rows, stride=step), :] = total
        else:
            outs[out][:, cols] = total


def finish(parts, moves, shapes, name):
    return pl.pallas_call(
        functools.partial(finish_kernel, moves, len(parts)),
        in_specs=[own_block(p.shape) for p in parts],
        out_specs=[own_block(s) for s in shapes],
        out_shape=[jax.ShapeDtypeStruct(s, f32) for s in shapes],
        name=name,
        **params(1, 16),
    )(*parts)


def fill_items(ref, first, high, keys, block, tile):
    filled = jnp.int32(0)
    for b in range(len(first)):
        count = (high[b] - first[b] * LANES + tile - 1) // tile

        def put(j, at, b=b):
            ref[0, at] = b
            ref[1, at] = first[b] + j * (tile // LANES)
            return at + 1

        filled = lax.fori_loop(0, count, put, filled)
    for j in range(PADDING):
        ref[0, filled + j] = len(first) - 1
        ref[1, filled + j] = keys // LANES
    for i, n in enumerate(EACH):
        ref[2, i] = (filled + n - 1) // n


def plan_kernel(block, tile, seg_ref, mem_ref, qid_ref, mid_ref, own_ref, cross_ref):
    def ends_of(ref):
        ends, total = [], jnp.int32(0)
        for i in range(ref.shape[1]):
            total += ref[0, i]
            ends.append(total)
        return ends

    ends, mem_ends = ends_of(seg_ref), ends_of(mem_ref)
    for ref, marks in ((qid_ref, ends), (mid_ref, mem_ends)):
        places = lax.broadcasted_iota(jnp.int32, ref.shape, 1)
        ids = jnp.zeros(ref.shape, jnp.int32)
        for mark in marks:
            ids += (places >= mark).astype(jnp.int32)
        ref[...] = ids
    total, keys = qid_ref.shape[1], mid_ref.shape[1]
    own, low, high = [], [], []
    for begin in range(0, total, block):
        own_first, first, last = jnp.int32(0), jnp.int32(0), mem_ref[0, 0]
        for i in range(seg_ref.shape[1]):
            passed = (ends[i] <= begin).astype(jnp.int32)
            own_first += passed * seg_ref[0, i]
            first += passed * mem_ref[0, i]
            if i + 1 < seg_ref.shape[1]:
                last += (ends[i] <= begin + block - 1).astype(jnp.int32) * mem_ref[0, i + 1]
        own.append(own_first // LANES)
        low.append(first // LANES)
        high.append(last)
    fill_items(own_ref, own, [begin + block for begin in range(0, total, block)], total, block, tile)
    fill_items(cross_ref, low, high, keys, block, tile)


def plan(seg, mem, total, keys, block=QROWS, tile=256):
    smem = pl.BlockSpec(memory_space=pltpu.SMEM)
    sds = jax.ShapeDtypeStruct
    more = PADDING
    return pl.pallas_call(
        functools.partial(plan_kernel, block, tile),
        in_specs=[smem, smem],
        out_specs=[own_block((1, total)), own_block((1, keys)), smem, smem],
        out_shape=[
            sds((1, total), jnp.int32), sds((1, keys), jnp.int32),
            sds((3, total // block * (total // tile) + more), jnp.int32), sds((3, total // block * (keys // tile) + more), jnp.int32),
        ],
        name="plan",
        **params(1, 16),
    )(seg, mem)

HEAD_START = 1


def mesh_size():
    return lax.axis_size("dp") * lax.axis_size("fsdp")


def position():
    return lax.axis_index("dp") * lax.axis_size("fsdp") + lax.axis_index("fsdp")


def bit_groups(wide):
    count = mesh_size().bit_length() - 1
    groups = [(0, 1)]
    while groups[-1][0] + groups[-1][1] < count:
        low = groups[-1][0] + groups[-1][1]
        groups.append((low, min(2 if len(groups) <= wide else 1, count - low)))
    return groups


def swap(x, mask):
    return lax.ppermute(x, ("dp", "fsdp"), [(i, i ^ mask) for i in range(mesh_size())])


def place_in(group):
    return (position() >> group[0]) & ((1 << group[1]) - 1)


def tie(x, *after):
    return lax.optimization_barrier((x, *after))[0] if after else x


def gather_step(x, group, after=(), lower=0, came=None):
    low, width = group
    here = place_in(group)
    if came is None:
        came = tie([swap(x, m << low) for m in range(1, 1 << width)], *after)
    blocks = [x] + came
    for j in range(width):
        flip = (here >> j) & 1 == 1
        blocks = [jnp.where(flip, blocks[p ^ (1 << j)], blocks[p]) for p in range(1 << width)]
    return jnp.stack(blocks, axis=x.ndim - 2 - lower)


def gathered(x):
    return x.reshape(x.shape[:1] + (-1, x.shape[-1]))


def swap_pieces(parts, group, after=()):
    return [parts[0]] + tie([swap(parts[m], m << group[0]) for m in range(1, len(parts))], *after)


def next_pieces(parts, groups, done):
    group = groups[done]
    outer = 1 << sum(g[1] for g in groups[done + 1 :])
    return add_split(place_in(group).reshape(1).astype(jnp.int32), parts, outer, 1 << group[1])


def norm_parts(norm_params, size):
    parts, left = [], norm_params
    for _ in range(3):
        part = left.astype(bf16)
        parts.append(jnp.pad(part, (0, LANES - part.size)))
        left = left - part.astype(f32)
    flat = jnp.concatenate(parts)
    return jnp.pad(flat, (0, size - flat.size))


def resplit(keep, send, devices, core, squares):
    halves = jnp.concatenate([keep, send])
    width = halves.shape[-1]
    first = halves[:, :squares].transpose(1, 0, 2, 3).reshape(squares, devices, -1, width).transpose(1, 0, 2, 3)
    rows = first.shape[2]
    if halves.shape[1] > squares:
        rest = halves[:, squares:].reshape(devices, halves.shape[1] - squares, rows, width)
        first = jnp.concatenate([first, rest], axis=1)
    both = first.reshape(devices // 2, 2, -1, rows, width)
    return [lax.dynamic_index_in_dim(both, core ^ m, 1, keepdims=False) for m in range(2)]


def body(
    inputs, memory, seg_lengths, mem_lengths, self_query, self_key, self_value, self_out,
    cross_query, cross_key, cross_value, cross_out, ffn_in, ffn_out, norm_params, cotangent,
):
    total, width = inputs.shape
    keys = memory.shape[0]
    devices = mesh_size()
    groups, single = bit_groups(8), bit_groups(1)
    down = groups[::-1]
    shard = norm_params.shape[0]
    size = self_query.shape[0]
    own_rows = size // width
    blocks = ffn_in.shape[0] // size
    whole_tiles = own_rows % 16 == 0
    core = place_in(groups[0]).reshape(1).astype(jnp.int32)

    firsts = (self_query, self_key, self_value)
    seconds = (self_out, cross_query, cross_key, cross_value, norm_parts(norm_params, size))
    if whole_tiles:
        lane_blocks = width // LANES
        three = [m for i in range(3) for m in square_moves(i, i, width)]
        five = three + [m for i in range(3, 5) for m in square_moves(i, i, width)]
        wide = [(0, c * lane_blocks + b, blocks * lane_blocks, c, b) for c in range(blocks) for b in range(lane_blocks)]
        tall = [(1, j * own_rows * lane_blocks + b, lane_blocks, blocks + 1 + j, b) for j in range(blocks) for b in range(lane_blocks)]
        first = pack(firsts, three, 3, own_rows, width, "pack_self")
        second = pack(tie(seconds, first), five, 5, own_rows, width, "pack_cross")
        last = square_moves(2, blocks, width)
        third = pack(tie((ffn_in, ffn_out, cross_out), first), wide + tall + last, 2 * blocks + 1, own_rows, width, "pack_ffn")
    else:
        first = jnp.concatenate(firsts).reshape(3, own_rows, width)
        second = jnp.concatenate(seconds).reshape(5, own_rows, width)
        fi = ffn_in.reshape(own_rows, blocks, width).transpose(1, 0, 2)
        third = jnp.concatenate([fi, cross_out.reshape(1, own_rows, width), ffn_out.reshape(blocks, own_rows, width)])
    third = third.reshape(-1, width)
    plane = groups[1]
    high_bits = [(b, 1) for b in reversed(range(plane[0] + plane[1], devices.bit_length() - 1))]
    for g in down[:-2]:
        first = gather_step(first, g)
    second = gather_step(second, high_bits[0])
    qid, mid, own_items, items = plan(*tie((seg_lengths, mem_lengths), first), total, keys)
    first = gather_step(first, plane, [second, own_items])
    for g in high_bits[1:]:
        second = gather_step(second, g)
    third = gather_step(third, high_bits[0])
    first = gathered(gather_step(first, down[-1], [second, third]))
    for g in high_bits[1:]:
        third = gather_step(third, g)
    low, high = (plane[0], 1), (plane[0] + 1, 1)
    cut = (blocks + 1) * own_rows
    part_a, part_b = tie((third[..., :cut, :], third[..., cut:, :]), first)
    early = [second, part_a, part_b]
    bits = jnp.stack([(position() >> b) & 1 for b in (low[0], high[0], 0)]).astype(jnp.int32)
    pairs = devices // 2 if whole_tiles else 1
    part_of = core if whole_tiles else jnp.zeros_like(core)

    q1, k1, v1, o1, l1 = self_forward(own_items, inputs, first, qid, early)
    def at(group):
        return place_in(group).reshape(1).astype(jnp.int32)

    second = gather_step(second, plane, [l1])
    came_a, came_b = tie((swap(part_a, 1 << low[0]), swap(part_b, 1 << high[0])), l1)
    second = tie(second, came_a, came_b)
    part_a, part_b = place(at(low), [part_a, came_a]), place(at(high), [part_b, came_b])
    second = gathered(gather_step(second, down[-1]))
    norm_all = second[4].reshape(devices, -1)[:, : 3 * LANES].reshape(devices, 3, LANES)[:, :, :shard].astype(f32)
    norms = jnp.sum(norm_all, axis=1).reshape(6, width)
    k2, v2, r1, h1b, q2, h1, o2, l2 = cross_forward(items, memory, inputs, o1, second, norms, qid, mid, [bits])
    part_a, part_b = [part_a, swap(part_a, 1 << high[0])], [part_b, swap(part_b, 1 << low[0])]
    came = [swap(part_a[0], 1), swap(part_b[0], 1)]
    part_a[1], part_b[1], came[0], came[1] = tie((part_a[1], part_b[1], came[0], came[1]), l2)
    part_a += [came[0], swap(part_a[1], 1)]
    part_b += [came[1], swap(part_b[1], 1)]
    if whole_tiles:
        pieces = [p.reshape((-1, 2) + p.shape[-2:]) for p in part_a + part_b]
    else:
        pieces = []
        for parts, group, lower in ((part_a, high, 1), (part_b, low, 0)):
            halves = [gather_step(parts[j], group, lower=lower, came=[parts[j + 1]]) for j in (0, 2)]
            both = gather_step(halves[0], down[-1], came=[halves[1]]).reshape(devices, -1, own_rows, width)
            pieces.append(both)
        pieces[0] = jnp.concatenate([pieces[0][:, i].reshape(width, width) for i in range(blocks + 1)])[None]
        pieces[1] = pieces[1].reshape(1, -1, width)
    out, dr3, dr2, do2, delta2, keep, send, gn23 = ffn(part_of, bits, pairs, h1, inputs, cotangent, o2, pieces, norms)

    one = [keep, send] if whole_tiles else resplit(keep, send, devices, core[0], blocks + 1)
    dq2a, dk2a, dv2a, gckva = cross_backward(items, q2, k2, v2, do2, l2, delta2, qid, mid, memory, 0, HEAD_START, 4, [])
    low, high = 1 << groups[1][0], 2 << groups[1][0]
    both = jnp.stack([(position() >> (groups[1][0] + j)) & 1 for j in range(2)]).astype(jnp.int32)
    one = swap_pieces(one, groups[0], [dq2a])
    one = first_pair(both, one[0], one[1], devices // 8, blocks + 1)
    more = width // LANES - HEAD_START
    dq2b, dk2b, dv2b, gckvb = cross_backward(
        items, q2, k2, v2, do2, l2, delta2, qid, mid, memory, HEAD_START, more, 2, [one[1], one[3]]
    )
    came = tie([swap(one[1], low), swap(one[3], high)], dq2b)
    one = second_pair(both, [one[0], came[0], one[2], came[1]])
    gm = memory_grad(dk2a, dk2b, dv2a, dv2b, second, 2, [one[1], one[3]])
    dsum, do1, delta1, keep, send, gn = between(
        part_of, pairs, gckva, gckvb, gn23, r1, dr2, dr3, dq2a, dq2b, h1b, o1, second, norms, placed(gm)
    )
    came = tie([swap(one[1], high), swap(one[3], low)], do1)
    one = join_split(
        place_in(single[2]).reshape(1).astype(jnp.int32), [one[0], came[0], one[2], came[1]],
        1 << sum(g[1] for g in single[3:]), 1 << single[2][1],
    )
    two = [keep, send]
    if not whole_tiles:
        two = resplit(keep, send, devices, core[0], 5)
        own_norms = jnp.pad(gn[:6].astype(bf16).reshape(devices, -1), ((0, 0), (0, size - shard)))
        own_norms = own_norms.reshape(devices // 2, 2, own_rows, width)
        two = [two[m].at[:, 4].set(lax.dynamic_index_in_dim(own_norms, core[0] ^ m, 1, keepdims=False)) for m in range(2)]
    two = next_pieces(swap_pieces(tie(two, one[1]), groups[0]), groups, 1)
    gx, keep, send = self_backward(part_of, pairs, own_items, q1, k1, v1, do1, l1, delta1, qid, inputs, first, dsum, one[1:] + two[1:])
    two = next_pieces(swap_pieces(two, groups[1], [gx]), single, 2)
    one = next_pieces(swap_pieces(one, single[2], [gx]), single, 3)
    keep, send = tie((keep, send), two[1], one[1])
    three = [keep, send] if whole_tiles else resplit(keep, send, devices, core[0], 3)
    three = next_pieces(swap_pieces(three, groups[0]), groups, 1)
    early_three = three[1]
    for i in range(2, len(groups)):
        three = next_pieces(swap_pieces(three, groups[i - 1]), groups, i)
    for i in range(3, len(single)):
        two = next_pieces(swap_pieces(two, single[i - 1]), single, i)
        if i > 3:
            one = next_pieces(swap_pieces(one, single[i - 1]), single, i)

    def flat(g):
        return g.reshape(-1)

    chains = [swap_pieces(one, single[-1], [early_three]), swap_pieces(two, single[-1], [three[1]]), swap_pieces(three, groups[-1])]
    chains = [[p.reshape(-1, own_rows, width) for p in chain] for chain in chains]
    if whole_tiles:
        lane_rows = size // LANES
        square, long = (lane_rows, LANES), (blocks * lane_rows, LANES)

        moves = [(c, b, 0, c * lane_blocks + b, blocks * lane_blocks) for c in range(blocks) for b in range(lane_blocks)]
        moves += [(blocks, b, 1, b, lane_blocks) for b in range(lane_blocks)]
        moves += [
            (blocks + 1 + j, b, 2, j * own_rows * lane_blocks + b, lane_blocks) for j in range(blocks) for b in range(lane_blocks)
        ]
        gfi, gco, gfo = finish(chains[0], moves, [long, square, long], "finish_ffn")
        moves = [(i, b, i, b, lane_blocks) for i in range(4) for b in range(lane_blocks)] + [(4, b, 4, 0, 0) for b in range(lane_blocks)]
        gck, gcv, gcq, gso, gn = finish(chains[1], moves, [square] * 4 + [(own_rows, width)], "finish_cross")
        gn = lax.dynamic_slice_in_dim(flat(gn[:6]), position() * shard, shard)
        moves = [(i, b, i, b, lane_blocks) for i in range(3) for b in range(lane_blocks)]
        gsq, gsk, gsv = finish(chains[2], moves, [square] * 3, "finish_self")
    else:
        one, two, three = (sum(p.astype(f32) for p in chain) for chain in chains)
        gfi, gco, gfo = one[:blocks].transpose(1, 0, 2), one[blocks], one[blocks + 1 :]
        gck, gcv, gcq, gso, gn = two[0], two[1], two[2], two[3], flat(two[4])[:shard]
        gsq, gsk, gsv = three[0], three[1], three[2]
    return (out, gx, gm) + tuple(flat(g) for g in (gsq, gsk, gsv, gso, gcq, gck, gcv, gco, gfi, gfo, gn))


def solution(mesh):
    rows, flat = P(("dp", "fsdp"), None), P(("dp", "fsdp"))
    return jax.shard_map(
        body,
        mesh=mesh,
        in_specs=(rows,) * 4 + (flat,) * 11 + (rows,),
        out_specs=(rows,) * 3 + (flat,) * 11,
        check_vma=False,
    )
```
